32 devices in a mesh: batch: 8 (over z, y), shard: 4 (over x, core).
Axes of the slice: x: 2, y: 2, z: 4, core: 2. Of those that a mesh axis runs over, the one named last changes fastest.
Arguments:
- tokens: bfloat16 [2, 32, 1024, 512], P(None, ('batch', 'shard')), may hold values from -6 to 6
- cotangent: bfloat16 [2, 32, 1024, 512], P(None, ('batch', 'shard')), may hold values from -6 to 6
- lengths: int32 [2, 32, 4], P(None, ('batch', 'shard')), may hold values from 1 to 512, 1024 in all within a row
- exit_layers: int32 [2, 32, 4], P(None, ('batch', 'shard')), may hold values from 1 to 8
- teacher: float32 [2, 32, 4, 14], P(None, ('batch', 'shard')), may hold values from -8 to 8
- blocks: bfloat16 [12, 512, 512], P('shard'), may hold values from -0.70710678 to 0.70710678
- left_stats: float32 [12, 512, 512], P('shard'), may hold values from -285212.7 to 6710886.4, as said below
- right_stats: float32 [12, 512, 512], P('shard'), may hold values from -285212.7 to 6710886.4, as said below
- left_root: float32 [12, 512, 512], P('shard'), may hold values from -0.17 to 2, as said below
- right_root: float32 [12, 512, 512], P('shard'), may hold values from -0.17 to 2, as said below
- vectors: float32 [12, 512], P('shard'), may hold values from -1.2 to 1.4
- vec_moment: float32 [12, 512], P('shard'), may hold values from 655.36 to 39321.6
- student: float32 [643, 128], replicated, may hold values from -8 to 8
- stu_moment: float32 [643, 128], replicated, may hold values from 0.512 to 12.8
- classifier: float32 [129, 14], replicated, may hold values from -0.70710677 to 0.70710677
- cls_moment: float32 [129, 14], replicated, may hold values from 0.512 to 12.8
Outputs:
- layer_out: bfloat16 [2, 32, 1024, 512], P(None, ('batch', 'shard'))
- grad_tokens: bfloat16 [2, 32, 1024, 512], P(None, ('batch', 'shard'))
- block_grads: float32 [12, 512, 512], P('shard')
- new_blocks: float32 [12, 512, 512], P('shard')
- new_left: float32 [12, 512, 512], P('shard')
- new_right: float32 [12, 512, 512], P('shard')
- vector_grads: float32 [12, 512], P('shard')
- new_vec_moment: float32 [12, 512], P('shard')
- new_vectors: float32 [12, 512], P('shard')
- student_grads: float32 [643, 128], replicated
- new_stu_moment: float32 [643, 128], replicated
- new_student: float32 [643, 128], replicated
- class_grads: float32 [129, 14], replicated
- new_cls_moment: float32 [129, 14], replicated
- new_classifier: float32 [129, 14], replicated
The draws below stay inside these ranges and needn't reach their ends.
Inputs may be any that keep to these rules, and one draw needn't show every extreme that they name: In each row the 4 lengths sum to 1024 and the longest is exactly 512. `left_stats`: symmetric. `right_stats`: symmetric. `left_root`: symmetric. `right_root`: symmetric.
All inputs are finite; a program needn't handle non-finite values.
Results may differ from the reference program's by a relative error of at most 0.019.
Values may be sent and summed in bfloat16 or wider, within the bound.
A program may use at most 256 MiB of HBM per device.

```python
import math
import jax
import jax.numpy as jnp
import numpy as np
from jax import lax

D = 512
H = 8
DH = 64
FF = 2048
NLAYER = 8
SW = 128
PH = 2
CLS = 14
NMAT = 12
ROW = 1024
MAXLEN = 512
SAMP = 4
LAYER = 4
MB = 2
RPD = 1
RW = 32
TOKENS = 65536
STU_R = 643
N_BATCH = 8
N_SHARD = 4


def statistic_matrix(key, unit_scale, low_end, high_end):
    key_diagonal, key_noise = jax.random.split(key)
    diagonal = jax.random.uniform(key_diagonal, (NMAT, D), jnp.float32, low_end, high_end) * unit_scale
    noise_part = jax.random.truncated_normal(key_noise, -4.0, 4.0, (NMAT, D, D), jnp.float32)
    symmetric = (noise_part + jnp.swapaxes(noise_part, 1, 2)) * (0.03 * unit_scale / math.sqrt(2.0))
    identity = jnp.eye(D, dtype=jnp.float32)
    return symmetric * (1.0 - identity) + diagonal[:, :, None] * identity


def draw_blocks(key, part):
    key = jax.random.fold_in(key, 1)
    noise_part = jax.random.truncated_normal(key, -4.0, 4.0, (NMAT, D, D), jnp.float32)
    block_index = jnp.arange(NMAT)
    scale_table = jnp.where(block_index == 3, 4.0 / math.sqrt(D), jnp.where(block_index >= 8, 1.0 / math.sqrt(FF), 1.0 / math.sqrt(D)))
    return (noise_part * scale_table[:, None, None]).astype(jnp.bfloat16)


def draw_left_stats(key, part):
    key = jax.random.fold_in(key, 2)
    return statistic_matrix(key, 0.05 * D * TOKENS, 1.0, 4.0)


def draw_right_stats(key, part):
    key = jax.random.fold_in(key, 3)
    return statistic_matrix(key, 0.05 * D * TOKENS, 1.0, 4.0)


def draw_left_root(key, part):
    key = jax.random.fold_in(key, 4)
    return statistic_matrix(key, 1.0, 0.5, 2.0)


def draw_right_root(key, part):
    key = jax.random.fold_in(key, 5)
    return statistic_matrix(key, 1.0, 0.5, 2.0)


def draw_vectors(key, part):
    key = jax.random.fold_in(key, 6)
    key_gain, key_bias = jax.random.split(key)
    gains = jax.random.uniform(key_gain, (NMAT, D), jnp.float32, 0.6, 1.4)
    biases = jax.random.truncated_normal(key_bias, -4.0, 4.0, (NMAT, D), jnp.float32) * 0.3
    row_index = jnp.arange(NMAT)[:, None]
    return jnp.where((row_index == 3) | (row_index == 10), gains, biases)


def draw_student(key, part):
    key = jax.random.fold_in(key, 7)
    noise_part = jax.random.truncated_normal(key, -4.0, 4.0, (STU_R, SW), jnp.float32)
    row_index = jnp.arange(STU_R)[:, None]
    scale_table = jnp.where(row_index < D, 1.0 / math.sqrt(D), jnp.where(row_index < D + SW, 1.0 / math.sqrt(SW), jnp.where(row_index == D + SW + 2, 2.0, 0.3)))
    return noise_part * scale_table


def with_ends(values, stream_key, low, high):
    shape = values.shape
    index_at = [jax.random.randint(jax.random.fold_in(stream_key, axis), (), 0, shape[axis]) for axis in range(len(shape))]
    values = values.at[tuple(index_at)].set(low)
    longest = shape.index(max(shape))
    index_at[longest] = (index_at[longest] + 1) % shape[longest]
    return values.at[tuple(index_at)].set(high)


def levels(own_key, shape, cuts, low, high):
    gain, own = 1.0, jax.random.fold_in(own_key, 6)
    for dim, shards_of in cuts:
        draws = jnp.exp(jax.random.uniform(jax.random.fold_in(own, dim), (shards_of,), jnp.float32, low / len(cuts), high / len(cuts)))
        gain = gain * jnp.repeat(draws, shape[dim] // shards_of).reshape([-1 if axis == dim else 1 for axis in range(len(shape))])
    return gain


def profile(amount, total, most, skew):
    loads = [(1 << 20) // math.isqrt(rank ** skew) + 1 for rank in range(2, amount + 1)]
    spare, given = total - most - (amount - 1), [1] * (amount - 1)
    while spare > 0:
        free = [i for i in range(amount - 1) if given[i] < most]
        whole, budget = sum([loads[i] for i in free]), spare
        for i in free:
            more = min(most - given[i], max(1, budget * loads[i] // whole), spare)
            given[i] = given[i] + more
            spare = spare - more
    return np.array([most] + given)


def ragged_sizes(key, amount, total, most, skew):
    if amount == 2:
        one = jax.random.randint(key, (), max(1, total - most), min(most, total - 1) + 1)
        return jnp.stack([one, total - one])
    tallies = jnp.asarray(profile(amount, total, most, skew), jnp.int32)
    pairs = (amount - 1) // 2
    source_of, taker = tallies[1:1 + 2 * pairs:2], tallies[2:2 + 2 * pairs:2]
    margin = jnp.minimum(source_of - 1, most - taker)
    shifted = jax.random.randint(jax.random.fold_in(key, 1), (pairs,), 0, 1 << 20) % (margin + 1)
    tallies = tallies.at[1:1 + 2 * pairs:2].set(source_of - shifted).at[2:2 + 2 * pairs:2].set(taker + shifted)
    return tallies[jax.random.permutation(jax.random.fold_in(key, 2), amount)]


def scatter_about(own_key, shape, scale, bound, shards=(), kind=jnp.bfloat16):
    gain = levels(own_key, shape, shards, -0.22, 0.18) if shards else 1.0
    drawn = jax.random.normal(own_key, shape, jnp.float32) * scale * gain
    return jnp.minimum(jnp.maximum(drawn, -bound), bound).astype(kind)


def setup_inputs(seed: int = 0) -> dict:
    streams_of = jax.random.split(jax.random.key(seed), 17)
    tokens = scatter_about(streams_of[0], (MB, RW, ROW, D), 1.0, 6.0, ((1, 32),))
    cotangent = scatter_about(streams_of[1], (MB, RW, ROW, D), 1.0, 6.0, ((1, 32),))
    lengths = jax.vmap(lambda own: ragged_sizes(own, SAMP, ROW, MAXLEN, 2))(jax.random.split(streams_of[2], MB * RW)).reshape((MB, RW, SAMP)).astype(jnp.int32)
    exit_layers = with_ends(jax.random.randint(streams_of[3], (MB, RW, SAMP), 1, NLAYER + 1), jax.random.fold_in(streams_of[3], 1), 1, NLAYER).astype(jnp.int32)
    teacher = scatter_about(streams_of[4], (MB, RW, SAMP, CLS), 2.0, 8.0, ((1, 32),), jnp.float32)
    blocks = draw_blocks(jax.random.fold_in(streams_of[16], 71), 0)
    left_stats = draw_left_stats(jax.random.fold_in(streams_of[16], 71), 0)
    right_stats = draw_right_stats(jax.random.fold_in(streams_of[16], 71), 0)
    left_root = draw_left_root(jax.random.fold_in(streams_of[16], 71), 0)
    right_root = draw_right_root(jax.random.fold_in(streams_of[16], 71), 0)
    vectors = draw_vectors(jax.random.fold_in(streams_of[16], 71), 0)
    vec_moment = jnp.clip(jnp.exp(math.log(39321.6) - 4.0943446 * jax.random.uniform(streams_of[11], (NMAT, D), jnp.float32) ** levels(streams_of[11], (NMAT, D), ((0, 4),), -0.2, 0.2)), 655.36, 39321.6)
    student = draw_student(jax.random.fold_in(streams_of[16], 71), 0)
    stu_moment = jnp.clip(jnp.exp(jax.random.uniform(streams_of[13], (STU_R, SW), jnp.float32, math.log(0.512), math.log(12.8))), 0.512, 12.8)
    classifier = scatter_about(streams_of[14], (SW + 1, CLS), (2.0 / SW ** 0.5), 0.70710677, (), jnp.float32)
    cls_moment = jnp.clip(jnp.exp(jax.random.uniform(streams_of[15], (SW + 1, CLS), jnp.float32, math.log(0.512), math.log(12.8))), 0.512, 12.8)
    return {"tokens": tokens, "cotangent": cotangent, "lengths": lengths, "exit_layers": exit_layers, "teacher": teacher, "blocks": blocks, "left_stats": left_stats, "right_stats": right_stats, "left_root": left_root, "right_root": right_root, "vectors": vectors, "vec_moment": vec_moment, "student": student, "stu_moment": stu_moment, "classifier": classifier, "cls_moment": cls_moment}


@jax.custom_vjp
def low(v):
    return lax.optimization_barrier(v.astype(jnp.bfloat16)).astype(jnp.float32)

@jax.custom_vjp
def low_back(v):
    return v

def low_keep(v):
    return (low(v), None)

def low_pass(kept, grad):
    return (grad,)

def back_keep(v):
    return (v, None)

def back_low(kept, grad):
    return (low(grad),)
low.defvjp(low_keep, low_pass)
low_back.defvjp(back_keep, back_low)
decay_rate = 0.5
block_rate = 0.04
vector_rate = 0.05
head_rate = 0.05

def product(left_side, right_side):
    return jnp.dot(left_side, right_side, precision=lax.Precision.HIGHEST, preferred_element_type=jnp.float32)

def layer_norm(values, gain_vec, shift_vec):
    center = values - lax.optimization_barrier(jnp.mean(values, axis=-1, keepdims=True))
    spread = lax.optimization_barrier(jnp.mean(center * center, axis=-1, keepdims=True))
    return center * lax.rsqrt(spread + 1e-06) * gain_vec + shift_vec

def segment_ids(lengths, row_len):
    bounds = jnp.cumsum(lengths, dtype=jnp.int32)
    places = jnp.arange(row_len, dtype=jnp.int32)
    return lax.optimization_barrier(jnp.sum((places[:, None] >= bounds[None, :]).astype(jnp.int32), axis=1, dtype=jnp.int32))

def alive_tokens(lengths, exit_layers, row_len):
    segments = segment_ids(lengths, row_len)
    alive_flags = (exit_layers >= LAYER).astype(jnp.int32)
    member = segments[:, None] == jnp.arange(SAMP, dtype=jnp.int32)[None, :]
    return lax.optimization_barrier(jnp.sum(jnp.where(member, alive_flags[None, :], 0), axis=1, dtype=jnp.int32))

def head_loss(hidden, segments, alive_flags, target, student, classifier):
    row_count = hidden.shape[0]
    head_width = SW // PH
    pool_weight = student[D:D + SW]
    pool_bias = student[D + SW + 1]
    query_vec = student[D + SW + 2].reshape(PH, head_width)
    split_heads = hidden.reshape(row_count, PH, head_width)
    scores = lax.optimization_barrier(jnp.sum(split_heads * query_vec, axis=-1)) * head_width ** (-0.5)
    member = segments[None, :] == jnp.arange(SAMP, dtype=jnp.int32)[:, None]
    masked = jnp.where(member[:, :, None], scores[None, :, :], -1000000000.0)
    peak_score = lax.optimization_barrier(jnp.max(masked, axis=1, keepdims=True))
    exponent = jnp.exp(masked - peak_score)
    weights = exponent / lax.optimization_barrier(jnp.sum(exponent, axis=1, keepdims=True))
    pooled = jnp.einsum('srh,rhc->shc', weights, split_heads, precision=lax.Precision.HIGHEST).reshape(SAMP, SW)
    mixed_head = jnp.tanh(product(pooled, pool_weight) + pool_bias)
    logits = product(mixed_head, classifier[:SW]) + classifier[SW]
    log_probs = jax.nn.log_softmax(logits, axis=-1)
    return -jnp.sum(alive_flags[:, None] * target * log_probs)

def attention(queries, keys, values, segments):
    row_count = queries.shape[0]
    span_rows = min(512, row_count)
    block_count = row_count // span_rows
    key_heads = keys.reshape(row_count, H, DH)
    value_heads = values.reshape(row_count, H, DH)

    def one_block(pieces):
        query_part, query_ids = pieces
        scores = jnp.einsum('qhd,khd->hqk', query_part.reshape(span_rows, H, DH), key_heads, precision=lax.Precision.HIGHEST) * DH ** (-0.5)
        scores = jnp.where(query_ids[None, :, None] == segments[None, None, :], scores, -1000000000.0)
        scores = low_back(scores)
        peak_score = lax.optimization_barrier(jnp.max(scores, axis=-1, keepdims=True))
        exponent = jnp.exp(scores - peak_score)
        probabilities = low(exponent / lax.optimization_barrier(jnp.sum(exponent, axis=-1, keepdims=True)))
        mixed_heads = jnp.einsum('hqk,khd->qhd', probabilities, value_heads, precision=lax.Precision.HIGHEST)
        return mixed_heads.reshape(span_rows, D)
    attended = lax.map(jax.checkpoint(one_block), (queries.reshape(block_count, span_rows, D), segments.reshape(block_count, span_rows)))
    return attended.reshape(row_count, D)

def row_forward(row_tokens, lengths, exit_layers, teacher, blocks, vectors, student_weight, student, classifier):
    segments = segment_ids(lengths, row_tokens.shape[0])
    alive_flags = (exit_layers >= LAYER).astype(jnp.float32)
    target = jax.nn.softmax(teacher, axis=-1)
    up_weight = jnp.concatenate([blocks[4], blocks[5], blocks[6], blocks[7]], axis=1)
    down_weight = jnp.concatenate([blocks[8], blocks[9], blocks[10], blocks[11]], axis=0)
    queries = low(low_back(product(row_tokens, blocks[0]) + vectors[0]))
    keys = low(low_back(product(row_tokens, blocks[1])))
    values = low(low_back(product(row_tokens, blocks[2]) + vectors[1]))
    attended = low(low_back(attention(queries, keys, values, segments)))
    branch = low_back(product(attended, blocks[3]) + vectors[2])
    first_norm = layer_norm(row_tokens + branch, vectors[3], vectors[4])
    hidden = low_back(product(low(first_norm), up_weight) + vectors[5:9].reshape(-1))
    activated = low(jax.nn.gelu(hidden, approximate=False))
    feed_out = low_back(product(activated, down_weight) + vectors[9])
    normed = low(layer_norm(first_norm + feed_out, vectors[10], vectors[11]))
    head_in = low_back(product(normed, student_weight) + student[D + SW])
    return (normed, head_loss(head_in, segments, alive_flags, target, student, classifier))

def repack(normed, live_flags):
    micro_count, row_total, row_len, model_width = normed.shape
    span_len = RPD * row_len
    whole_len = N_BATCH * span_len
    grouped = normed.reshape(micro_count, N_BATCH, N_SHARD, span_len, model_width).transpose(0, 2, 1, 3, 4).reshape(micro_count, N_SHARD, whole_len, model_width)
    flag_group = live_flags.reshape(micro_count, N_BATCH, N_SHARD, span_len).transpose(0, 2, 1, 3).reshape(micro_count, N_SHARD, whole_len)
    rank_index = jnp.cumsum(flag_group, axis=-1, dtype=jnp.int32) - 1
    target = jnp.where(flag_group > 0, rank_index % N_BATCH * span_len + rank_index // N_BATCH, whole_len)

    def place_rows(row_values, where_to):
        return jnp.zeros((whole_len + 1, model_width), row_values.dtype).at[where_to].set(row_values)[:whole_len]
    placed = jax.vmap(jax.vmap(place_rows))(grouped, target)
    placed = placed.reshape(micro_count, N_SHARD, N_BATCH, span_len, model_width).transpose(0, 2, 1, 3, 4)
    return placed.reshape(micro_count, row_total, row_len, model_width)

def forward(tokens_f, blocks_f, vectors_f, student, classifier, lengths, exit_layers, teacher):
    micro_count, row_total, row_len, model_width = tokens_f.shape
    student_weight = low(student[:D])

    def one_row(pieces):
        row_tokens, row_lengths, row_exits, row_teacher = pieces
        return row_forward(row_tokens, row_lengths, row_exits, row_teacher, blocks_f, vectors_f, student_weight, student, classifier)
    normed, losses = lax.map(jax.checkpoint(one_row), (tokens_f.reshape(micro_count * row_total, row_len, model_width), lengths.reshape(-1, SAMP), exit_layers.reshape(-1, SAMP), teacher.reshape(-1, SAMP, CLS)))
    live_flags = jax.vmap(lambda row_lengths, row_exits: alive_tokens(row_lengths, row_exits, row_len))(lengths.reshape(-1, SAMP), exit_layers.reshape(-1, SAMP))
    dense = repack(normed.reshape(micro_count, row_total, row_len, model_width), live_flags.reshape(micro_count, row_total, row_len))
    return (dense, jnp.sum(losses))

def diagonal_rule(old_values, moment, grads, rate):
    new_moment = decay_rate * moment + (1.0 - decay_rate) * grads * grads
    return (new_moment, old_values - rate * grads / (jnp.sqrt(new_moment) + 1e-08))

def reference(tokens, cotangent, lengths, exit_layers, teacher, blocks, left_stats, right_stats, left_root, right_root, vectors, vec_moment, student, stu_moment, classifier, cls_moment):
    tokens_f = tokens.astype(jnp.float32)
    blocks_f = blocks.astype(jnp.float32)
    vectors_f = lax.optimization_barrier(vectors.astype(jnp.bfloat16)).astype(jnp.float32)

    def run(tok_in, blk_in, vec_in, stu_in, cls_in):
        return forward(tok_in, blk_in, vec_in, stu_in, cls_in, lengths, exit_layers, teacher)
    (dense, total_loss), pull = jax.vjp(run, tokens_f, blocks_f, vectors_f, student, classifier)
    grad_in, grad_blocks, grad_vectors, grad_student, grad_class = pull((cotangent.astype(jnp.float32), jnp.ones((), jnp.float32)))
    gram_left = jnp.einsum('bij,bkj->bik', grad_blocks, grad_blocks, precision=lax.Precision.HIGHEST)
    gram_right = jnp.einsum('bji,bjk->bik', grad_blocks, grad_blocks, precision=lax.Precision.HIGHEST)
    new_left = decay_rate * left_stats + (1.0 - decay_rate) * gram_left
    new_right = decay_rate * right_stats + (1.0 - decay_rate) * gram_right
    steered = jnp.einsum('bij,bjk->bik', left_root, grad_blocks, precision=lax.Precision.HIGHEST)
    steered = jnp.einsum('bij,bjk->bik', steered, right_root, precision=lax.Precision.HIGHEST)
    size_norm = jnp.sqrt(lax.optimization_barrier(jnp.mean(steered * steered, axis=(1, 2), keepdims=True)) + 1e-06)
    new_blocks = blocks_f - block_rate * steered / size_norm
    new_vec_moment, new_vectors = diagonal_rule(vectors, vec_moment, grad_vectors, vector_rate)
    new_stu_moment, new_student = diagonal_rule(student, stu_moment, grad_student, head_rate)
    new_cls_moment, new_classifier = diagonal_rule(classifier, cls_moment, grad_class, head_rate)
    return (dense.astype(jnp.bfloat16), grad_in.astype(jnp.bfloat16), grad_blocks, new_blocks, new_left, new_right, grad_vectors, new_vec_moment, new_vectors, grad_student, new_stu_moment, new_student, grad_class, new_cls_moment, new_classifier)
```

```python
import functools

import jax
import jax.numpy as jnp
from jax import lax
from jax.experimental import pallas as pl
from jax.experimental.pallas import tpu as pltpu
from jax.sharding import PartitionSpec as P

D = 512
H = 8
DH = 64
FF = 2048
SW = 128
NMAT = 12
SAMP = 4
LAYER = 4
CLS = 14

decay_rate = 0.5
block_rate = 0.04
vector_rate = 0.05
head_rate = 0.05

QT = 256
KG = 128
PAIRS = H // 2
LANES = 128
BIG = float(2**30)
EPS = 1e-6
VMEM = 60 * 1024 * 1024

F32 = jnp.float32
BF16 = jnp.bfloat16


def nn(a, b):
    return jnp.dot(a, b, preferred_element_type=F32)


def nt(a, b):
    return lax.dot_general(a, b, (((1,), (1,)), ((), ())), preferred_element_type=F32)


def tn(a, b):
    return lax.dot_general(a, b, (((0,), (0,)), ((), ())), preferred_element_type=F32)


def exact(a, b, dims=(((1,), (0,)), ((), ()))):
    return lax.dot_general(
        a, b, dims, preferred_element_type=F32, precision=lax.Precision.HIGHEST
    )


def row_sum(v):
    return jnp.sum(v, axis=0, keepdims=True)


def split_low(v):
    high = v.astype(BF16).astype(F32)
    rest = v - high
    mid = rest.astype(BF16).astype(F32)
    return high, mid, rest - mid


def ends_of(info, row):
    return [info[row, j] for j in range(SAMP)]


def live_of(info, row):
    return [info[row, SAMP + j] for j in range(SAMP)]


def sample_column(ends, first, count):
    place = first + lax.broadcasted_iota(jnp.int32, (count, 1), 0)
    total = jnp.zeros((count, 1), jnp.int32)
    for j in range(SAMP - 1):
        total = total + (place >= ends[j]).astype(jnp.int32)
    return total


def reach(ends, live, first, count, row_len):
    low, high = jnp.int32(row_len), jnp.int32(0)
    start = jnp.int32(0)
    for j in range(SAMP):
        end = ends[j]
        meets = (start < first + count) & (end > first) & (end > start) & (live[j] > 0)
        low = jnp.where(meets, jnp.minimum(low, start), low)
        high = jnp.where(meets, jnp.maximum(high, end), high)
        start = end
    begin = low // KG
    number = jnp.maximum((high + KG - 1) // KG - begin, 0)
    return begin, number


def lane_index(rows):
    return lax.broadcasted_iota(jnp.int32, (rows, LANES), 1)


def key_spare(sample, rows):
    lane = lane_index(rows) % DH
    return jnp.where(
        lane < SAMP, (lane == sample).astype(F32), (lane < SAMP + 3).astype(F32)
    )


def query_spare(sample, rows):
    lane = lane_index(rows) % DH
    return jnp.where((lane < SAMP) & (lane != sample), -BIG, 0.0)


def halves(pair, spare, first):
    return jnp.where(first, pair, spare), jnp.where(first, spare, pair)


def attend_kernel(
    info, x_ref, w_ref, vec_ref, a1_ref, q_ref, k_ref, v_ref, o_ref, kx, vx
):
    row = pl.program_id(0)
    row_len = x_ref.shape[1]
    ends, live = ends_of(info, row), live_of(info, row)
    first = lane_index(QT) < DH

    @pl.loop(0, row_len // QT)
    def _(t):
        rows = pl.ds(pl.multiple_of(t * QT, QT), QT)
        x = x_ref[0, rows, :]
        sample = sample_column(ends, t * QT, QT)
        k_extra, q_extra = key_spare(sample, QT), query_spare(sample, QT)
        q = (nn(x, w_ref[0]) + vec_ref[0:1, :]).astype(BF16).astype(F32) * DH**-0.5
        k = nn(x, w_ref[1]).astype(BF16)
        v = (nn(x, w_ref[2]) + vec_ref[1:2, :]).astype(BF16)
        k_ref[0, rows, :] = k
        v_ref[0, rows, :] = v
        for p in range(PAIRS):
            pair = slice(p * LANES, (p + 1) * LANES)
            for ref, values, spare in (
                (q_ref.at[0], q, q_extra),
                (kx, k.astype(F32), k_extra),
                (vx, v.astype(F32), jnp.ones((QT, LANES), F32)),
            ):
                left, right = halves(values[:, pair], spare, first)
                ref[rows, 2 * p * LANES : (2 * p + 1) * LANES] = left.astype(BF16)
                ref[rows, (2 * p + 1) * LANES : (2 * p + 2) * LANES] = right.astype(BF16)

    @pl.loop(0, row_len // QT)
    def _(t):
        rows = pl.ds(pl.multiple_of(t * QT, QT), QT)
        begin, number = reach(ends, live, t * QT, QT, row_len)

        @pl.when(number == 0)
        def _():
            o_ref[0, rows, :] = jnp.zeros((QT, D), BF16)

        for n in range(1, row_len // KG + 1):

            @pl.when(number == n)
            def _(n=n):
                span = pl.ds(pl.multiple_of(begin * KG, KG), n * KG)
                lane = lane_index(QT)

                @pl.loop(0, PAIRS)
                def _(p):
                    parts = []
                    for head in range(2):
                        cols = pl.ds(
                            pl.multiple_of((2 * p + head) * LANES, LANES), LANES
                        )
                        q = q_ref[0, rows, cols]
                        s = nt(q, kx[span, cols])
                        peak = jnp.max(s, axis=1, keepdims=True)
                        e = jnp.exp(s - peak).astype(BF16)
                        got = nn(e, vx[span, cols])
                        parts.append(got)
                        other = (lane >= DH) if head == 0 else (lane < DH)
                        total = peak + jnp.log(jnp.where(other, got, 1.0))
                        high, mid, rest = split_low(
                            jnp.where(peak > -0.5 * BIG, total, 0.0)
                        )
                        at = lane % DH
                        fill = jnp.where(
                            at == SAMP, -high, jnp.where(at == SAMP + 1, -mid, -rest)
                        )
                        spot = other & (at >= SAMP) & (at < SAMP + 3)
                        q_ref[0, rows, cols] = jnp.where(
                            spot, fill, q.astype(F32)
                        ).astype(BF16)
                    top = jnp.where(first, parts[0], parts[1])
                    total = pltpu.roll(jnp.where(first, parts[1], parts[0]), DH, 1)
                    cols = pl.ds(pl.multiple_of(p * LANES, LANES), LANES)
                    o_ref[0, rows, cols] = (top / total).astype(BF16)

    @pl.loop(0, row_len // QT)
    def _(t):
        rows = pl.ds(pl.multiple_of(t * QT, QT), QT)
        a1_ref[0, rows, :] = x_ref[0, rows, :].astype(F32) + (
            nn(o_ref[0, rows, :], w_ref[3]) + vec_ref[2:3, :]
        )


def attend(info, tokens, blocks, vec):
    micro, row_len, _ = tokens.shape
    row_spec = lambda width: pl.BlockSpec((1, row_len, width), lambda r: (r, 0, 0))
    return pl.pallas_call(
        attend_kernel,
        grid=(micro,),
        in_specs=[
            pl.BlockSpec(memory_space=pltpu.SMEM),
            row_spec(D),
            pl.BlockSpec((4, D, D), lambda r: (0, 0, 0)),
            pl.BlockSpec((NMAT, D), lambda r: (0, 0)),
        ],
        out_specs=[row_spec(D), row_spec(2 * D), row_spec(D), row_spec(D), row_spec(D)],
        out_shape=[
            jax.ShapeDtypeStruct((micro, row_len, D), F32),
            jax.ShapeDtypeStruct((micro, row_len, 2 * D), BF16),
            jax.ShapeDtypeStruct((micro, row_len, D), BF16),
            jax.ShapeDtypeStruct((micro, row_len, D), BF16),
            jax.ShapeDtypeStruct((micro, row_len, D), BF16),
        ],
        scratch_shapes=[
            pltpu.VMEM((row_len, 2 * D), BF16),
            pltpu.VMEM((row_len, 2 * D), BF16),
        ],
        compiler_params=pltpu.CompilerParams(vmem_limit_bytes=VMEM),
        cost_estimate=pl.CostEstimate(
            flops=micro * row_len * D * D * 8 + micro * H * row_len * row_len * DH * 4,
            bytes_accessed=micro * row_len * D * 16,
            transcendentals=micro * H * row_len * row_len,
        ),
    )(info, tokens, blocks, vec)


def gelu_both(u):
    t = 1.0 / (1.0 + (0.3275911 * 0.5**0.5) * jnp.abs(u))
    bell = jnp.exp(-0.5 * (u * u))
    tail = (
        t
        * (
            0.127414796
            + t * (-0.142248368 + t * (0.7107068705 + t * (-0.7265760135 + t * 0.5307027145)))
        )
        * bell
    )
    share = jnp.where(u >= 0, 1.0 - tail, tail)
    return u * share, share + u * bell * 0.3989422804014327


def norm_parts(a):
    center = a - jnp.mean(a, axis=-1, keepdims=True)
    rate = lax.rsqrt(jnp.mean(center * center, axis=-1, keepdims=True) + EPS)
    return center * rate, rate


def norm_back(grad, unit, rate):
    return rate * (
        grad
        - jnp.mean(grad, axis=-1, keepdims=True)
        - unit * jnp.mean(grad * unit, axis=-1, keepdims=True)
    )


def feed_kernel(
    info,
    a1_ref,
    w_ref,
    vec_ref,
    stu_ref,
    cls_ref,
    goal_ref,
    send_row,
    send_col,
    back_ref,
    da1_ref,
    out_ref,
    wg_ref,
    vg_ref,
    sg_ref,
    cg_ref,
    unit1,
    rate1,
    h1b,
    act,
    slope,
    unit2,
    rate2,
    zb,
    head_in,
    head_low,
    feed_low,
    *,
    tile,
    micro,
    row_len,
):
    step = pl.program_id(0)
    tiles = micro * row_len // tile
    group, _, slots, _ = out_ref.shape

    @pl.when(step == 0)
    def _():
        vg_ref[...] = jnp.zeros_like(vg_ref)

    @pl.when(step < tiles)
    def _():
        rows = pl.ds(pl.multiple_of(step * tile, tile), tile)
        unit, rate = norm_parts(a1_ref[...])
        unit1[rows, :] = unit
        rate1[rows, :] = rate
        h1 = unit * vec_ref[3:4, :] + vec_ref[4:5, :]
        low = h1.astype(BF16)
        h1b[rows, :] = low
        total = h1 + vec_ref[9:10, :]
        for c in range(FF // D):
            cols = slice(c * D, (c + 1) * D)
            value, grad = gelu_both(nn(low, w_ref[4 + c]) + vec_ref[5 + c : 6 + c, :])
            value = value.astype(BF16)
            act[rows, cols] = value
            slope[rows, cols] = grad.astype(BF16)
            total = total + nn(value, w_ref[8 + c])
        unit, rate = norm_parts(total)
        unit2[rows, :] = unit
        rate2[rows, :] = rate
        z = (unit * vec_ref[10:11, :] + vec_ref[11:12, :]).astype(BF16)
        zb[rows, :] = z
        head_in[rows, :] = nn(z, stu_ref[0:D, :].astype(BF16)) + stu_ref[D + SW : D + SW + 1, :]

    @pl.when(step == tiles)
    def _():
        head_phase(
            info, stu_ref, cls_ref, goal_ref, sg_ref, cg_ref, head_in, head_low, micro, row_len
        )
        sg_ref[0:D, :] = tn(zb[...], head_low[...])
        for m in range(micro):
            place = send_row[m : m + 1, :]
            spot = lax.broadcasted_iota(jnp.int32, (group * slots, row_len), 0)
            pick = jnp.where(spot == place, 1.0, 0.0).astype(BF16)
            moved = nn(pick, zb[m * row_len : (m + 1) * row_len, :]).astype(BF16)
            out_ref[:, m] = moved.reshape(group, slots, D)

    @pl.when(step >= tiles)
    def _():
        t = step - tiles
        rows = pl.ds(pl.multiple_of(t * tile, tile), tile)
        m = (t * tile) // row_len
        spot = lax.broadcasted_iota(jnp.int32, (tile, group * slots), 1)
        pick = jnp.where(spot == send_col[...], 1.0, 0.0).astype(BF16)
        dz = nn(pick, back_ref[:, m].reshape(group * slots, D))
        dz = dz + nt(head_low[rows, :], stu_ref[0:D, :].astype(BF16))
        unit = unit2[rows, :]
        vg_ref[10:11, :] += row_sum(dz * unit)
        vg_ref[11:12, :] += row_sum(dz)
        da2 = norm_back(dz * vec_ref[10:11, :], unit, rate2[rows, :])
        low = da2.astype(BF16)
        feed_low[rows, :] = low
        vg_ref[9:10, :] += row_sum(low.astype(F32))
        dh1 = da2
        for c in range(FF // D):
            cols = slice(c * D, (c + 1) * D)
            du = (nt(low, w_ref[8 + c]) * slope[rows, cols].astype(F32)).astype(BF16)
            slope[rows, cols] = du
            vg_ref[5 + c : 6 + c, :] += row_sum(du.astype(F32))
            dh1 = dh1 + nt(du, w_ref[4 + c])
        unit = unit1[rows, :]
        vg_ref[3:4, :] += row_sum(dh1 * unit)
        vg_ref[4:5, :] += row_sum(dh1)
        da1_ref[...] = norm_back(dh1 * vec_ref[3:4, :], unit, rate1[rows, :])

    @pl.when(step == 2 * tiles - 1)
    def _():
        for c in range(FF // D):
            cols = slice(c * D, (c + 1) * D)
            wg_ref[c] = tn(h1b[...], slope[:, cols]).astype(BF16)
            wg_ref[4 + c] = tn(act[:, cols], feed_low[...]).astype(BF16)


def head_phase(info, stu_ref, cls_ref, goal_ref, sg_ref, cg_ref, head_in, head_low, micro, row_len):
    scale = DH**-0.5
    query = stu_ref[D + SW + 2 : D + SW + 3, :]
    same = (
        lax.broadcasted_iota(jnp.int32, (SW, SW), 0) // DH
        == lax.broadcasted_iota(jnp.int32, (SW, SW), 1) // DH
    ).astype(F32)
    pooled, weights, members = [], [], []
    for m in range(micro):
        rows = slice(m * row_len, (m + 1) * row_len)
        s = head_in[rows, :]
        e = exact(s * query, same) * scale
        sample = sample_column(ends_of(info, m), 0, row_len)
        share = jnp.zeros_like(e)
        for j in range(SAMP):
            member = sample == j
            peak = jnp.max(jnp.where(member, e, -1e30), axis=0, keepdims=True)
            up = jnp.where(member, jnp.exp(jnp.where(member, e - peak, 0.0)), 0.0)
            up = up / row_sum(up)
            share = share + up
            pooled.append(row_sum(up * s))
            members.append(member)
        weights.append(share)
    pooled = jnp.concatenate(pooled, axis=0)
    pool_weight = stu_ref[D : D + SW, :]
    mixed = jnp.tanh(exact(pooled, pool_weight) + stu_ref[D + SW + 1 : D + SW + 2, :])
    classes = cls_ref[0:SW, :]
    logits = exact(mixed, classes) + cls_ref[SW : SW + 1, :]
    logits = logits - jnp.max(logits, axis=-1, keepdims=True)
    chance = jnp.exp(logits)
    chance = chance / jnp.sum(chance, axis=-1, keepdims=True)
    goal = goal_ref[:, 0:CLS]
    alive = goal_ref[:, CLS : CLS + 1]
    target = jnp.exp(goal - jnp.max(goal, axis=-1, keepdims=True))
    target = target / jnp.sum(target, axis=-1, keepdims=True)
    d_logits = alive * (chance - target)
    cg_ref[0:SW, :] = exact(mixed, d_logits, (((0,), (0,)), ((), ())))
    cg_ref[SW : SW + 1, :] = row_sum(d_logits)
    d_pre = exact(d_logits, classes, (((1,), (1,)), ((), ()))) * (1.0 - mixed * mixed)
    sg_ref[D : D + SW, :] = exact(pooled, d_pre, (((0,), (0,)), ((), ())))
    sg_ref[D + SW + 1 : D + SW + 2, :] = row_sum(d_pre)
    d_pooled = exact(d_pre, pool_weight, (((1,), (1,)), ((), ())))
    inner = exact(pooled * d_pooled, same)
    d_bias = jnp.zeros((1, SW), F32)
    d_query = jnp.zeros((1, SW), F32)
    for m in range(micro):
        rows = slice(m * row_len, (m + 1) * row_len)
        s = head_in[rows, :]
        spread = jnp.zeros((row_len, SW), F32)
        center = jnp.zeros((row_len, SW), F32)
        for j in range(SAMP):
            member = members[m * SAMP + j]
            at = m * SAMP + j
            spread = jnp.where(member, d_pooled[at : at + 1, :], spread)
            center = jnp.where(member, inner[at : at + 1, :], center)
        share = weights[m]
        d_e = share * (exact(s * spread, same) - center) * scale
        d_s = (share * spread + d_e * query).astype(BF16)
        head_low[rows, :] = d_s
        d_bias = d_bias + row_sum(d_s.astype(F32))
        d_query = d_query + row_sum(d_e * s)
    sg_ref[D + SW : D + SW + 1, :] = d_bias
    sg_ref[D + SW + 2 : D + SW + 3, :] = d_query


def feed(info, a1, blocks, vec, student, classifier, goals, send_row, send_col, returned):
    micro, row_len, _ = a1.shape
    tokens = micro * row_len
    tile = 256
    tiles = tokens // tile
    group, _, slots, _ = returned.shape
    whole = lambda *shape: pl.BlockSpec(shape, lambda i: (0,) * len(shape))
    once = lambda *shape: pl.BlockSpec(
        shape, lambda i: (0,) * len(shape), pipeline_mode=pl.Buffered(1)
    )
    ahead = lambda width: pl.BlockSpec((tile, width), lambda i: (jnp.minimum(i, tiles - 1), 0))
    behind = lambda width: pl.BlockSpec((tile, width), lambda i: (jnp.maximum(i - tiles, 0), 0))
    return pl.pallas_call(
        functools.partial(feed_kernel, tile=tile, micro=micro, row_len=row_len),
        grid=(2 * tiles,),
        in_specs=[
            pl.BlockSpec(memory_space=pltpu.SMEM),
            ahead(D),
            once(NMAT, D, D),
            once(NMAT, D),
            once(*student.shape),
            once(*classifier.shape),
            once(*goals.shape),
            once(*send_row.shape),
            behind(1),
            once(*returned.shape),
        ],
        out_specs=[
            behind(D),
            once(*returned.shape),
            once(8, D, D),
            once(NMAT, D),
            once(*student.shape),
            once(*classifier.shape),
        ],
        out_shape=[
            jax.ShapeDtypeStruct((tokens, D), F32),
            jax.ShapeDtypeStruct(returned.shape, BF16),
            jax.ShapeDtypeStruct((8, D, D), BF16),
            jax.ShapeDtypeStruct((NMAT, D), F32),
            jax.ShapeDtypeStruct(student.shape, F32),
            jax.ShapeDtypeStruct(classifier.shape, F32),
        ],
        scratch_shapes=[
            pltpu.VMEM((tokens, D), F32),
            pltpu.VMEM((tokens, 1), F32),
            pltpu.VMEM((tokens, D), BF16),
            pltpu.VMEM((tokens, FF), BF16),
            pltpu.VMEM((tokens, FF), BF16),
            pltpu.VMEM((tokens, D), F32),
            pltpu.VMEM((tokens, 1), F32),
            pltpu.VMEM((tokens, D), BF16),
            pltpu.VMEM((tokens, SW), F32),
            pltpu.VMEM((tokens, SW), BF16),
            pltpu.VMEM((tokens, D), BF16),
        ],
        compiler_params=pltpu.CompilerParams(vmem_limit_bytes=VMEM),
        cost_estimate=pl.CostEstimate(
            flops=tokens * D * FF * 12, bytes_accessed=tokens * D * 16, transcendentals=tokens * FF
        ),
    )(
        info,
        a1.reshape(tokens, D),
        blocks,
        vec,
        student,
        classifier,
        goals,
        send_row,
        send_col,
        returned,
    )


def attend_back_kernel(
    info,
    x_ref,
    da1_ref,
    q_ref,
    k_ref,
    v_ref,
    o_ref,
    w_ref,
    dx_ref,
    wg_ref,
    vg_ref,
    kx,
    vx,
    dox,
    dq,
    dk,
    dv,
    wsum,
    *,
    micro,
):
    row = pl.program_id(0)
    row_len = x_ref.shape[1]
    ends, live = ends_of(info, row), live_of(info, row)
    first = lane_index(QT) < DH

    @pl.when(row == 0)
    def _():
        vg_ref[...] = jnp.zeros_like(vg_ref)
        wsum[...] = jnp.zeros_like(wsum)

    crossed = (
        lax.broadcasted_iota(jnp.int32, (LANES, LANES), 0) // DH
        != lax.broadcasted_iota(jnp.int32, (LANES, LANES), 1) // DH
    )
    crossed = jnp.where(crossed, 1.0, 0.0).astype(BF16)

    dq[...] = jnp.zeros_like(dq)

    @pl.loop(0, row_len // QT)
    def _(t):
        rows = pl.ds(pl.multiple_of(t * QT, QT), QT)
        sample = sample_column(ends, t * QT, QT)
        k_extra = key_spare(sample, QT)
        branch = da1_ref[0, rows, :].astype(BF16)
        vg_ref[2:3, :] += row_sum(branch.astype(F32))
        do = nt(branch, w_ref[3]).astype(BF16).astype(F32)
        inner = do * o_ref[0, rows, :].astype(F32)
        lane = lane_index(QT) % DH
        for p in range(PAIRS):
            pair = slice(p * LANES, (p + 1) * LANES)
            high = inner[:, pair].astype(BF16)
            rest = (inner[:, pair] - high.astype(F32)).astype(BF16)
            delta = nn(high, crossed) + nn(rest, crossed)
            high, mid, _rest = split_low(delta)
            do_extra = jnp.where(lane == 0, -high, jnp.where(lane == 1, -mid, 0.0))
            for ref, values, spare in (
                (dox, do[:, pair], do_extra),
                (kx, k_ref[0, rows, pair].astype(F32), k_extra),
                (vx, v_ref[0, rows, pair].astype(F32), jnp.ones((QT, LANES), F32)),
            ):
                left, right = halves(values, spare, first)
                ref[rows, 2 * p * LANES : (2 * p + 1) * LANES] = left.astype(BF16)
                ref[rows, (2 * p + 1) * LANES : (2 * p + 2) * LANES] = right.astype(BF16)

    @pl.loop(0, row_len // QT)
    def _(t):
        rows = pl.ds(pl.multiple_of(t * QT, QT), QT)
        begin, number = reach(ends, live, t * QT, QT, row_len)

        @pl.when(number == 0)
        def _():
            dk[rows, :] = jnp.zeros((QT, D), BF16)
            dv[rows, :] = jnp.zeros((QT, D), BF16)

        for n in range(1, row_len // KG + 1):

            @pl.when(number == n)
            def _(n=n):
                span = pl.ds(pl.multiple_of(begin * KG, KG), n * KG)
                wide = lane_index(n * KG) < DH

                @pl.loop(0, PAIRS)
                def _(p):
                    got = []
                    for head in range(2):
                        cols = pl.ds(
                            pl.multiple_of((2 * p + head) * LANES, LANES), LANES
                        )
                        q, k = q_ref[0, span, cols], kx[rows, cols]
                        do = dox[span, cols]
                        prob = jnp.exp(nt(k, q))
                        ds = (prob * nt(vx[rows, cols], do)).astype(BF16)
                        got.append(
                            (nn(prob.astype(BF16), do), nn(ds, q), tn(ds, k))
                        )
                    cols = pl.ds(pl.multiple_of(p * LANES, LANES), LANES)
                    dv[rows, cols] = jnp.where(first, got[0][0], got[1][0]).astype(BF16)
                    dk[rows, cols] = jnp.where(first, got[0][1], got[1][1]).astype(BF16)
                    dq[span, cols] += jnp.where(wide, got[0][2], got[1][2])

    @pl.loop(0, row_len // QT)
    def _(t):
        rows = pl.ds(pl.multiple_of(t * QT, QT), QT)
        dq_low = (dq[rows, :] * DH**-0.5).astype(BF16)
        dk_low, dv_low = dk[rows, :], dv[rows, :]
        vg_ref[0:1, :] += row_sum(dq_low.astype(F32))
        vg_ref[1:2, :] += row_sum(dv_low.astype(F32))
        dx_ref[0, rows, :] = (
            da1_ref[0, rows, :]
            + nt(dq_low, w_ref[0])
            + nt(dk_low, w_ref[1])
            + nt(dv_low, w_ref[2])
        ).astype(BF16)

    x = x_ref[0]
    wsum[0] += tn(x, (dq[...] * DH**-0.5).astype(BF16))
    wsum[1] += tn(x, dk[...])
    wsum[2] += tn(x, dv[...])
    wsum[3] += tn(o_ref[0], da1_ref[0].astype(BF16))

    @pl.when(row == micro - 1)
    def _():
        wg_ref[...] = wsum[...].astype(BF16)


def attend_back(info, tokens, da1, q, k, v, o, blocks):
    micro, row_len, _ = tokens.shape
    row_spec = lambda width: pl.BlockSpec((1, row_len, width), lambda r: (r, 0, 0))
    return pl.pallas_call(
        functools.partial(attend_back_kernel, micro=micro),
        grid=(micro,),
        in_specs=[
            pl.BlockSpec(memory_space=pltpu.SMEM),
            row_spec(D),
            row_spec(D),
            row_spec(2 * D),
            row_spec(D),
            row_spec(D),
            row_spec(D),
            pl.BlockSpec((4, D, D), lambda r: (0, 0, 0)),
        ],
        out_specs=[
            row_spec(D),
            pl.BlockSpec((4, D, D), lambda r: (0, 0, 0)),
            pl.BlockSpec((8, D), lambda r: (0, 0)),
        ],
        out_shape=[
            jax.ShapeDtypeStruct((micro, row_len, D), BF16),
            jax.ShapeDtypeStruct((4, D, D), BF16),
            jax.ShapeDtypeStruct((8, D), F32),
        ],
        scratch_shapes=[
            pltpu.VMEM((row_len, 2 * D), BF16),
            pltpu.VMEM((row_len, 2 * D), BF16),
            pltpu.VMEM((row_len, 2 * D), BF16),
            pltpu.VMEM((row_len, D), F32),
            pltpu.VMEM((row_len, D), BF16),
            pltpu.VMEM((row_len, D), BF16),
            pltpu.VMEM((4, D, D), F32),
        ],
        compiler_params=pltpu.CompilerParams(vmem_limit_bytes=VMEM),
        cost_estimate=pl.CostEstimate(
            flops=micro * row_len * D * D * 16 + micro * H * row_len * row_len * DH * 10,
            bytes_accessed=micro * row_len * D * 16,
            transcendentals=micro * H * row_len * row_len,
        ),
    )(info, tokens, da1, q, k, v, o, blocks)


def pick_kernel(place_ref, rows_ref, out_ref):
    group, _, slots, _ = out_ref.shape
    places = group * slots
    spot = lax.broadcasted_iota(jnp.int32, (places, rows_ref.shape[1]), 1)
    pick = jnp.where(spot == place_ref[0], 1.0, 0.0).astype(BF16)
    out_ref[:, 0] = nn(pick, rows_ref[0]).astype(BF16).reshape(group, slots, D)


def pick_rows(place_col, rows, group):
    micro, row_len, _ = rows.shape
    slots = row_len // group
    return pl.pallas_call(
        pick_kernel,
        grid=(micro,),
        in_specs=[
            pl.BlockSpec((1, row_len, 1), lambda m: (m, 0, 0)),
            pl.BlockSpec((1, row_len, D), lambda m: (m, 0, 0)),
        ],
        out_specs=pl.BlockSpec((group, 1, slots, D), lambda m: (0, m, 0, 0)),
        out_shape=jax.ShapeDtypeStruct((group, micro, slots, D), BF16),
        compiler_params=pltpu.CompilerParams(vmem_limit_bytes=VMEM),
    )(place_col, rows)


def place_kernel(place_ref, rows_ref, out_ref):
    row_len = out_ref.shape[1]
    spot = lax.broadcasted_iota(jnp.int32, (row_len, row_len), 0)
    pick = jnp.where(spot == place_ref[0], 1.0, 0.0).astype(BF16)
    out_ref[0] = nn(pick, rows_ref[:, 0].reshape(row_len, D)).astype(BF16)


def place_rows(place_row, rows):
    group, micro, slots, _ = rows.shape
    row_len = group * slots
    return pl.pallas_call(
        place_kernel,
        grid=(micro,),
        in_specs=[
            pl.BlockSpec((1, 1, row_len), lambda m: (m, 0, 0)),
            pl.BlockSpec((group, 1, slots, D), lambda m: (0, m, 0, 0)),
        ],
        out_specs=pl.BlockSpec((1, row_len, D), lambda m: (m, 0, 0)),
        out_shape=jax.ShapeDtypeStruct((micro, row_len, D), BF16),
        compiler_params=pltpu.CompilerParams(vmem_limit_bytes=VMEM),
    )(place_row, rows)


def diagonal_rule(old_values, moment, grads, rate):
    new_moment = decay_rate * moment + (1.0 - decay_rate) * grads * grads
    return (new_moment, old_values - rate * grads / (jnp.sqrt(new_moment) + 1e-08))


def local(
    tokens,
    cotangent,
    lengths,
    exit_layers,
    teacher,
    blocks,
    left_stats,
    right_stats,
    left_root,
    right_root,
    vectors,
    vec_moment,
    student,
    stu_moment,
    classifier,
    cls_moment,
):
    group = lax.axis_size("batch")
    me = lax.axis_index("batch")
    micro, _, row_len, _ = tokens.shape
    slots = row_len // group
    tokens, cotangent = tokens[:, 0], cotangent[:, 0]
    ends = jnp.cumsum(lengths[:, 0], axis=-1, dtype=jnp.int32)
    live = (exit_layers[:, 0] >= LAYER).astype(jnp.int32)
    info = jnp.concatenate([ends, live], axis=1)
    alive_len = lengths[:, 0] * live
    counts = jnp.sum(alive_len, axis=1, dtype=jnp.int32)
    everyone = lax.all_gather(counts[None, :], "batch", axis=0, tiled=True)
    starts = jnp.cumsum(everyone, axis=0, dtype=jnp.int32) - everyone

    places = jnp.arange(row_len, dtype=jnp.int32)
    before = jnp.cumsum(alive_len, axis=1, dtype=jnp.int32) - alive_len
    sample = jnp.sum((places[None, :, None] >= ends[:, None, : SAMP - 1]).astype(jnp.int32), axis=-1)
    chosen = sample[..., None] == jnp.arange(SAMP, dtype=jnp.int32)
    shift = jnp.sum(jnp.where(chosen, (before - ends + lengths[:, 0])[:, None, :], 0), axis=-1)
    alive_tok = jnp.sum(jnp.where(chosen, live[:, None, :], 0), axis=-1)
    rank = places[None, :] + shift
    send = (starts[me][:, None] + rank) % group * slots + rank // group
    send = jnp.where(alive_tok > 0, send, row_len)
    start_of = jnp.repeat(starts.T, slots, axis=1)
    count_of = jnp.repeat(everyone.T, slots, axis=1)
    turn = (me - start_of) % group + group * (places % slots)[None, :]
    back = jnp.where(turn < count_of, (start_of + turn) // group, row_len)

    grad_outgoing = pick_rows(back[:, :, None], cotangent, group)
    returned = lax.all_to_all(grad_outgoing, "batch", split_axis=0, concat_axis=0, tiled=True)

    matrices = lax.all_gather(blocks, "shard", axis=0, tiled=True)
    vec = lax.all_gather(vectors.astype(BF16), "shard", axis=0, tiled=True).astype(F32)

    a1, q, k, v, o = attend(info, tokens, matrices, vec)
    goals = jnp.concatenate(
        [teacher[:, 0], live[..., None].astype(F32)], axis=-1
    ).reshape(micro * SAMP, CLS + 1)
    da1, outgoing, ff_grads, ff_vecs, stu_grads, cls_grads = feed(
        info, a1, matrices, vec, student, classifier, goals, send, send.reshape(-1, 1), returned
    )
    arrived = lax.all_to_all(outgoing, "batch", split_axis=0, concat_axis=0, tiled=True)
    input_grads, at_grads, at_vecs = attend_back(
        info, tokens, da1.reshape(micro, row_len, D), q, k, v, o, matrices
    )
    layer_out = place_rows(back[:, None, :], arrived)

    grads = jnp.concatenate([at_grads, ff_grads], axis=0)
    vec_grads = jnp.concatenate([at_vecs[:3], ff_vecs[3:]], axis=0)
    owned = lax.psum_scatter(grads, "shard", scatter_dimension=0, tiled=True)
    owned = lax.psum(owned, "batch")
    small = jnp.concatenate(
        [vec_grads.reshape(-1), stu_grads.reshape(-1), cls_grads.reshape(-1)]
    )
    small = lax.psum(small, ("batch", "shard"))
    whole_vecs = small[: NMAT * D].reshape(NMAT, D)
    head_student = small[NMAT * D : NMAT * D + student.size].reshape(student.shape)
    head_class = small[NMAT * D + student.size :].reshape(classifier.shape)
    owners = lax.axis_size("shard")
    owned_vecs = lax.dynamic_slice_in_dim(
        whole_vecs, lax.axis_index("shard") * (NMAT // owners), NMAT // owners, 0
    )

    owned_f32 = owned.astype(F32)
    gram_left = jnp.einsum("bij,bkj->bik", owned, owned, preferred_element_type=F32)
    gram_right = jnp.einsum("bji,bjk->bik", owned, owned, preferred_element_type=F32)
    new_left = decay_rate * left_stats + (1.0 - decay_rate) * gram_left
    new_right = decay_rate * right_stats + (1.0 - decay_rate) * gram_right
    steered = jnp.einsum("bij,bjk->bik", left_root, owned_f32)
    steered = jnp.einsum("bij,bjk->bik", steered, right_root)
    size_norm = jnp.sqrt(jnp.mean(steered * steered, axis=(1, 2), keepdims=True) + 1e-06)
    new_blocks = blocks.astype(F32) - block_rate * steered / size_norm
    new_vec_moment, new_vectors = diagonal_rule(vectors, vec_moment, owned_vecs, vector_rate)
    new_stu_moment, new_student = diagonal_rule(student, stu_moment, head_student, head_rate)
    new_cls_moment, new_classifier = diagonal_rule(classifier, cls_moment, head_class, head_rate)
    return (
        layer_out[:, None],
        input_grads[:, None],
        owned_f32,
        new_blocks,
        new_left,
        new_right,
        owned_vecs,
        new_vec_moment,
        new_vectors,
        head_student,
        new_stu_moment,
        new_student,
        head_class,
        new_cls_moment,
        new_classifier,
    )


def solution(mesh):
    rows = P(None, ("batch", "shard"), None, None)
    tags = P(None, ("batch", "shard"), None)
    mats = P("shard", None, None)
    vecs = P("shard", None)
    return jax.shard_map(
        local,
        mesh=mesh,
        in_specs=(rows, rows, tags, tags, rows, mats, mats, mats, mats, mats, vecs, vecs)
        + (P(),) * 4,
        out_specs=(rows, rows, mats, mats, mats, mats, vecs, vecs, vecs) + (P(),) * 6,
        check_vma=False,
    )
```

```python
import functools

import jax
import jax.numpy as jnp
from jax import lax
from jax.experimental import pallas as pl
from jax.experimental.pallas import tpu as pltpu
from jax.sharding import PartitionSpec as P

D = 512
H = 8
DH = 64
FF = 2048
SW = 128
NMAT = 12
SAMP = 4
LAYER = 4
CLS = 14

decay_rate = 0.5
block_rate = 0.04
vector_rate = 0.05
head_rate = 0.05

QT = 256
KG = 128
PAIRS = H // 2
LANES = 128
BIG = float(2**30)
EPS = 1e-6
VMEM = 60 * 1024 * 1024

F32 = jnp.float32
BF16 = jnp.bfloat16


def nn(a, b):
    return jnp.dot(a, b, preferred_element_type=F32)


def nt(a, b):
    return lax.dot_general(a, b, (((1,), (1,)), ((), ())), preferred_element_type=F32)


def tn(a, b):
    return lax.dot_general(a, b, (((0,), (0,)), ((), ())), preferred_element_type=F32)


def exact(a, b, dims=(((1,), (0,)), ((), ()))):
    return lax.dot_general(
        a, b, dims, preferred_element_type=F32, precision=lax.Precision.HIGHEST
    )


def row_sum(v):
    return jnp.sum(v, axis=0, keepdims=True)


def split_low(v):
    high = v.astype(BF16).astype(F32)
    rest = v - high
    mid = rest.astype(BF16).astype(F32)
    return high, mid, rest - mid


def ends_of(info, row):
    return [info[row, j] for j in range(SAMP)]


def live_of(info, row):
    return [info[row, SAMP + j] for j in range(SAMP)]


def sample_column(ends, first, count):
    place = first + lax.broadcasted_iota(jnp.int32, (count, 1), 0)
    total = jnp.zeros((count, 1), jnp.int32)
    for j in range(SAMP - 1):
        total = total + (place >= ends[j]).astype(jnp.int32)
    return total


def reach(ends, live, first, count, row_len):
    low, high = jnp.int32(row_len), jnp.int32(0)
    start = jnp.int32(0)
    for j in range(SAMP):
        end = ends[j]
        meets = (start < first + count) & (end > first) & (end > start) & (live[j] > 0)
        low = jnp.where(meets, jnp.minimum(low, start), low)
        high = jnp.where(meets, jnp.maximum(high, end), high)
        start = end
    begin = low // KG
    number = jnp.maximum((high + KG - 1) // KG - begin, 0)
    return begin, number


def lane_index(rows):
    return lax.broadcasted_iota(jnp.int32, (rows, LANES), 1)


def key_spare(sample, rows):
    lane = lane_index(rows) % DH
    return jnp.where(
        lane < SAMP, (lane == sample).astype(F32), (lane < SAMP + 3).astype(F32)
    )


def query_spare(sample, rows):
    lane = lane_index(rows) % DH
    return jnp.where((lane < SAMP) & (lane != sample), -BIG, 0.0)


def halves(pair, spare, first):
    return jnp.where(first, pair, spare), jnp.where(first, spare, pair)


def attend_kernel(
    info, x_ref, w_ref, vec_ref, a1_ref, q_ref, k_ref, v_ref, o_ref, kx, vx
):
    row = pl.program_id(0)
    row_len = x_ref.shape[1]
    ends, live = ends_of(info, row), live_of(info, row)
    first = lane_index(QT) < DH

    @pl.loop(0, row_len // QT)
    def _(t):
        rows = pl.ds(pl.multiple_of(t * QT, QT), QT)
        x = x_ref[0, rows, :]
        sample = sample_column(ends, t * QT, QT)
        k_extra, q_extra = key_spare(sample, QT), query_spare(sample, QT)
        q = (nn(x, w_ref[0]) + vec_ref[0:1, :]).astype(BF16).astype(F32) * DH**-0.5
        k = nn(x, w_ref[1]).astype(BF16)
        v = (nn(x, w_ref[2]) + vec_ref[1:2, :]).astype(BF16)
        k_ref[0, rows, :] = k
        v_ref[0, rows, :] = v
        for p in range(PAIRS):
            pair = slice(p * LANES, (p + 1) * LANES)
            for ref, values, spare in (
                (q_ref.at[0], q, q_extra),
                (kx, k.astype(F32), k_extra),
                (vx, v.astype(F32), jnp.ones((QT, LANES), F32)),
            ):
                left, right = halves(values[:, pair], spare, first)
                ref[rows, 2 * p * LANES : (2 * p + 1) * LANES] = left.astype(BF16)
                ref[rows, (2 * p + 1) * LANES : (2 * p + 2) * LANES] = right.astype(BF16)

    @pl.loop(0, row_len // QT)
    def _(t):
        rows = pl.ds(pl.multiple_of(t * QT, QT), QT)
        begin, number = reach(ends, live, t * QT, QT, row_len)

        @pl.when(number == 0)
        def _():
            o_ref[0, rows, :] = jnp.zeros((QT, D), BF16)

        for n in range(1, row_len // KG + 1):

            @pl.when(number == n)
            def _(n=n):
                span = pl.ds(pl.multiple_of(begin * KG, KG), n * KG)
                lane = lane_index(QT)

                @pl.loop(0, PAIRS)
                def _(p):
                    parts = []
                    for head in range(2):
                        cols = pl.ds(
                            pl.multiple_of((2 * p + head) * LANES, LANES), LANES
                        )
                        q = q_ref[0, rows, cols]
                        s = nt(q, kx[span, cols])
                        peak = jnp.max(s, axis=1, keepdims=True)
                        e = jnp.exp(s - peak).astype(BF16)
                        got = nn(e, vx[span, cols])
                        parts.append(got)
                        other = (lane >= DH) if head == 0 else (lane < DH)
                        total = peak + jnp.log(jnp.where(other, got, 1.0))
                        high, mid, rest = split_low(
                            jnp.where(peak > -0.5 * BIG, total, 0.0)
                        )
                        at = lane % DH
                        fill = jnp.where(
                            at == SAMP, -high, jnp.where(at == SAMP + 1, -mid, -rest)
                        )
                        spot = other & (at >= SAMP) & (at < SAMP + 3)
                        q_ref[0, rows, cols] = jnp.where(
                            spot, fill, q.astype(F32)
                        ).astype(BF16)
                    top = jnp.where(first, parts[0], parts[1])
                    total = pltpu.roll(jnp.where(first, parts[1], parts[0]), DH, 1)
                    cols = pl.ds(pl.multiple_of(p * LANES, LANES), LANES)
                    o_ref[0, rows, cols] = (top / total).astype(BF16)

    @pl.loop(0, row_len // QT)
    def _(t):
        rows = pl.ds(pl.multiple_of(t * QT, QT), QT)
        a1_ref[0, rows, :] = x_ref[0, rows, :].astype(F32) + (
            nn(o_ref[0, rows, :], w_ref[3]) + vec_ref[2:3, :]
        )


def attend(info, tokens, blocks, vec):
    micro, row_len, _ = tokens.shape
    row_spec = lambda width: pl.BlockSpec((1, row_len, width), lambda r: (r, 0, 0))
    return pl.pallas_call(
        attend_kernel,
        grid=(micro,),
        in_specs=[
            pl.BlockSpec(memory_space=pltpu.SMEM),
            row_spec(D),
            pl.BlockSpec((4, D, D), lambda r: (0, 0, 0)),
            pl.BlockSpec((NMAT, D), lambda r: (0, 0)),
        ],
        out_specs=[row_spec(D), row_spec(2 * D), row_spec(D), row_spec(D), row_spec(D)],
        out_shape=[
            jax.ShapeDtypeStruct((micro, row_len, D), F32),
            jax.ShapeDtypeStruct((micro, row_len, 2 * D), BF16),
            jax.ShapeDtypeStruct((micro, row_len, D), BF16),
            jax.ShapeDtypeStruct((micro, row_len, D), BF16),
            jax.ShapeDtypeStruct((micro, row_len, D), BF16),
        ],
        scratch_shapes=[
            pltpu.VMEM((row_len, 2 * D), BF16),
            pltpu.VMEM((row_len, 2 * D), BF16),
        ],
        compiler_params=pltpu.CompilerParams(vmem_limit_bytes=VMEM),
        cost_estimate=pl.CostEstimate(
            flops=micro * row_len * D * D * 8 + micro * H * row_len * row_len * DH * 4,
            bytes_accessed=micro * row_len * D * 16,
            transcendentals=micro * H * row_len * row_len,
        ),
    )(info, tokens, blocks, vec)


def gelu_both(u):
    t = 1.0 / (1.0 + (0.3275911 * 0.5**0.5) * jnp.abs(u))
    bell = jnp.exp(-0.5 * (u * u))
    tail = (
        t
        * (
            0.127414796
            + t * (-0.142248368 + t * (0.7107068705 + t * (-0.7265760135 + t * 0.5307027145)))
        )
        * bell
    )
    share = jnp.where(u >= 0, 1.0 - tail, tail)
    return u * share, share + u * bell * 0.3989422804014327


def norm_parts(a):
    center = a - jnp.mean(a, axis=-1, keepdims=True)
    rate = lax.rsqrt(jnp.mean(center * center, axis=-1, keepdims=True) + EPS)
    return center * rate, rate


def norm_back(grad, unit, rate):
    return rate * (
        grad
        - jnp.mean(grad, axis=-1, keepdims=True)
        - unit * jnp.mean(grad * unit, axis=-1, keepdims=True)
    )


def feed_kernel(
    info,
    a1_ref,
    w_ref,
    vec_ref,
    stu_ref,
    cls_ref,
    goal_ref,
    send_row,
    send_col,
    back_ref,
    da1_ref,
    out_ref,
    wg_ref,
    vg_ref,
    sg_ref,
    cg_ref,
    unit1,
    rate1,
    h1b,
    act,
    slope,
    unit2,
    rate2,
    zb,
    head_in,
    head_low,
    feed_low,
    *,
    tile,
    micro,
    row_len,
):
    step = pl.program_id(0)
    tiles = micro * row_len // tile
    group, _, slots, _ = out_ref.shape

    @pl.when(step == 0)
    def _():
        vg_ref[...] = jnp.zeros_like(vg_ref)

    @pl.when(step < tiles)
    def _():
        rows = pl.ds(pl.multiple_of(step * tile, tile), tile)
        unit, rate = norm_parts(a1_ref[...])
        unit1[rows, :] = unit
        rate1[rows, :] = rate
        h1 = unit * vec_ref[3:4, :] + vec_ref[4:5, :]
        low = h1.astype(BF16)
        h1b[rows, :] = low
        total = h1 + vec_ref[9:10, :]
        for c in range(FF // D):
            cols = slice(c * D, (c + 1) * D)
            value, grad = gelu_both(nn(low, w_ref[4 + c]) + vec_ref[5 + c : 6 + c, :])
            value = value.astype(BF16)
            act[rows, cols] = value
            slope[rows, cols] = grad.astype(BF16)
            total = total + nn(value, w_ref[8 + c])
        unit, rate = norm_parts(total)
        unit2[rows, :] = unit
        rate2[rows, :] = rate
        z = (unit * vec_ref[10:11, :] + vec_ref[11:12, :]).astype(BF16)
        zb[rows, :] = z
        head_in[rows, :] = nn(z, stu_ref[0:D, :].astype(BF16)) + stu_ref[D + SW : D + SW + 1, :]

    @pl.when(step == tiles)
    def _():
        head_phase(
            info, stu_ref, cls_ref, goal_ref, sg_ref, cg_ref, head_in, head_low, micro, row_len
        )
        sg_ref[0:D, :] = tn(zb[...], head_low[...])
        for m in range(micro):
            place = send_row[m : m + 1, :]
            spot = lax.broadcasted_iota(jnp.int32, (group * slots, row_len), 0)
            pick = jnp.where(spot == place, 1.0, 0.0).astype(BF16)
            moved = nn(pick, zb[m * row_len : (m + 1) * row_len, :]).astype(BF16)
            out_ref[:, m] = moved.reshape(group, slots, D)

    @pl.when(step >= tiles)
    def _():
        t = step - tiles
        rows = pl.ds(pl.multiple_of(t * tile, tile), tile)
        m = (t * tile) // row_len
        spot = lax.broadcasted_iota(jnp.int32, (tile, group * slots), 1)
        pick = jnp.where(spot == send_col[...], 1.0, 0.0).astype(BF16)
        dz = nn(pick, back_ref[:, m].reshape(group * slots, D))
        dz = dz + nt(head_low[rows, :], stu_ref[0:D, :].astype(BF16))
        unit = unit2[rows, :]
        vg_ref[10:11, :] += row_sum(dz * unit)
        vg_ref[11:12, :] += row_sum(dz)
        da2 = norm_back(dz * vec_ref[10:11, :], unit, rate2[rows, :])
        low = da2.astype(BF16)
        feed_low[rows, :] = low
        vg_ref[9:10, :] += row_sum(low.astype(F32))
        dh1 = da2
        for c in range(FF // D):
            cols = slice(c * D, (c + 1) * D)
            du = (nt(low, w_ref[8 + c]) * slope[rows, cols].astype(F32)).astype(BF16)
            slope[rows, cols] = du
            vg_ref[5 + c : 6 + c, :] += row_sum(du.astype(F32))
            dh1 = dh1 + nt(du, w_ref[4 + c])
        unit = unit1[rows, :]
        vg_ref[3:4, :] += row_sum(dh1 * unit)
        vg_ref[4:5, :] += row_sum(dh1)
        da1_ref[...] = norm_back(dh1 * vec_ref[3:4, :], unit, rate1[rows, :])

    @pl.when(step == 2 * tiles - 1)
    def _():
        for c in range(FF // D):
            cols = slice(c * D, (c + 1) * D)
            wg_ref[c] = tn(h1b[...], slope[:, cols]).astype(BF16)
            wg_ref[4 + c] = tn(act[:, cols], feed_low[...]).astype(BF16)


def head_phase(info, stu_ref, cls_ref, goal_ref, sg_ref, cg_ref, head_in, head_low, micro, row_len):
    scale = DH**-0.5
    query = stu_ref[D + SW + 2 : D + SW + 3, :]
    same = (
        lax.broadcasted_iota(jnp.int32, (SW, SW), 0) // DH
        == lax.broadcasted_iota(jnp.int32, (SW, SW), 1) // DH
    ).astype(F32)
    pooled, weights, members = [], [], []
    for m in range(micro):
        rows = slice(m * row_len, (m + 1) * row_len)
        s = head_in[rows, :]
        e = exact(s * query, same) * scale
        sample = sample_column(ends_of(info, m), 0, row_len)
        share = jnp.zeros_like(e)
        for j in range(SAMP):
            member = sample == j
            peak = jnp.max(jnp.where(member, e, -1e30), axis=0, keepdims=True)
            up = jnp.where(member, jnp.exp(jnp.where(member, e - peak, 0.0)), 0.0)
            up = up / row_sum(up)
            share = share + up
            pooled.append(row_sum(up * s))
            members.append(member)
        weights.append(share)
    pooled = jnp.concatenate(pooled, axis=0)
    pool_weight = stu_ref[D : D + SW, :]
    mixed = jnp.tanh(exact(pooled, pool_weight) + stu_ref[D + SW + 1 : D + SW + 2, :])
    classes = cls_ref[0:SW, :]
    logits = exact(mixed, classes) + cls_ref[SW : SW + 1, :]
    logits = logits - jnp.max(logits, axis=-1, keepdims=True)
    chance = jnp.exp(logits)
    chance = chance / jnp.sum(chance, axis=-1, keepdims=True)
    goal = goal_ref[:, 0:CLS]
    alive = goal_ref[:, CLS : CLS + 1]
    target = jnp.exp(goal - jnp.max(goal, axis=-1, keepdims=True))
    target = target / jnp.sum(target, axis=-1, keepdims=True)
    d_logits = alive * (chance - target)
    cg_ref[0:SW, :] = exact(mixed, d_logits, (((0,), (0,)), ((), ())))
    cg_ref[SW : SW + 1, :] = row_sum(d_logits)
    d_pre = exact(d_logits, classes, (((1,), (1,)), ((), ()))) * (1.0 - mixed * mixed)
    sg_ref[D : D + SW, :] = exact(pooled, d_pre, (((0,), (0,)), ((), ())))
    sg_ref[D + SW + 1 : D + SW + 2, :] = row_sum(d_pre)
    d_pooled = exact(d_pre, pool_weight, (((1,), (1,)), ((), ())))
    inner = exact(pooled * d_pooled, same)
    d_bias = jnp.zeros((1, SW), F32)
    d_query = jnp.zeros((1, SW), F32)
    for m in range(micro):
        rows = slice(m * row_len, (m + 1) * row_len)
        s = head_in[rows, :]
        spread = jnp.zeros((row_len, SW), F32)
        center = jnp.zeros((row_len, SW), F32)
        for j in range(SAMP):
            member = members[m * SAMP + j]
            at = m * SAMP + j
            spread = jnp.where(member, d_pooled[at : at + 1, :], spread)
            center = jnp.where(member, inner[at : at + 1, :], center)
        share = weights[m]
        d_e = share * (exact(s * spread, same) - center) * scale
        d_s = (share * spread + d_e * query).astype(BF16)
        head_low[rows, :] = d_s
        d_bias = d_bias + row_sum(d_s.astype(F32))
        d_query = d_query + row_sum(d_e * s)
    sg_ref[D + SW : D + SW + 1, :] = d_bias
    sg_ref[D + SW + 2 : D + SW + 3, :] = d_query


def feed(info, a1, blocks, vec, student, classifier, goals, send_row, send_col, returned):
    micro, row_len, _ = a1.shape
    tokens = micro * row_len
    tile = 256
    tiles = tokens // tile
    group, _, slots, _ = returned.shape
    whole = lambda *shape: pl.BlockSpec(shape, lambda i: (0,) * len(shape))
    once = lambda *shape: pl.BlockSpec(
        shape, lambda i: (0,) * len(shape), pipeline_mode=pl.Buffered(1)
    )
    ahead = lambda width: pl.BlockSpec((tile, width), lambda i: (jnp.minimum(i, tiles - 1), 0))
    behind = lambda width: pl.BlockSpec((tile, width), lambda i: (jnp.maximum(i - tiles, 0), 0))
    return pl.pallas_call(
        functools.partial(feed_kernel, tile=tile, micro=micro, row_len=row_len),
        grid=(2 * tiles,),
        in_specs=[
            pl.BlockSpec(memory_space=pltpu.SMEM),
            ahead(D),
            once(NMAT, D, D),
            once(NMAT, D),
            once(*student.shape),
            once(*classifier.shape),
            once(*goals.shape),
            once(*send_row.shape),
            behind(1),
            once(*returned.shape),
        ],
        out_specs=[
            behind(D),
            once(*returned.shape),
            once(8, D, D),
            once(NMAT, D),
            once(*student.shape),
            once(*classifier.shape),
        ],
        out_shape=[
            jax.ShapeDtypeStruct((tokens, D), F32),
            jax.ShapeDtypeStruct(returned.shape, BF16),
            jax.ShapeDtypeStruct((NMAT, D, D), BF16),
            jax.ShapeDtypeStruct((NMAT, D), F32),
            jax.ShapeDtypeStruct(student.shape, F32),
            jax.ShapeDtypeStruct(classifier.shape, F32),
        ],
        scratch_shapes=[
            pltpu.VMEM((tokens, D), F32),
            pltpu.VMEM((tokens, 1), F32),
            pltpu.VMEM((tokens, D), BF16),
            pltpu.VMEM((tokens, FF), BF16),
            pltpu.VMEM((tokens, FF), BF16),
            pltpu.VMEM((tokens, D), F32),
            pltpu.VMEM((tokens, 1), F32),
            pltpu.VMEM((tokens, D), BF16),
            pltpu.VMEM((tokens, SW), F32),
            pltpu.VMEM((tokens, SW), BF16),
            pltpu.VMEM((tokens, D), BF16),
        ],
        compiler_params=pltpu.CompilerParams(vmem_limit_bytes=VMEM),
        cost_estimate=pl.CostEstimate(
            flops=tokens * D * FF * 12, bytes_accessed=tokens * D * 16, transcendentals=tokens * FF
        ),
    )(
        info,
        a1.reshape(tokens, D),
        blocks,
        vec,
        student,
        classifier,
        goals,
        send_row,
        send_col,
        returned,
    )


def attend_back_kernel(
    info,
    x_ref,
    da1_ref,
    q_ref,
    k_ref,
    v_ref,
    o_ref,
    w_ref,
    _,
    dx_ref,
    wg_ref,
    vg_ref,
    kx,
    vx,
    dox,
    dq,
    dk,
    dv,
    wsum,
    *,
    micro,
):
    row = pl.program_id(0)
    row_len = x_ref.shape[1]
    ends, live = ends_of(info, row), live_of(info, row)
    first = lane_index(QT) < DH

    @pl.when(row == 0)
    def _():
        vg_ref[...] = jnp.zeros_like(vg_ref)
        wsum[...] = jnp.zeros_like(wsum)

    crossed = (
        lax.broadcasted_iota(jnp.int32, (LANES, LANES), 0) // DH
        != lax.broadcasted_iota(jnp.int32, (LANES, LANES), 1) // DH
    )
    crossed = jnp.where(crossed, 1.0, 0.0).astype(BF16)

    dq[...] = jnp.zeros_like(dq)

    @pl.loop(0, row_len // QT)
    def _(t):
        rows = pl.ds(pl.multiple_of(t * QT, QT), QT)
        sample = sample_column(ends, t * QT, QT)
        k_extra = key_spare(sample, QT)
        branch = da1_ref[0, rows, :].astype(BF16)
        vg_ref[2:3, :] += row_sum(branch.astype(F32))
        do = nt(branch, w_ref[3]).astype(BF16).astype(F32)
        inner = do * o_ref[0, rows, :].astype(F32)
        lane = lane_index(QT) % DH
        for p in range(PAIRS):
            pair = slice(p * LANES, (p + 1) * LANES)
            high = inner[:, pair].astype(BF16)
            rest = (inner[:, pair] - high.astype(F32)).astype(BF16)
            delta = nn(high, crossed) + nn(rest, crossed)
            high, mid, _rest = split_low(delta)
            do_extra = jnp.where(lane == 0, -high, jnp.where(lane == 1, -mid, 0.0))
            for ref, values, spare in (
                (dox, do[:, pair], do_extra),
                (kx, k_ref[0, rows, pair].astype(F32), k_extra),
                (vx, v_ref[0, rows, pair].astype(F32), jnp.ones((QT, LANES), F32)),
            ):
                left, right = halves(values, spare, first)
                ref[rows, 2 * p * LANES : (2 * p + 1) * LANES] = left.astype(BF16)
                ref[rows, (2 * p + 1) * LANES : (2 * p + 2) * LANES] = right.astype(BF16)

    @pl.loop(0, row_len // QT)
    def _(t):
        rows = pl.ds(pl.multiple_of(t * QT, QT), QT)
        begin, number = reach(ends, live, t * QT, QT, row_len)

        @pl.when(number == 0)
        def _():
            dk[rows, :] = jnp.zeros((QT, D), BF16)
            dv[rows, :] = jnp.zeros((QT, D), BF16)

        for n in range(1, row_len // KG + 1):

            @pl.when(number == n)
            def _(n=n):
                span = pl.ds(pl.multiple_of(begin * KG, KG), n * KG)
                wide = lane_index(n * KG) < DH

                @pl.loop(0, PAIRS)
                def _(p):
                    got = []
                    for head in range(2):
                        cols = pl.ds(
                            pl.multiple_of((2 * p + head) * LANES, LANES), LANES
                        )
                        q, k = q_ref[0, span, cols], kx[rows, cols]
                        do = dox[span, cols]
                        prob = jnp.exp(nt(k, q))
                        ds = (prob * nt(vx[rows, cols], do)).astype(BF16)
                        got.append(
                            (nn(prob.astype(BF16), do), nn(ds, q), tn(ds, k))
                        )
                    cols = pl.ds(pl.multiple_of(p * LANES, LANES), LANES)
                    dv[rows, cols] = jnp.where(first, got[0][0], got[1][0]).astype(BF16)
                    dk[rows, cols] = jnp.where(first, got[0][1], got[1][1]).astype(BF16)
                    dq[span, cols] += jnp.where(wide, got[0][2], got[1][2])

    @pl.loop(0, row_len // QT)
    def _(t):
        rows = pl.ds(pl.multiple_of(t * QT, QT), QT)
        dq_low = (dq[rows, :] * DH**-0.5).astype(BF16)
        dk_low, dv_low = dk[rows, :], dv[rows, :]
        vg_ref[0:1, :] += row_sum(dq_low.astype(F32))
        vg_ref[1:2, :] += row_sum(dv_low.astype(F32))
        dx_ref[0, rows, :] = (
            da1_ref[0, rows, :]
            + nt(dq_low, w_ref[0])
            + nt(dk_low, w_ref[1])
            + nt(dv_low, w_ref[2])
        ).astype(BF16)

    x = x_ref[0]
    wsum[0] += tn(x, (dq[...] * DH**-0.5).astype(BF16))
    wsum[1] += tn(x, dk[...])
    wsum[2] += tn(x, dv[...])
    wsum[3] += tn(o_ref[0], da1_ref[0].astype(BF16))

    @pl.when(row == micro - 1)
    def _():
        wg_ref[...] = wsum[...].astype(BF16)


def attend_back(info, tokens, da1, q, k, v, o, blocks, grads):
    micro, row_len, _ = tokens.shape
    row_spec = lambda width: pl.BlockSpec((1, row_len, width), lambda r: (r, 0, 0))
    return pl.pallas_call(
        functools.partial(attend_back_kernel, micro=micro),
        grid=(micro,),
        in_specs=[
            pl.BlockSpec(memory_space=pltpu.SMEM),
            row_spec(D),
            row_spec(D),
            row_spec(2 * D),
            row_spec(D),
            row_spec(D),
            row_spec(D),
            pl.BlockSpec((4, D, D), lambda r: (0, 0, 0)),
            pl.BlockSpec(memory_space=pl.ANY),
        ],
        out_specs=[
            row_spec(D),
            pl.BlockSpec((4, D, D), lambda r: (2, 0, 0)),
            pl.BlockSpec((8, D), lambda r: (0, 0)),
        ],
        out_shape=[
            jax.ShapeDtypeStruct((micro, row_len, D), BF16),
            jax.ShapeDtypeStruct((NMAT, D, D), BF16),
            jax.ShapeDtypeStruct((8, D), F32),
        ],
        scratch_shapes=[
            pltpu.VMEM((row_len, 2 * D), BF16),
            pltpu.VMEM((row_len, 2 * D), BF16),
            pltpu.VMEM((row_len, 2 * D), BF16),
            pltpu.VMEM((row_len, D), F32),
            pltpu.VMEM((row_len, D), BF16),
            pltpu.VMEM((row_len, D), BF16),
            pltpu.VMEM((4, D, D), F32),
        ],
        input_output_aliases={8: 1},
        compiler_params=pltpu.CompilerParams(vmem_limit_bytes=VMEM),
        cost_estimate=pl.CostEstimate(
            flops=micro * row_len * D * D * 16 + micro * H * row_len * row_len * DH * 10,
            bytes_accessed=micro * row_len * D * 16,
            transcendentals=micro * H * row_len * row_len,
        ),
    )(info, tokens, da1, q, k, v, o, blocks, grads)


def pick_kernel(place_ref, rows_ref, out_ref):
    group, _, slots, _ = out_ref.shape
    places = group * slots
    spot = lax.broadcasted_iota(jnp.int32, (places, rows_ref.shape[1]), 1)
    pick = jnp.where(spot == place_ref[0], 1.0, 0.0).astype(BF16)
    out_ref[:, 0] = nn(pick, rows_ref[0]).astype(BF16).reshape(group, slots, D)


def pick_rows(place_col, rows, group):
    micro, row_len, _ = rows.shape
    slots = row_len // group
    return pl.pallas_call(
        pick_kernel,
        grid=(micro,),
        in_specs=[
            pl.BlockSpec((1, row_len, 1), lambda m: (m, 0, 0)),
            pl.BlockSpec((1, row_len, D), lambda m: (m, 0, 0)),
        ],
        out_specs=pl.BlockSpec((group, 1, slots, D), lambda m: (0, m, 0, 0)),
        out_shape=jax.ShapeDtypeStruct((group, micro, slots, D), BF16),
        compiler_params=pltpu.CompilerParams(vmem_limit_bytes=VMEM),
    )(place_col, rows)


def place_kernel(place_ref, rows_ref, out_ref):
    row_len = out_ref.shape[1]
    spot = lax.broadcasted_iota(jnp.int32, (row_len, row_len), 0)
    pick = jnp.where(spot == place_ref[0], 1.0, 0.0).astype(BF16)
    out_ref[0] = nn(pick, rows_ref[:, 0].reshape(row_len, D)).astype(BF16)


def place_rows(place_row, rows):
    group, micro, slots, _ = rows.shape
    row_len = group * slots
    return pl.pallas_call(
        place_kernel,
        grid=(micro,),
        in_specs=[
            pl.BlockSpec((1, 1, row_len), lambda m: (m, 0, 0)),
            pl.BlockSpec((group, 1, slots, D), lambda m: (0, m, 0, 0)),
        ],
        out_specs=pl.BlockSpec((1, row_len, D), lambda m: (m, 0, 0)),
        out_shape=jax.ShapeDtypeStruct((micro, row_len, D), BF16),
        compiler_params=pltpu.CompilerParams(vmem_limit_bytes=VMEM),
    )(place_row, rows)


CHUNKS = 6
STU_ROWS, CLS_ROWS, VEC_ROWS = 656, 144, 16
SMALL_ROWS = STU_ROWS + CLS_ROWS + 4 * VEC_ROWS


def bits_of(size):
    return [1 << i for i in range(size.bit_length() - 1)]


def reduce_kernel(
    group,
    owners,
    grad_ref,
    ff_vec,
    at_vec,
    stu_ref,
    cls_ref,
    own_ref,
    vec_out,
    stu_out,
    cls_out,
    got_a,
    sum_a,
    got_b,
    part,
    got_c,
    final,
    small,
    small_got,
    small_sum,
    small_end,
    send_sem,
    recv_sem,
    small_send,
    small_recv,
):
    b, s = lax.axis_index("batch"), lax.axis_index("shard")
    per = NMAT // owners
    rows = per * D // CHUNKS
    batch_bits, shard_bits = bits_of(group), bits_of(owners)
    half = SMALL_ROWS // 2

    def copy(src, dst, sems, at, where):
        return pltpu.make_async_remote_copy(
            src_ref=src,
            dst_ref=dst,
            send_sem=sems[0].at[at],
            recv_sem=sems[1].at[at],
            device_id=where,
            device_id_type=pl.DeviceIdType.MESH,
        )

    peers = [(b, s ^ bit) for bit in shard_bits] + [(b ^ bit, s) for bit in batch_bits]
    barrier = pltpu.get_barrier_semaphore()
    for peer in peers:
        pl.semaphore_signal(
            barrier, inc=1, device_id=peer, device_id_type=pl.DeviceIdType.MESH
        )
    pl.semaphore_wait(barrier, len(peers))

    sems = (send_sem, recv_sem)
    small_sems = (small_send, small_recv)
    waits = []

    def begin(op):
        op.start()
        waits.append(op)
        return op

    def piece(owner, c):
        at = lax.rem(owner * per + c * per // CHUNKS + 8, NMAT)
        if rows == D:
            return grad_ref.at[at]
        step = D // rows
        return grad_ref.at[at, pl.ds((c % step) * rows, rows)]

    far = shard_bits[1]
    first = {}
    for c in range(CHUNKS):
        first[c] = [
            begin(copy(piece(s ^ 1 ^ far, c), got_a.at[c, 0], sems, (c, 0), peers[0])),
            begin(copy(piece(s ^ 1, c), got_a.at[c, 1], sems, (c, 1), peers[0])),
        ]

    small[...] = jnp.zeros_like(small)
    stu_count, cls_count = stu_ref.shape[0], cls_ref.shape[0]
    small[0:stu_count, :] = stu_ref[...].astype(BF16)
    small[STU_ROWS : STU_ROWS + cls_count, 0:CLS] = cls_ref[...].astype(BF16)
    for i in range(4):
        at = STU_ROWS + CLS_ROWS + i * VEC_ROWS
        lanes = slice(i * LANES, (i + 1) * LANES)
        small[at : at + 3, :] = at_vec[0:3, lanes].astype(BF16)
        small[at + 3 : at + NMAT, :] = ff_vec[3:NMAT, lanes].astype(BF16)
    core = lax.rem(s, 2)
    mine = pl.ds(pl.multiple_of(core * half, 16), half)
    other = pl.ds(pl.multiple_of((1 - core) * half, 16), half)
    small_op = begin(copy(small.at[other], small_got.at[0], small_sems, 0, peers[0]))

    def add(x, y):
        return (x.astype(F32) + y.astype(F32)).astype(BF16)

    second = {}

    def start_second(c):
        for i, op in enumerate(first[c]):
            op.wait_recv()
            owner = s ^ far if i == 0 else s
            sum_a[c, i] = add(piece(owner, c)[...], got_a[c, i])
        second[c] = begin(copy(sum_a.at[c, 0], got_b.at[c], sems, (c, 2), peers[1]))

    start_second(0)
    start_second(1)

    spans = []
    size = rows
    for bit in batch_bits:
        halving = size >= 32
        spans.append((bit, size, halving))
        if halving:
            size //= 2
    offset_of = []
    offset = jnp.int32(0)
    slot_of = []
    slot = 0
    for bit, now, halving in spans:
        place = lax.rem(b // bit, 2)
        offset_of.append((offset, place))
        slot_of.append(slot)
        if halving:
            offset = offset + place * (now // 2)
            slot += now // 2
        else:
            slot += now
    last = offset

    def ranged(ref, c, start, count):
        return ref.at[c, pl.ds(pl.multiple_of(start, 16), count)]

    moving = {}

    def start_batch(c, k):
        bit, now, halving = spans[k]
        start, place = offset_of[k]
        if halving:
            count = now // 2
            src = ranged(part.at[k], c, start + (1 - place) * count, count)
        else:
            count = now
            src = ranged(part.at[k], c, start, count)
        dst = got_c.at[c, pl.ds(slot_of[k], count)]
        moving[c, k] = begin(copy(src, dst, sems, (c, 3 + k), (b ^ bit, s)))

    def end_batch(c, k):
        bit, now, halving = spans[k]
        start, place = offset_of[k]
        moving[c, k].wait_recv()
        count = now // 2 if halving else now
        if halving:
            start = start + place * count
        here = pl.ds(pl.multiple_of(start, 16), count)
        total = add(part[k, c, here, :], got_c[c, slot_of[k] : slot_of[k] + count])
        if k + 1 < len(spans):
            part[k + 1, c, here, :] = total
        else:
            final[c, here, :] = total

    gathers = [k for k in reversed(range(len(spans))) if spans[k][2]]
    gathering = {}

    def start_gather(c, g):
        k = gathers[g]
        bit, now, _ = spans[k]
        start, place = offset_of[k]
        count = now // 2
        at = ranged(final, c, start + place * count, count)
        gathering[c, g] = begin(
            copy(at, at, sems, (c, 3 + len(spans) + g), (b ^ bit, s))
        )

    def stage(c, k):
        if k == 0:
            second[c].wait_recv()
            if c + 2 < CHUNKS:
                start_second(c + 2)
            part[0, c] = add(sum_a[c, 1], got_b[c])
            start_batch(c, 0)
        elif k <= len(spans):
            end_batch(c, k - 1)
            if k < len(spans):
                start_batch(c, k)
            else:
                start_gather(c, 0)
        else:
            g = k - len(spans) - 1
            gathering[c, g].wait_recv()
            if g + 1 < len(gathers):
                start_gather(c, g + 1)
            else:
                per_block = CHUNKS // per
                block, within = c // per_block, c % per_block
                own_ref[block, within * rows : (within + 1) * rows, :] = final[c]

    stages = 1 + len(spans) + len(gathers)
    rest = [(b, s ^ bit) for bit in shard_bits[1:]] + [(b ^ bit, s) for bit in batch_bits]

    def small_stage(k):
        nonlocal small_op
        small_op.wait_recv()
        if k == 0:
            small_sum[0] = add(small[mine, :], small_got[0])
        elif k <= len(rest):
            small_sum[k] = add(small_sum[k - 1], small_got[k])
        if k < len(rest):
            small_op = begin(
                copy(small_sum.at[k], small_got.at[k + 1], small_sems, k + 1, rest[k])
            )
        elif k == len(rest):
            small_end[mine, :] = small_sum[k]
            small_op = begin(
                copy(small_sum.at[k], small_end.at[mine], small_sems, k + 1, peers[0])
            )

    small_k = 0
    for tick in range(CHUNKS + stages - 1):
        for k in reversed(range(stages)):
            c = tick - k
            if 0 <= c < CHUNKS:
                stage(c, k)
        if small_k <= len(rest) + 1:
            small_stage(small_k)
            small_k += 1
    while small_k <= len(rest) + 1:
        small_stage(small_k)
        small_k += 1

    for i in range(4):
        at = STU_ROWS + CLS_ROWS + i * VEC_ROWS
        lanes = slice(i * LANES, (i + 1) * LANES)
        vec_out[:, lanes] = small_end[at : at + VEC_ROWS, :].astype(F32)
    stu_out[...] = small_end[0:STU_ROWS, :].astype(F32)
    cls_out[...] = small_end[STU_ROWS : STU_ROWS + CLS_ROWS, :].astype(F32)
    for op in waits:
        op.wait_send()


def reduce_grads(grads, ff_vec, at_vec, stu, cls):
    group, owners = lax.axis_size("batch"), lax.axis_size("shard")
    per = NMAT // owners
    rows = per * D // CHUNKS
    batch_count = len(bits_of(group))
    copies = 3 + 2 * batch_count
    small_count = len(bits_of(owners)) + batch_count + 1
    vmem = pl.BlockSpec(memory_space=pltpu.VMEM)
    return pl.pallas_call(
        functools.partial(reduce_kernel, group, owners),
        in_specs=[vmem] * 5,
        out_specs=[vmem] * 4,
        out_shape=[
            jax.ShapeDtypeStruct((per, D, D), BF16),
            jax.ShapeDtypeStruct((VEC_ROWS, D), F32),
            jax.ShapeDtypeStruct((STU_ROWS, SW), F32),
            jax.ShapeDtypeStruct((CLS_ROWS, LANES), F32),
        ],
        scratch_shapes=[
            pltpu.VMEM((CHUNKS, 2, rows, D), BF16),
            pltpu.VMEM((CHUNKS, 2, rows, D), BF16),
            pltpu.VMEM((CHUNKS, rows, D), BF16),
            pltpu.VMEM((batch_count, CHUNKS, rows, D), BF16),
            pltpu.VMEM((CHUNKS, rows + 16 * batch_count, D), BF16),
            pltpu.VMEM((CHUNKS, rows, D), BF16),
            pltpu.VMEM((SMALL_ROWS, LANES), BF16),
            pltpu.VMEM((small_count - 1, SMALL_ROWS // 2, LANES), BF16),
            pltpu.VMEM((small_count - 1, SMALL_ROWS // 2, LANES), BF16),
            pltpu.VMEM((SMALL_ROWS, LANES), BF16),
            pltpu.SemaphoreType.DMA((CHUNKS, copies)),
            pltpu.SemaphoreType.DMA((CHUNKS, copies)),
            pltpu.SemaphoreType.DMA((small_count,)),
            pltpu.SemaphoreType.DMA((small_count,)),
        ],
        compiler_params=pltpu.CompilerParams(
            collective_id=1, has_side_effects=True, vmem_limit_bytes=VMEM
        ),
        cost_estimate=pl.CostEstimate(
            flops=NMAT * D * D * 4, bytes_accessed=NMAT * D * D * 8, transcendentals=0
        ),
    )(grads, ff_vec, at_vec, stu, cls)


def update_kernel(
    own_ref,
    blocks_ref,
    left_ref,
    right_ref,
    lroot_ref,
    rroot_ref,
    shard_ref,
    vsum_ref,
    vec_ref,
    vmom_ref,
    ssum_ref,
    stu_ref,
    smom_ref,
    csum_ref,
    cls_ref,
    cmom_ref,
    grad_out,
    new_out,
    left_out,
    right_out,
    vg_out,
    vm_out,
    v_out,
    sg_out,
    sm_out,
    s_out,
    cg_out,
    cm_out,
    c_out,
    *,
    owners,
):
    g = own_ref[0]
    grad_out[0] = g.astype(F32)
    left_out[0] = decay_rate * left_ref[0] + (1.0 - decay_rate) * nt(g, g)
    right_out[0] = decay_rate * right_ref[0] + (1.0 - decay_rate) * tn(g, g)
    steered = nn(lroot_ref[0].astype(BF16), g).astype(BF16)
    steered = nn(steered, rroot_ref[0].astype(BF16))
    size = jnp.mean(steered * steered, keepdims=True)
    new_out[0] = blocks_ref[0].astype(F32) - steered * (block_rate * lax.rsqrt(size + 1e-06))

    @pl.when(pl.program_id(0) == 0)
    def _():
        per = NMAT // owners
        mine = vsum_ref[0:per, :]
        for i in range(1, owners):
            mine = jnp.where(shard_ref[0] == i, vsum_ref[i * per : (i + 1) * per, :], mine)

        def rule(grads, old, moment, rate, outs):
            renewed = decay_rate * moment + (1.0 - decay_rate) * grads * grads
            outs[0][...] = grads
            outs[1][...] = renewed
            outs[2][...] = old - rate * grads / (jnp.sqrt(renewed) + 1e-08)

        rule(mine, vec_ref[...], vmom_ref[...], vector_rate, (vg_out, vm_out, v_out))
        rule(
            ssum_ref[0 : stu_ref.shape[0], :],
            stu_ref[...],
            smom_ref[...],
            head_rate,
            (sg_out, sm_out, s_out),
        )
        rule(
            csum_ref[0 : cls_ref.shape[0], 0:CLS],
            cls_ref[...],
            cmom_ref[...],
            head_rate,
            (cg_out, cm_out, c_out),
        )


def update(own, blocks, left, right, lroot, rroot, shard, vsum, vec, vmom, ssum, stu, smom, csum, cls, cmom):
    per = own.shape[0]
    mat = pl.BlockSpec((1, D, D), lambda i: (i, 0, 0))
    whole = lambda a: pl.BlockSpec(a.shape, lambda i: (0,) * a.ndim)
    like = lambda a: jax.ShapeDtypeStruct(a.shape, F32)
    return pl.pallas_call(
        functools.partial(update_kernel, owners=NMAT // per),
        grid=(per,),
        in_specs=[mat] * 6
        + [pl.BlockSpec(memory_space=pltpu.SMEM)]
        + [whole(a) for a in (vsum, vec, vmom, ssum, stu, smom, csum, cls, cmom)],
        out_specs=[mat] * 4 + [whole(a) for a in (vec,) * 3 + (stu,) * 3 + (cls,) * 3],
        out_shape=[like(left)] * 4 + [like(a) for a in (vec,) * 3 + (stu,) * 3 + (cls,) * 3],
        compiler_params=pltpu.CompilerParams(vmem_limit_bytes=VMEM),
    )(own, blocks, left, right, lroot, rroot, shard, vsum, vec, vmom, ssum, stu, smom, csum, cls, cmom)


def local(
    tokens,
    cotangent,
    lengths,
    exit_layers,
    teacher,
    blocks,
    left_stats,
    right_stats,
    left_root,
    right_root,
    vectors,
    vec_moment,
    student,
    stu_moment,
    classifier,
    cls_moment,
):
    group = lax.axis_size("batch")
    me = lax.axis_index("batch")
    micro, _, row_len, _ = tokens.shape
    slots = row_len // group
    tokens, cotangent = tokens[:, 0], cotangent[:, 0]
    ends = jnp.cumsum(lengths[:, 0], axis=-1, dtype=jnp.int32)
    live = (exit_layers[:, 0] >= LAYER).astype(jnp.int32)
    info = jnp.concatenate([ends, live], axis=1)
    alive_len = lengths[:, 0] * live
    counts = jnp.sum(alive_len, axis=1, dtype=jnp.int32)
    everyone = lax.all_gather(counts[None, :], "batch", axis=0, tiled=True)
    starts = jnp.cumsum(everyone, axis=0, dtype=jnp.int32) - everyone

    places = jnp.arange(row_len, dtype=jnp.int32)
    before = jnp.cumsum(alive_len, axis=1, dtype=jnp.int32) - alive_len
    sample = jnp.sum((places[None, :, None] >= ends[:, None, : SAMP - 1]).astype(jnp.int32), axis=-1)
    chosen = sample[..., None] == jnp.arange(SAMP, dtype=jnp.int32)
    shift = jnp.sum(jnp.where(chosen, (before - ends + lengths[:, 0])[:, None, :], 0), axis=-1)
    alive_tok = jnp.sum(jnp.where(chosen, live[:, None, :], 0), axis=-1)
    rank = places[None, :] + shift
    send = (starts[me][:, None] + rank) % group * slots + rank // group
    send = jnp.where(alive_tok > 0, send, row_len)
    start_of = jnp.repeat(starts.T, slots, axis=1)
    count_of = jnp.repeat(everyone.T, slots, axis=1)
    turn = (me - start_of) % group + group * (places % slots)[None, :]
    back = jnp.where(turn < count_of, (start_of + turn) // group, row_len)

    grad_outgoing = pick_rows(back[:, :, None], cotangent, group)
    returned = lax.all_to_all(grad_outgoing, "batch", split_axis=0, concat_axis=0, tiled=True)

    matrices = lax.all_gather(blocks, "shard", axis=0, tiled=True)
    vec = lax.all_gather(vectors.astype(BF16), "shard", axis=0, tiled=True).astype(F32)

    a1, q, k, v, o = attend(info, tokens, matrices, vec)
    goals = jnp.concatenate(
        [teacher[:, 0], live[..., None].astype(F32)], axis=-1
    ).reshape(micro * SAMP, CLS + 1)
    da1, outgoing, ff_grads, ff_vecs, stu_grads, cls_grads = feed(
        info, a1, matrices, vec, student, classifier, goals, send, send.reshape(-1, 1), returned
    )
    arrived = lax.all_to_all(outgoing, "batch", split_axis=0, concat_axis=0, tiled=True)
    input_grads, grads, at_vecs = attend_back(
        info, tokens, da1.reshape(micro, row_len, D), q, k, v, o, matrices, ff_grads
    )
    layer_out = place_rows(back[:, None, :], arrived)
    own, vec_sum, stu_sum, cls_sum = reduce_grads(grads, ff_vecs, at_vecs, stu_grads, cls_grads)
    shard = lax.axis_index("shard").astype(jnp.int32).reshape(1)
    updated = update(
        own,
        blocks,
        left_stats,
        right_stats,
        left_root,
        right_root,
        shard,
        vec_sum,
        vectors,
        vec_moment,
        stu_sum,
        student,
        stu_moment,
        cls_sum,
        classifier,
        cls_moment,
    )
    return (layer_out[:, None], input_grads[:, None], *updated)


def solution(mesh):
    rows = P(None, ("batch", "shard"), None, None)
    tags = P(None, ("batch", "shard"), None)
    mats = P("shard", None, None)
    vecs = P("shard", None)
    return jax.shard_map(
        local,
        mesh=mesh,
        in_specs=(rows, rows, tags, tags, rows, mats, mats, mats, mats, mats, vecs, vecs)
        + (P(),) * 4,
        out_specs=(rows, rows, mats, mats, mats, mats, vecs, vecs, vecs) + (P(),) * 6,
        check_vma=False,
    )
```

```python
import functools

import jax
import jax.numpy as jnp
from jax import lax
from jax.experimental import pallas as pl
from jax.experimental.pallas import tpu as pltpu
from jax.sharding import PartitionSpec as P

D = 512
H = 8
DH = 64
FF = 2048
SW = 128
NMAT = 12
SAMP = 4
LAYER = 4
CLS = 14

decay_rate = 0.5
block_rate = 0.04
vector_rate = 0.05
head_rate = 0.05

QT = 256
KG = 128
PAIRS = H // 2
LANES = 128
PART = 512
PARTS, CUT = FF // PART, D // PART
BIG = float(2**30)
EPS = 1e-6
VMEM = 60 * 1024 * 1024

F32 = jnp.float32
BF16 = jnp.bfloat16


def nn(a, b):
    return jnp.dot(a, b, preferred_element_type=F32)


def nt(a, b):
    return lax.dot_general(a, b, (((1,), (1,)), ((), ())), preferred_element_type=F32)


def tn(a, b):
    return lax.dot_general(a, b, (((0,), (0,)), ((), ())), preferred_element_type=F32)


def exact(a, b, dims=(((1,), (0,)), ((), ()))):
    return lax.dot_general(
        a, b, dims, preferred_element_type=F32, precision=lax.Precision.HIGHEST
    )


def row_sum(v):
    return jnp.sum(v, axis=0, keepdims=True)


def two_low(v, b):
    high = v.astype(BF16)
    return nn(high, b) + nn((v - high.astype(F32)).astype(BF16), b)


def split_low(v):
    high = v.astype(BF16).astype(F32)
    rest = v - high
    mid = rest.astype(BF16).astype(F32)
    return high, mid, rest - mid


def ends_of(info, row):
    return [info[row, j] for j in range(SAMP)]


def live_of(info, row):
    return [info[row, SAMP + j] for j in range(SAMP)]


def sample_column(ends, first, count):
    place = first + lax.broadcasted_iota(jnp.int32, (count, 1), 0)
    total = jnp.zeros((count, 1), jnp.int32)
    for j in range(SAMP - 1):
        total = total + (place >= ends[j]).astype(jnp.int32)
    return total


def reach(ends, live, first, count, row_len):
    low, high = jnp.int32(row_len), jnp.int32(0)
    start = jnp.int32(0)
    for j in range(SAMP):
        end = ends[j]
        meets = (start < first + count) & (end > first) & (end > start) & (live[j] > 0)
        low = jnp.where(meets, jnp.minimum(low, start), low)
        high = jnp.where(meets, jnp.maximum(high, end), high)
        start = end
    begin = low // KG
    number = jnp.maximum((high + KG - 1) // KG - begin, 0)
    return begin, number


def lane_index(rows):
    return lax.broadcasted_iota(jnp.int32, (rows, LANES), 1)


TAG = 16


def key_spare(sample, rows, pair):
    lane = lane_index(rows) % DH
    own = (lane < 3 * PAIRS) & (lane % PAIRS == pair)
    return jnp.where(own | (lane == sample + TAG), 1.0, 0.0)


def query_spare(sample, rows):
    lane = lane_index(rows) % DH
    tag = (lane >= TAG) & (lane < TAG + SAMP) & (lane != sample + TAG)
    return jnp.where(tag, -BIG, 0.0)


def store_heads(ref, rows, p, pair, spare, first):
    ref[rows, 2 * p * LANES : (2 * p + 1) * LANES] = jnp.where(first, pair, spare).astype(BF16)
    ref[rows, (2 * p + 1) * LANES : (2 * p + 2) * LANES] = jnp.where(
        first, spare, pair
    ).astype(BF16)


def head_lanes(h):
    return slice(h * LANES, (h + 1) * LANES)


def widths(row_len):
    most = row_len // KG
    return list(range(most // 2, most + 1))


def chosen_span(ends, live, t, row_len):
    begin, number = reach(ends, live, t * QT, QT, row_len)
    least, most = widths(row_len)[0], row_len // KG
    number = jnp.where(number > 0, jnp.maximum(number, least), 0)
    return jnp.minimum(begin, most - number), number


def attend_kernel(info, x_ref, w_ref, vec_ref, q_ref, k_ref, v_ref, o_ref, l_ref, qx, kx, vx):
    row = pl.program_id(0)
    row_len = x_ref.shape[1]
    ends, live = ends_of(info, row), live_of(info, row)
    first = lane_index(QT) < DH
    ones = jnp.ones((QT, LANES), F32)

    @pl.loop(0, row_len // QT)
    def _(t):
        rows = pl.ds(pl.multiple_of(t * QT, QT), QT)
        x = x_ref[0, rows, :]
        sample = sample_column(ends, t * QT, QT)
        q_extra = query_spare(sample, QT)
        q = ((nn(x, w_ref[0]) + vec_ref[0:1, :]).astype(BF16).astype(F32) * DH**-0.5).astype(BF16)
        k = nn(x, w_ref[1]).astype(BF16)
        v = (nn(x, w_ref[2]) + vec_ref[1:2, :]).astype(BF16)
        q_ref[0, rows, :] = q
        k_ref[0, rows, :] = k
        v_ref[0, rows, :] = v
        for p in range(PAIRS):
            pair = head_lanes(p)
            store_heads(qx, rows, p, q[:, pair].astype(F32), q_extra, first)
            store_heads(kx, rows, p, k[:, pair].astype(F32), key_spare(sample, QT, p), first)
            store_heads(vx, rows, p, v[:, pair].astype(F32), ones, first)

    @pl.loop(0, row_len // QT)
    def _(t):
        rows = pl.ds(pl.multiple_of(t * QT, QT), QT)
        begin, number = chosen_span(ends, live, t, row_len)

        @pl.when(number == 0)
        def _():
            o_ref[0, rows, :] = jnp.zeros((QT, D), BF16)
            l_ref[0, rows, :] = jnp.zeros((QT, LANES), F32)

        for n in widths(row_len):

            @pl.when(number == n)
            def _(n=n):
                span = pl.ds(pl.multiple_of(begin * KG, KG), n * KG)
                lane = lane_index(QT)
                scores, powers, got = {}, {}, {}
                peaks = jnp.zeros((QT, LANES), F32)
                totals = jnp.ones((QT, LANES), F32)
                for step in range(H + 2):
                    if step < H:
                        cols = head_lanes(step)
                        scores[step] = nt(qx[rows, cols], kx[span, cols])
                    h = step - 1
                    if 0 <= h < H:
                        s = scores.pop(h)
                        peak = jnp.max(s, axis=1, keepdims=True)
                        powers[h] = jnp.exp(s - peak).astype(BF16)
                        spot = lane == (h // 2 + DH if h % 2 == 0 else h // 2)
                        peaks = jnp.where(spot, peak, peaks)
                    h = step - 2
                    if 0 <= h < H:
                        got[h] = nn(powers.pop(h), vx[span, head_lanes(h)])
                        spot = lane == (h // 2 + DH if h % 2 == 0 else h // 2)
                        totals = jnp.where(spot, got[h], totals)
                        if h % 2 == 1:
                            left, right = got.pop(h - 1), got.pop(h)
                            top = jnp.where(first, left, right)
                            total = pltpu.roll(jnp.where(first, right, left), DH, 1)
                            o_ref[0, rows, head_lanes(h // 2)] = (top / total).astype(BF16)
                l_ref[0, rows, :] = jnp.where(
                    peaks > -0.5 * BIG, peaks + jnp.log(totals), 0.0
                )


def attend(info, tokens, blocks, vec):
    micro, row_len, _ = tokens.shape
    row_spec = lambda width: pl.BlockSpec((1, row_len, width), lambda r: (r, 0, 0))
    low = jax.ShapeDtypeStruct((micro, row_len, D), BF16)
    return pl.pallas_call(
        attend_kernel,
        grid=(micro,),
        in_specs=[
            pl.BlockSpec(memory_space=pltpu.SMEM),
            row_spec(D),
            pl.BlockSpec((3, D, D), lambda r: (0, 0, 0)),
            pl.BlockSpec((NMAT, D), lambda r: (0, 0)),
        ],
        out_specs=[row_spec(D)] * 4 + [row_spec(LANES)],
        out_shape=[low] * 4 + [jax.ShapeDtypeStruct((micro, row_len, LANES), F32)],
        scratch_shapes=[pltpu.VMEM((row_len, 2 * D), BF16)] * 3,
        compiler_params=pltpu.CompilerParams(vmem_limit_bytes=VMEM),
        cost_estimate=pl.CostEstimate(
            flops=micro * row_len * D * D * 6 + micro * H * row_len * row_len * DH * 16,
            bytes_accessed=micro * row_len * D * 16,
            transcendentals=micro * H * row_len * row_len,
        ),
    )(info, tokens, blocks, vec)


def gelu_both(u):
    share = 0.5 + 0.5 * lax.erf(u * 0.5**0.5)
    bell = jnp.exp2((-0.5 * 1.4426950408889634) * (u * u))
    return u * share, share + (u * 0.3989422804014327) * bell


def norm_parts(a):
    center = a - jnp.mean(a, axis=-1, keepdims=True)
    rate = lax.rsqrt(jnp.mean(center * center, axis=-1, keepdims=True) + EPS)
    return center * rate, rate


def norm_back(grad, unit, rate):
    return rate * (
        grad
        - jnp.mean(grad, axis=-1, keepdims=True)
        - unit * jnp.mean(grad * unit, axis=-1, keepdims=True)
    )


def feed_kernel(
    info,
    x_ref,
    o_ref,
    w_ref,
    vec_ref,
    stu_ref,
    cls_ref,
    goal_ref,
    send_row,
    send_col,
    back_ref,
    da1_ref,
    out_ref,
    wg_ref,
    vg_ref,
    sg_ref,
    cg_ref,
    unit1,
    rate1,
    h1b,
    act,
    slope,
    unit2,
    rate2,
    zb,
    head_in,
    head_low,
    *,
    tile,
    micro,
    row_len,
):
    step = pl.program_id(0)
    tiles = micro * row_len // tile
    group, _, slots, _ = out_ref.shape

    @pl.when(step == 0)
    def _():
        vg_ref[...] = jnp.zeros_like(vg_ref)

    @pl.when(step < tiles)
    def _():
        rows = pl.ds(pl.multiple_of(step * tile, tile), tile)
        a1 = x_ref[...].astype(F32) + (nn(o_ref[...], w_ref[3]) + vec_ref[2:3, :])
        unit, rate = norm_parts(a1)
        unit1[rows, :] = unit
        rate1[rows, :] = rate
        h1 = unit * vec_ref[3:4, :] + vec_ref[4:5, :]
        low = h1.astype(BF16)
        h1b[rows, :] = low
        total = h1 + vec_ref[9:10, :]
        raw, value = {}, {}
        for turn in range(PARTS + 2):
            if turn < PARTS:
                c, at = turn // CUT, slice(turn % CUT * PART, (turn % CUT + 1) * PART)
                raw[turn] = nn(low, w_ref[4 + c, :, at]) + vec_ref[5 + c : 6 + c, at]
            if 0 <= turn - 1 < PARTS:
                cols = slice((turn - 1) * PART, turn * PART)
                up, grad = gelu_both(raw.pop(turn - 1))
                value[turn - 1] = up.astype(BF16)
                act[rows, cols] = value[turn - 1]
                slope[rows, cols] = grad.astype(BF16)
            if 0 <= turn - 2 < PARTS:
                c = (turn - 2) // CUT
                at = slice((turn - 2) % CUT * PART, ((turn - 2) % CUT + 1) * PART)
                total = total + nn(value.pop(turn - 2), w_ref[8 + c, at, :])
        unit, rate = norm_parts(total)
        unit2[rows, :] = unit
        rate2[rows, :] = rate
        z = (unit * vec_ref[10:11, :] + vec_ref[11:12, :]).astype(BF16)
        zb[rows, :] = z
        head_in[rows, :] = nn(z, stu_ref[0:D, :].astype(BF16)) + stu_ref[D + SW : D + SW + 1, :]

    @pl.when(step == tiles)
    def _():
        head_phase(
            info, stu_ref, cls_ref, goal_ref, sg_ref, cg_ref, head_in, head_low, micro, row_len
        )
        sg_ref[0:D, :] = tn(zb[...], head_low[...])
        for m in range(micro):
            place = send_row[m : m + 1, :]
            spot = lax.broadcasted_iota(jnp.int32, (group * slots, row_len), 0)
            pick = jnp.where(spot == place, 1.0, 0.0).astype(BF16)
            moved = nn(pick, zb[m * row_len : (m + 1) * row_len, :]).astype(BF16)
            out_ref[:, m] = moved.reshape(group, slots, D)

    @pl.when(step >= tiles)
    def _():
        t = step - tiles
        rows = pl.ds(pl.multiple_of(t * tile, tile), tile)
        m = (t * tile) // row_len
        spot = lax.broadcasted_iota(jnp.int32, (tile, group * slots), 1)
        pick = jnp.where(spot == send_col[...], 1.0, 0.0).astype(BF16)
        dz = nn(pick, back_ref[:, m].reshape(group * slots, D))
        dz = dz + nt(head_low[rows, :], stu_ref[0:D, :].astype(BF16))
        unit = unit2[rows, :]
        vg_ref[10:11, :] += row_sum(dz * unit)
        vg_ref[11:12, :] += row_sum(dz)
        da2 = norm_back(dz * vec_ref[10:11, :], unit, rate2[rows, :])
        low = da2.astype(BF16)
        zb[rows, :] = low
        vg_ref[9:10, :] += row_sum(low.astype(F32))
        dh1 = da2
        raw, value = {}, {}
        for turn in range(PARTS + 2):
            if turn < PARTS:
                c, at = turn // CUT, slice(turn % CUT * PART, (turn % CUT + 1) * PART)
                raw[turn] = nt(low, w_ref[8 + c, at, :])
            if 0 <= turn - 1 < PARTS:
                cols = slice((turn - 1) * PART, turn * PART)
                c = (turn - 1) // CUT
                at = slice((turn - 1) % CUT * PART, ((turn - 1) % CUT + 1) * PART)
                du = (raw.pop(turn - 1) * slope[rows, cols].astype(F32)).astype(BF16)
                value[turn - 1] = du
                slope[rows, cols] = du
                vg_ref[5 + c : 6 + c, at] += row_sum(du.astype(F32))
            if 0 <= turn - 2 < PARTS:
                c = (turn - 2) // CUT
                at = slice((turn - 2) % CUT * PART, ((turn - 2) % CUT + 1) * PART)
                dh1 = dh1 + nt(value.pop(turn - 2), w_ref[4 + c, :, at])
        unit = unit1[rows, :]
        vg_ref[3:4, :] += row_sum(dh1 * unit)
        vg_ref[4:5, :] += row_sum(dh1)
        da1_ref[...] = norm_back(dh1 * vec_ref[3:4, :], unit, rate1[rows, :])

    @pl.when(step == 2 * tiles - 1)
    def _():
        for c in range(FF // D):
            cols = slice(c * D, (c + 1) * D)
            wg_ref[c] = tn(h1b[...], slope[:, cols]).astype(BF16)
            wg_ref[4 + c] = tn(act[:, cols], zb[...]).astype(BF16)


def head_phase(info, stu_ref, cls_ref, goal_ref, sg_ref, cg_ref, head_in, head_low, micro, row_len):
    scale = DH**-0.5
    query = stu_ref[D + SW + 2 : D + SW + 3, :]
    same = (
        lax.broadcasted_iota(jnp.int32, (SW, SW), 0) // DH
        == lax.broadcasted_iota(jnp.int32, (SW, SW), 1) // DH
    )
    same = jnp.where(same, 1.0, 0.0).astype(BF16)
    pooled, weights, members = [], [], []
    for m in range(micro):
        rows = slice(m * row_len, (m + 1) * row_len)
        s = head_in[rows, :]
        e = two_low(s * query, same) * scale
        sample = sample_column(ends_of(info, m), 0, row_len)
        share = jnp.zeros_like(e)
        for j in range(SAMP):
            member = sample == j
            peak = jnp.max(jnp.where(member, e, -1e30), axis=0, keepdims=True)
            up = jnp.where(member, jnp.exp(jnp.where(member, e - peak, 0.0)), 0.0)
            up = up / row_sum(up)
            share = share + up
            pooled.append(row_sum(up * s))
            members.append(member)
        weights.append(share)
    pooled = jnp.concatenate(pooled, axis=0)
    pool_weight = stu_ref[D : D + SW, :]
    mixed = jnp.tanh(exact(pooled, pool_weight) + stu_ref[D + SW + 1 : D + SW + 2, :])
    classes = cls_ref[0:SW, :]
    logits = exact(mixed, classes) + cls_ref[SW : SW + 1, :]
    logits = logits - jnp.max(logits, axis=-1, keepdims=True)
    chance = jnp.exp(logits)
    chance = chance / jnp.sum(chance, axis=-1, keepdims=True)
    goal = goal_ref[:, 0:CLS]
    alive = goal_ref[:, CLS : CLS + 1]
    target = jnp.exp(goal - jnp.max(goal, axis=-1, keepdims=True))
    target = target / jnp.sum(target, axis=-1, keepdims=True)
    d_logits = alive * (chance - target)
    cg_ref[0:SW, :] = exact(mixed, d_logits, (((0,), (0,)), ((), ())))
    cg_ref[SW : SW + 1, :] = row_sum(d_logits)
    d_pre = exact(d_logits, classes, (((1,), (1,)), ((), ()))) * (1.0 - mixed * mixed)
    sg_ref[D : D + SW, :] = exact(pooled, d_pre, (((0,), (0,)), ((), ())))
    sg_ref[D + SW + 1 : D + SW + 2, :] = row_sum(d_pre)
    d_pooled = exact(d_pre, pool_weight, (((1,), (1,)), ((), ())))
    inner = two_low(pooled * d_pooled, same)
    d_bias = jnp.zeros((1, SW), F32)
    d_query = jnp.zeros((1, SW), F32)
    for m in range(micro):
        rows = slice(m * row_len, (m + 1) * row_len)
        s = head_in[rows, :]
        spread = jnp.zeros((row_len, SW), F32)
        center = jnp.zeros((row_len, SW), F32)
        for j in range(SAMP):
            member = members[m * SAMP + j]
            at = m * SAMP + j
            spread = jnp.where(member, d_pooled[at : at + 1, :], spread)
            center = jnp.where(member, inner[at : at + 1, :], center)
        share = weights[m]
        d_e = share * (two_low(s * spread, same) - center) * scale
        d_s = (share * spread + d_e * query).astype(BF16)
        head_low[rows, :] = d_s
        d_bias = d_bias + row_sum(d_s.astype(F32))
        d_query = d_query + row_sum(d_e * s)
    sg_ref[D + SW : D + SW + 1, :] = d_bias
    sg_ref[D + SW + 2 : D + SW + 3, :] = d_query


def feed(info, x, o, blocks, vec, student, classifier, goals, send_row, send_col, returned):
    micro, row_len, _ = x.shape
    tokens = micro * row_len
    tile = 512
    tiles = tokens // tile
    group, _, slots, _ = returned.shape
    whole = lambda *shape: pl.BlockSpec(shape, lambda i: (0,) * len(shape))
    once = lambda *shape: pl.BlockSpec(
        shape, lambda i: (0,) * len(shape), pipeline_mode=pl.Buffered(1)
    )
    ahead = lambda width: pl.BlockSpec((tile, width), lambda i: (jnp.minimum(i, tiles - 1), 0))
    behind = lambda width: pl.BlockSpec((tile, width), lambda i: (jnp.maximum(i - tiles, 0), 0))
    return pl.pallas_call(
        functools.partial(feed_kernel, tile=tile, micro=micro, row_len=row_len),
        grid=(2 * tiles,),
        in_specs=[
            pl.BlockSpec(memory_space=pltpu.SMEM),
            ahead(D),
            ahead(D),
            once(NMAT, D, D),
            once(NMAT, D),
            once(*student.shape),
            once(*classifier.shape),
            once(*goals.shape),
            once(*send_row.shape),
            behind(1),
            once(*returned.shape),
        ],
        out_specs=[
            behind(D),
            once(*returned.shape),
            once(8, D, D),
            once(NMAT, D),
            once(*student.shape),
            once(*classifier.shape),
        ],
        out_shape=[
            jax.ShapeDtypeStruct((tokens, D), F32),
            jax.ShapeDtypeStruct(returned.shape, BF16),
            jax.ShapeDtypeStruct((NMAT, D, D), BF16),
            jax.ShapeDtypeStruct((NMAT, D), F32),
            jax.ShapeDtypeStruct(student.shape, F32),
            jax.ShapeDtypeStruct(classifier.shape, F32),
        ],
        scratch_shapes=[
            pltpu.VMEM((tokens, D), F32),
            pltpu.VMEM((tokens, 1), F32),
            pltpu.VMEM((tokens, D), BF16),
            pltpu.VMEM((tokens, FF), BF16),
            pltpu.VMEM((tokens, FF), BF16),
            pltpu.VMEM((tokens, D), F32),
            pltpu.VMEM((tokens, 1), F32),
            pltpu.VMEM((tokens, D), BF16),
            pltpu.VMEM((tokens, SW), F32),
            pltpu.VMEM((tokens, SW), BF16),
        ],
        compiler_params=pltpu.CompilerParams(vmem_limit_bytes=VMEM),
        cost_estimate=pl.CostEstimate(
            flops=tokens * D * FF * 12, bytes_accessed=tokens * D * 16, transcendentals=tokens * FF
        ),
    )(
        info,
        x.reshape(tokens, D),
        o.reshape(tokens, D),
        blocks,
        vec,
        student,
        classifier,
        goals,
        send_row,
        send_col,
        returned,
    )


def attend_back_kernel(
    info,
    x_ref,
    da1_ref,
    q_ref,
    k_ref,
    v_ref,
    o_ref,
    l_ref,
    w_ref,
    _,
    dx_ref,
    wg_ref,
    vg_ref,
    qx,
    kx,
    vx,
    dox,
    dq,
    dk,
    dv,
    wsum,
    *,
    micro,
):
    row = pl.program_id(0)
    row_len = x_ref.shape[1]
    ends, live = ends_of(info, row), live_of(info, row)
    first = lane_index(QT) < DH
    ones = jnp.ones((QT, LANES), F32)

    @pl.when(row == 0)
    def _():
        vg_ref[...] = jnp.zeros_like(vg_ref)
        wsum[...] = jnp.zeros_like(wsum)

    crossed = (
        lax.broadcasted_iota(jnp.int32, (LANES, LANES), 0) // DH
        != lax.broadcasted_iota(jnp.int32, (LANES, LANES), 1) // DH
    )
    crossed = jnp.where(crossed, 1.0, 0.0).astype(BF16)

    dq[...] = jnp.zeros_like(dq)

    @pl.loop(0, row_len // QT)
    def _(t):
        rows = pl.ds(pl.multiple_of(t * QT, QT), QT)
        sample = sample_column(ends, t * QT, QT)
        lane = lane_index(QT) % DH
        high, mid, rest = split_low(jnp.where(lane < PAIRS, -l_ref[0, rows, :], 0.0))
        q_extra = (
            query_spare(sample, QT)
            + high
            + pltpu.roll(mid, PAIRS, 1)
            + pltpu.roll(rest, 2 * PAIRS, 1)
        )
        branch = da1_ref[0, rows, :].astype(BF16)
        vg_ref[2:3, :] += row_sum(branch.astype(F32))
        do = nt(branch, w_ref[3]).astype(BF16).astype(F32)
        inner = do * o_ref[0, rows, :].astype(F32)
        for p in range(PAIRS):
            pair = head_lanes(p)
            high = inner[:, pair].astype(BF16)
            rest = (inner[:, pair] - high.astype(F32)).astype(BF16)
            delta = nn(high, crossed) + nn(rest, crossed)
            high = delta.astype(BF16).astype(F32)
            do_extra = jnp.where(lane == 0, -high, jnp.where(lane == 1, high - delta, 0.0))
            store_heads(dox, rows, p, do[:, pair], do_extra, first)
            store_heads(qx, rows, p, q_ref[0, rows, pair].astype(F32), q_extra, first)
            store_heads(
                kx, rows, p, k_ref[0, rows, pair].astype(F32), key_spare(sample, QT, p), first
            )
            store_heads(vx, rows, p, v_ref[0, rows, pair].astype(F32), ones, first)

    @pl.loop(0, row_len // QT)
    def _(t):
        rows = pl.ds(pl.multiple_of(t * QT, QT), QT)
        begin, number = chosen_span(ends, live, t, row_len)

        @pl.when(number == 0)
        def _():
            dk[rows, :] = jnp.zeros((QT, D), BF16)
            dv[rows, :] = jnp.zeros((QT, D), BF16)

        for n in widths(row_len):

            @pl.when(number == n)
            def _(n=n):
                span = pl.ds(pl.multiple_of(begin * KG, KG), n * KG)
                wide = lane_index(n * KG) < DH
                raw, done, got = {}, {}, {}
                for step in range(H + 2):
                    if step < H:
                        cols = head_lanes(step)
                        raw[step] = (
                            nt(kx[rows, cols], qx[span, cols]),
                            nt(vx[rows, cols], dox[span, cols]),
                        )
                    h = step - 1
                    if 0 <= h < H:
                        s, dp = raw.pop(h)
                        prob = jnp.exp(s)
                        done[h] = (prob.astype(BF16), (prob * dp).astype(BF16))
                    h = step - 2
                    if 0 <= h < H:
                        cols = head_lanes(h)
                        prob, ds = done.pop(h)
                        got[h] = (
                            nn(prob, dox[span, cols]),
                            nn(ds, qx[span, cols]),
                            tn(ds, kx[rows, cols]),
                        )
                        if h % 2 == 1:
                            left, right = got.pop(h - 1), got.pop(h)
                            cols = head_lanes(h // 2)
                            dv[rows, cols] = jnp.where(first, left[0], right[0]).astype(BF16)
                            dk[rows, cols] = jnp.where(first, left[1], right[1]).astype(BF16)
                            dq[span, cols] += jnp.where(wide, left[2], right[2])

    @pl.loop(0, row_len // QT)
    def _(t):
        rows = pl.ds(pl.multiple_of(t * QT, QT), QT)
        dq_low = (dq[rows, :] * DH**-0.5).astype(BF16)
        dk_low, dv_low = dk[rows, :], dv[rows, :]
        vg_ref[0:1, :] += row_sum(dq_low.astype(F32))
        vg_ref[1:2, :] += row_sum(dv_low.astype(F32))
        dx_ref[0, rows, :] = (
            da1_ref[0, rows, :]
            + nt(dq_low, w_ref[0])
            + nt(dk_low, w_ref[1])
            + nt(dv_low, w_ref[2])
        ).astype(BF16)

    x = x_ref[0]
    wsum[0] += tn(x, (dq[...] * DH**-0.5).astype(BF16))
    wsum[1] += tn(x, dk[...])
    wsum[2] += tn(x, dv[...])
    wsum[3] += tn(o_ref[0], da1_ref[0].astype(BF16))

    @pl.when(row == micro - 1)
    def _():
        wg_ref[...] = wsum[...].astype(BF16)


def attend_back(info, tokens, da1, q, k, v, o, logs, blocks, grads):
    micro, row_len, _ = tokens.shape
    row_spec = lambda width: pl.BlockSpec((1, row_len, width), lambda r: (r, 0, 0))
    return pl.pallas_call(
        functools.partial(attend_back_kernel, micro=micro),
        grid=(micro,),
        in_specs=[
            pl.BlockSpec(memory_space=pltpu.SMEM),
            *[row_spec(D)] * 6,
            row_spec(LANES),
            pl.BlockSpec((4, D, D), lambda r: (0, 0, 0)),
            pl.BlockSpec(memory_space=pl.ANY),
        ],
        out_specs=[
            row_spec(D),
            pl.BlockSpec((4, D, D), lambda r: (2, 0, 0)),
            pl.BlockSpec((8, D), lambda r: (0, 0)),
        ],
        out_shape=[
            jax.ShapeDtypeStruct((micro, row_len, D), BF16),
            jax.ShapeDtypeStruct((NMAT, D, D), BF16),
            jax.ShapeDtypeStruct((8, D), F32),
        ],
        scratch_shapes=[
            *[pltpu.VMEM((row_len, 2 * D), BF16)] * 4,
            pltpu.VMEM((row_len, D), F32),
            pltpu.VMEM((row_len, D), BF16),
            pltpu.VMEM((row_len, D), BF16),
            pltpu.VMEM((4, D, D), F32),
        ],
        input_output_aliases={9: 1},
        compiler_params=pltpu.CompilerParams(vmem_limit_bytes=VMEM),
        cost_estimate=pl.CostEstimate(
            flops=micro * row_len * D * D * 16 + micro * H * row_len * row_len * DH * 10,
            bytes_accessed=micro * row_len * D * 16,
            transcendentals=micro * H * row_len * row_len,
        ),
    )(info, tokens, da1, q, k, v, o, logs, blocks, grads)


def pick_kernel(place_ref, rows_ref, out_ref):
    group, _, slots, _ = out_ref.shape
    places = group * slots
    spot = lax.broadcasted_iota(jnp.int32, (places, rows_ref.shape[1]), 1)
    pick = jnp.where(spot == place_ref[0], 1.0, 0.0).astype(BF16)
    out_ref[:, 0] = nn(pick, rows_ref[0]).astype(BF16).reshape(group, slots, D)


def pick_rows(place_col, rows, group):
    micro, row_len, _ = rows.shape
    slots = row_len // group
    return pl.pallas_call(
        pick_kernel,
        grid=(micro,),
        in_specs=[
            pl.BlockSpec((1, row_len, 1), lambda m: (m, 0, 0)),
            pl.BlockSpec((1, row_len, D), lambda m: (m, 0, 0)),
        ],
        out_specs=pl.BlockSpec((group, 1, slots, D), lambda m: (0, m, 0, 0)),
        out_shape=jax.ShapeDtypeStruct((group, micro, slots, D), BF16),
        compiler_params=pltpu.CompilerParams(vmem_limit_bytes=VMEM),
    )(place_col, rows)


def place_kernel(place_ref, rows_ref, out_ref):
    row_len = out_ref.shape[1]
    spot = lax.broadcasted_iota(jnp.int32, (row_len, row_len), 0)
    pick = jnp.where(spot == place_ref[0], 1.0, 0.0).astype(BF16)
    out_ref[0] = nn(pick, rows_ref[:, 0].reshape(row_len, D)).astype(BF16)


def place_rows(place_row, rows):
    group, micro, slots, _ = rows.shape
    row_len = group * slots
    return pl.pallas_call(
        place_kernel,
        grid=(micro,),
        in_specs=[
            pl.BlockSpec((1, 1, row_len), lambda m: (m, 0, 0)),
            pl.BlockSpec((group, 1, slots, D), lambda m: (0, m, 0, 0)),
        ],
        out_specs=pl.BlockSpec((1, row_len, D), lambda m: (m, 0, 0)),
        out_shape=jax.ShapeDtypeStruct((micro, row_len, D), BF16),
        compiler_params=pltpu.CompilerParams(vmem_limit_bytes=VMEM),
    )(place_row, rows)


CHUNKS = 6
STU_ROWS, CLS_ROWS, VEC_ROWS = 656, 144, 16
SMALL_ROWS = STU_ROWS + CLS_ROWS + 4 * VEC_ROWS


def bits_of(size):
    return [1 << i for i in range(size.bit_length() - 1)]


def reduce_kernel(
    group,
    owners,
    grad_ref,
    ff_vec,
    at_vec,
    stu_ref,
    cls_ref,
    own_ref,
    vec_out,
    stu_out,
    cls_out,
    got_a,
    sum_a,
    got_b,
    part,
    got_c,
    final,
    small,
    small_got,
    small_sum,
    small_end,
    send_sem,
    recv_sem,
    small_send,
    small_recv,
):
    b, s = lax.axis_index("batch"), lax.axis_index("shard")
    per = NMAT // owners
    rows = per * D // CHUNKS
    batch_bits, shard_bits = bits_of(group), bits_of(owners)
    half = SMALL_ROWS // 2

    def copy(src, dst, sems, at, where):
        return pltpu.make_async_remote_copy(
            src_ref=src,
            dst_ref=dst,
            send_sem=sems[0].at[at],
            recv_sem=sems[1].at[at],
            device_id=where,
            device_id_type=pl.DeviceIdType.MESH,
        )

    peers = [(b, s ^ bit) for bit in shard_bits] + [(b ^ bit, s) for bit in batch_bits]
    barrier = pltpu.get_barrier_semaphore()
    for peer in peers:
        pl.semaphore_signal(
            barrier, inc=1, device_id=peer, device_id_type=pl.DeviceIdType.MESH
        )
    pl.semaphore_wait(barrier, len(peers))

    sems = (send_sem, recv_sem)
    small_sems = (small_send, small_recv)
    waits = []

    def begin(op):
        op.start()
        waits.append(op)
        return op

    def piece(owner, c):
        at = lax.rem(owner * per + c * per // CHUNKS + 8, NMAT)
        if rows == D:
            return grad_ref.at[at]
        step = D // rows
        return grad_ref.at[at, pl.ds((c % step) * rows, rows)]

    far = shard_bits[1]
    first = {}
    for c in range(CHUNKS):
        first[c] = [
            begin(copy(piece(s ^ 1 ^ far, c), got_a.at[c, 0], sems, (c, 0), peers[0])),
            begin(copy(piece(s ^ 1, c), got_a.at[c, 1], sems, (c, 1), peers[0])),
        ]

    small[...] = jnp.zeros_like(small)
    stu_count, cls_count = stu_ref.shape[0], cls_ref.shape[0]
    small[0:stu_count, :] = stu_ref[...].astype(BF16)
    small[STU_ROWS : STU_ROWS + cls_count, 0:CLS] = cls_ref[...].astype(BF16)
    for i in range(4):
        at = STU_ROWS + CLS_ROWS + i * VEC_ROWS
        lanes = slice(i * LANES, (i + 1) * LANES)
        small[at : at + 3, :] = at_vec[0:3, lanes].astype(BF16)
        small[at + 3 : at + NMAT, :] = ff_vec[3:NMAT, lanes].astype(BF16)
    core = lax.rem(s, 2)
    mine = pl.ds(pl.multiple_of(core * half, 16), half)
    other = pl.ds(pl.multiple_of((1 - core) * half, 16), half)
    small_op = begin(copy(small.at[other], small_got.at[0], small_sems, 0, peers[0]))

    def add(x, y):
        return (x.astype(F32) + y.astype(F32)).astype(BF16)

    second = {}

    def start_second(c):
        for i, op in enumerate(first[c]):
            op.wait_recv()
            owner = s ^ far if i == 0 else s
            sum_a[c, i] = add(piece(owner, c)[...], got_a[c, i])
        second[c] = begin(copy(sum_a.at[c, 0], got_b.at[c], sems, (c, 2), peers[1]))

    start_second(0)
    start_second(1)

    spans = []
    size = rows
    for bit in batch_bits:
        halving = size >= 32
        spans.append((bit, size, halving))
        if halving:
            size //= 2
    offset_of = []
    offset = jnp.int32(0)
    slot_of = []
    slot = 0
    for bit, now, halving in spans:
        place = lax.rem(b // bit, 2)
        offset_of.append((offset, place))
        slot_of.append(slot)
        if halving:
            offset = offset + place * (now // 2)
            slot += now // 2
        else:
            slot += now
    last = offset

    def ranged(ref, c, start, count):
        return ref.at[c, pl.ds(pl.multiple_of(start, 16), count)]

    moving = {}

    def start_batch(c, k):
        bit, now, halving = spans[k]
        start, place = offset_of[k]
        if halving:
            count = now // 2
            src = ranged(part.at[k], c, start + (1 - place) * count, count)
        else:
            count = now
            src = ranged(part.at[k], c, start, count)
        dst = got_c.at[c, pl.ds(slot_of[k], count)]
        moving[c, k] = begin(copy(src, dst, sems, (c, 3 + k), (b ^ bit, s)))

    def end_batch(c, k):
        bit, now, halving = spans[k]
        start, place = offset_of[k]
        moving[c, k].wait_recv()
        count = now // 2 if halving else now
        if halving:
            start = start + place * count
        here = pl.ds(pl.multiple_of(start, 16), count)
        total = add(part[k, c, here, :], got_c[c, slot_of[k] : slot_of[k] + count])
        if k + 1 < len(spans):
            part[k + 1, c, here, :] = total
        else:
            final[c, here, :] = total

    gathers = [k for k in reversed(range(len(spans))) if spans[k][2]]
    gathering = {}

    def start_gather(c, g):
        k = gathers[g]
        bit, now, _ = spans[k]
        start, place = offset_of[k]
        count = now // 2
        at = ranged(final, c, start + place * count, count)
        gathering[c, g] = begin(
            copy(at, at, sems, (c, 3 + len(spans) + g), (b ^ bit, s))
        )

    def stage(c, k):
        if k == 0:
            second[c].wait_recv()
            if c + 2 < CHUNKS:
                start_second(c + 2)
            part[0, c] = add(sum_a[c, 1], got_b[c])
            start_batch(c, 0)
        elif k <= len(spans):
            end_batch(c, k - 1)
            if k < len(spans):
                start_batch(c, k)
            else:
                start_gather(c, 0)
        else:
            g = k - len(spans) - 1
            gathering[c, g].wait_recv()
            if g + 1 < len(gathers):
                start_gather(c, g + 1)
            else:
                per_block = CHUNKS // per
                block, within = c // per_block, c % per_block
                own_ref[block, within * rows : (within + 1) * rows, :] = final[c]

    stages = 1 + len(spans) + len(gathers)
    rest = [(b, s ^ bit) for bit in shard_bits[1:]] + [(b ^ bit, s) for bit in batch_bits]

    def small_stage(k):
        nonlocal small_op
        small_op.wait_recv()
        if k == 0:
            small_sum[0] = add(small[mine, :], small_got[0])
        elif k <= len(rest):
            small_sum[k] = add(small_sum[k - 1], small_got[k])
        if k < len(rest):
            small_op = begin(
                copy(small_sum.at[k], small_got.at[k + 1], small_sems, k + 1, rest[k])
            )
        elif k == len(rest):
            small_end[mine, :] = small_sum[k]
            small_op = begin(
                copy(small_sum.at[k], small_end.at[mine], small_sems, k + 1, peers[0])
            )

    small_k = 0
    for tick in range(CHUNKS + stages - 1):
        for k in reversed(range(stages)):
            c = tick - k
            if 0 <= c < CHUNKS:
                stage(c, k)
        if small_k <= len(rest) + 1:
            small_stage(small_k)
            small_k += 1
    while small_k <= len(rest) + 1:
        small_stage(small_k)
        small_k += 1

    for i in range(4):
        at = STU_ROWS + CLS_ROWS + i * VEC_ROWS
        lanes = slice(i * LANES, (i + 1) * LANES)
        vec_out[:, lanes] = small_end[at : at + VEC_ROWS, :].astype(F32)
    stu_out[...] = small_end[0:STU_ROWS, :].astype(F32)
    cls_out[...] = small_end[STU_ROWS : STU_ROWS + CLS_ROWS, :].astype(F32)
    for op in waits:
        op.wait_send()


def reduce_grads(grads, ff_vec, at_vec, stu, cls):
    group, owners = lax.axis_size("batch"), lax.axis_size("shard")
    per = NMAT // owners
    rows = per * D // CHUNKS
    batch_count = len(bits_of(group))
    copies = 3 + 2 * batch_count
    small_count = len(bits_of(owners)) + batch_count + 1
    vmem = pl.BlockSpec(memory_space=pltpu.VMEM)
    return pl.pallas_call(
        functools.partial(reduce_kernel, group, owners),
        in_specs=[vmem] * 5,
        out_specs=[vmem] * 4,
        out_shape=[
            jax.ShapeDtypeStruct((per, D, D), BF16),
            jax.ShapeDtypeStruct((VEC_ROWS, D), F32),
            jax.ShapeDtypeStruct((STU_ROWS, SW), F32),
            jax.ShapeDtypeStruct((CLS_ROWS, LANES), F32),
        ],
        scratch_shapes=[
            pltpu.VMEM((CHUNKS, 2, rows, D), BF16),
            pltpu.VMEM((CHUNKS, 2, rows, D), BF16),
            pltpu.VMEM((CHUNKS, rows, D), BF16),
            pltpu.VMEM((batch_count, CHUNKS, rows, D), BF16),
            pltpu.VMEM((CHUNKS, rows + 16 * batch_count, D), BF16),
            pltpu.VMEM((CHUNKS, rows, D), BF16),
            pltpu.VMEM((SMALL_ROWS, LANES), BF16),
            pltpu.VMEM((small_count - 1, SMALL_ROWS // 2, LANES), BF16),
            pltpu.VMEM((small_count - 1, SMALL_ROWS // 2, LANES), BF16),
            pltpu.VMEM((SMALL_ROWS, LANES), BF16),
            pltpu.SemaphoreType.DMA((CHUNKS, copies)),
            pltpu.SemaphoreType.DMA((CHUNKS, copies)),
            pltpu.SemaphoreType.DMA((small_count,)),
            pltpu.SemaphoreType.DMA((small_count,)),
        ],
        compiler_params=pltpu.CompilerParams(
            collective_id=1, has_side_effects=True, vmem_limit_bytes=VMEM
        ),
        cost_estimate=pl.CostEstimate(
            flops=NMAT * D * D * 4, bytes_accessed=NMAT * D * D * 8, transcendentals=0
        ),
    )(grads, ff_vec, at_vec, stu, cls)


def update_kernel(
    own_ref,
    blocks_ref,
    left_ref,
    right_ref,
    lroot_ref,
    rroot_ref,
    shard_ref,
    vsum_ref,
    vec_ref,
    vmom_ref,
    ssum_ref,
    stu_ref,
    smom_ref,
    csum_ref,
    cls_ref,
    cmom_ref,
    grad_out,
    new_out,
    left_out,
    right_out,
    vg_out,
    vm_out,
    v_out,
    sg_out,
    sm_out,
    s_out,
    cg_out,
    cm_out,
    c_out,
    *,
    owners,
):
    g = own_ref[0]
    grad_out[0] = g.astype(F32)
    left_out[0] = decay_rate * left_ref[0] + (1.0 - decay_rate) * nt(g, g)
    right_out[0] = decay_rate * right_ref[0] + (1.0 - decay_rate) * tn(g, g)
    steered = nn(lroot_ref[0].astype(BF16), g).astype(BF16)
    steered = nn(steered, rroot_ref[0].astype(BF16))
    size = jnp.mean(steered * steered, keepdims=True)
    new_out[0] = blocks_ref[0].astype(F32) - steered * (block_rate * lax.rsqrt(size + 1e-06))

    @pl.when(pl.program_id(0) == 0)
    def _():
        per = NMAT // owners
        mine = vsum_ref[0:per, :]
        for i in range(1, owners):
            mine = jnp.where(shard_ref[0] == i, vsum_ref[i * per : (i + 1) * per, :], mine)

        def rule(grads, old, moment, rate, outs):
            renewed = decay_rate * moment + (1.0 - decay_rate) * grads * grads
            outs[0][...] = grads
            outs[1][...] = renewed
            outs[2][...] = old - rate * grads / (jnp.sqrt(renewed) + 1e-08)

        rule(mine, vec_ref[...], vmom_ref[...], vector_rate, (vg_out, vm_out, v_out))
        rule(
            ssum_ref[0 : stu_ref.shape[0], :],
            stu_ref[...],
            smom_ref[...],
            head_rate,
            (sg_out, sm_out, s_out),
        )
        rule(
            csum_ref[0 : cls_ref.shape[0], 0:CLS],
            cls_ref[...],
            cmom_ref[...],
            head_rate,
            (cg_out, cm_out, c_out),
        )


def update(own, blocks, left, right, lroot, rroot, shard, vsum, vec, vmom, ssum, stu, smom, csum, cls, cmom):
    per = own.shape[0]
    mat = pl.BlockSpec((1, D, D), lambda i: (i, 0, 0))
    whole = lambda a: pl.BlockSpec(a.shape, lambda i: (0,) * a.ndim)
    like = lambda a: jax.ShapeDtypeStruct(a.shape, F32)
    return pl.pallas_call(
        functools.partial(update_kernel, owners=NMAT // per),
        grid=(per,),
        in_specs=[mat] * 6
        + [pl.BlockSpec(memory_space=pltpu.SMEM)]
        + [whole(a) for a in (vsum, vec, vmom, ssum, stu, smom, csum, cls, cmom)],
        out_specs=[mat] * 4 + [whole(a) for a in (vec,) * 3 + (stu,) * 3 + (cls,) * 3],
        out_shape=[like(left)] * 4 + [like(a) for a in (vec,) * 3 + (stu,) * 3 + (cls,) * 3],
        compiler_params=pltpu.CompilerParams(vmem_limit_bytes=VMEM),
    )(own, blocks, left, right, lroot, rroot, shard, vsum, vec, vmom, ssum, stu, smom, csum, cls, cmom)


def local(
    tokens,
    cotangent,
    lengths,
    exit_layers,
    teacher,
    blocks,
    left_stats,
    right_stats,
    left_root,
    right_root,
    vectors,
    vec_moment,
    student,
    stu_moment,
    classifier,
    cls_moment,
):
    group = lax.axis_size("batch")
    me = lax.axis_index("batch")
    micro, _, row_len, _ = tokens.shape
    slots = row_len // group
    tokens, cotangent = tokens[:, 0], cotangent[:, 0]
    ends = jnp.cumsum(lengths[:, 0], axis=-1, dtype=jnp.int32)
    live = (exit_layers[:, 0] >= LAYER).astype(jnp.int32)
    info = jnp.concatenate([ends, live], axis=1)
    alive_len = lengths[:, 0] * live
    counts = jnp.sum(alive_len, axis=1, dtype=jnp.int32)
    everyone = lax.all_gather(counts[None, :], "batch", axis=0, tiled=True)
    starts = jnp.cumsum(everyone, axis=0, dtype=jnp.int32) - everyone

    places = jnp.arange(row_len, dtype=jnp.int32)
    before = jnp.cumsum(alive_len, axis=1, dtype=jnp.int32) - alive_len
    sample = jnp.sum((places[None, :, None] >= ends[:, None, : SAMP - 1]).astype(jnp.int32), axis=-1)
    chosen = sample[..., None] == jnp.arange(SAMP, dtype=jnp.int32)
    shift = jnp.sum(jnp.where(chosen, (before - ends + lengths[:, 0])[:, None, :], 0), axis=-1)
    alive_tok = jnp.sum(jnp.where(chosen, live[:, None, :], 0), axis=-1)
    rank = places[None, :] + shift
    send = (starts[me][:, None] + rank) % group * slots + rank // group
    send = jnp.where(alive_tok > 0, send, row_len)
    start_of = jnp.repeat(starts.T, slots, axis=1)
    count_of = jnp.repeat(everyone.T, slots, axis=1)
    turn = (me - start_of) % group + group * (places % slots)[None, :]
    back = jnp.where(turn < count_of, (start_of + turn) // group, row_len)

    grad_outgoing = pick_rows(back[:, :, None], cotangent, group)
    returned = lax.all_to_all(grad_outgoing, "batch", split_axis=0, concat_axis=0, tiled=True)

    matrices = lax.all_gather(blocks, "shard", axis=0, tiled=True)
    vec = lax.all_gather(vectors.astype(BF16), "shard", axis=0, tiled=True).astype(F32)

    q, k, v, o, logs = attend(info, tokens, matrices, vec)
    goals = jnp.concatenate(
        [teacher[:, 0], live[..., None].astype(F32)], axis=-1
    ).reshape(micro * SAMP, CLS + 1)
    da1, outgoing, ff_grads, ff_vecs, stu_grads, cls_grads = feed(
        info, tokens, o, matrices, vec, student, classifier, goals, send, send.reshape(-1, 1), returned
    )
    arrived = lax.all_to_all(outgoing, "batch", split_axis=0, concat_axis=0, tiled=True)
    input_grads, grads, at_vecs = attend_back(
        info, tokens, da1.reshape(micro, row_len, D), q, k, v, o, logs, matrices, ff_grads
    )
    layer_out = place_rows(back[:, None, :], arrived)
    own, vec_sum, stu_sum, cls_sum = reduce_grads(grads, ff_vecs, at_vecs, stu_grads, cls_grads)
    shard = lax.axis_index("shard").astype(jnp.int32).reshape(1)
    updated = update(
        own,
        blocks,
        left_stats,
        right_stats,
        left_root,
        right_root,
        shard,
        vec_sum,
        vectors,
        vec_moment,
        stu_sum,
        student,
        stu_moment,
        cls_sum,
        classifier,
        cls_moment,
    )
    return (layer_out[:, None], input_grads[:, None], *updated)


def solution(mesh):
    rows = P(None, ("batch", "shard"), None, None)
    tags = P(None, ("batch", "shard"), None)
    mats = P("shard", None, None)
    vecs = P("shard", None)
    return jax.shard_map(
        local,
        mesh=mesh,
        in_specs=(rows, rows, tags, tags, rows, mats, mats, mats, mats, mats, vecs, vecs)
        + (P(),) * 4,
        out_specs=(rows, rows, mats, mats, mats, mats, vecs, vecs, vecs) + (P(),) * 6,
        check_vma=False,
    )
```

```python
import functools

import jax
import jax.numpy as jnp
from jax import lax
from jax.experimental import pallas as pl
from jax.experimental.pallas import tpu as pltpu
from jax.sharding import PartitionSpec as P

D = 512
H = 8
DH = 64
FF = 2048
SW = 128
NMAT = 12
SAMP = 4
LAYER = 4
CLS = 14

decay_rate = 0.5
block_rate = 0.04
vector_rate = 0.05
head_rate = 0.05

QT = 256
STEP = 2
KG = 128
PAIRS = H // 2
LANES = 128
PART = 512
PARTS, CUT = FF // PART, D // PART
BIG = float(2**30)
EPS = 1e-6
VMEM = 60 * 1024 * 1024

F32 = jnp.float32
BF16 = jnp.bfloat16


def nn(a, b):
    return jnp.dot(a, b, preferred_element_type=F32)


def nt(a, b):
    return lax.dot_general(a, b, (((1,), (1,)), ((), ())), preferred_element_type=F32)


def tn(a, b):
    return lax.dot_general(a, b, (((0,), (0,)), ((), ())), preferred_element_type=F32)


def exact(a, b, dims=(((1,), (0,)), ((), ()))):
    return lax.dot_general(
        a, b, dims, preferred_element_type=F32, precision=lax.Precision.HIGHEST
    )


def row_sum(v):
    return jnp.sum(v, axis=0, keepdims=True)


def two_low(v, b):
    high = v.astype(BF16)
    return nn(high, b) + nn((v - high.astype(F32)).astype(BF16), b)


def split_low(v):
    high = v.astype(BF16).astype(F32)
    rest = v - high
    mid = rest.astype(BF16).astype(F32)
    return high, mid, rest - mid


def ends_of(info, row):
    return [info[row, j] for j in range(SAMP)]


def live_of(info, row):
    return [info[row, SAMP + j] for j in range(SAMP)]


def sample_column(ends, first, count):
    place = first + lax.broadcasted_iota(jnp.int32, (count, 1), 0)
    total = jnp.zeros((count, 1), jnp.int32)
    for j in range(SAMP - 1):
        total = total + (place >= ends[j]).astype(jnp.int32)
    return total


def reach(ends, live, first, count, row_len):
    low, high = jnp.int32(row_len), jnp.int32(0)
    start = jnp.int32(0)
    for j in range(SAMP):
        end = ends[j]
        meets = (start < first + count) & (end > first) & (end > start) & (live[j] > 0)
        low = jnp.where(meets, jnp.minimum(low, start), low)
        high = jnp.where(meets, jnp.maximum(high, end), high)
        start = end
    begin = low // KG
    number = jnp.maximum((high + KG - 1) // KG - begin, 0)
    return begin, number


def lane_index(rows):
    return lax.broadcasted_iota(jnp.int32, (rows, LANES), 1)


TAG = 16


def key_spare(sample, rows, pair):
    lane = lane_index(rows) % DH
    own = (lane < 3 * PAIRS) & (lane % PAIRS == pair)
    return jnp.where(own | (lane == sample + TAG), 1.0, 0.0)


def query_spare(sample, rows):
    lane = lane_index(rows) % DH
    tag = (lane >= TAG) & (lane < TAG + SAMP) & (lane != sample + TAG)
    return jnp.where(tag, -BIG, 0.0)


def store_heads(ref, rows, p, pair, spare, first):
    ref[rows, 2 * p * LANES : (2 * p + 1) * LANES] = jnp.where(first, pair, spare).astype(BF16)
    ref[rows, (2 * p + 1) * LANES : (2 * p + 2) * LANES] = jnp.where(
        first, spare, pair
    ).astype(BF16)


def head_lanes(h):
    return slice(h * LANES, (h + 1) * LANES)


def widths(row_len):
    most = row_len // KG
    return list(range(most // 2, most + 1))


def chosen_span(ends, live, t, row_len):
    begin, number = reach(ends, live, t * QT, QT, row_len)
    least, most = widths(row_len)[0], row_len // KG
    number = jnp.where(number > 0, jnp.maximum(number, least), 0)
    return jnp.minimum(begin, most - number), number


def attend_kernel(info, x_ref, w_ref, vec_ref, q_ref, k_ref, v_ref, o_ref, l_ref, qx, kx, vx):
    row = pl.program_id(0)
    row_len = x_ref.shape[1]
    ends, live = ends_of(info, row), live_of(info, row)
    first = lane_index(QT) < DH
    ones = jnp.ones((QT, LANES), F32)

    @pl.loop(0, row_len // QT)
    def _(t):
        rows = pl.ds(pl.multiple_of(t * QT, QT), QT)
        x = x_ref[0, rows, :]
        sample = sample_column(ends, t * QT, QT)
        q_extra = query_spare(sample, QT)
        q = ((nn(x, w_ref[0]) + vec_ref[0:1, :]).astype(BF16).astype(F32) * DH**-0.5).astype(BF16)
        k = nn(x, w_ref[1]).astype(BF16)
        v = (nn(x, w_ref[2]) + vec_ref[1:2, :]).astype(BF16)
        q_ref[0, rows, :] = q
        k_ref[0, rows, :] = k
        v_ref[0, rows, :] = v
        for p in range(PAIRS):
            pair = head_lanes(p)
            store_heads(qx, rows, p, q[:, pair].astype(F32), q_extra, first)
            store_heads(kx, rows, p, k[:, pair].astype(F32), key_spare(sample, QT, p), first)
            store_heads(vx, rows, p, v[:, pair].astype(F32), ones, first)

    @pl.loop(0, row_len // QT)
    def _(t):
        rows = pl.ds(pl.multiple_of(t * QT, QT), QT)
        begin, number = chosen_span(ends, live, t, row_len)

        @pl.when(number == 0)
        def _():
            o_ref[0, rows, :] = jnp.zeros((QT, D), BF16)
            l_ref[0, rows, :] = jnp.zeros((QT, LANES), F32)

        for n in widths(row_len):

            @pl.when(number == n)
            def _(n=n):
                span = pl.ds(pl.multiple_of(begin * KG, KG), n * KG)
                lane = lane_index(QT)
                scores, powers, got = {}, {}, {}
                peaks = jnp.zeros((QT, LANES), F32)
                totals = jnp.ones((QT, LANES), F32)
                for step in range(H + 2):
                    if step < H:
                        cols = head_lanes(step)
                        scores[step] = nt(qx[rows, cols], kx[span, cols])
                    h = step - 1
                    if 0 <= h < H:
                        s = scores.pop(h)
                        peak = jnp.max(s, axis=1, keepdims=True)
                        powers[h] = jnp.exp(s - peak).astype(BF16)
                        spot = lane == (h // 2 + DH if h % 2 == 0 else h // 2)
                        peaks = jnp.where(spot, peak, peaks)
                    h = step - 2
                    if 0 <= h < H:
                        got[h] = nn(powers.pop(h), vx[span, head_lanes(h)])
                        spot = lane == (h // 2 + DH if h % 2 == 0 else h // 2)
                        totals = jnp.where(spot, got[h], totals)
                        if h % 2 == 1:
                            left, right = got.pop(h - 1), got.pop(h)
                            top = jnp.where(first, left, right)
                            total = pltpu.roll(jnp.where(first, right, left), DH, 1)
                            o_ref[0, rows, head_lanes(h // 2)] = (top / total).astype(BF16)
                l_ref[0, rows, :] = jnp.where(
                    peaks > -0.5 * BIG, peaks + jnp.log(totals), 0.0
                )


def attend(info, tokens, blocks, vec):
    micro, row_len, _ = tokens.shape
    row_spec = lambda width: pl.BlockSpec((1, row_len, width), lambda r: (r, 0, 0))
    low = jax.ShapeDtypeStruct((micro, row_len, D), BF16)
    return pl.pallas_call(
        attend_kernel,
        grid=(micro,),
        in_specs=[
            pl.BlockSpec(memory_space=pltpu.SMEM),
            row_spec(D),
            pl.BlockSpec((3, D, D), lambda r: (0, 0, 0)),
            pl.BlockSpec((NMAT, D), lambda r: (0, 0)),
        ],
        out_specs=[row_spec(D)] * 4 + [row_spec(LANES)],
        out_shape=[low] * 4 + [jax.ShapeDtypeStruct((micro, row_len, LANES), F32)],
        scratch_shapes=[pltpu.VMEM((row_len, 2 * D), BF16)] * 3,
        compiler_params=pltpu.CompilerParams(vmem_limit_bytes=VMEM),
        cost_estimate=pl.CostEstimate(
            flops=micro * row_len * D * D * 6 + micro * H * row_len * row_len * DH * 16,
            bytes_accessed=micro * row_len * D * 16,
            transcendentals=micro * H * row_len * row_len,
        ),
    )(info, tokens, blocks, vec)


def gelu_both(u):
    share = 0.5 + 0.5 * lax.erf(u * 0.5**0.5)
    bell = jnp.exp2((-0.5 * 1.4426950408889634) * (u * u))
    return u * share, share + (u * 0.3989422804014327) * bell


def norm_parts(a):
    center = a - jnp.mean(a, axis=-1, keepdims=True)
    rate = lax.rsqrt(jnp.mean(center * center, axis=-1, keepdims=True) + EPS)
    return center * rate, rate


def norm_back(grad, unit, rate):
    return rate * (
        grad
        - jnp.mean(grad, axis=-1, keepdims=True)
        - unit * jnp.mean(grad * unit, axis=-1, keepdims=True)
    )


def feed_kernel(
    info,
    x_ref,
    o_ref,
    w_ref,
    vec_ref,
    stu_ref,
    cls_ref,
    goal_ref,
    send_row,
    send_col,
    back_ref,
    da1_ref,
    out_ref,
    wg_ref,
    vg_ref,
    sg_ref,
    cg_ref,
    unit1,
    rate1,
    h1b,
    act,
    slope,
    unit2,
    rate2,
    zb,
    head_in,
    head_low,
    *,
    tile,
    micro,
    row_len,
):
    step = pl.program_id(0)
    tiles = micro * row_len // tile
    group, _, slots, _ = out_ref.shape

    @pl.when(step == 0)
    def _():
        vg_ref[...] = jnp.zeros_like(vg_ref)

    @pl.when(step < tiles)
    def _():
        rows = pl.ds(pl.multiple_of(step * tile, tile), tile)
        a1 = x_ref[...].astype(F32) + (nn(o_ref[...], w_ref[3]) + vec_ref[2:3, :])
        unit, rate = norm_parts(a1)
        unit1[rows, :] = unit
        rate1[rows, :] = rate
        h1 = unit * vec_ref[3:4, :] + vec_ref[4:5, :]
        low = h1.astype(BF16)
        h1b[rows, :] = low
        total = h1 + vec_ref[9:10, :]
        raw, value = {}, {}
        for turn in range(PARTS + 2):
            if turn < PARTS:
                c, at = turn // CUT, slice(turn % CUT * PART, (turn % CUT + 1) * PART)
                raw[turn] = nn(low, w_ref[4 + c, :, at]) + vec_ref[5 + c : 6 + c, at]
            if 0 <= turn - 1 < PARTS:
                cols = slice((turn - 1) * PART, turn * PART)
                up, grad = gelu_both(raw.pop(turn - 1))
                value[turn - 1] = up.astype(BF16)
                act[rows, cols] = value[turn - 1]
                slope[rows, cols] = grad.astype(BF16)
            if 0 <= turn - 2 < PARTS:
                c = (turn - 2) // CUT
                at = slice((turn - 2) % CUT * PART, ((turn - 2) % CUT + 1) * PART)
                total = total + nn(value.pop(turn - 2), w_ref[8 + c, at, :])
        unit, rate = norm_parts(total)
        unit2[rows, :] = unit
        rate2[rows, :] = rate
        z = (unit * vec_ref[10:11, :] + vec_ref[11:12, :]).astype(BF16)
        zb[rows, :] = z
        head_in[rows, :] = nn(z, stu_ref[0:D, :].astype(BF16)) + stu_ref[D + SW : D + SW + 1, :]

    @pl.when(step == tiles)
    def _():
        head_phase(
            info, stu_ref, cls_ref, goal_ref, sg_ref, cg_ref, head_in, head_low, micro, row_len
        )
        sg_ref[0:D, :] = tn(zb[...], head_low[...])
        @pl.loop(0, micro)
        def _(m):
            place = send_row[pl.ds(m, 1), :]
            spot = lax.broadcasted_iota(jnp.int32, (group * slots, row_len), 0)
            pick = jnp.where(spot == place, 1.0, 0.0).astype(BF16)
            here = pl.ds(pl.multiple_of(m * row_len, row_len), row_len)
            moved = nn(pick, zb[here, :]).astype(BF16)
            out_ref[:, m] = moved.reshape(group, slots, D)

    @pl.when(step >= tiles)
    def _():
        t = step - tiles
        rows = pl.ds(pl.multiple_of(t * tile, tile), tile)
        m = (t * tile) // row_len
        spot = lax.broadcasted_iota(jnp.int32, (tile, group * slots), 1)
        pick = jnp.where(spot == send_col[...], 1.0, 0.0).astype(BF16)
        dz = nn(pick, back_ref[:, m].reshape(group * slots, D))
        dz = dz + nt(head_low[rows, :], stu_ref[0:D, :].astype(BF16))
        unit = unit2[rows, :]
        vg_ref[10:11, :] += row_sum(dz * unit)
        vg_ref[11:12, :] += row_sum(dz)
        da2 = norm_back(dz * vec_ref[10:11, :], unit, rate2[rows, :])
        low = da2.astype(BF16)
        zb[rows, :] = low
        vg_ref[9:10, :] += row_sum(low.astype(F32))
        dh1 = da2
        raw, value = {}, {}
        for turn in range(PARTS + 2):
            if turn < PARTS:
                c, at = turn // CUT, slice(turn % CUT * PART, (turn % CUT + 1) * PART)
                raw[turn] = nt(low, w_ref[8 + c, at, :])
            if 0 <= turn - 1 < PARTS:
                cols = slice((turn - 1) * PART, turn * PART)
                c = (turn - 1) // CUT
                at = slice((turn - 1) % CUT * PART, ((turn - 1) % CUT + 1) * PART)
                du = (raw.pop(turn - 1) * slope[rows, cols].astype(F32)).astype(BF16)
                value[turn - 1] = du
                slope[rows, cols] = du
                vg_ref[5 + c : 6 + c, at] += row_sum(du.astype(F32))
            if 0 <= turn - 2 < PARTS:
                c = (turn - 2) // CUT
                at = slice((turn - 2) % CUT * PART, ((turn - 2) % CUT + 1) * PART)
                dh1 = dh1 + nt(value.pop(turn - 2), w_ref[4 + c, :, at])
        unit = unit1[rows, :]
        vg_ref[3:4, :] += row_sum(dh1 * unit)
        vg_ref[4:5, :] += row_sum(dh1)
        da1_ref[...] = norm_back(dh1 * vec_ref[3:4, :], unit, rate1[rows, :])

    @pl.when(step == 2 * tiles - 1)
    def _():
        @pl.loop(0, FF // D)
        def _(c):
            cols = pl.ds(pl.multiple_of(c * D, D), D)
            wg_ref[c] = tn(h1b[...], slope[:, cols]).astype(BF16)
            wg_ref[4 + c] = tn(act[:, cols], zb[...]).astype(BF16)


def head_phase(info, stu_ref, cls_ref, goal_ref, sg_ref, cg_ref, head_in, head_low, micro, row_len):
    scale = DH**-0.5
    query = stu_ref[D + SW + 2 : D + SW + 3, :]
    same = (
        lax.broadcasted_iota(jnp.int32, (SW, SW), 0) // DH
        == lax.broadcasted_iota(jnp.int32, (SW, SW), 1) // DH
    )
    same = jnp.where(same, 1.0, 0.0).astype(BF16)
    pooled, weights, members = [], [], []
    for m in range(micro):
        rows = slice(m * row_len, (m + 1) * row_len)
        s = head_in[rows, :]
        e = two_low(s * query, same) * scale
        sample = sample_column(ends_of(info, m), 0, row_len)
        share = jnp.zeros_like(e)
        for j in range(SAMP):
            member = sample == j
            peak = jnp.max(jnp.where(member, e, -1e30), axis=0, keepdims=True)
            up = jnp.where(member, jnp.exp(jnp.where(member, e - peak, 0.0)), 0.0)
            up = up / row_sum(up)
            share = share + up
            pooled.append(row_sum(up * s))
            members.append(member)
        weights.append(share)
    pooled = jnp.concatenate(pooled, axis=0)
    pool_weight = stu_ref[D : D + SW, :]
    mixed = jnp.tanh(exact(pooled, pool_weight) + stu_ref[D + SW + 1 : D + SW + 2, :])
    classes = cls_ref[0:SW, :]
    logits = exact(mixed, classes) + cls_ref[SW : SW + 1, :]
    logits = logits - jnp.max(logits, axis=-1, keepdims=True)
    chance = jnp.exp(logits)
    chance = chance / jnp.sum(chance, axis=-1, keepdims=True)
    goal = goal_ref[:, 0:CLS]
    alive = goal_ref[:, CLS : CLS + 1]
    target = jnp.exp(goal - jnp.max(goal, axis=-1, keepdims=True))
    target = target / jnp.sum(target, axis=-1, keepdims=True)
    d_logits = alive * (chance - target)
    cg_ref[0:SW, :] = exact(mixed, d_logits, (((0,), (0,)), ((), ())))
    cg_ref[SW : SW + 1, :] = row_sum(d_logits)
    d_pre = exact(d_logits, classes, (((1,), (1,)), ((), ()))) * (1.0 - mixed * mixed)
    sg_ref[D : D + SW, :] = exact(pooled, d_pre, (((0,), (0,)), ((), ())))
    sg_ref[D + SW + 1 : D + SW + 2, :] = row_sum(d_pre)
    d_pooled = exact(d_pre, pool_weight, (((1,), (1,)), ((), ())))
    inner = two_low(pooled * d_pooled, same)
    d_bias = jnp.zeros((1, SW), F32)
    d_query = jnp.zeros((1, SW), F32)
    for m in range(micro):
        rows = slice(m * row_len, (m + 1) * row_len)
        s = head_in[rows, :]
        spread = jnp.zeros((row_len, SW), F32)
        center = jnp.zeros((row_len, SW), F32)
        for j in range(SAMP):
            member = members[m * SAMP + j]
            at = m * SAMP + j
            spread = jnp.where(member, d_pooled[at : at + 1, :], spread)
            center = jnp.where(member, inner[at : at + 1, :], center)
        share = weights[m]
        d_e = share * (two_low(s * spread, same) - center) * scale
        d_s = (share * spread + d_e * query).astype(BF16)
        head_low[rows, :] = d_s
        d_bias = d_bias + row_sum(d_s.astype(F32))
        d_query = d_query + row_sum(d_e * s)
    sg_ref[D + SW : D + SW + 1, :] = d_bias
    sg_ref[D + SW + 2 : D + SW + 3, :] = d_query


def feed(info, x, o, blocks, vec, student, classifier, goals, send_row, send_col, returned):
    micro, row_len, _ = x.shape
    tokens = micro * row_len
    tile = 512
    tiles = tokens // tile
    group, _, slots, _ = returned.shape
    whole = lambda *shape: pl.BlockSpec(shape, lambda i: (0,) * len(shape))
    once = lambda *shape: pl.BlockSpec(
        shape, lambda i: (0,) * len(shape), pipeline_mode=pl.Buffered(1)
    )
    ahead = lambda width: pl.BlockSpec((tile, width), lambda i: (jnp.minimum(i, tiles - 1), 0))
    behind = lambda width: pl.BlockSpec((tile, width), lambda i: (jnp.maximum(i - tiles, 0), 0))
    return pl.pallas_call(
        functools.partial(feed_kernel, tile=tile, micro=micro, row_len=row_len),
        grid=(2 * tiles,),
        in_specs=[
            pl.BlockSpec(memory_space=pltpu.SMEM),
            ahead(D),
            ahead(D),
            once(NMAT, D, D),
            once(NMAT, D),
            once(*student.shape),
            once(*classifier.shape),
            once(*goals.shape),
            once(*send_row.shape),
            behind(1),
            once(*returned.shape),
        ],
        out_specs=[
            behind(D),
            once(*returned.shape),
            once(8, D, D),
            once(NMAT, D),
            once(*student.shape),
            once(*classifier.shape),
        ],
        out_shape=[
            jax.ShapeDtypeStruct((tokens, D), F32),
            jax.ShapeDtypeStruct(returned.shape, BF16),
            jax.ShapeDtypeStruct((NMAT, D, D), BF16),
            jax.ShapeDtypeStruct((NMAT, D), F32),
            jax.ShapeDtypeStruct(student.shape, F32),
            jax.ShapeDtypeStruct(classifier.shape, F32),
        ],
        scratch_shapes=[
            pltpu.VMEM((tokens, D), F32),
            pltpu.VMEM((tokens, 1), F32),
            pltpu.VMEM((tokens, D), BF16),
            pltpu.VMEM((tokens, FF), BF16),
            pltpu.VMEM((tokens, FF), BF16),
            pltpu.VMEM((tokens, D), F32),
            pltpu.VMEM((tokens, 1), F32),
            pltpu.VMEM((tokens, D), BF16),
            pltpu.VMEM((tokens, SW), F32),
            pltpu.VMEM((tokens, SW), BF16),
        ],
        compiler_params=pltpu.CompilerParams(vmem_limit_bytes=VMEM),
        cost_estimate=pl.CostEstimate(
            flops=tokens * D * FF * 12, bytes_accessed=tokens * D * 16, transcendentals=tokens * FF
        ),
    )(
        info,
        x.reshape(tokens, D),
        o.reshape(tokens, D),
        blocks,
        vec,
        student,
        classifier,
        goals,
        send_row,
        send_col,
        returned,
    )


def attend_back_kernel(
    info,
    x_ref,
    da1_ref,
    q_ref,
    k_ref,
    v_ref,
    o_ref,
    l_ref,
    w_ref,
    _,
    dx_ref,
    wg_ref,
    vg_ref,
    qx,
    kx,
    vx,
    dox,
    dq,
    dk,
    dv,
    dk_sum,
    dv_sum,
    wsum,
    *,
    micro,
):
    row = pl.program_id(0)
    row_len = x_ref.shape[1]
    ends, live = ends_of(info, row), live_of(info, row)
    first = lane_index(QT) < DH
    ones = jnp.ones((QT, LANES), F32)

    @pl.when(row == 0)
    def _():
        vg_ref[...] = jnp.zeros_like(vg_ref)
        wsum[...] = jnp.zeros_like(wsum)

    head = lax.broadcasted_iota(jnp.int32, (D, LANES), 0) // DH
    spot = head // 2 + DH * (1 - head % 2)
    gather = lax.broadcasted_iota(jnp.int32, (D, LANES), 1) == spot
    gather = jnp.where(gather, 1.0, 0.0).astype(BF16)

    dq[...] = jnp.zeros_like(dq)

    @pl.loop(0, row_len // QT)
    def _(t):
        rows = pl.ds(pl.multiple_of(t * QT, QT), QT)
        sample = sample_column(ends, t * QT, QT)
        lane = lane_index(QT) % DH
        high, mid, rest = split_low(jnp.where(lane < PAIRS, -l_ref[0, rows, :], 0.0))
        q_extra = (
            query_spare(sample, QT)
            + high
            + pltpu.roll(mid, PAIRS, 1)
            + pltpu.roll(rest, 2 * PAIRS, 1)
        )
        branch = da1_ref[0, rows, :].astype(BF16)
        vg_ref[2:3, :] += row_sum(branch.astype(F32))
        do = nt(branch, w_ref[3]).astype(BF16).astype(F32)
        delta = two_low(do * o_ref[0, rows, :].astype(F32), gather)
        high = delta.astype(BF16).astype(F32)
        do_extra = pltpu.roll(high - delta, PAIRS, 1) - high
        for p in range(PAIRS):
            pair = head_lanes(p)
            k_extra = key_spare(sample, QT, p)
            store_heads(dox, rows, p, do[:, pair], do_extra, first)
            store_heads(qx, rows, p, q_ref[0, rows, pair].astype(F32), q_extra, first)
            store_heads(kx, rows, p, k_ref[0, rows, pair].astype(F32), k_extra, first)
            store_heads(vx, rows, p, v_ref[0, rows, pair].astype(F32), k_extra, first)

    @pl.loop(0, row_len // QT)
    def _(t):
        rows = pl.ds(pl.multiple_of(t * QT, QT), QT)
        begin, number = reach(ends, live, t * QT, QT, row_len)
        number = (number + STEP - 1) // STEP
        begin = jnp.minimum(begin, row_len // KG - number * STEP)
        dk_sum[...] = jnp.zeros_like(dk_sum)
        dv_sum[...] = jnp.zeros_like(dv_sum)

        @pl.loop(0, number)
        def _(j):
            span = pl.ds(pl.multiple_of((begin + j * STEP) * KG, KG), STEP * KG)
            wide = lane_index(STEP * KG) < DH
            raw, done, got = {}, {}, {}
            for step in range(H + 2):
                if step < H:
                    cols = head_lanes(step)
                    raw[step] = (
                        nt(kx[rows, cols], qx[span, cols]),
                        nt(vx[rows, cols], dox[span, cols]),
                    )
                h = step - 1
                if 0 <= h < H:
                    s, dp = raw.pop(h)
                    prob = jnp.exp(s)
                    done[h] = (prob.astype(BF16), (prob * dp).astype(BF16))
                h = step - 2
                if 0 <= h < H:
                    cols = head_lanes(h)
                    prob, ds = done.pop(h)
                    got[h] = (
                        nn(prob, dox[span, cols]),
                        nn(ds, qx[span, cols]),
                        tn(ds, kx[rows, cols]),
                    )
                    if h % 2 == 1:
                        left, right = got.pop(h - 1), got.pop(h)
                        cols = head_lanes(h // 2)
                        dv_sum[:, cols] += jnp.where(first, left[0], right[0])
                        dk_sum[:, cols] += jnp.where(first, left[1], right[1])
                        dq[span, cols] += jnp.where(wide, left[2], right[2])

        dk[rows, :] = dk_sum[...].astype(BF16)
        dv[rows, :] = dv_sum[...].astype(BF16)

    @pl.loop(0, row_len // QT)
    def _(t):
        rows = pl.ds(pl.multiple_of(t * QT, QT), QT)
        dq_low = (dq[rows, :] * DH**-0.5).astype(BF16)
        dk_low, dv_low = dk[rows, :], dv[rows, :]
        vg_ref[0:1, :] += row_sum(dq_low.astype(F32))
        vg_ref[1:2, :] += row_sum(dv_low.astype(F32))
        dx_ref[0, rows, :] = (
            da1_ref[0, rows, :]
            + nt(dq_low, w_ref[0])
            + nt(dk_low, w_ref[1])
            + nt(dv_low, w_ref[2])
        ).astype(BF16)

    x = x_ref[0]
    wsum[0] += tn(x, (dq[...] * DH**-0.5).astype(BF16))
    wsum[1] += tn(x, dk[...])
    wsum[2] += tn(x, dv[...])
    wsum[3] += tn(o_ref[0], da1_ref[0].astype(BF16))

    @pl.when(row == micro - 1)
    def _():
        wg_ref[...] = wsum[...].astype(BF16)


def attend_back(info, tokens, da1, q, k, v, o, logs, blocks, grads):
    micro, row_len, _ = tokens.shape
    row_spec = lambda width: pl.BlockSpec((1, row_len, width), lambda r: (r, 0, 0))
    return pl.pallas_call(
        functools.partial(attend_back_kernel, micro=micro),
        grid=(micro,),
        in_specs=[
            pl.BlockSpec(memory_space=pltpu.SMEM),
            *[row_spec(D)] * 6,
            row_spec(LANES),
            pl.BlockSpec((4, D, D), lambda r: (0, 0, 0)),
            pl.BlockSpec(memory_space=pl.ANY),
        ],
        out_specs=[
            row_spec(D),
            pl.BlockSpec((4, D, D), lambda r: (2, 0, 0)),
            pl.BlockSpec((8, D), lambda r: (0, 0)),
        ],
        out_shape=[
            jax.ShapeDtypeStruct((micro, row_len, D), BF16),
            jax.ShapeDtypeStruct((NMAT, D, D), BF16),
            jax.ShapeDtypeStruct((8, D), F32),
        ],
        scratch_shapes=[
            *[pltpu.VMEM((row_len, 2 * D), BF16)] * 4,
            pltpu.VMEM((row_len, D), F32),
            pltpu.VMEM((row_len, D), BF16),
            pltpu.VMEM((row_len, D), BF16),
            pltpu.VMEM((QT, D), F32),
            pltpu.VMEM((QT, D), F32),
            pltpu.VMEM((4, D, D), F32),
        ],
        input_output_aliases={9: 1},
        compiler_params=pltpu.CompilerParams(vmem_limit_bytes=VMEM),
        cost_estimate=pl.CostEstimate(
            flops=micro * row_len * D * D * 16 + micro * H * row_len * row_len * DH * 10,
            bytes_accessed=micro * row_len * D * 16,
            transcendentals=micro * H * row_len * row_len,
        ),
    )(info, tokens, da1, q, k, v, o, logs, blocks, grads)


def pick_kernel(place_ref, rows_ref, out_ref):
    group, _, slots, _ = out_ref.shape
    places = group * slots
    spot = lax.broadcasted_iota(jnp.int32, (places, rows_ref.shape[1]), 1)
    pick = jnp.where(spot == place_ref[0], 1.0, 0.0).astype(BF16)
    out_ref[:, 0] = nn(pick, rows_ref[0]).astype(BF16).reshape(group, slots, D)


def pick_rows(place_col, rows, group):
    micro, row_len, _ = rows.shape
    slots = row_len // group
    return pl.pallas_call(
        pick_kernel,
        grid=(micro,),
        in_specs=[
            pl.BlockSpec((1, row_len, 1), lambda m: (m, 0, 0)),
            pl.BlockSpec((1, row_len, D), lambda m: (m, 0, 0)),
        ],
        out_specs=pl.BlockSpec((group, 1, slots, D), lambda m: (0, m, 0, 0)),
        out_shape=jax.ShapeDtypeStruct((group, micro, slots, D), BF16),
        compiler_params=pltpu.CompilerParams(vmem_limit_bytes=VMEM),
    )(place_col, rows)


def place_kernel(place_ref, rows_ref, out_ref):
    row_len = out_ref.shape[1]
    spot = lax.broadcasted_iota(jnp.int32, (row_len, row_len), 0)
    pick = jnp.where(spot == place_ref[0], 1.0, 0.0).astype(BF16)
    out_ref[0] = nn(pick, rows_ref[:, 0].reshape(row_len, D)).astype(BF16)


def place_rows(place_row, rows):
    group, micro, slots, _ = rows.shape
    row_len = group * slots
    return pl.pallas_call(
        place_kernel,
        grid=(micro,),
        in_specs=[
            pl.BlockSpec((1, 1, row_len), lambda m: (m, 0, 0)),
            pl.BlockSpec((group, 1, slots, D), lambda m: (0, m, 0, 0)),
        ],
        out_specs=pl.BlockSpec((1, row_len, D), lambda m: (m, 0, 0)),
        out_shape=jax.ShapeDtypeStruct((micro, row_len, D), BF16),
        compiler_params=pltpu.CompilerParams(vmem_limit_bytes=VMEM),
    )(place_row, rows)


CHUNKS = 6
STU_ROWS, CLS_ROWS, VEC_ROWS = 656, 144, 16
SMALL_ROWS = STU_ROWS + CLS_ROWS + 4 * VEC_ROWS


def bits_of(size):
    return [1 << i for i in range(size.bit_length() - 1)]


def reduce_kernel(
    group,
    owners,
    grad_ref,
    ff_vec,
    at_vec,
    stu_ref,
    cls_ref,
    own_ref,
    vec_out,
    stu_out,
    cls_out,
    got_a,
    sum_a,
    got_b,
    part,
    got_c,
    final,
    small,
    small_got,
    small_sum,
    small_end,
    send_sem,
    recv_sem,
    small_send,
    small_recv,
):
    b, s = lax.axis_index("batch"), lax.axis_index("shard")
    per = NMAT // owners
    rows = per * D // CHUNKS
    batch_bits, shard_bits = bits_of(group), bits_of(owners)
    half = SMALL_ROWS // 2

    def copy(src, dst, sems, at, where):
        return pltpu.make_async_remote_copy(
            src_ref=src,
            dst_ref=dst,
            send_sem=sems[0].at[at],
            recv_sem=sems[1].at[at],
            device_id=where,
            device_id_type=pl.DeviceIdType.MESH,
        )

    peers = [(b, s ^ bit) for bit in shard_bits] + [(b ^ bit, s) for bit in batch_bits]
    barrier = pltpu.get_barrier_semaphore()
    for peer in peers:
        pl.semaphore_signal(
            barrier, inc=1, device_id=peer, device_id_type=pl.DeviceIdType.MESH
        )
    pl.semaphore_wait(barrier, len(peers))

    sems = (send_sem, recv_sem)
    small_sems = (small_send, small_recv)
    waits = []

    def begin(op):
        op.start()
        waits.append(op)
        return op

    def piece(owner, c):
        at = lax.rem(owner * per + c * per // CHUNKS + 8, NMAT)
        if rows == D:
            return grad_ref.at[at]
        step = D // rows
        return grad_ref.at[at, pl.ds((c % step) * rows, rows)]

    far = shard_bits[1]
    first = {}
    for c in range(CHUNKS):
        first[c] = [
            begin(copy(piece(s ^ 1 ^ far, c), got_a.at[c, 0], sems, (c, 0), peers[0])),
            begin(copy(piece(s ^ 1, c), got_a.at[c, 1], sems, (c, 1), peers[0])),
        ]

    small[...] = jnp.zeros_like(small)
    stu_count, cls_count = stu_ref.shape[0], cls_ref.shape[0]
    small[0:stu_count, :] = stu_ref[...].astype(BF16)
    small[STU_ROWS : STU_ROWS + cls_count, 0:CLS] = cls_ref[...].astype(BF16)
    for i in range(4):
        at = STU_ROWS + CLS_ROWS + i * VEC_ROWS
        lanes = slice(i * LANES, (i + 1) * LANES)
        small[at : at + 3, :] = at_vec[0:3, lanes].astype(BF16)
        small[at + 3 : at + NMAT, :] = ff_vec[3:NMAT, lanes].astype(BF16)
    core = lax.rem(s, 2)
    mine = pl.ds(pl.multiple_of(core * half, 16), half)
    other = pl.ds(pl.multiple_of((1 - core) * half, 16), half)
    small_op = begin(copy(small.at[other], small_got.at[0], small_sems, 0, peers[0]))

    def add(x, y):
        return (x.astype(F32) + y.astype(F32)).astype(BF16)

    second = {}

    def start_second(c):
        for i, op in enumerate(first[c]):
            op.wait_recv()
            owner = s ^ far if i == 0 else s
            sum_a[c, i] = add(piece(owner, c)[...], got_a[c, i])
        second[c] = begin(copy(sum_a.at[c, 0], got_b.at[c], sems, (c, 2), peers[1]))

    start_second(0)
    start_second(1)

    spans = []
    size = rows
    for bit in batch_bits:
        halving = size >= 32
        spans.append((bit, size, halving))
        if halving:
            size //= 2
    offset_of = []
    offset = jnp.int32(0)
    slot_of = []
    slot = 0
    for bit, now, halving in spans:
        place = lax.rem(b // bit, 2)
        offset_of.append((offset, place))
        slot_of.append(slot)
        if halving:
            offset = offset + place * (now // 2)
            slot += now // 2
        else:
            slot += now
    last = offset

    def ranged(ref, c, start, count):
        return ref.at[c, pl.ds(pl.multiple_of(start, 16), count)]

    moving = {}

    def start_batch(c, k):
        bit, now, halving = spans[k]
        start, place = offset_of[k]
        if halving:
            count = now // 2
            src = ranged(part.at[k], c, start + (1 - place) * count, count)
        else:
            count = now
            src = ranged(part.at[k], c, start, count)
        dst = got_c.at[c, pl.ds(slot_of[k], count)]
        moving[c, k] = begin(copy(src, dst, sems, (c, 3 + k), (b ^ bit, s)))

    def end_batch(c, k):
        bit, now, halving = spans[k]
        start, place = offset_of[k]
        moving[c, k].wait_recv()
        count = now // 2 if halving else now
        if halving:
            start = start + place * count
        here = pl.ds(pl.multiple_of(start, 16), count)
        total = add(part[k, c, here, :], got_c[c, slot_of[k] : slot_of[k] + count])
        if k + 1 < len(spans):
            part[k + 1, c, here, :] = total
        else:
            final[c, here, :] = total

    gathers = [k for k in reversed(range(len(spans))) if spans[k][2]]
    gathering = {}

    def start_gather(c, g):
        k = gathers[g]
        bit, now, _ = spans[k]
        start, place = offset_of[k]
        count = now // 2
        at = ranged(final, c, start + place * count, count)
        gathering[c, g] = begin(
            copy(at, at, sems, (c, 3 + len(spans) + g), (b ^ bit, s))
        )

    def stage(c, k):
        if k == 0:
            second[c].wait_recv()
            if c + 2 < CHUNKS:
                start_second(c + 2)
            part[0, c] = add(sum_a[c, 1], got_b[c])
            start_batch(c, 0)
        elif k <= len(spans):
            end_batch(c, k - 1)
            if k < len(spans):
                start_batch(c, k)
            else:
                start_gather(c, 0)
        else:
            g = k - len(spans) - 1
            gathering[c, g].wait_recv()
            if g + 1 < len(gathers):
                start_gather(c, g + 1)
            else:
                per_block = CHUNKS // per
                block, within = c // per_block, c % per_block
                own_ref[block, within * rows : (within + 1) * rows, :] = final[c]

    stages = 1 + len(spans) + len(gathers)
    rest = [(b, s ^ bit) for bit in shard_bits[1:]] + [(b ^ bit, s) for bit in batch_bits]

    def small_stage(k):
        nonlocal small_op
        small_op.wait_recv()
        if k == 0:
            small_sum[0] = add(small[mine, :], small_got[0])
        elif k <= len(rest):
            small_sum[k] = add(small_sum[k - 1], small_got[k])
        if k < len(rest):
            small_op = begin(
                copy(small_sum.at[k], small_got.at[k + 1], small_sems, k + 1, rest[k])
            )
        elif k == len(rest):
            small_end[mine, :] = small_sum[k]
            small_op = begin(
                copy(small_sum.at[k], small_end.at[mine], small_sems, k + 1, peers[0])
            )

    small_k = 0
    for tick in range(CHUNKS + stages - 1):
        for k in reversed(range(stages)):
            c = tick - k
            if 0 <= c < CHUNKS:
                stage(c, k)
        if small_k <= len(rest) + 1:
            small_stage(small_k)
            small_k += 1
    while small_k <= len(rest) + 1:
        small_stage(small_k)
        small_k += 1

    for i in range(4):
        at = STU_ROWS + CLS_ROWS + i * VEC_ROWS
        lanes = slice(i * LANES, (i + 1) * LANES)
        vec_out[:, lanes] = small_end[at : at + VEC_ROWS, :].astype(F32)
    stu_out[...] = small_end[0:STU_ROWS, :].astype(F32)
    cls_out[...] = small_end[STU_ROWS : STU_ROWS + CLS_ROWS, :].astype(F32)
    for op in waits:
        op.wait_send()


def reduce_grads(grads, ff_vec, at_vec, stu, cls):
    group, owners = lax.axis_size("batch"), lax.axis_size("shard")
    per = NMAT // owners
    rows = per * D // CHUNKS
    batch_count = len(bits_of(group))
    copies = 3 + 2 * batch_count
    small_count = len(bits_of(owners)) + batch_count + 1
    vmem = pl.BlockSpec(memory_space=pltpu.VMEM)
    return pl.pallas_call(
        functools.partial(reduce_kernel, group, owners),
        in_specs=[vmem] * 5,
        out_specs=[vmem] * 4,
        out_shape=[
            jax.ShapeDtypeStruct((per, D, D), BF16),
            jax.ShapeDtypeStruct((VEC_ROWS, D), F32),
            jax.ShapeDtypeStruct((STU_ROWS, SW), F32),
            jax.ShapeDtypeStruct((CLS_ROWS, LANES), F32),
        ],
        scratch_shapes=[
            pltpu.VMEM((CHUNKS, 2, rows, D), BF16),
            pltpu.VMEM((CHUNKS, 2, rows, D), BF16),
            pltpu.VMEM((CHUNKS, rows, D), BF16),
            pltpu.VMEM((batch_count, CHUNKS, rows, D), BF16),
            pltpu.VMEM((CHUNKS, rows + 16 * batch_count, D), BF16),
            pltpu.VMEM((CHUNKS, rows, D), BF16),
            pltpu.VMEM((SMALL_ROWS, LANES), BF16),
            pltpu.VMEM((small_count - 1, SMALL_ROWS // 2, LANES), BF16),
            pltpu.VMEM((small_count - 1, SMALL_ROWS // 2, LANES), BF16),
            pltpu.VMEM((SMALL_ROWS, LANES), BF16),
            pltpu.SemaphoreType.DMA((CHUNKS, copies)),
            pltpu.SemaphoreType.DMA((CHUNKS, copies)),
            pltpu.SemaphoreType.DMA((small_count,)),
            pltpu.SemaphoreType.DMA((small_count,)),
        ],
        compiler_params=pltpu.CompilerParams(
            collective_id=1, has_side_effects=True, vmem_limit_bytes=VMEM
        ),
        cost_estimate=pl.CostEstimate(
            flops=NMAT * D * D * 4, bytes_accessed=NMAT * D * D * 8, transcendentals=0
        ),
    )(grads, ff_vec, at_vec, stu, cls)


def update_kernel(
    own_ref,
    blocks_ref,
    left_ref,
    right_ref,
    lroot_ref,
    rroot_ref,
    shard_ref,
    vsum_ref,
    vec_ref,
    vmom_ref,
    ssum_ref,
    stu_ref,
    smom_ref,
    csum_ref,
    cls_ref,
    cmom_ref,
    grad_out,
    new_out,
    left_out,
    right_out,
    vg_out,
    vm_out,
    v_out,
    sg_out,
    sm_out,
    s_out,
    cg_out,
    cm_out,
    c_out,
    *,
    owners,
):
    g = own_ref[0]
    grad_out[0] = g.astype(F32)
    left_out[0] = decay_rate * left_ref[0] + (1.0 - decay_rate) * nt(g, g)
    right_out[0] = decay_rate * right_ref[0] + (1.0 - decay_rate) * tn(g, g)
    steered = nn(lroot_ref[0].astype(BF16), g).astype(BF16)
    steered = nn(steered, rroot_ref[0].astype(BF16))
    size = jnp.mean(steered * steered, keepdims=True)
    new_out[0] = blocks_ref[0].astype(F32) - steered * (block_rate * lax.rsqrt(size + 1e-06))

    @pl.when(pl.program_id(0) == 0)
    def _():
        per = NMAT // owners
        mine = vsum_ref[0:per, :]
        for i in range(1, owners):
            mine = jnp.where(shard_ref[0] == i, vsum_ref[i * per : (i + 1) * per, :], mine)

        def rule(grads, old, moment, rate, outs):
            renewed = decay_rate * moment + (1.0 - decay_rate) * grads * grads
            outs[0][...] = grads
            outs[1][...] = renewed
            outs[2][...] = old - rate * grads / (jnp.sqrt(renewed) + 1e-08)

        rule(mine, vec_ref[...], vmom_ref[...], vector_rate, (vg_out, vm_out, v_out))
        rule(
            ssum_ref[0 : stu_ref.shape[0], :],
            stu_ref[...],
            smom_ref[...],
            head_rate,
            (sg_out, sm_out, s_out),
        )
        rule(
            csum_ref[0 : cls_ref.shape[0], 0:CLS],
            cls_ref[...],
            cmom_ref[...],
            head_rate,
            (cg_out, cm_out, c_out),
        )


def update(own, blocks, left, right, lroot, rroot, shard, vsum, vec, vmom, ssum, stu, smom, csum, cls, cmom):
    per = own.shape[0]
    mat = pl.BlockSpec((1, D, D), lambda i: (i, 0, 0))
    whole = lambda a: pl.BlockSpec(a.shape, lambda i: (0,) * a.ndim)
    like = lambda a: jax.ShapeDtypeStruct(a.shape, F32)
    return pl.pallas_call(
        functools.partial(update_kernel, owners=NMAT // per),
        grid=(per,),
        in_specs=[mat] * 6
        + [pl.BlockSpec(memory_space=pltpu.SMEM)]
        + [whole(a) for a in (vsum, vec, vmom, ssum, stu, smom, csum, cls, cmom)],
        out_specs=[mat] * 4 + [whole(a) for a in (vec,) * 3 + (stu,) * 3 + (cls,) * 3],
        out_shape=[like(left)] * 4 + [like(a) for a in (vec,) * 3 + (stu,) * 3 + (cls,) * 3],
        compiler_params=pltpu.CompilerParams(vmem_limit_bytes=VMEM),
    )(own, blocks, left, right, lroot, rroot, shard, vsum, vec, vmom, ssum, stu, smom, csum, cls, cmom)


def local(
    tokens,
    cotangent,
    lengths,
    exit_layers,
    teacher,
    blocks,
    left_stats,
    right_stats,
    left_root,
    right_root,
    vectors,
    vec_moment,
    student,
    stu_moment,
    classifier,
    cls_moment,
):
    group = lax.axis_size("batch")
    me = lax.axis_index("batch")
    micro, _, row_len, _ = tokens.shape
    slots = row_len // group
    tokens, cotangent = tokens[:, 0], cotangent[:, 0]
    ends = jnp.cumsum(lengths[:, 0], axis=-1, dtype=jnp.int32)
    live = (exit_layers[:, 0] >= LAYER).astype(jnp.int32)
    info = jnp.concatenate([ends, live], axis=1)
    alive_len = lengths[:, 0] * live
    counts = jnp.sum(alive_len, axis=1, dtype=jnp.int32)
    everyone = lax.all_gather(counts[None, :], "batch", axis=0, tiled=True)
    starts = jnp.cumsum(everyone, axis=0, dtype=jnp.int32) - everyone

    places = jnp.arange(row_len, dtype=jnp.int32)
    before = jnp.cumsum(alive_len, axis=1, dtype=jnp.int32) - alive_len
    sample = jnp.sum((places[None, :, None] >= ends[:, None, : SAMP - 1]).astype(jnp.int32), axis=-1)
    chosen = sample[..., None] == jnp.arange(SAMP, dtype=jnp.int32)
    shift = jnp.sum(jnp.where(chosen, (before - ends + lengths[:, 0])[:, None, :], 0), axis=-1)
    alive_tok = jnp.sum(jnp.where(chosen, live[:, None, :], 0), axis=-1)
    rank = places[None, :] + shift
    send = (starts[me][:, None] + rank) % group * slots + rank // group
    send = jnp.where(alive_tok > 0, send, row_len)
    start_of = jnp.repeat(starts.T, slots, axis=1)
    count_of = jnp.repeat(everyone.T, slots, axis=1)
    turn = (me - start_of) % group + group * (places % slots)[None, :]
    back = jnp.where(turn < count_of, (start_of + turn) // group, row_len)

    grad_outgoing = pick_rows(back[:, :, None], cotangent, group)
    returned = lax.all_to_all(grad_outgoing, "batch", split_axis=0, concat_axis=0, tiled=True)

    matrices = lax.all_gather(blocks, "shard", axis=0, tiled=True)
    vec = lax.all_gather(vectors.astype(BF16), "shard", axis=0, tiled=True).astype(F32)

    q, k, v, o, logs = attend(info, tokens, matrices, vec)
    goals = jnp.concatenate(
        [teacher[:, 0], live[..., None].astype(F32)], axis=-1
    ).reshape(micro * SAMP, CLS + 1)
    da1, outgoing, ff_grads, ff_vecs, stu_grads, cls_grads = feed(
        info, tokens, o, matrices, vec, student, classifier, goals, send, send.reshape(-1, 1), returned
    )
    arrived = lax.all_to_all(outgoing, "batch", split_axis=0, concat_axis=0, tiled=True)
    input_grads, grads, at_vecs = attend_back(
        info, tokens, da1.reshape(micro, row_len, D), q, k, v, o, logs, matrices, ff_grads
    )
    layer_out = place_rows(back[:, None, :], arrived)
    own, vec_sum, stu_sum, cls_sum = reduce_grads(grads, ff_vecs, at_vecs, stu_grads, cls_grads)
    shard = lax.axis_index("shard").astype(jnp.int32).reshape(1)
    updated = update(
        own,
        blocks,
        left_stats,
        right_stats,
        left_root,
        right_root,
        shard,
        vec_sum,
        vectors,
        vec_moment,
        stu_sum,
        student,
        stu_moment,
        cls_sum,
        classifier,
        cls_moment,
    )
    return (layer_out[:, None], input_grads[:, None], *updated)


def solution(mesh):
    rows = P(None, ("batch", "shard"), None, None)
    tags = P(None, ("batch", "shard"), None)
    mats = P("shard", None, None)
    vecs = P("shard", None)
    return jax.shard_map(
        local,
        mesh=mesh,
        in_specs=(rows, rows, tags, tags, rows, mats, mats, mats, mats, mats, vecs, vecs)
        + (P(),) * 4,
        out_specs=(rows, rows, mats, mats, mats, mats, vecs, vecs, vecs) + (P(),) * 6,
        check_vma=False,
    )
```

```python
import functools

import jax
import jax.numpy as jnp
from jax import lax
from jax.experimental import pallas as pl
from jax.experimental.pallas import tpu as pltpu
from jax.sharding import PartitionSpec as P

D = 512
H = 8
DH = 64
FF = 2048
SW = 128
NMAT = 12
SAMP = 4
LAYER = 4
CLS = 14

decay_rate = 0.5
block_rate = 0.04
vector_rate = 0.05
head_rate = 0.05

QT = 256
STEP = 2
KG = 128
PAIRS = H // 2
LANES = 128
PART = 512
PARTS, CUT = FF // PART, D // PART
BIG = float(2**30)
EPS = 1e-6
VMEM = 60 * 1024 * 1024

F32 = jnp.float32
BF16 = jnp.bfloat16


def nn(a, b):
    return jnp.dot(a, b, preferred_element_type=F32)


def nt(a, b):
    return lax.dot_general(a, b, (((1,), (1,)), ((), ())), preferred_element_type=F32)


def tn(a, b):
    return lax.dot_general(a, b, (((0,), (0,)), ((), ())), preferred_element_type=F32)


def exact(a, b, dims=(((1,), (0,)), ((), ()))):
    return lax.dot_general(
        a, b, dims, preferred_element_type=F32, precision=lax.Precision.HIGHEST
    )


def row_sum(v):
    return jnp.sum(v, axis=0, keepdims=True)


def two_low(v, b):
    high = v.astype(BF16)
    return nn(high, b) + nn((v - high.astype(F32)).astype(BF16), b)


def split_low(v):
    high = v.astype(BF16).astype(F32)
    rest = v - high
    mid = rest.astype(BF16).astype(F32)
    return high, mid, rest - mid


def ends_of(info, row):
    ends, total = [], jnp.int32(0)
    for j in range(SAMP):
        total = total + info[row, j]
        ends.append(total)
    return ends


def live_of(info, row):
    return [(info[row, SAMP + j] >= LAYER).astype(jnp.int32) for j in range(SAMP)]


def sample_column(ends, first, count):
    place = first + lax.broadcasted_iota(jnp.int32, (count, 1), 0)
    total = jnp.zeros((count, 1), jnp.int32)
    for j in range(SAMP - 1):
        total = total + (place >= ends[j]).astype(jnp.int32)
    return total


def reach(ends, live, first, count, row_len):
    low, high = jnp.int32(row_len), jnp.int32(0)
    start = jnp.int32(0)
    for j in range(SAMP):
        end = ends[j]
        meets = (start < first + count) & (end > first) & (end > start) & (live[j] > 0)
        low = jnp.where(meets, jnp.minimum(low, start), low)
        high = jnp.where(meets, jnp.maximum(high, end), high)
        start = end
    begin = low // KG
    number = jnp.maximum((high + KG - 1) // KG - begin, 0)
    return begin, number


def lane_index(rows):
    return lax.broadcasted_iota(jnp.int32, (rows, LANES), 1)


TAG = 16


def key_spare(sample, rows, pair):
    lane = lane_index(rows) % DH
    own = (lane < 3 * PAIRS) & (lane % PAIRS == pair)
    return jnp.where(own | (lane == sample + TAG), 1.0, 0.0)


def query_spare(sample, rows):
    lane = lane_index(rows) % DH
    tag = (lane >= TAG) & (lane < TAG + SAMP) & (lane != sample + TAG)
    return jnp.where(tag, -BIG, 0.0)


def store_heads(ref, rows, p, pair, spare, first):
    ref[rows, 2 * p * LANES : (2 * p + 1) * LANES] = jnp.where(first, pair, spare).astype(BF16)
    ref[rows, (2 * p + 1) * LANES : (2 * p + 2) * LANES] = jnp.where(
        first, spare, pair
    ).astype(BF16)


def head_lanes(h):
    return slice(h * LANES, (h + 1) * LANES)


def widths(row_len):
    most = row_len // KG
    return list(range(most // 2, most + 1))


def chosen_span(ends, live, t, row_len):
    begin, number = reach(ends, live, t * QT, QT, row_len)
    least, most = widths(row_len)[0], row_len // KG
    number = jnp.where(number > 0, jnp.maximum(number, least), 0)
    return jnp.minimum(begin, most - number), number


WEIGHT_PARTS = 4


def bits_of(size):
    return [1 << i for i in range(size.bit_length() - 1)]


def token_spots(place, ends, live, start, group, slots):
    shift, keep = jnp.zeros_like(place), jnp.zeros_like(place)
    before, begin = jnp.int32(0), jnp.int32(0)
    for j in range(SAMP):
        inside = (place >= begin) & (place < ends[j])
        shift = jnp.where(inside, before - begin, shift)
        keep = jnp.where(inside, live[j], keep)
        before = before + live[j] * (ends[j] - begin)
        begin = ends[j]
    rank = place + shift
    fold = group.bit_length() - 1
    spot = ((start + rank) & (group - 1)) * slots + (rank >> fold)
    return jnp.where(keep > 0, spot, group * slots)


def open_kernel(
    group,
    owners,
    info,
    blocks_ref,
    vec_ref,
    cot_ref,
    w_out,
    vec_out,
    out_ref,
    send_row,
    send_col,
    back_row,
    tally,
    tallies,
    vecs,
    own_sem,
    count_send,
    count_recv,
    vec_send,
    vec_recv,
    w_send,
    w_recv,
):
    b, s = lax.axis_index("batch"), lax.axis_index("shard")
    micro, row_len, _ = cot_ref.shape
    slots = row_len // group
    per = NMAT // owners
    far = bits_of(owners)[1]
    near = 1
    mesh_id = pl.DeviceIdType.MESH

    batch_peers = [(lax.rem(b + i, group), s) for i in range(1, group)]
    shard_peers = [(b, s ^ i) for i in range(1, owners)]
    barrier = pltpu.get_barrier_semaphore()
    for peer in batch_peers + shard_peers:
        pl.semaphore_signal(barrier, inc=1, device_id=peer, device_id_type=mesh_id)

    lane = lax.broadcasted_iota(jnp.int32, (8, LANES), 1)
    mine = jnp.zeros((8, LANES), jnp.int32)
    for m in range(micro):
        total = jnp.int32(0)
        for j in range(SAMP):
            alive = (info[m, SAMP + j] >= LAYER).astype(jnp.int32)
            total = total + alive * info[m, j]
        mine = jnp.where(lane == m, total, mine)
    tally[...] = mine
    low = vec_ref[...].astype(BF16).astype(F32)
    vecs[owners] = jnp.concatenate([low, jnp.zeros((8 - per, D), F32)], axis=0)
    pl.semaphore_wait(barrier, len(batch_peers) + len(shard_peers))

    def remote(src, dst, sems, at, peer):
        op = pltpu.make_async_remote_copy(
            src_ref=src,
            dst_ref=dst,
            send_sem=sems[0].at[at],
            recv_sem=sems[1].at[at],
            device_id=peer,
            device_id_type=mesh_id,
        )
        op.start()
        return op

    counts = [
        remote(tally, tallies.at[i - 1], (count_send, count_recv), i - 1, batch_peers[i - 1])
        for i in range(1, group)
    ]
    half = per * D // 2
    rows = half // WEIGHT_PARTS
    side = lax.rem(b, 2)
    x_peer, y_peer, core_peer = (b, s ^ far), (b ^ 1, s), (b, s ^ near)
    w_sems = (w_send, w_recv)

    def part_of(owner, which, c):
        at = pl.multiple_of(owner * per * D + which * half + c * rows, 16)
        return w_out.at[pl.ds(at, rows)]

    def own_part(which, c):
        at = pl.multiple_of(which * half + c * rows, 16)
        return blocks_ref.at[pl.ds(at, rows)]

    kept = pltpu.make_async_copy(
        blocks_ref,
        w_out.at[pl.ds(pl.multiple_of(s * per * D, 16), per * D)],
        own_sem.at[0],
    )
    kept.start()
    over_x = [
        remote(own_part(side, c), part_of(s, side, c), w_sems, (0, c), x_peer)
        for c in range(WEIGHT_PARTS)
    ]
    over_core = [
        remote(
            blocks_ref,
            w_out.at[pl.ds(pl.multiple_of(s * per * D, 16), per * D)],
            w_sems,
            (1, 0),
            core_peer,
        )
    ]
    vec_ops = [
        remote(vecs.at[owners], vecs.at[s], (vec_send, vec_recv), i - 1, shard_peers[i - 1])
        for i in range(1, owners)
    ]

    for op in counts:
        op.wait_recv()
    start = jnp.zeros((8, LANES), jnp.int32)
    place_row = lax.broadcasted_iota(jnp.int32, (1, row_len), 1)
    place_col = lax.broadcasted_iota(jnp.int32, (row_len, 1), 0)
    for i in range(1, group):
        start = start + jnp.where(b >= i, tallies[i - 1], 0)

    for m in range(micro):
        ends, live = ends_of(info, m), live_of(info, m)
        begin = start[0:1, m : m + 1]
        send_row[m : m + 1, :] = token_spots(place_row, ends, live, begin, group, slots)
        send_col[m * row_len : (m + 1) * row_len, :] = token_spots(
            place_col, ends, live, begin, group, slots
        )

    def home_slots(place, m):
        source = place // slots
        first = jnp.zeros_like(place)
        number = jnp.zeros_like(place)
        for i in range(group):
            other = tally if i == 0 else tallies.at[i - 1]
            at = lax.rem(b - i + group, group)
            here = other[0:1, m : m + 1]
            number = jnp.where(source == at, here, number)
            first = first + jnp.where(source > at, here, 0)
        turn = ((b - first) & (group - 1)) + group * (place & (slots - 1))
        slot = (first + turn) >> (group.bit_length() - 1)
        return jnp.where(turn < number, slot, row_len)

    for m in range(micro):
        back_row[m : m + 1, :] = home_slots(place_row, m)

    chunk = min(256, row_len)

    @pl.loop(0, micro * row_len // chunk)
    def _(k):
        m = (k * chunk) // row_len
        at = lax.rem(k * chunk, row_len)
        place = at + lax.broadcasted_iota(jnp.int32, (chunk, 1), 0)
        home = jnp.where(m == 0, home_slots(place, 0), home_slots(place, micro - 1))
        spot = lax.broadcasted_iota(jnp.int32, (chunk, row_len), 1)
        pick = jnp.where(spot == home, 1.0, 0.0).astype(BF16)
        moved = nn(pick, cot_ref[m]).astype(BF16)
        count = chunk // slots
        out_ref[pl.ds(at // slots, count), m] = moved.reshape(count, slots, D)

    over_y, fill = [], []
    for c in range(WEIGHT_PARTS):
        over_x[c].wait_recv()
        came = part_of(s ^ far, side, c)
        over_y.append(remote(came, came, w_sems, (2, c), y_peer))
        fill.append(remote(came, came, w_sems, (3, c), core_peer))
    for c in range(WEIGHT_PARTS):
        over_y[c].wait_recv()
        came = part_of(s ^ far, 1 - side, c)
        fill.append(remote(came, came, w_sems, (4, c), core_peer))
    for op in vec_ops:
        op.wait_recv()
    vecs[s] = vecs[owners]
    for o in range(owners):
        vec_out[o * per : (o + 1) * per, :] = vecs[o, 0:per, :]
    over_core[0].wait_recv()
    for op in fill:
        op.wait_recv()
    kept.wait()
    for op in counts + vec_ops + over_x + over_core + over_y + fill:
        op.wait_send()


def opening(info, blocks, vectors, cotangent):
    group, owners = lax.axis_size("batch"), lax.axis_size("shard")
    micro, row_len, _ = cotangent.shape
    slots = row_len // group
    vmem = pl.BlockSpec(memory_space=pltpu.VMEM)
    any_ = pl.BlockSpec(memory_space=pl.ANY)
    dma = pltpu.SemaphoreType.DMA
    ints = lambda *shape: jax.ShapeDtypeStruct(shape, jnp.int32)
    return pl.pallas_call(
        functools.partial(open_kernel, group, owners),
        in_specs=[pl.BlockSpec(memory_space=pltpu.SMEM), any_, vmem, vmem],
        out_specs=[any_] + [vmem] * 5,
        out_shape=[
            jax.ShapeDtypeStruct((NMAT * D, D), BF16),
            jax.ShapeDtypeStruct((NMAT, D), F32),
            jax.ShapeDtypeStruct((group, micro, slots, D), BF16),
            ints(micro, row_len),
            ints(micro * row_len, 1),
            ints(micro, row_len),
        ],
        scratch_shapes=[
            pltpu.VMEM((8, LANES), jnp.int32),
            pltpu.VMEM((group - 1, 8, LANES), jnp.int32),
            pltpu.VMEM((owners + 1, 8, D), F32),
            dma((1,)),
            dma((group - 1,)),
            dma((group - 1,)),
            dma((owners - 1,)),
            dma((owners - 1,)),
            dma((5, WEIGHT_PARTS)),
            dma((5, WEIGHT_PARTS)),
        ],
        compiler_params=pltpu.CompilerParams(
            collective_id=2, has_side_effects=True, vmem_limit_bytes=24 * 1024 * 1024
        ),
        cost_estimate=pl.CostEstimate(
            flops=micro * row_len * row_len * D * 2,
            bytes_accessed=NMAT * D * D * 4,
            transcendentals=0,
        ),
    )(info, blocks.reshape(-1, D), vectors, cotangent)


def attend_kernel(info, x_ref, w_ref, vec_ref, q_ref, k_ref, v_ref, o_ref, l_ref, qx, kx, vx):
    row = pl.program_id(0)
    row_len = x_ref.shape[1]
    ends, live = ends_of(info, row), live_of(info, row)
    first = lane_index(QT) < DH
    ones = jnp.ones((QT, LANES), F32)

    @pl.loop(0, row_len // QT)
    def _(t):
        rows = pl.ds(pl.multiple_of(t * QT, QT), QT)
        x = x_ref[0, rows, :]
        sample = sample_column(ends, t * QT, QT)
        q_extra = query_spare(sample, QT)
        q = ((nn(x, w_ref[0]) + vec_ref[0:1, :]).astype(BF16).astype(F32) * DH**-0.5).astype(BF16)
        k = nn(x, w_ref[1]).astype(BF16)
        v = (nn(x, w_ref[2]) + vec_ref[1:2, :]).astype(BF16)
        q_ref[0, rows, :] = q
        k_ref[0, rows, :] = k
        v_ref[0, rows, :] = v
        for p in range(PAIRS):
            pair = head_lanes(p)
            store_heads(qx, rows, p, q[:, pair].astype(F32), q_extra, first)
            store_heads(kx, rows, p, k[:, pair].astype(F32), key_spare(sample, QT, p), first)
            store_heads(vx, rows, p, v[:, pair].astype(F32), ones, first)

    @pl.loop(0, row_len // QT)
    def _(t):
        rows = pl.ds(pl.multiple_of(t * QT, QT), QT)
        begin, number = chosen_span(ends, live, t, row_len)

        @pl.when(number == 0)
        def _():
            o_ref[0, rows, :] = jnp.zeros((QT, D), BF16)
            l_ref[0, rows, :] = jnp.zeros((QT, LANES), F32)

        for n in widths(row_len):

            @pl.when(number == n)
            def _(n=n):
                span = pl.ds(pl.multiple_of(begin * KG, KG), n * KG)
                lane = lane_index(QT)
                scores, powers, got = {}, {}, {}
                peaks = jnp.zeros((QT, LANES), F32)
                totals = jnp.ones((QT, LANES), F32)
                for step in range(H + 2):
                    if step < H:
                        cols = head_lanes(step)
                        scores[step] = nt(qx[rows, cols], kx[span, cols])
                    h = step - 1
                    if 0 <= h < H:
                        s = scores.pop(h)
                        peak = jnp.max(s, axis=1, keepdims=True)
                        powers[h] = jnp.exp(s - peak).astype(BF16)
                        spot = lane == (h // 2 + DH if h % 2 == 0 else h // 2)
                        peaks = jnp.where(spot, peak, peaks)
                    h = step - 2
                    if 0 <= h < H:
                        got[h] = nn(powers.pop(h), vx[span, head_lanes(h)])
                        spot = lane == (h // 2 + DH if h % 2 == 0 else h // 2)
                        totals = jnp.where(spot, got[h], totals)
                        if h % 2 == 1:
                            left, right = got.pop(h - 1), got.pop(h)
                            top = jnp.where(first, left, right)
                            total = pltpu.roll(jnp.where(first, right, left), DH, 1)
                            o_ref[0, rows, head_lanes(h // 2)] = (top / total).astype(BF16)
                l_ref[0, rows, :] = jnp.where(
                    peaks > -0.5 * BIG, peaks + jnp.log(totals), 0.0
                )


def attend(info, tokens, blocks, vec):
    micro, row_len, _ = tokens.shape
    row_spec = lambda width: pl.BlockSpec((1, row_len, width), lambda r: (r, 0, 0))
    low = jax.ShapeDtypeStruct((micro, row_len, D), BF16)
    return pl.pallas_call(
        attend_kernel,
        grid=(micro,),
        in_specs=[
            pl.BlockSpec(memory_space=pltpu.SMEM),
            row_spec(D),
            pl.BlockSpec((3, D, D), lambda r: (0, 0, 0)),
            pl.BlockSpec((NMAT, D), lambda r: (0, 0)),
        ],
        out_specs=[row_spec(D)] * 4 + [row_spec(LANES)],
        out_shape=[low] * 4 + [jax.ShapeDtypeStruct((micro, row_len, LANES), F32)],
        scratch_shapes=[pltpu.VMEM((row_len, 2 * D), BF16)] * 3,
        compiler_params=pltpu.CompilerParams(vmem_limit_bytes=VMEM),
        cost_estimate=pl.CostEstimate(
            flops=micro * row_len * D * D * 6 + micro * H * row_len * row_len * DH * 16,
            bytes_accessed=micro * row_len * D * 16,
            transcendentals=micro * H * row_len * row_len,
        ),
    )(info, tokens, blocks, vec)


def gelu_both(u):
    share = 0.5 + 0.5 * lax.erf(u * 0.5**0.5)
    bell = jnp.exp2((-0.5 * 1.4426950408889634) * (u * u))
    return u * share, share + (u * 0.3989422804014327) * bell


def norm_parts(a):
    center = a - jnp.mean(a, axis=-1, keepdims=True)
    rate = lax.rsqrt(jnp.mean(center * center, axis=-1, keepdims=True) + EPS)
    return center * rate, rate


def norm_back(grad, unit, rate):
    return rate * (
        grad
        - jnp.mean(grad, axis=-1, keepdims=True)
        - unit * jnp.mean(grad * unit, axis=-1, keepdims=True)
    )


def feed_kernel(
    info,
    x_ref,
    o_ref,
    w_ref,
    vec_ref,
    stu_ref,
    cls_ref,
    goal_ref,
    send_row,
    send_col,
    back_ref,
    da1_ref,
    out_ref,
    wg_ref,
    vg_ref,
    sg_ref,
    cg_ref,
    unit1,
    rate1,
    h1b,
    act,
    slope,
    unit2,
    rate2,
    zb,
    head_in,
    head_low,
    *,
    tile,
    micro,
    row_len,
):
    step = pl.program_id(0)
    tiles = micro * row_len // tile
    group, _, slots, _ = out_ref.shape

    @pl.when(step == 0)
    def _():
        vg_ref[...] = jnp.zeros_like(vg_ref)

    @pl.when(step < tiles)
    def _():
        rows = pl.ds(pl.multiple_of(step * tile, tile), tile)
        a1 = x_ref[...].astype(F32) + (nn(o_ref[...], w_ref[3]) + vec_ref[2:3, :])
        unit, rate = norm_parts(a1)
        unit1[rows, :] = unit
        rate1[rows, :] = rate
        h1 = unit * vec_ref[3:4, :] + vec_ref[4:5, :]
        low = h1.astype(BF16)
        h1b[rows, :] = low
        total = h1 + vec_ref[9:10, :]
        raw, value = {}, {}
        for turn in range(PARTS + 2):
            if turn < PARTS:
                c, at = turn // CUT, slice(turn % CUT * PART, (turn % CUT + 1) * PART)
                raw[turn] = nn(low, w_ref[4 + c, :, at]) + vec_ref[5 + c : 6 + c, at]
            if 0 <= turn - 1 < PARTS:
                cols = slice((turn - 1) * PART, turn * PART)
                up, grad = gelu_both(raw.pop(turn - 1))
                value[turn - 1] = up.astype(BF16)
                act[rows, cols] = value[turn - 1]
                slope[rows, cols] = grad.astype(BF16)
            if 0 <= turn - 2 < PARTS:
                c = (turn - 2) // CUT
                at = slice((turn - 2) % CUT * PART, ((turn - 2) % CUT + 1) * PART)
                total = total + nn(value.pop(turn - 2), w_ref[8 + c, at, :])
        unit, rate = norm_parts(total)
        unit2[rows, :] = unit
        rate2[rows, :] = rate
        z = (unit * vec_ref[10:11, :] + vec_ref[11:12, :]).astype(BF16)
        zb[rows, :] = z
        head_in[rows, :] = nn(z, stu_ref[0:D, :].astype(BF16)) + stu_ref[D + SW : D + SW + 1, :]

    @pl.when(step == tiles)
    def _():
        head_phase(
            info, stu_ref, cls_ref, goal_ref, sg_ref, cg_ref, head_in, head_low, micro, row_len
        )
        sg_ref[0:D, :] = tn(zb[...], head_low[...])
        @pl.loop(0, micro)
        def _(m):
            place = send_row[pl.ds(m, 1), :]
            spot = lax.broadcasted_iota(jnp.int32, (group * slots, row_len), 0)
            pick = jnp.where(spot == place, 1.0, 0.0).astype(BF16)
            here = pl.ds(pl.multiple_of(m * row_len, row_len), row_len)
            moved = nn(pick, zb[here, :]).astype(BF16)
            out_ref[:, m] = moved.reshape(group, slots, D)

    @pl.when(step >= tiles)
    def _():
        t = step - tiles
        rows = pl.ds(pl.multiple_of(t * tile, tile), tile)
        m = (t * tile) // row_len
        spot = lax.broadcasted_iota(jnp.int32, (tile, group * slots), 1)
        pick = jnp.where(spot == send_col[...], 1.0, 0.0).astype(BF16)
        dz = nn(pick, back_ref[:, m].reshape(group * slots, D))
        dz = dz + nt(head_low[rows, :], stu_ref[0:D, :].astype(BF16))
        unit = unit2[rows, :]
        vg_ref[10:11, :] += row_sum(dz * unit)
        vg_ref[11:12, :] += row_sum(dz)
        da2 = norm_back(dz * vec_ref[10:11, :], unit, rate2[rows, :])
        low = da2.astype(BF16)
        zb[rows, :] = low
        vg_ref[9:10, :] += row_sum(low.astype(F32))
        dh1 = da2
        raw, value = {}, {}
        for turn in range(PARTS + 2):
            if turn < PARTS:
                c, at = turn // CUT, slice(turn % CUT * PART, (turn % CUT + 1) * PART)
                raw[turn] = nt(low, w_ref[8 + c, at, :])
            if 0 <= turn - 1 < PARTS:
                cols = slice((turn - 1) * PART, turn * PART)
                c = (turn - 1) // CUT
                at = slice((turn - 1) % CUT * PART, ((turn - 1) % CUT + 1) * PART)
                du = (raw.pop(turn - 1) * slope[rows, cols].astype(F32)).astype(BF16)
                value[turn - 1] = du
                slope[rows, cols] = du
                vg_ref[5 + c : 6 + c, at] += row_sum(du.astype(F32))
            if 0 <= turn - 2 < PARTS:
                c = (turn - 2) // CUT
                at = slice((turn - 2) % CUT * PART, ((turn - 2) % CUT + 1) * PART)
                dh1 = dh1 + nt(value.pop(turn - 2), w_ref[4 + c, :, at])
        unit = unit1[rows, :]
        vg_ref[3:4, :] += row_sum(dh1 * unit)
        vg_ref[4:5, :] += row_sum(dh1)
        da1_ref[...] = norm_back(dh1 * vec_ref[3:4, :], unit, rate1[rows, :])

    @pl.when(step == 2 * tiles - 1)
    def _():
        @pl.loop(0, FF // D)
        def _(c):
            cols = pl.ds(pl.multiple_of(c * D, D), D)
            wg_ref[c] = tn(h1b[...], slope[:, cols]).astype(BF16)
            wg_ref[4 + c] = tn(act[:, cols], zb[...]).astype(BF16)


def head_phase(info, stu_ref, cls_ref, goal_ref, sg_ref, cg_ref, head_in, head_low, micro, row_len):
    scale = DH**-0.5
    query = stu_ref[D + SW + 2 : D + SW + 3, :]
    same = (
        lax.broadcasted_iota(jnp.int32, (SW, SW), 0) // DH
        == lax.broadcasted_iota(jnp.int32, (SW, SW), 1) // DH
    )
    same = jnp.where(same, 1.0, 0.0).astype(BF16)
    pooled, weights, members = [], [], []
    for m in range(micro):
        rows = slice(m * row_len, (m + 1) * row_len)
        s = head_in[rows, :]
        e = two_low(s * query, same) * scale
        sample = sample_column(ends_of(info, m), 0, row_len)
        share = jnp.zeros_like(e)
        for j in range(SAMP):
            member = sample == j
            peak = jnp.max(jnp.where(member, e, -1e30), axis=0, keepdims=True)
            up = jnp.where(member, jnp.exp(jnp.where(member, e - peak, 0.0)), 0.0)
            up = up / row_sum(up)
            share = share + up
            pooled.append(row_sum(up * s))
            members.append(member)
        weights.append(share)
    pooled = jnp.concatenate(pooled, axis=0)
    pool_weight = stu_ref[D : D + SW, :]
    mixed = jnp.tanh(exact(pooled, pool_weight) + stu_ref[D + SW + 1 : D + SW + 2, :])
    classes = cls_ref[:, 0:SW]
    bias = cls_ref[:, SW : SW + 1].T
    logits = exact(mixed, classes, (((1,), (1,)), ((), ()))) + bias
    logits = logits - jnp.max(logits, axis=-1, keepdims=True)
    chance = jnp.exp(logits)
    chance = chance / jnp.sum(chance, axis=-1, keepdims=True)
    goal = goal_ref[...]
    index = lax.broadcasted_iota(jnp.int32, (micro * SAMP, 1), 0)
    alive = jnp.zeros((micro * SAMP, 1), F32)
    for m in range(micro):
        for j, flag in enumerate(live_of(info, m)):
            alive = jnp.where(index == m * SAMP + j, flag.astype(F32), alive)
    target = jnp.exp(goal - jnp.max(goal, axis=-1, keepdims=True))
    target = target / jnp.sum(target, axis=-1, keepdims=True)
    d_logits = alive * (chance - target)
    cg_ref[:, 0:SW] = exact(d_logits, mixed, (((0,), (0,)), ((), ())))
    cg_ref[:, SW : SW + 1] = row_sum(d_logits).T
    d_pre = exact(d_logits, classes) * (1.0 - mixed * mixed)
    sg_ref[D : D + SW, :] = exact(pooled, d_pre, (((0,), (0,)), ((), ())))
    sg_ref[D + SW + 1 : D + SW + 2, :] = row_sum(d_pre)
    d_pooled = exact(d_pre, pool_weight, (((1,), (1,)), ((), ())))
    inner = two_low(pooled * d_pooled, same)
    d_bias = jnp.zeros((1, SW), F32)
    d_query = jnp.zeros((1, SW), F32)
    for m in range(micro):
        rows = slice(m * row_len, (m + 1) * row_len)
        s = head_in[rows, :]
        spread = jnp.zeros((row_len, SW), F32)
        center = jnp.zeros((row_len, SW), F32)
        for j in range(SAMP):
            member = members[m * SAMP + j]
            at = m * SAMP + j
            spread = jnp.where(member, d_pooled[at : at + 1, :], spread)
            center = jnp.where(member, inner[at : at + 1, :], center)
        share = weights[m]
        d_e = share * (two_low(s * spread, same) - center) * scale
        d_s = (share * spread + d_e * query).astype(BF16)
        head_low[rows, :] = d_s
        d_bias = d_bias + row_sum(d_s.astype(F32))
        d_query = d_query + row_sum(d_e * s)
    sg_ref[D + SW : D + SW + 1, :] = d_bias
    sg_ref[D + SW + 2 : D + SW + 3, :] = d_query


def feed(info, x, o, blocks, vec, student, classifier, goals, send_row, send_col, returned):
    micro, row_len, _ = x.shape
    tokens = micro * row_len
    tile = 512
    tiles = tokens // tile
    group, _, slots, _ = returned.shape
    whole = lambda *shape: pl.BlockSpec(shape, lambda i: (0,) * len(shape))
    once = lambda *shape: pl.BlockSpec(
        shape, lambda i: (0,) * len(shape), pipeline_mode=pl.Buffered(1)
    )
    ahead = lambda width: pl.BlockSpec((tile, width), lambda i: (jnp.minimum(i, tiles - 1), 0))
    behind = lambda width: pl.BlockSpec((tile, width), lambda i: (jnp.maximum(i - tiles, 0), 0))
    return pl.pallas_call(
        functools.partial(feed_kernel, tile=tile, micro=micro, row_len=row_len),
        grid=(2 * tiles,),
        in_specs=[
            pl.BlockSpec(memory_space=pltpu.SMEM),
            ahead(D),
            ahead(D),
            once(NMAT, D, D),
            once(NMAT, D),
            once(*student.shape),
            once(*classifier.shape),
            once(*goals.shape),
            once(*send_row.shape),
            behind(1),
            once(*returned.shape),
        ],
        out_specs=[
            behind(D),
            once(*returned.shape),
            once(8, D, D),
            once(NMAT, D),
            once(*student.shape),
            once(*classifier.shape),
        ],
        out_shape=[
            jax.ShapeDtypeStruct((tokens, D), F32),
            jax.ShapeDtypeStruct(returned.shape, BF16),
            jax.ShapeDtypeStruct((NMAT, D, D), BF16),
            jax.ShapeDtypeStruct((NMAT, D), F32),
            jax.ShapeDtypeStruct(student.shape, F32),
            jax.ShapeDtypeStruct(classifier.shape, F32),
        ],
        scratch_shapes=[
            pltpu.VMEM((tokens, D), F32),
            pltpu.VMEM((tokens, 1), F32),
            pltpu.VMEM((tokens, D), BF16),
            pltpu.VMEM((tokens, FF), BF16),
            pltpu.VMEM((tokens, FF), BF16),
            pltpu.VMEM((tokens, D), F32),
            pltpu.VMEM((tokens, 1), F32),
            pltpu.VMEM((tokens, D), BF16),
            pltpu.VMEM((tokens, SW), F32),
            pltpu.VMEM((tokens, SW), BF16),
        ],
        compiler_params=pltpu.CompilerParams(vmem_limit_bytes=VMEM),
        cost_estimate=pl.CostEstimate(
            flops=tokens * D * FF * 12, bytes_accessed=tokens * D * 16, transcendentals=tokens * FF
        ),
    )(
        info,
        x.reshape(tokens, D),
        o.reshape(tokens, D),
        blocks,
        vec,
        student,
        classifier,
        goals,
        send_row,
        send_col,
        returned,
    )


def attend_back_kernel(
    info,
    x_ref,
    da1_ref,
    q_ref,
    k_ref,
    v_ref,
    o_ref,
    l_ref,
    w_ref,
    _,
    dx_ref,
    wg_ref,
    vg_ref,
    qx,
    kx,
    vx,
    dox,
    dq,
    dk,
    dv,
    dk_sum,
    dv_sum,
    wsum,
    *,
    micro,
):
    row = pl.program_id(0)
    row_len = x_ref.shape[1]
    ends, live = ends_of(info, row), live_of(info, row)
    first = lane_index(QT) < DH
    ones = jnp.ones((QT, LANES), F32)

    @pl.when(row == 0)
    def _():
        vg_ref[...] = jnp.zeros_like(vg_ref)
        wsum[...] = jnp.zeros_like(wsum)

    head = lax.broadcasted_iota(jnp.int32, (D, LANES), 0) // DH
    spot = head // 2 + DH * (1 - head % 2)
    gather = lax.broadcasted_iota(jnp.int32, (D, LANES), 1) == spot
    gather = jnp.where(gather, 1.0, 0.0).astype(BF16)

    dq[...] = jnp.zeros_like(dq)

    @pl.loop(0, row_len // QT)
    def _(t):
        rows = pl.ds(pl.multiple_of(t * QT, QT), QT)
        sample = sample_column(ends, t * QT, QT)
        lane = lane_index(QT) % DH
        high, mid, rest = split_low(jnp.where(lane < PAIRS, -l_ref[0, rows, :], 0.0))
        q_extra = (
            query_spare(sample, QT)
            + high
            + pltpu.roll(mid, PAIRS, 1)
            + pltpu.roll(rest, 2 * PAIRS, 1)
        )
        branch = da1_ref[0, rows, :].astype(BF16)
        vg_ref[2:3, :] += row_sum(branch.astype(F32))
        do = nt(branch, w_ref[3]).astype(BF16).astype(F32)
        delta = two_low(do * o_ref[0, rows, :].astype(F32), gather)
        high = delta.astype(BF16).astype(F32)
        do_extra = pltpu.roll(high - delta, PAIRS, 1) - high
        for p in range(PAIRS):
            pair = head_lanes(p)
            k_extra = key_spare(sample, QT, p)
            store_heads(dox, rows, p, do[:, pair], do_extra, first)
            store_heads(qx, rows, p, q_ref[0, rows, pair].astype(F32), q_extra, first)
            store_heads(kx, rows, p, k_ref[0, rows, pair].astype(F32), k_extra, first)
            store_heads(vx, rows, p, v_ref[0, rows, pair].astype(F32), k_extra, first)

    @pl.loop(0, row_len // QT)
    def _(t):
        rows = pl.ds(pl.multiple_of(t * QT, QT), QT)
        begin, number = reach(ends, live, t * QT, QT, row_len)
        number = (number + STEP - 1) // STEP
        begin = jnp.minimum(begin, row_len // KG - number * STEP)
        dk_sum[...] = jnp.zeros_like(dk_sum)
        dv_sum[...] = jnp.zeros_like(dv_sum)

        @pl.loop(0, number)
        def _(j):
            span = pl.ds(pl.multiple_of((begin + j * STEP) * KG, KG), STEP * KG)
            wide = lane_index(STEP * KG) < DH
            raw, done, got = {}, {}, {}
            for step in range(H + 2):
                if step < H:
                    cols = head_lanes(step)
                    raw[step] = (
                        nt(kx[rows, cols], qx[span, cols]),
                        nt(vx[rows, cols], dox[span, cols]),
                    )
                h = step - 1
                if 0 <= h < H:
                    s, dp = raw.pop(h)
                    prob = jnp.exp(s)
                    done[h] = (prob.astype(BF16), (prob * dp).astype(BF16))
                h = step - 2
                if 0 <= h < H:
                    cols = head_lanes(h)
                    prob, ds = done.pop(h)
                    got[h] = (
                        nn(prob, dox[span, cols]),
                        nn(ds, qx[span, cols]),
                        tn(ds, kx[rows, cols]),
                    )
                    if h % 2 == 1:
                        left, right = got.pop(h - 1), got.pop(h)
                        cols = head_lanes(h // 2)
                        dv_sum[:, cols] += jnp.where(first, left[0], right[0])
                        dk_sum[:, cols] += jnp.where(first, left[1], right[1])
                        dq[span, cols] += jnp.where(wide, left[2], right[2])

        dk[rows, :] = dk_sum[...].astype(BF16)
        dv[rows, :] = dv_sum[...].astype(BF16)

    @pl.loop(0, row_len // QT)
    def _(t):
        rows = pl.ds(pl.multiple_of(t * QT, QT), QT)
        dq_low = (dq[rows, :] * DH**-0.5).astype(BF16)
        dk_low, dv_low = dk[rows, :], dv[rows, :]
        vg_ref[0:1, :] += row_sum(dq_low.astype(F32))
        vg_ref[1:2, :] += row_sum(dv_low.astype(F32))
        dx_ref[0, rows, :] = (
            da1_ref[0, rows, :]
            + nt(dq_low, w_ref[0])
            + nt(dk_low, w_ref[1])
            + nt(dv_low, w_ref[2])
        ).astype(BF16)

    x = x_ref[0]
    wsum[0] += tn(x, (dq[...] * DH**-0.5).astype(BF16))
    wsum[1] += tn(x, dk[...])
    wsum[2] += tn(x, dv[...])
    wsum[3] += tn(o_ref[0], da1_ref[0].astype(BF16))

    @pl.when(row == micro - 1)
    def _():
        wg_ref[...] = wsum[...].astype(BF16)


def attend_back(info, tokens, da1, q, k, v, o, logs, blocks, grads):
    micro, row_len, _ = tokens.shape
    row_spec = lambda width: pl.BlockSpec((1, row_len, width), lambda r: (r, 0, 0))
    return pl.pallas_call(
        functools.partial(attend_back_kernel, micro=micro),
        grid=(micro,),
        in_specs=[
            pl.BlockSpec(memory_space=pltpu.SMEM),
            *[row_spec(D)] * 6,
            row_spec(LANES),
            pl.BlockSpec((4, D, D), lambda r: (0, 0, 0)),
            pl.BlockSpec(memory_space=pl.ANY),
        ],
        out_specs=[
            row_spec(D),
            pl.BlockSpec((4, D, D), lambda r: (2, 0, 0)),
            pl.BlockSpec((8, D), lambda r: (0, 0)),
        ],
        out_shape=[
            jax.ShapeDtypeStruct((micro, row_len, D), BF16),
            jax.ShapeDtypeStruct((NMAT, D, D), BF16),
            jax.ShapeDtypeStruct((8, D), F32),
        ],
        scratch_shapes=[
            *[pltpu.VMEM((row_len, 2 * D), BF16)] * 4,
            pltpu.VMEM((row_len, D), F32),
            pltpu.VMEM((row_len, D), BF16),
            pltpu.VMEM((row_len, D), BF16),
            pltpu.VMEM((QT, D), F32),
            pltpu.VMEM((QT, D), F32),
            pltpu.VMEM((4, D, D), F32),
        ],
        input_output_aliases={9: 1},
        compiler_params=pltpu.CompilerParams(vmem_limit_bytes=VMEM),
        cost_estimate=pl.CostEstimate(
            flops=micro * row_len * D * D * 16 + micro * H * row_len * row_len * DH * 10,
            bytes_accessed=micro * row_len * D * 16,
            transcendentals=micro * H * row_len * row_len,
        ),
    )(info, tokens, da1, q, k, v, o, logs, blocks, grads)


CHUNKS = 6
STU_ROWS, CLS_ROWS, VEC_ROWS = 656, 16, 16
SMALL_ROWS = STU_ROWS + 2 * CLS_ROWS + 4 * VEC_ROWS + 16


def reduce_kernel(
    group,
    owners,
    grad_ref,
    ff_vec,
    at_vec,
    stu_ref,
    cls_ref,
    own_ref,
    vec_out,
    stu_out,
    cls_out,
    got_a,
    sum_a,
    got_b,
    part,
    got_c,
    final,
    small,
    small_got,
    small_sum,
    small_end,
    send_sem,
    recv_sem,
    small_send,
    small_recv,
):
    b, s = lax.axis_index("batch"), lax.axis_index("shard")
    per = NMAT // owners
    rows = per * D // CHUNKS
    batch_bits, shard_bits = bits_of(group), bits_of(owners)
    half = SMALL_ROWS // 2

    def copy(src, dst, sems, at, where):
        return pltpu.make_async_remote_copy(
            src_ref=src,
            dst_ref=dst,
            send_sem=sems[0].at[at],
            recv_sem=sems[1].at[at],
            device_id=where,
            device_id_type=pl.DeviceIdType.MESH,
        )

    peers = [(b, s ^ bit) for bit in shard_bits] + [(b ^ bit, s) for bit in batch_bits]
    barrier = pltpu.get_barrier_semaphore()
    for peer in peers:
        pl.semaphore_signal(
            barrier, inc=1, device_id=peer, device_id_type=pl.DeviceIdType.MESH
        )
    pl.semaphore_wait(barrier, len(peers))

    sems = (send_sem, recv_sem)
    small_sems = (small_send, small_recv)
    waits = []

    def begin(op):
        op.start()
        waits.append(op)
        return op

    def piece(owner, c):
        at = lax.rem(owner * per + c * per // CHUNKS + 8, NMAT)
        if rows == D:
            return grad_ref.at[at]
        step = D // rows
        return grad_ref.at[at, pl.ds((c % step) * rows, rows)]

    far = shard_bits[1]
    first = {}
    for c in range(CHUNKS):
        first[c] = [
            begin(copy(piece(s ^ 1 ^ far, c), got_a.at[c, 0], sems, (c, 0), peers[0])),
            begin(copy(piece(s ^ 1, c), got_a.at[c, 1], sems, (c, 1), peers[0])),
        ]

    small[...] = jnp.zeros_like(small)
    stu_count = stu_ref.shape[0]
    small[0:stu_count, :] = stu_ref[...].astype(BF16)
    small[STU_ROWS : STU_ROWS + CLS, :] = cls_ref[:, 0:SW].astype(BF16)
    small[STU_ROWS + CLS_ROWS : STU_ROWS + CLS_ROWS + CLS, 0:1] = cls_ref[:, SW:].astype(BF16)
    for i in range(4):
        at = STU_ROWS + 2 * CLS_ROWS + i * VEC_ROWS
        lanes = slice(i * LANES, (i + 1) * LANES)
        small[at : at + 3, :] = at_vec[0:3, lanes].astype(BF16)
        small[at + 3 : at + NMAT, :] = ff_vec[3:NMAT, lanes].astype(BF16)
    core = lax.rem(s, 2)
    mine = pl.ds(pl.multiple_of(core * half, 16), half)
    other = pl.ds(pl.multiple_of((1 - core) * half, 16), half)
    small_op = begin(copy(small.at[other], small_got.at[0], small_sems, 0, peers[0]))

    def add(x, y):
        return (x.astype(F32) + y.astype(F32)).astype(BF16)

    second = {}

    def start_second(c):
        for i, op in enumerate(first[c]):
            op.wait_recv()
            owner = s ^ far if i == 0 else s
            sum_a[c, i] = add(piece(owner, c)[...], got_a[c, i])
        second[c] = begin(copy(sum_a.at[c, 0], got_b.at[c], sems, (c, 2), peers[1]))

    start_second(0)
    start_second(1)

    spans = []
    size = rows
    for bit in batch_bits:
        halving = size >= 32
        spans.append((bit, size, halving))
        if halving:
            size //= 2
    offset_of = []
    offset = jnp.int32(0)
    slot_of = []
    slot = 0
    for bit, now, halving in spans:
        place = lax.rem(b // bit, 2)
        offset_of.append((offset, place))
        slot_of.append(slot)
        if halving:
            offset = offset + place * (now // 2)
            slot += now // 2
        else:
            slot += now
    last = offset

    def ranged(ref, c, start, count):
        return ref.at[c, pl.ds(pl.multiple_of(start, 16), count)]

    moving = {}

    def start_batch(c, k):
        bit, now, halving = spans[k]
        start, place = offset_of[k]
        if halving:
            count = now // 2
            src = ranged(part.at[k], c, start + (1 - place) * count, count)
        else:
            count = now
            src = ranged(part.at[k], c, start, count)
        dst = got_c.at[c, pl.ds(slot_of[k], count)]
        moving[c, k] = begin(copy(src, dst, sems, (c, 3 + k), (b ^ bit, s)))

    def end_batch(c, k):
        bit, now, halving = spans[k]
        start, place = offset_of[k]
        moving[c, k].wait_recv()
        count = now // 2 if halving else now
        if halving:
            start = start + place * count
        here = pl.ds(pl.multiple_of(start, 16), count)
        total = add(part[k, c, here, :], got_c[c, slot_of[k] : slot_of[k] + count])
        if k + 1 < len(spans):
            part[k + 1, c, here, :] = total
        else:
            final[c, here, :] = total

    gathers = [k for k in reversed(range(len(spans))) if spans[k][2]]
    gathering = {}

    def start_gather(c, g):
        k = gathers[g]
        bit, now, _ = spans[k]
        start, place = offset_of[k]
        count = now // 2
        at = ranged(final, c, start + place * count, count)
        gathering[c, g] = begin(
            copy(at, at, sems, (c, 3 + len(spans) + g), (b ^ bit, s))
        )

    def stage(c, k):
        if k == 0:
            second[c].wait_recv()
            if c + 2 < CHUNKS:
                start_second(c + 2)
            part[0, c] = add(sum_a[c, 1], got_b[c])
            start_batch(c, 0)
        elif k <= len(spans):
            end_batch(c, k - 1)
            if k < len(spans):
                start_batch(c, k)
            else:
                start_gather(c, 0)
        else:
            g = k - len(spans) - 1
            gathering[c, g].wait_recv()
            if g + 1 < len(gathers):
                start_gather(c, g + 1)
            else:
                per_block = CHUNKS // per
                block, within = c // per_block, c % per_block
                own_ref[block, within * rows : (within + 1) * rows, :] = final[c]

    stages = 1 + len(spans) + len(gathers)
    rest = [(b, s ^ bit) for bit in shard_bits[1:]] + [(b ^ bit, s) for bit in batch_bits]

    def small_stage(k):
        nonlocal small_op
        small_op.wait_recv()
        if k == 0:
            small_sum[0] = add(small[mine, :], small_got[0])
        elif k <= len(rest):
            small_sum[k] = add(small_sum[k - 1], small_got[k])
        if k < len(rest):
            small_op = begin(
                copy(small_sum.at[k], small_got.at[k + 1], small_sems, k + 1, rest[k])
            )
        elif k == len(rest):
            small_end[mine, :] = small_sum[k]
            small_op = begin(
                copy(small_sum.at[k], small_end.at[mine], small_sems, k + 1, peers[0])
            )

    small_k = 0
    for tick in range(CHUNKS + stages - 1):
        for k in reversed(range(stages)):
            c = tick - k
            if 0 <= c < CHUNKS:
                stage(c, k)
        if small_k <= len(rest) + 1:
            small_stage(small_k)
            small_k += 1
    while small_k <= len(rest) + 1:
        small_stage(small_k)
        small_k += 1

    for i in range(4):
        at = STU_ROWS + 2 * CLS_ROWS + i * VEC_ROWS
        lanes = slice(i * LANES, (i + 1) * LANES)
        vec_out[:, lanes] = small_end[at : at + VEC_ROWS, :].astype(F32)
    stu_out[...] = small_end[0:STU_ROWS, :].astype(F32)
    cls_out[:, 0:LANES] = small_end[STU_ROWS : STU_ROWS + CLS_ROWS, :].astype(F32)
    at = STU_ROWS + CLS_ROWS
    cls_out[:, LANES:] = small_end[at : at + CLS_ROWS, :].astype(F32)
    for op in waits:
        op.wait_send()


def reduce_grads(grads, ff_vec, at_vec, stu, cls):
    group, owners = lax.axis_size("batch"), lax.axis_size("shard")
    per = NMAT // owners
    rows = per * D // CHUNKS
    batch_count = len(bits_of(group))
    copies = 3 + 2 * batch_count
    small_count = len(bits_of(owners)) + batch_count + 1
    vmem = pl.BlockSpec(memory_space=pltpu.VMEM)
    return pl.pallas_call(
        functools.partial(reduce_kernel, group, owners),
        in_specs=[vmem] * 5,
        out_specs=[vmem] * 4,
        out_shape=[
            jax.ShapeDtypeStruct((per, D, D), BF16),
            jax.ShapeDtypeStruct((VEC_ROWS, D), F32),
            jax.ShapeDtypeStruct((STU_ROWS, SW), F32),
            jax.ShapeDtypeStruct((CLS_ROWS, 2 * LANES), F32),
        ],
        scratch_shapes=[
            pltpu.VMEM((CHUNKS, 2, rows, D), BF16),
            pltpu.VMEM((CHUNKS, 2, rows, D), BF16),
            pltpu.VMEM((CHUNKS, rows, D), BF16),
            pltpu.VMEM((batch_count, CHUNKS, rows, D), BF16),
            pltpu.VMEM((CHUNKS, rows + 16 * batch_count, D), BF16),
            pltpu.VMEM((CHUNKS, rows, D), BF16),
            pltpu.VMEM((SMALL_ROWS, LANES), BF16),
            pltpu.VMEM((small_count - 1, SMALL_ROWS // 2, LANES), BF16),
            pltpu.VMEM((small_count - 1, SMALL_ROWS // 2, LANES), BF16),
            pltpu.VMEM((SMALL_ROWS, LANES), BF16),
            pltpu.SemaphoreType.DMA((CHUNKS, copies)),
            pltpu.SemaphoreType.DMA((CHUNKS, copies)),
            pltpu.SemaphoreType.DMA((small_count,)),
            pltpu.SemaphoreType.DMA((small_count,)),
        ],
        compiler_params=pltpu.CompilerParams(
            collective_id=1, has_side_effects=True, vmem_limit_bytes=32 * 1024 * 1024
        ),
        cost_estimate=pl.CostEstimate(
            flops=NMAT * D * D * 4, bytes_accessed=NMAT * D * D * 8, transcendentals=0
        ),
    )(grads, ff_vec, at_vec, stu, cls)


def update_kernel(
    own_ref,
    blocks_ref,
    left_ref,
    right_ref,
    lroot_ref,
    rroot_ref,
    shard_ref,
    vsum_ref,
    vec_ref,
    vmom_ref,
    ssum_ref,
    stu_ref,
    smom_ref,
    csum_ref,
    cls_ref,
    cmom_ref,
    back_ref,
    rows_ref,
    grad_out,
    new_out,
    left_out,
    right_out,
    vg_out,
    vm_out,
    v_out,
    sg_out,
    sm_out,
    s_out,
    cg_out,
    cm_out,
    c_out,
    layer_out,
    *,
    owners,
):
    step = pl.program_id(0)
    row_len = layer_out.shape[1]

    @pl.when(step < rows_ref.shape[1])
    def _():
        arrived = rows_ref[:, step].reshape(row_len, D)
        chunk = min(256, row_len)

        @pl.loop(0, row_len // chunk)
        def _(k):
            at = pl.multiple_of(k * chunk, chunk)
            spot = at + lax.broadcasted_iota(jnp.int32, (chunk, row_len), 0)
            pick = jnp.where(spot == back_ref[pl.ds(step, 1), :], 1.0, 0.0).astype(BF16)
            layer_out[0, pl.ds(at, chunk), :] = nn(pick, arrived).astype(BF16)

    g = own_ref[0]
    grad_out[0] = g.astype(F32)
    left_out[0] = decay_rate * left_ref[0] + (1.0 - decay_rate) * nt(g, g)
    right_out[0] = decay_rate * right_ref[0] + (1.0 - decay_rate) * tn(g, g)
    steered = nn(lroot_ref[0].astype(BF16), g).astype(BF16)
    steered = nn(steered, rroot_ref[0].astype(BF16))
    size = jnp.mean(steered * steered, keepdims=True)
    new_out[0] = blocks_ref[0].astype(F32) - steered * (block_rate * lax.rsqrt(size + 1e-06))

    @pl.when(pl.program_id(0) == 0)
    def _():
        per = NMAT // owners
        mine = vsum_ref[0:per, :]
        for i in range(1, owners):
            mine = jnp.where(shard_ref[0] == i, vsum_ref[i * per : (i + 1) * per, :], mine)

        def rule(grads, old, moment, rate, outs):
            renewed = decay_rate * moment + (1.0 - decay_rate) * grads * grads
            outs[0][...] = grads
            outs[1][...] = renewed
            outs[2][...] = old - rate * grads / (jnp.sqrt(renewed) + 1e-08)

        rule(mine, vec_ref[...], vmom_ref[...], vector_rate, (vg_out, vm_out, v_out))
        rule(
            ssum_ref[0 : stu_ref.shape[0], :],
            stu_ref[...],
            smom_ref[...],
            head_rate,
            (sg_out, sm_out, s_out),
        )
        rule(
            csum_ref[0:CLS, 0 : SW + 1],
            cls_ref[...],
            cmom_ref[...],
            head_rate,
            (cg_out, cm_out, c_out),
        )


def update(own, blocks, left, right, lroot, rroot, shard, vsum, vec, vmom, ssum, stu, smom, csum, cls, cmom, back, arrived):
    per = own.shape[0]
    micro, row_len = back.shape
    mat = pl.BlockSpec((1, D, D), lambda i: (i, 0, 0))
    whole = lambda a: pl.BlockSpec(a.shape, lambda i: (0,) * a.ndim)
    like = lambda a: jax.ShapeDtypeStruct(a.shape, F32)
    return pl.pallas_call(
        functools.partial(update_kernel, owners=NMAT // per),
        grid=(per,),
        in_specs=[mat] * 6
        + [pl.BlockSpec(memory_space=pltpu.SMEM)]
        + [whole(a) for a in (vsum, vec, vmom, ssum, stu, smom, csum, cls, cmom, back, arrived)],
        out_specs=[mat] * 4
        + [whole(a) for a in (vec,) * 3 + (stu,) * 3 + (cls,) * 3]
        + [pl.BlockSpec((1, row_len, D), lambda i: (jnp.minimum(i, micro - 1), 0, 0))],
        out_shape=[like(left)] * 4
        + [like(a) for a in (vec,) * 3 + (stu,) * 3 + (cls,) * 3]
        + [jax.ShapeDtypeStruct((micro, row_len, D), BF16)],
        compiler_params=pltpu.CompilerParams(vmem_limit_bytes=44 * 1024 * 1024),
    )(
        own,
        blocks,
        left,
        right,
        lroot,
        rroot,
        shard,
        vsum,
        vec,
        vmom,
        ssum,
        stu,
        smom,
        csum,
        cls,
        cmom,
        back,
        arrived,
    )


def local(
    tokens,
    cotangent,
    lengths,
    exit_layers,
    teacher,
    blocks,
    left_stats,
    right_stats,
    left_root,
    right_root,
    vectors,
    vec_moment,
    student,
    stu_moment,
    classifier,
    cls_moment,
):
    micro, _, row_len, _ = tokens.shape
    tokens, cotangent = tokens[:, 0], cotangent[:, 0]
    info = jnp.concatenate([lengths[:, 0], exit_layers[:, 0]], axis=1)
    matrices, vec, grad_outgoing, send, send_col, back = opening(
        info, blocks, vectors, cotangent
    )
    matrices = matrices.reshape(NMAT, D, D)
    returned = lax.all_to_all(grad_outgoing, "batch", split_axis=0, concat_axis=0, tiled=True)

    q, k, v, o, logs = attend(info, tokens, matrices, vec)
    goals = teacher.reshape(micro * SAMP, CLS)
    classifier, cls_moment = classifier.T, cls_moment.T
    da1, outgoing, ff_grads, ff_vecs, stu_grads, cls_grads = feed(
        info, tokens, o, matrices, vec, student, classifier, goals, send, send_col, returned
    )
    arrived = lax.all_to_all(outgoing, "batch", split_axis=0, concat_axis=0, tiled=True)
    input_grads, grads, at_vecs = attend_back(
        info, tokens, da1.reshape(micro, row_len, D), q, k, v, o, logs, matrices, ff_grads
    )
    own, vec_sum, stu_sum, cls_sum = reduce_grads(grads, ff_vecs, at_vecs, stu_grads, cls_grads)
    shard = lax.axis_index("shard").astype(jnp.int32).reshape(1)
    *updated, layer_out = update(
        own,
        blocks,
        left_stats,
        right_stats,
        left_root,
        right_root,
        shard,
        vec_sum,
        vectors,
        vec_moment,
        stu_sum,
        student,
        stu_moment,
        cls_sum,
        classifier,
        cls_moment,
        back,
        arrived,
    )
    classes = [a.T for a in updated[-3:]]
    return (layer_out[:, None], input_grads[:, None], *updated[:-3], *classes)


def solution(mesh):
    rows = P(None, ("batch", "shard"), None, None)
    tags = P(None, ("batch", "shard"), None)
    mats = P("shard", None, None)
    vecs = P("shard", None)
    return jax.shard_map(
        local,
        mesh=mesh,
        in_specs=(rows, rows, tags, tags, rows, mats, mats, mats, mats, mats, vecs, vecs)
        + (P(),) * 4,
        out_specs=(rows, rows, mats, mats, mats, mats, vecs, vecs, vecs) + (P(),) * 6,
        check_vma=False,
    )
```

```python
import functools

import jax
import jax.numpy as jnp
from jax import lax
from jax.experimental import pallas as pl
from jax.experimental.pallas import tpu as pltpu
from jax.sharding import PartitionSpec as P

D = 512
H = 8
DH = 64
FF = 2048
SW = 128
NMAT = 12
SAMP = 4
LAYER = 4
CLS = 14

decay_rate = 0.5
block_rate = 0.04
vector_rate = 0.05
head_rate = 0.05

QT = 256
STEP = 2
KG = 128
PAIRS = H // 2
LANES = 128
PART = 512
PARTS, CUT = FF // PART, D // PART
BIG = float(2**30)
EPS = 1e-6
VMEM = 60 * 1024 * 1024

F32 = jnp.float32
BF16 = jnp.bfloat16


def nn(a, b):
    return jnp.dot(a, b, preferred_element_type=F32)


def nt(a, b):
    return lax.dot_general(a, b, (((1,), (1,)), ((), ())), preferred_element_type=F32)


def tn(a, b):
    return lax.dot_general(a, b, (((0,), (0,)), ((), ())), preferred_element_type=F32)


def exact(a, b, dims=(((1,), (0,)), ((), ()))):
    return lax.dot_general(
        a, b, dims, preferred_element_type=F32, precision=lax.Precision.HIGHEST
    )


def row_sum(v):
    return jnp.sum(v, axis=0, keepdims=True)


def two_low(v, b):
    high = v.astype(BF16)
    return nn(high, b) + nn((v - high.astype(F32)).astype(BF16), b)


def split_low(v):
    high = v.astype(BF16).astype(F32)
    rest = v - high
    mid = rest.astype(BF16).astype(F32)
    return high, mid, rest - mid


def ends_of(info, row):
    ends, total = [], jnp.int32(0)
    for j in range(SAMP):
        total = total + info[row, j]
        ends.append(total)
    return ends


def live_of(info, row):
    return [(info[row, SAMP + j] >= LAYER).astype(jnp.int32) for j in range(SAMP)]


def sample_column(ends, first, count):
    place = first + lax.broadcasted_iota(jnp.int32, (count, 1), 0)
    total = jnp.zeros((count, 1), jnp.int32)
    for j in range(SAMP - 1):
        total = total + (place >= ends[j]).astype(jnp.int32)
    return total


def reach(ends, live, first, count, row_len):
    low, high = jnp.int32(row_len), jnp.int32(0)
    start = jnp.int32(0)
    for j in range(SAMP):
        end = ends[j]
        meets = (start < first + count) & (end > first) & (end > start) & (live[j] > 0)
        low = jnp.where(meets, jnp.minimum(low, start), low)
        high = jnp.where(meets, jnp.maximum(high, end), high)
        start = end
    begin = low // KG
    number = jnp.maximum((high + KG - 1) // KG - begin, 0)
    return begin, number


def lane_index(rows):
    return lax.broadcasted_iota(jnp.int32, (rows, LANES), 1)


TAG = 16


def key_spare(sample, rows, pair):
    lane = lane_index(rows) % DH
    own = (lane < 3 * PAIRS) & (lane % PAIRS == pair)
    return jnp.where(own | (lane == sample + TAG), 1.0, 0.0)


def query_spare(sample, rows):
    lane = lane_index(rows) % DH
    tag = (lane >= TAG) & (lane < TAG + SAMP) & (lane != sample + TAG)
    return jnp.where(tag, -BIG, 0.0)


def store_heads(ref, rows, p, pair, spare, first):
    ref[rows, 2 * p * LANES : (2 * p + 1) * LANES] = jnp.where(first, pair, spare).astype(BF16)
    ref[rows, (2 * p + 1) * LANES : (2 * p + 2) * LANES] = jnp.where(
        first, spare, pair
    ).astype(BF16)


def head_lanes(h):
    return slice(h * LANES, (h + 1) * LANES)


def widths(row_len):
    most = row_len // KG
    return list(range(most // 2, most + 1))


def chosen_span(ends, live, t, row_len):
    begin, number = reach(ends, live, t * QT, QT, row_len)
    least, most = widths(row_len)[0], row_len // KG
    number = jnp.where(number > 0, jnp.maximum(number, least), 0)
    return jnp.minimum(begin, most - number), number


WEIGHT_PARTS = 4


def bits_of(size):
    return [1 << i for i in range(size.bit_length() - 1)]


def token_spots(place, ends, live, start, group, slots):
    shift, keep = jnp.zeros_like(place), jnp.zeros_like(place)
    before, begin = jnp.int32(0), jnp.int32(0)
    for j in range(SAMP):
        inside = (place >= begin) & (place < ends[j])
        shift = jnp.where(inside, before - begin, shift)
        keep = jnp.where(inside, live[j], keep)
        before = before + live[j] * (ends[j] - begin)
        begin = ends[j]
    rank = place + shift
    fold = group.bit_length() - 1
    spot = ((start + rank) & (group - 1)) * slots + (rank >> fold)
    return jnp.where(keep > 0, spot, group * slots)


def count_kernel(
    group,
    info,
    cot_ref,
    out_ref,
    send_row,
    send_col,
    back_row,
    tally,
    tallies,
    count_send,
    count_recv,
):
    b, s = lax.axis_index("batch"), lax.axis_index("shard")
    micro, row_len, _ = cot_ref.shape
    slots = row_len // group
    mesh_id = pl.DeviceIdType.MESH

    peers = [(lax.rem(b + i, group), s) for i in range(1, group)]
    barrier = pltpu.get_barrier_semaphore()
    for peer in peers:
        pl.semaphore_signal(barrier, inc=1, device_id=peer, device_id_type=mesh_id)

    lane = lax.broadcasted_iota(jnp.int32, (8, LANES), 1)
    mine = jnp.zeros((8, LANES), jnp.int32)
    for m in range(micro):
        total = jnp.int32(0)
        for j in range(SAMP):
            alive = (info[m, SAMP + j] >= LAYER).astype(jnp.int32)
            total = total + alive * info[m, j]
        mine = jnp.where(lane == m, total, mine)
    tally[...] = mine
    pl.semaphore_wait(barrier, len(peers))

    counts = []
    for i in range(1, group):
        op = pltpu.make_async_remote_copy(
            src_ref=tally,
            dst_ref=tallies.at[i - 1],
            send_sem=count_send.at[i - 1],
            recv_sem=count_recv.at[i - 1],
            device_id=peers[i - 1],
            device_id_type=mesh_id,
        )
        op.start()
        counts.append(op)
    for op in counts:
        op.wait_recv()
    start = jnp.zeros((8, LANES), jnp.int32)
    place_row = lax.broadcasted_iota(jnp.int32, (1, row_len), 1)
    place_col = lax.broadcasted_iota(jnp.int32, (row_len, 1), 0)
    for i in range(1, group):
        start = start + jnp.where(b >= i, tallies[i - 1], 0)

    for m in range(micro):
        ends, live = ends_of(info, m), live_of(info, m)
        begin = start[0:1, m : m + 1]
        send_row[m : m + 1, :] = token_spots(place_row, ends, live, begin, group, slots)
        send_col[m * row_len : (m + 1) * row_len, :] = token_spots(
            place_col, ends, live, begin, group, slots
        )

    def home_slots(place, m):
        source = place // slots
        first = jnp.zeros_like(place)
        number = jnp.zeros_like(place)
        for i in range(group):
            other = tally if i == 0 else tallies.at[i - 1]
            at = lax.rem(b - i + group, group)
            here = other[0:1, m : m + 1]
            number = jnp.where(source == at, here, number)
            first = first + jnp.where(source > at, here, 0)
        turn = ((b - first) & (group - 1)) + group * (place & (slots - 1))
        slot = (first + turn) >> (group.bit_length() - 1)
        return jnp.where(turn < number, slot, row_len)

    for m in range(micro):
        back_row[m : m + 1, :] = home_slots(place_row, m)

    chunk = min(256, row_len)

    @pl.loop(0, micro * row_len // chunk)
    def _(k):
        m = (k * chunk) // row_len
        at = lax.rem(k * chunk, row_len)
        place = at + lax.broadcasted_iota(jnp.int32, (chunk, 1), 0)
        home = jnp.where(m == 0, home_slots(place, 0), home_slots(place, micro - 1))
        spot = lax.broadcasted_iota(jnp.int32, (chunk, row_len), 1)
        pick = jnp.where(spot == home, 1.0, 0.0).astype(BF16)
        moved = nn(pick, cot_ref[m]).astype(BF16)
        count = chunk // slots
        out_ref[pl.ds(at // slots, count), m] = moved.reshape(count, slots, D)

    for op in counts:
        op.wait_send()


def weight_kernel(
    group,
    owners,
    blocks_ref,
    vec_ref,
    w_out,
    vec_out,
    vecs,
    own_sem,
    vec_send,
    vec_recv,
    w_send,
    w_recv,
):
    b, s = lax.axis_index("batch"), lax.axis_index("shard")
    per = NMAT // owners
    far = bits_of(owners)[1]
    near = 1
    mesh_id = pl.DeviceIdType.MESH
    shard_peers = [(b, s ^ i) for i in range(1, owners)]
    x_peer, y_peer, core_peer = (b, s ^ far), (b ^ 1, s), (b, s ^ near)
    barrier = pltpu.get_barrier_semaphore()
    for peer in shard_peers + [y_peer]:
        pl.semaphore_signal(barrier, inc=1, device_id=peer, device_id_type=mesh_id)
    low = vec_ref[...].astype(BF16).astype(F32)
    vecs[owners] = jnp.concatenate([low, jnp.zeros((8 - per, D), F32)], axis=0)
    pl.semaphore_wait(barrier, len(shard_peers) + 1)

    def remote(src, dst, sems, at, peer):
        op = pltpu.make_async_remote_copy(
            src_ref=src,
            dst_ref=dst,
            send_sem=sems[0].at[at],
            recv_sem=sems[1].at[at],
            device_id=peer,
            device_id_type=mesh_id,
        )
        op.start()
        return op

    half = per * D // 2
    rows = half // WEIGHT_PARTS
    side = lax.rem(b, 2)
    w_sems = (w_send, w_recv)

    def part_of(owner, which, c):
        at = pl.multiple_of(owner * per * D + which * half + c * rows, 16)
        return w_out.at[pl.ds(at, rows)]

    def own_part(which, c):
        at = pl.multiple_of(which * half + c * rows, 16)
        return blocks_ref.at[pl.ds(at, rows)]

    kept = pltpu.make_async_copy(
        blocks_ref,
        w_out.at[pl.ds(pl.multiple_of(s * per * D, 16), per * D)],
        own_sem.at[0],
    )
    kept.start()
    over_x = [
        remote(own_part(side, c), part_of(s, side, c), w_sems, (0, c), x_peer)
        for c in range(WEIGHT_PARTS)
    ]
    over_core = [
        remote(
            blocks_ref,
            w_out.at[pl.ds(pl.multiple_of(s * per * D, 16), per * D)],
            w_sems,
            (1, 0),
            core_peer,
        )
    ]
    vec_ops = [
        remote(vecs.at[owners], vecs.at[s], (vec_send, vec_recv), i - 1, shard_peers[i - 1])
        for i in range(1, owners)
    ]

    over_y, fill = [], []
    for c in range(WEIGHT_PARTS):
        over_x[c].wait_recv()
        came = part_of(s ^ far, side, c)
        over_y.append(remote(came, came, w_sems, (2, c), y_peer))
        fill.append(remote(came, came, w_sems, (3, c), core_peer))
    for c in range(WEIGHT_PARTS):
        over_y[c].wait_recv()
        came = part_of(s ^ far, 1 - side, c)
        fill.append(remote(came, came, w_sems, (4, c), core_peer))
    for op in vec_ops:
        op.wait_recv()
    vecs[s] = vecs[owners]
    for o in range(owners):
        vec_out[o * per : (o + 1) * per, :] = vecs[o, 0:per, :]
    over_core[0].wait_recv()
    for op in fill:
        op.wait_recv()
    kept.wait()
    for op in vec_ops + over_x + over_core + over_y + fill:
        op.wait_send()


def exchange_counts(info, cotangent):
    group = lax.axis_size("batch")
    micro, row_len, _ = cotangent.shape
    slots = row_len // group
    vmem = pl.BlockSpec(memory_space=pltpu.VMEM)
    dma = pltpu.SemaphoreType.DMA
    ints = lambda *shape: jax.ShapeDtypeStruct(shape, jnp.int32)
    return pl.pallas_call(
        functools.partial(count_kernel, group),
        in_specs=[pl.BlockSpec(memory_space=pltpu.SMEM), vmem],
        out_specs=[vmem] * 4,
        out_shape=[
            jax.ShapeDtypeStruct((group, micro, slots, D), BF16),
            ints(micro, row_len),
            ints(micro * row_len, 1),
            ints(micro, row_len),
        ],
        scratch_shapes=[
            pltpu.VMEM((8, LANES), jnp.int32),
            pltpu.VMEM((group - 1, 8, LANES), jnp.int32),
            dma((group - 1,)),
            dma((group - 1,)),
        ],
        compiler_params=pltpu.CompilerParams(
            collective_id=2, has_side_effects=True, vmem_limit_bytes=VMEM
        ),
        cost_estimate=pl.CostEstimate(
            flops=micro * row_len * row_len * D * 2,
            bytes_accessed=micro * row_len * D * 4,
            transcendentals=0,
        ),
    )(info, cotangent)


def gather_weights(blocks, vectors):
    group, owners = lax.axis_size("batch"), lax.axis_size("shard")
    vmem = pl.BlockSpec(memory_space=pltpu.VMEM)
    any_ = pl.BlockSpec(memory_space=pl.ANY)
    dma = pltpu.SemaphoreType.DMA
    matrices, vec = pl.pallas_call(
        functools.partial(weight_kernel, group, owners),
        in_specs=[any_, vmem],
        out_specs=[any_, vmem],
        out_shape=[
            jax.ShapeDtypeStruct((NMAT * D, D), BF16),
            jax.ShapeDtypeStruct((NMAT, D), F32),
        ],
        scratch_shapes=[
            pltpu.VMEM((owners + 1, 8, D), F32),
            dma((1,)),
            dma((owners - 1,)),
            dma((owners - 1,)),
            dma((5, WEIGHT_PARTS)),
            dma((5, WEIGHT_PARTS)),
        ],
        compiler_params=pltpu.CompilerParams(
            collective_id=3, has_side_effects=True, vmem_limit_bytes=VMEM
        ),
        cost_estimate=pl.CostEstimate(
            flops=0, bytes_accessed=NMAT * D * D * 4, transcendentals=0
        ),
    )(blocks.reshape(-1, D), vectors)
    return matrices.reshape(NMAT, D, D), vec


def attend_kernel(info, x_ref, w_ref, vec_ref, q_ref, k_ref, v_ref, o_ref, l_ref, qx, kx, vx):
    row = pl.program_id(0)
    row_len = x_ref.shape[1]
    ends, live = ends_of(info, row), live_of(info, row)
    first = lane_index(QT) < DH
    ones = jnp.ones((QT, LANES), F32)

    @pl.loop(0, row_len // QT)
    def _(t):
        rows = pl.ds(pl.multiple_of(t * QT, QT), QT)
        x = x_ref[0, rows, :]
        sample = sample_column(ends, t * QT, QT)
        q_extra = query_spare(sample, QT)
        q = ((nn(x, w_ref[0]) + vec_ref[0:1, :]).astype(BF16).astype(F32) * DH**-0.5).astype(BF16)
        k = nn(x, w_ref[1]).astype(BF16)
        v = (nn(x, w_ref[2]) + vec_ref[1:2, :]).astype(BF16)
        q_ref[0, rows, :] = q
        k_ref[0, rows, :] = k
        v_ref[0, rows, :] = v
        for p in range(PAIRS):
            pair = head_lanes(p)
            store_heads(qx, rows, p, q[:, pair].astype(F32), q_extra, first)
            store_heads(kx, rows, p, k[:, pair].astype(F32), key_spare(sample, QT, p), first)
            store_heads(vx, rows, p, v[:, pair].astype(F32), ones, first)

    @pl.loop(0, row_len // QT)
    def _(t):
        rows = pl.ds(pl.multiple_of(t * QT, QT), QT)
        begin, number = chosen_span(ends, live, t, row_len)

        @pl.when(number == 0)
        def _():
            o_ref[0, rows, :] = jnp.zeros((QT, D), BF16)
            l_ref[0, rows, :] = jnp.zeros((QT, LANES), F32)

        for n in widths(row_len):

            @pl.when(number == n)
            def _(n=n):
                span = pl.ds(pl.multiple_of(begin * KG, KG), n * KG)
                lane = lane_index(QT)
                scores, powers, got = {}, {}, {}
                peaks = jnp.zeros((QT, LANES), F32)
                totals = jnp.ones((QT, LANES), F32)
                for step in range(H + 2):
                    if step < H:
                        cols = head_lanes(step)
                        scores[step] = nt(qx[rows, cols], kx[span, cols])
                    h = step - 1
                    if 0 <= h < H:
                        s = scores.pop(h)
                        peak = jnp.max(s, axis=1, keepdims=True)
                        powers[h] = jnp.exp(s - peak).astype(BF16)
                        spot = lane == (h // 2 + DH if h % 2 == 0 else h // 2)
                        peaks = jnp.where(spot, peak, peaks)
                    h = step - 2
                    if 0 <= h < H:
                        got[h] = nn(powers.pop(h), vx[span, head_lanes(h)])
                        spot = lane == (h // 2 + DH if h % 2 == 0 else h // 2)
                        totals = jnp.where(spot, got[h], totals)
                        if h % 2 == 1:
                            left, right = got.pop(h - 1), got.pop(h)
                            top = jnp.where(first, left, right)
                            total = pltpu.roll(jnp.where(first, right, left), DH, 1)
                            o_ref[0, rows, head_lanes(h // 2)] = (top / total).astype(BF16)
                l_ref[0, rows, :] = jnp.where(
                    peaks > -0.5 * BIG, peaks + jnp.log(totals), 0.0
                )


def attend(info, tokens, blocks, vec):
    micro, row_len, _ = tokens.shape
    row_spec = lambda width: pl.BlockSpec((1, row_len, width), lambda r: (r, 0, 0))
    low = jax.ShapeDtypeStruct((micro, row_len, D), BF16)
    return pl.pallas_call(
        attend_kernel,
        grid=(micro,),
        in_specs=[
            pl.BlockSpec(memory_space=pltpu.SMEM),
            row_spec(D),
            pl.BlockSpec((3, D, D), lambda r: (0, 0, 0)),
            pl.BlockSpec((NMAT, D), lambda r: (0, 0)),
        ],
        out_specs=[row_spec(D)] * 4 + [row_spec(LANES)],
        out_shape=[low] * 4 + [jax.ShapeDtypeStruct((micro, row_len, LANES), F32)],
        scratch_shapes=[pltpu.VMEM((row_len, 2 * D), BF16)] * 3,
        compiler_params=pltpu.CompilerParams(vmem_limit_bytes=VMEM),
        cost_estimate=pl.CostEstimate(
            flops=micro * row_len * D * D * 6 + micro * H * row_len * row_len * DH * 16,
            bytes_accessed=micro * row_len * D * 16,
            transcendentals=micro * H * row_len * row_len,
        ),
    )(info, tokens, blocks, vec)


def gelu_both(u):
    share = 0.5 + 0.5 * lax.erf(u * 0.5**0.5)
    bell = jnp.exp2((-0.5 * 1.4426950408889634) * (u * u))
    return u * share, share + (u * 0.3989422804014327) * bell


def norm_parts(a):
    center = a - jnp.mean(a, axis=-1, keepdims=True)
    rate = lax.rsqrt(jnp.mean(center * center, axis=-1, keepdims=True) + EPS)
    return center * rate, rate


def norm_back(grad, unit, rate):
    return rate * (
        grad
        - jnp.mean(grad, axis=-1, keepdims=True)
        - unit * jnp.mean(grad * unit, axis=-1, keepdims=True)
    )


def feed_kernel(
    info,
    x_ref,
    o_ref,
    w_ref,
    vec_ref,
    stu_ref,
    cls_ref,
    goal_ref,
    send_row,
    send_col,
    back_ref,
    da1_ref,
    out_ref,
    wg_ref,
    vg_ref,
    sg_ref,
    cg_ref,
    unit1,
    rate1,
    h1b,
    act,
    slope,
    unit2,
    rate2,
    zb,
    head_in,
    head_low,
    *,
    tile,
    micro,
    row_len,
):
    step = pl.program_id(0)
    tiles = micro * row_len // tile
    group, _, slots, _ = out_ref.shape

    @pl.when(step == 0)
    def _():
        vg_ref[...] = jnp.zeros_like(vg_ref)

    @pl.when(step < tiles)
    def _():
        rows = pl.ds(pl.multiple_of(step * tile, tile), tile)
        a1 = x_ref[...].astype(F32) + (nn(o_ref[...], w_ref[3]) + vec_ref[2:3, :])
        unit, rate = norm_parts(a1)
        unit1[rows, :] = unit
        rate1[rows, :] = rate
        h1 = unit * vec_ref[3:4, :] + vec_ref[4:5, :]
        low = h1.astype(BF16)
        h1b[rows, :] = low
        total = h1 + vec_ref[9:10, :]
        raw, value = {}, {}
        for turn in range(PARTS + 2):
            if turn < PARTS:
                c, at = turn // CUT, slice(turn % CUT * PART, (turn % CUT + 1) * PART)
                raw[turn] = nn(low, w_ref[4 + c, :, at]) + vec_ref[5 + c : 6 + c, at]
            if 0 <= turn - 1 < PARTS:
                cols = slice((turn - 1) * PART, turn * PART)
                up, grad = gelu_both(raw.pop(turn - 1))
                value[turn - 1] = up.astype(BF16)
                act[rows, cols] = value[turn - 1]
                slope[rows, cols] = grad.astype(BF16)
            if 0 <= turn - 2 < PARTS:
                c = (turn - 2) // CUT
                at = slice((turn - 2) % CUT * PART, ((turn - 2) % CUT + 1) * PART)
                total = total + nn(value.pop(turn - 2), w_ref[8 + c, at, :])
        unit, rate = norm_parts(total)
        unit2[rows, :] = unit
        rate2[rows, :] = rate
        z = (unit * vec_ref[10:11, :] + vec_ref[11:12, :]).astype(BF16)
        zb[rows, :] = z
        head_in[rows, :] = nn(z, stu_ref[0:D, :].astype(BF16)) + stu_ref[D + SW : D + SW + 1, :]

    @pl.when(step == tiles)
    def _():
        head_phase(
            info, stu_ref, cls_ref, goal_ref, sg_ref, cg_ref, head_in, head_low, micro, row_len
        )
        sg_ref[0:D, :] = tn(zb[...], head_low[...])
        @pl.loop(0, micro)
        def _(m):
            place = send_row[pl.ds(m, 1), :]
            spot = lax.broadcasted_iota(jnp.int32, (group * slots, row_len), 0)
            pick = jnp.where(spot == place, 1.0, 0.0).astype(BF16)
            here = pl.ds(pl.multiple_of(m * row_len, row_len), row_len)
            moved = nn(pick, zb[here, :]).astype(BF16)
            out_ref[:, m] = moved.reshape(group, slots, D)

    @pl.when(step >= tiles)
    def _():
        t = step - tiles
        rows = pl.ds(pl.multiple_of(t * tile, tile), tile)
        m = (t * tile) // row_len
        spot = lax.broadcasted_iota(jnp.int32, (tile, group * slots), 1)
        pick = jnp.where(spot == send_col[...], 1.0, 0.0).astype(BF16)
        dz = nn(pick, back_ref[:, m].reshape(group * slots, D))
        dz = dz + nt(head_low[rows, :], stu_ref[0:D, :].astype(BF16))
        unit = unit2[rows, :]
        vg_ref[10:11, :] += row_sum(dz * unit)
        vg_ref[11:12, :] += row_sum(dz)
        da2 = norm_back(dz * vec_ref[10:11, :], unit, rate2[rows, :])
        low = da2.astype(BF16)
        zb[rows, :] = low
        vg_ref[9:10, :] += row_sum(low.astype(F32))
        dh1 = da2
        raw, value = {}, {}
        for turn in range(PARTS + 2):
            if turn < PARTS:
                c, at = turn // CUT, slice(turn % CUT * PART, (turn % CUT + 1) * PART)
                raw[turn] = nt(low, w_ref[8 + c, at, :])
            if 0 <= turn - 1 < PARTS:
                cols = slice((turn - 1) * PART, turn * PART)
                c = (turn - 1) // CUT
                at = slice((turn - 1) % CUT * PART, ((turn - 1) % CUT + 1) * PART)
                du = (raw.pop(turn - 1) * slope[rows, cols].astype(F32)).astype(BF16)
                value[turn - 1] = du
                slope[rows, cols] = du
                vg_ref[5 + c : 6 + c, at] += row_sum(du.astype(F32))
            if 0 <= turn - 2 < PARTS:
                c = (turn - 2) // CUT
                at = slice((turn - 2) % CUT * PART, ((turn - 2) % CUT + 1) * PART)
                dh1 = dh1 + nt(value.pop(turn - 2), w_ref[4 + c, :, at])
        unit = unit1[rows, :]
        vg_ref[3:4, :] += row_sum(dh1 * unit)
        vg_ref[4:5, :] += row_sum(dh1)
        da1_ref[...] = norm_back(dh1 * vec_ref[3:4, :], unit, rate1[rows, :])

    @pl.when(step == 2 * tiles - 1)
    def _():
        @pl.loop(0, FF // D)
        def _(c):
            cols = pl.ds(pl.multiple_of(c * D, D), D)
            wg_ref[c] = tn(h1b[...], slope[:, cols]).astype(BF16)
            wg_ref[4 + c] = tn(act[:, cols], zb[...]).astype(BF16)


def head_phase(info, stu_ref, cls_ref, goal_ref, sg_ref, cg_ref, head_in, head_low, micro, row_len):
    scale = DH**-0.5
    query = stu_ref[D + SW + 2 : D + SW + 3, :]
    same = (
        lax.broadcasted_iota(jnp.int32, (SW, SW), 0) // DH
        == lax.broadcasted_iota(jnp.int32, (SW, SW), 1) // DH
    )
    same = jnp.where(same, 1.0, 0.0).astype(BF16)
    pooled, weights, members = [], [], []
    for m in range(micro):
        rows = slice(m * row_len, (m + 1) * row_len)
        s = head_in[rows, :]
        e = two_low(s * query, same) * scale
        sample = sample_column(ends_of(info, m), 0, row_len)
        share = jnp.zeros_like(e)
        for j in range(SAMP):
            member = sample == j
            peak = jnp.max(jnp.where(member, e, -1e30), axis=0, keepdims=True)
            up = jnp.where(member, jnp.exp(jnp.where(member, e - peak, 0.0)), 0.0)
            up = up / row_sum(up)
            share = share + up
            pooled.append(row_sum(up * s))
            members.append(member)
        weights.append(share)
    pooled = jnp.concatenate(pooled, axis=0)
    pool_weight = stu_ref[D : D + SW, :]
    mixed = jnp.tanh(exact(pooled, pool_weight) + stu_ref[D + SW + 1 : D + SW + 2, :])
    classes = cls_ref[:, 0:SW]
    bias = cls_ref[:, SW : SW + 1].T
    logits = exact(mixed, classes, (((1,), (1,)), ((), ()))) + bias
    logits = logits - jnp.max(logits, axis=-1, keepdims=True)
    chance = jnp.exp(logits)
    chance = chance / jnp.sum(chance, axis=-1, keepdims=True)
    goal = goal_ref[...]
    index = lax.broadcasted_iota(jnp.int32, (micro * SAMP, 1), 0)
    alive = jnp.zeros((micro * SAMP, 1), F32)
    for m in range(micro):
        for j, flag in enumerate(live_of(info, m)):
            alive = jnp.where(index == m * SAMP + j, flag.astype(F32), alive)
    target = jnp.exp(goal - jnp.max(goal, axis=-1, keepdims=True))
    target = target / jnp.sum(target, axis=-1, keepdims=True)
    d_logits = alive * (chance - target)
    cg_ref[:, 0:SW] = exact(d_logits, mixed, (((0,), (0,)), ((), ())))
    cg_ref[:, SW : SW + 1] = row_sum(d_logits).T
    d_pre = exact(d_logits, classes) * (1.0 - mixed * mixed)
    sg_ref[D : D + SW, :] = exact(pooled, d_pre, (((0,), (0,)), ((), ())))
    sg_ref[D + SW + 1 : D + SW + 2, :] = row_sum(d_pre)
    d_pooled = exact(d_pre, pool_weight, (((1,), (1,)), ((), ())))
    inner = two_low(pooled * d_pooled, same)
    d_bias = jnp.zeros((1, SW), F32)
    d_query = jnp.zeros((1, SW), F32)
    for m in range(micro):
        rows = slice(m * row_len, (m + 1) * row_len)
        s = head_in[rows, :]
        spread = jnp.zeros((row_len, SW), F32)
        center = jnp.zeros((row_len, SW), F32)
        for j in range(SAMP):
            member = members[m * SAMP + j]
            at = m * SAMP + j
            spread = jnp.where(member, d_pooled[at : at + 1, :], spread)
            center = jnp.where(member, inner[at : at + 1, :], center)
        share = weights[m]
        d_e = share * (two_low(s * spread, same) - center) * scale
        d_s = (share * spread + d_e * query).astype(BF16)
        head_low[rows, :] = d_s
        d_bias = d_bias + row_sum(d_s.astype(F32))
        d_query = d_query + row_sum(d_e * s)
    sg_ref[D + SW : D + SW + 1, :] = d_bias
    sg_ref[D + SW + 2 : D + SW + 3, :] = d_query


def feed(info, x, o, blocks, vec, student, classifier, goals, send_row, send_col, returned):
    micro, row_len, _ = x.shape
    tokens = micro * row_len
    tile = 512
    tiles = tokens // tile
    group, _, slots, _ = returned.shape
    whole = lambda *shape: pl.BlockSpec(shape, lambda i: (0,) * len(shape))
    once = lambda *shape: pl.BlockSpec(
        shape, lambda i: (0,) * len(shape), pipeline_mode=pl.Buffered(1)
    )
    ahead = lambda width: pl.BlockSpec((tile, width), lambda i: (jnp.minimum(i, tiles - 1), 0))
    behind = lambda width: pl.BlockSpec((tile, width), lambda i: (jnp.maximum(i - tiles, 0), 0))
    return pl.pallas_call(
        functools.partial(feed_kernel, tile=tile, micro=micro, row_len=row_len),
        grid=(2 * tiles,),
        in_specs=[
            pl.BlockSpec(memory_space=pltpu.SMEM),
            ahead(D),
            ahead(D),
            once(NMAT, D, D),
            once(NMAT, D),
            once(*student.shape),
            once(*classifier.shape),
            once(*goals.shape),
            once(*send_row.shape),
            behind(1),
            once(*returned.shape),
        ],
        out_specs=[
            behind(D),
            once(*returned.shape),
            once(8, D, D),
            once(NMAT, D),
            once(*student.shape),
            once(*classifier.shape),
        ],
        out_shape=[
            jax.ShapeDtypeStruct((tokens, D), F32),
            jax.ShapeDtypeStruct(returned.shape, BF16),
            jax.ShapeDtypeStruct((NMAT, D, D), BF16),
            jax.ShapeDtypeStruct((NMAT, D), F32),
            jax.ShapeDtypeStruct(student.shape, F32),
            jax.ShapeDtypeStruct(classifier.shape, F32),
        ],
        scratch_shapes=[
            pltpu.VMEM((tokens, D), F32),
            pltpu.VMEM((tokens, 1), F32),
            pltpu.VMEM((tokens, D), BF16),
            pltpu.VMEM((tokens, FF), BF16),
            pltpu.VMEM((tokens, FF), BF16),
            pltpu.VMEM((tokens, D), F32),
            pltpu.VMEM((tokens, 1), F32),
            pltpu.VMEM((tokens, D), BF16),
            pltpu.VMEM((tokens, SW), F32),
            pltpu.VMEM((tokens, SW), BF16),
        ],
        compiler_params=pltpu.CompilerParams(vmem_limit_bytes=VMEM),
        cost_estimate=pl.CostEstimate(
            flops=tokens * D * FF * 12, bytes_accessed=tokens * D * 16, transcendentals=tokens * FF
        ),
    )(
        info,
        x.reshape(tokens, D),
        o.reshape(tokens, D),
        blocks,
        vec,
        student,
        classifier,
        goals,
        send_row,
        send_col,
        returned,
    )


def attend_back_kernel(
    info,
    x_ref,
    da1_ref,
    q_ref,
    k_ref,
    v_ref,
    o_ref,
    l_ref,
    w_ref,
    _,
    dx_ref,
    wg_ref,
    vg_ref,
    qx,
    kx,
    vx,
    dox,
    dq,
    dk,
    dv,
    dk_sum,
    dv_sum,
    wsum,
    *,
    micro,
):
    row = pl.program_id(0)
    row_len = x_ref.shape[1]
    ends, live = ends_of(info, row), live_of(info, row)
    first = lane_index(QT) < DH
    ones = jnp.ones((QT, LANES), F32)

    @pl.when(row == 0)
    def _():
        vg_ref[...] = jnp.zeros_like(vg_ref)
        wsum[...] = jnp.zeros_like(wsum)

    head = lax.broadcasted_iota(jnp.int32, (D, LANES), 0) // DH
    spot = head // 2 + DH * (1 - head % 2)
    gather = lax.broadcasted_iota(jnp.int32, (D, LANES), 1) == spot
    gather = jnp.where(gather, 1.0, 0.0).astype(BF16)

    dq[...] = jnp.zeros_like(dq)

    @pl.loop(0, row_len // QT)
    def _(t):
        rows = pl.ds(pl.multiple_of(t * QT, QT), QT)
        sample = sample_column(ends, t * QT, QT)
        lane = lane_index(QT) % DH
        high, mid, rest = split_low(jnp.where(lane < PAIRS, -l_ref[0, rows, :], 0.0))
        q_extra = (
            query_spare(sample, QT)
            + high
            + pltpu.roll(mid, PAIRS, 1)
            + pltpu.roll(rest, 2 * PAIRS, 1)
        )
        branch = da1_ref[0, rows, :].astype(BF16)
        vg_ref[2:3, :] += row_sum(branch.astype(F32))
        do = nt(branch, w_ref[3]).astype(BF16).astype(F32)
        delta = two_low(do * o_ref[0, rows, :].astype(F32), gather)
        high = delta.astype(BF16).astype(F32)
        do_extra = pltpu.roll(high - delta, PAIRS, 1) - high
        for p in range(PAIRS):
            pair = head_lanes(p)
            k_extra = key_spare(sample, QT, p)
            store_heads(dox, rows, p, do[:, pair], do_extra, first)
            store_heads(qx, rows, p, q_ref[0, rows, pair].astype(F32), q_extra, first)
            store_heads(kx, rows, p, k_ref[0, rows, pair].astype(F32), k_extra, first)
            store_heads(vx, rows, p, v_ref[0, rows, pair].astype(F32), k_extra, first)

    @pl.loop(0, row_len // QT)
    def _(t):
        rows = pl.ds(pl.multiple_of(t * QT, QT), QT)
        begin, number = reach(ends, live, t * QT, QT, row_len)
        number = (number + STEP - 1) // STEP
        begin = jnp.minimum(begin, row_len // KG - number * STEP)
        dk_sum[...] = jnp.zeros_like(dk_sum)
        dv_sum[...] = jnp.zeros_like(dv_sum)

        @pl.loop(0, number)
        def _(j):
            span = pl.ds(pl.multiple_of((begin + j * STEP) * KG, KG), STEP * KG)
            wide = lane_index(STEP * KG) < DH
            raw, done, got = {}, {}, {}
            for step in range(H + 2):
                if step < H:
                    cols = head_lanes(step)
                    raw[step] = (
                        nt(kx[rows, cols], qx[span, cols]),
                        nt(vx[rows, cols], dox[span, cols]),
                    )
                h = step - 1
                if 0 <= h < H:
                    s, dp = raw.pop(h)
                    prob = jnp.exp(s)
                    done[h] = (prob.astype(BF16), (prob * dp).astype(BF16))
                h = step - 2
                if 0 <= h < H:
                    cols = head_lanes(h)
                    prob, ds = done.pop(h)
                    got[h] = (
                        nn(prob, dox[span, cols]),
                        nn(ds, qx[span, cols]),
                        tn(ds, kx[rows, cols]),
                    )
                    if h % 2 == 1:
                        left, right = got.pop(h - 1), got.pop(h)
                        cols = head_lanes(h // 2)
                        dv_sum[:, cols] += jnp.where(first, left[0], right[0])
                        dk_sum[:, cols] += jnp.where(first, left[1], right[1])
                        dq[span, cols] += jnp.where(wide, left[2], right[2])

        dk[rows, :] = dk_sum[...].astype(BF16)
        dv[rows, :] = dv_sum[...].astype(BF16)

    @pl.loop(0, row_len // QT)
    def _(t):
        rows = pl.ds(pl.multiple_of(t * QT, QT), QT)
        dq_low = (dq[rows, :] * DH**-0.5).astype(BF16)
        dk_low, dv_low = dk[rows, :], dv[rows, :]
        vg_ref[0:1, :] += row_sum(dq_low.astype(F32))
        vg_ref[1:2, :] += row_sum(dv_low.astype(F32))
        dx_ref[0, rows, :] = (
            da1_ref[0, rows, :]
            + nt(dq_low, w_ref[0])
            + nt(dk_low, w_ref[1])
            + nt(dv_low, w_ref[2])
        ).astype(BF16)

    x = x_ref[0]
    wsum[0] += tn(x, (dq[...] * DH**-0.5).astype(BF16))
    wsum[1] += tn(x, dk[...])
    wsum[2] += tn(x, dv[...])
    wsum[3] += tn(o_ref[0], da1_ref[0].astype(BF16))

    @pl.when(row == micro - 1)
    def _():
        wg_ref[...] = wsum[...].astype(BF16)


def attend_back(info, tokens, da1, q, k, v, o, logs, blocks, grads):
    micro, row_len, _ = tokens.shape
    row_spec = lambda width: pl.BlockSpec((1, row_len, width), lambda r: (r, 0, 0))
    return pl.pallas_call(
        functools.partial(attend_back_kernel, micro=micro),
        grid=(micro,),
        in_specs=[
            pl.BlockSpec(memory_space=pltpu.SMEM),
            *[row_spec(D)] * 6,
            row_spec(LANES),
            pl.BlockSpec((4, D, D), lambda r: (0, 0, 0)),
            pl.BlockSpec(memory_space=pl.ANY),
        ],
        out_specs=[
            row_spec(D),
            pl.BlockSpec((4, D, D), lambda r: (2, 0, 0)),
            pl.BlockSpec((8, D), lambda r: (0, 0)),
        ],
        out_shape=[
            jax.ShapeDtypeStruct((micro, row_len, D), BF16),
            jax.ShapeDtypeStruct((NMAT, D, D), BF16),
            jax.ShapeDtypeStruct((8, D), F32),
        ],
        scratch_shapes=[
            *[pltpu.VMEM((row_len, 2 * D), BF16)] * 4,
            pltpu.VMEM((row_len, D), F32),
            pltpu.VMEM((row_len, D), BF16),
            pltpu.VMEM((row_len, D), BF16),
            pltpu.VMEM((QT, D), F32),
            pltpu.VMEM((QT, D), F32),
            pltpu.VMEM((4, D, D), F32),
        ],
        input_output_aliases={9: 1},
        compiler_params=pltpu.CompilerParams(vmem_limit_bytes=VMEM),
        cost_estimate=pl.CostEstimate(
            flops=micro * row_len * D * D * 16 + micro * H * row_len * row_len * DH * 10,
            bytes_accessed=micro * row_len * D * 16,
            transcendentals=micro * H * row_len * row_len,
        ),
    )(info, tokens, da1, q, k, v, o, logs, blocks, grads)


CHUNKS = 12
STU_ROWS, CLS_ROWS, VEC_ROWS = 656, 16, 16
SMALL_ROWS = STU_ROWS + 2 * CLS_ROWS + 4 * VEC_ROWS + 16


def reduce_kernel(
    group,
    owners,
    grad_ref,
    ff_vec,
    at_vec,
    stu_ref,
    cls_ref,
    own_ref,
    vec_out,
    stu_out,
    cls_out,
    got_a,
    sum_a,
    got_b,
    part,
    got_c,
    final,
    small,
    small_got,
    small_sum,
    small_end,
    send_sem,
    recv_sem,
    small_send,
    small_recv,
):
    b, s = lax.axis_index("batch"), lax.axis_index("shard")
    per = NMAT // owners
    rows = per * D // CHUNKS
    batch_bits, shard_bits = bits_of(group), bits_of(owners)
    half = SMALL_ROWS // 2

    def copy(src, dst, sems, at, where):
        return pltpu.make_async_remote_copy(
            src_ref=src,
            dst_ref=dst,
            send_sem=sems[0].at[at],
            recv_sem=sems[1].at[at],
            device_id=where,
            device_id_type=pl.DeviceIdType.MESH,
        )

    peers = [(b, s ^ bit) for bit in shard_bits] + [(b ^ bit, s) for bit in batch_bits]
    barrier = pltpu.get_barrier_semaphore()
    for peer in peers:
        pl.semaphore_signal(
            barrier, inc=1, device_id=peer, device_id_type=pl.DeviceIdType.MESH
        )
    pl.semaphore_wait(barrier, len(peers))

    sems = (send_sem, recv_sem)
    small_sems = (small_send, small_recv)
    waits = []

    def begin(op):
        op.start()
        waits.append(op)
        return op

    def piece(owner, c):
        at = lax.rem(owner * per + c * per // CHUNKS + 8, NMAT)
        if rows == D:
            return grad_ref.at[at]
        step = D // rows
        return grad_ref.at[at, pl.ds((c % step) * rows, rows)]

    far = shard_bits[1]
    first = {}
    for c in range(CHUNKS):
        first[c] = [
            begin(copy(piece(s ^ 1 ^ far, c), got_a.at[c, 0], sems, (c, 0), peers[0])),
            begin(copy(piece(s ^ 1, c), got_a.at[c, 1], sems, (c, 1), peers[0])),
        ]

    small[...] = jnp.zeros_like(small)
    stu_count = stu_ref.shape[0]
    small[0:stu_count, :] = stu_ref[...].astype(BF16)
    small[STU_ROWS : STU_ROWS + CLS, :] = cls_ref[:, 0:SW].astype(BF16)
    small[STU_ROWS + CLS_ROWS : STU_ROWS + CLS_ROWS + CLS, 0:1] = cls_ref[:, SW:].astype(BF16)
    for i in range(4):
        at = STU_ROWS + 2 * CLS_ROWS + i * VEC_ROWS
        lanes = slice(i * LANES, (i + 1) * LANES)
        small[at : at + 3, :] = at_vec[0:3, lanes].astype(BF16)
        small[at + 3 : at + NMAT, :] = ff_vec[3:NMAT, lanes].astype(BF16)
    core = lax.rem(s, 2)
    mine = pl.ds(pl.multiple_of(core * half, 16), half)
    other = pl.ds(pl.multiple_of((1 - core) * half, 16), half)
    small_op = begin(copy(small.at[other], small_got.at[0], small_sems, 0, peers[0]))

    def add(x, y):
        return (x.astype(F32) + y.astype(F32)).astype(BF16)

    def add_into(out, x, y, x_at=0, y_at=0, out_at=0):
        count = out[1]
        slab = 16 if count % 32 else 32

        @pl.loop(0, count // slab)
        def _(i):
            def rows_at(first):
                return pl.ds(pl.multiple_of(first + i * slab, 16), slab)

            out[0][rows_at(out_at), :] = add(x[rows_at(x_at), :], y[rows_at(y_at), :])

    second = {}

    def start_second(c):
        for i, op in enumerate(first[c]):
            op.wait_recv()
            owner = s ^ far if i == 0 else s
            add_into((sum_a.at[c, i], rows), piece(owner, c), got_a.at[c, i])
        second[c] = begin(copy(sum_a.at[c, 0], got_b.at[c], sems, (c, 2), peers[1]))

    start_second(0)
    start_second(1)

    spans = []
    size = rows
    for bit in batch_bits:
        halving = size >= 32
        spans.append((bit, size, halving))
        if halving:
            size //= 2
    offset_of = []
    offset = jnp.int32(0)
    slot_of = []
    slot = 0
    for bit, now, halving in spans:
        place = lax.rem(b // bit, 2)
        offset_of.append((offset, place))
        slot_of.append(slot)
        if halving:
            offset = offset + place * (now // 2)
            slot += now // 2
        else:
            slot += now
    last = offset

    def ranged(ref, c, start, count):
        return ref.at[c, pl.ds(pl.multiple_of(start, 16), count)]

    moving = {}

    def start_batch(c, k):
        bit, now, halving = spans[k]
        start, place = offset_of[k]
        if halving:
            count = now // 2
            src = ranged(part.at[k], c, start + (1 - place) * count, count)
        else:
            count = now
            src = ranged(part.at[k], c, start, count)
        dst = got_c.at[c, pl.ds(slot_of[k], count)]
        moving[c, k] = begin(copy(src, dst, sems, (c, 3 + k), (b ^ bit, s)))

    def end_batch(c, k):
        bit, now, halving = spans[k]
        start, place = offset_of[k]
        moving[c, k].wait_recv()
        count = now // 2 if halving else now
        if halving:
            start = start + place * count
        target = part.at[k + 1, c] if k + 1 < len(spans) else final.at[c]
        add_into(
            (target, count), part.at[k, c], got_c.at[c], x_at=start, y_at=slot_of[k], out_at=start
        )

    gathers = [k for k in reversed(range(len(spans))) if spans[k][2]]
    gathering = {}

    def start_gather(c, g):
        k = gathers[g]
        bit, now, _ = spans[k]
        start, place = offset_of[k]
        count = now // 2
        at = ranged(final, c, start + place * count, count)
        gathering[c, g] = begin(
            copy(at, at, sems, (c, 3 + len(spans) + g), (b ^ bit, s))
        )

    def stage(c, k):
        if k == 0:
            second[c].wait_recv()
            if c + 2 < CHUNKS:
                start_second(c + 2)
            add_into((part.at[0, c], rows), sum_a.at[c, 1], got_b.at[c])
            start_batch(c, 0)
        elif k <= len(spans):
            end_batch(c, k - 1)
            if k < len(spans):
                start_batch(c, k)
            else:
                start_gather(c, 0)
        else:
            g = k - len(spans) - 1
            gathering[c, g].wait_recv()
            if g + 1 < len(gathers):
                start_gather(c, g + 1)
            else:
                per_block = CHUNKS // per
                block, within = c // per_block, c % per_block
                own_ref[block, within * rows : (within + 1) * rows, :] = final[c]

    stages = 1 + len(spans) + len(gathers)
    rest = [(b, s ^ bit) for bit in shard_bits[1:]] + [(b ^ bit, s) for bit in batch_bits]

    def small_stage(k):
        nonlocal small_op
        small_op.wait_recv()
        if k == 0:
            small_sum[0] = add(small[mine, :], small_got[0])
        elif k <= len(rest):
            small_sum[k] = add(small_sum[k - 1], small_got[k])
        if k < len(rest):
            small_op = begin(
                copy(small_sum.at[k], small_got.at[k + 1], small_sems, k + 1, rest[k])
            )
        elif k == len(rest):
            small_end[mine, :] = small_sum[k]
            small_op = begin(
                copy(small_sum.at[k], small_end.at[mine], small_sems, k + 1, peers[0])
            )

    small_k = 0
    for tick in range(CHUNKS + stages - 1):
        for k in reversed(range(stages)):
            c = tick - k
            if 0 <= c < CHUNKS:
                stage(c, k)
        if small_k <= len(rest) + 1:
            small_stage(small_k)
            small_k += 1
    while small_k <= len(rest) + 1:
        small_stage(small_k)
        small_k += 1

    for i in range(4):
        at = STU_ROWS + 2 * CLS_ROWS + i * VEC_ROWS
        lanes = slice(i * LANES, (i + 1) * LANES)
        vec_out[:, lanes] = small_end[at : at + VEC_ROWS, :].astype(F32)
    stu_out[...] = small_end[0:STU_ROWS, :].astype(F32)
    cls_out[:, 0:LANES] = small_end[STU_ROWS : STU_ROWS + CLS_ROWS, :].astype(F32)
    at = STU_ROWS + CLS_ROWS
    cls_out[:, LANES:] = small_end[at : at + CLS_ROWS, :].astype(F32)
    for op in waits:
        op.wait_send()


def reduce_grads(grads, ff_vec, at_vec, stu, cls):
    group, owners = lax.axis_size("batch"), lax.axis_size("shard")
    per = NMAT // owners
    rows = per * D // CHUNKS
    batch_count = len(bits_of(group))
    copies = 3 + 2 * batch_count
    small_count = len(bits_of(owners)) + batch_count + 1
    vmem = pl.BlockSpec(memory_space=pltpu.VMEM)
    return pl.pallas_call(
        functools.partial(reduce_kernel, group, owners),
        in_specs=[vmem] * 5,
        out_specs=[vmem] * 4,
        out_shape=[
            jax.ShapeDtypeStruct((per, D, D), BF16),
            jax.ShapeDtypeStruct((VEC_ROWS, D), F32),
            jax.ShapeDtypeStruct((STU_ROWS, SW), F32),
            jax.ShapeDtypeStruct((CLS_ROWS, 2 * LANES), F32),
        ],
        scratch_shapes=[
            pltpu.VMEM((CHUNKS, 2, rows, D), BF16),
            pltpu.VMEM((CHUNKS, 2, rows, D), BF16),
            pltpu.VMEM((CHUNKS, rows, D), BF16),
            pltpu.VMEM((batch_count, CHUNKS, rows, D), BF16),
            pltpu.VMEM((CHUNKS, rows + 16 * batch_count, D), BF16),
            pltpu.VMEM((CHUNKS, rows, D), BF16),
            pltpu.VMEM((SMALL_ROWS, LANES), BF16),
            pltpu.VMEM((small_count - 1, SMALL_ROWS // 2, LANES), BF16),
            pltpu.VMEM((small_count - 1, SMALL_ROWS // 2, LANES), BF16),
            pltpu.VMEM((SMALL_ROWS, LANES), BF16),
            pltpu.SemaphoreType.DMA((CHUNKS, copies)),
            pltpu.SemaphoreType.DMA((CHUNKS, copies)),
            pltpu.SemaphoreType.DMA((small_count,)),
            pltpu.SemaphoreType.DMA((small_count,)),
        ],
        compiler_params=pltpu.CompilerParams(
            collective_id=1, has_side_effects=True, vmem_limit_bytes=VMEM
        ),
        cost_estimate=pl.CostEstimate(
            flops=NMAT * D * D * 4, bytes_accessed=NMAT * D * D * 8, transcendentals=0
        ),
    )(grads, ff_vec, at_vec, stu, cls)


def update_kernel(
    own_ref,
    blocks_ref,
    left_ref,
    right_ref,
    lroot_ref,
    rroot_ref,
    shard_ref,
    vsum_ref,
    vec_ref,
    vmom_ref,
    ssum_ref,
    stu_ref,
    smom_ref,
    csum_ref,
    cls_ref,
    cmom_ref,
    back_ref,
    rows_ref,
    grad_out,
    new_out,
    left_out,
    right_out,
    vg_out,
    vm_out,
    v_out,
    sg_out,
    sm_out,
    s_out,
    cg_out,
    cm_out,
    c_out,
    layer_out,
    *,
    owners,
):
    step = pl.program_id(0)
    row_len = layer_out.shape[1]

    @pl.when(step < rows_ref.shape[1])
    def _():
        arrived = rows_ref[:, step].reshape(row_len, D)
        chunk = min(256, row_len)

        @pl.loop(0, row_len // chunk)
        def _(k):
            at = pl.multiple_of(k * chunk, chunk)
            spot = at + lax.broadcasted_iota(jnp.int32, (chunk, row_len), 0)
            pick = jnp.where(spot == back_ref[pl.ds(step, 1), :], 1.0, 0.0).astype(BF16)
            layer_out[0, pl.ds(at, chunk), :] = nn(pick, arrived).astype(BF16)

    g = own_ref[0]
    grad_out[0] = g.astype(F32)
    left_out[0] = decay_rate * left_ref[0] + (1.0 - decay_rate) * nt(g, g)
    right_out[0] = decay_rate * right_ref[0] + (1.0 - decay_rate) * tn(g, g)
    steered = nn(lroot_ref[0].astype(BF16), g).astype(BF16)
    steered = nn(steered, rroot_ref[0].astype(BF16))
    size = jnp.mean(steered * steered, keepdims=True)
    new_out[0] = blocks_ref[0].astype(F32) - steered * (block_rate * lax.rsqrt(size + 1e-06))

    @pl.when(pl.program_id(0) == 0)
    def _():
        per = NMAT // owners
        mine = vsum_ref[0:per, :]
        for i in range(1, owners):
            mine = jnp.where(shard_ref[0] == i, vsum_ref[i * per : (i + 1) * per, :], mine)

        def rule(grads, old, moment, rate, outs):
            renewed = decay_rate * moment + (1.0 - decay_rate) * grads * grads
            outs[0][...] = grads
            outs[1][...] = renewed
            outs[2][...] = old - rate * grads / (jnp.sqrt(renewed) + 1e-08)

        rule(mine, vec_ref[...], vmom_ref[...], vector_rate, (vg_out, vm_out, v_out))
        rule(
            ssum_ref[0 : stu_ref.shape[0], :],
            stu_ref[...],
            smom_ref[...],
            head_rate,
            (sg_out, sm_out, s_out),
        )
        rule(
            csum_ref[0:CLS, 0 : SW + 1],
            cls_ref[...],
            cmom_ref[...],
            head_rate,
            (cg_out, cm_out, c_out),
        )


def update(own, blocks, left, right, lroot, rroot, shard, vsum, vec, vmom, ssum, stu, smom, csum, cls, cmom, back, arrived):
    per = own.shape[0]
    micro, row_len = back.shape
    mat = pl.BlockSpec((1, D, D), lambda i: (i, 0, 0))
    whole = lambda a: pl.BlockSpec(a.shape, lambda i: (0,) * a.ndim)
    like = lambda a: jax.ShapeDtypeStruct(a.shape, F32)
    return pl.pallas_call(
        functools.partial(update_kernel, owners=NMAT // per),
        grid=(per,),
        in_specs=[mat] * 6
        + [pl.BlockSpec(memory_space=pltpu.SMEM)]
        + [whole(a) for a in (vsum, vec, vmom, ssum, stu, smom, csum, cls, cmom, back, arrived)],
        out_specs=[mat] * 4
        + [whole(a) for a in (vec,) * 3 + (stu,) * 3 + (cls,) * 3]
        + [pl.BlockSpec((1, row_len, D), lambda i: (jnp.minimum(i, micro - 1), 0, 0))],
        out_shape=[like(left)] * 4
        + [like(a) for a in (vec,) * 3 + (stu,) * 3 + (cls,) * 3]
        + [jax.ShapeDtypeStruct((micro, row_len, D), BF16)],
        compiler_params=pltpu.CompilerParams(vmem_limit_bytes=VMEM),
    )(
        own,
        blocks,
        left,
        right,
        lroot,
        rroot,
        shard,
        vsum,
        vec,
        vmom,
        ssum,
        stu,
        smom,
        csum,
        cls,
        cmom,
        back,
        arrived,
    )


def local(
    tokens,
    cotangent,
    lengths,
    exit_layers,
    teacher,
    blocks,
    left_stats,
    right_stats,
    left_root,
    right_root,
    vectors,
    vec_moment,
    student,
    stu_moment,
    classifier,
    cls_moment,
):
    micro, _, row_len, _ = tokens.shape
    tokens, cotangent = tokens[:, 0], cotangent[:, 0]
    info = jnp.concatenate([lengths[:, 0], exit_layers[:, 0]], axis=1)
    grad_outgoing, send, send_col, back = exchange_counts(info, cotangent)
    returned = lax.all_to_all(grad_outgoing, "batch", split_axis=0, concat_axis=0, tiled=True)
    blocks, vectors, _ = lax.optimization_barrier((blocks, vectors, back))
    matrices, vec = gather_weights(blocks, vectors)

    q, k, v, o, logs = attend(info, tokens, matrices, vec)
    goals = teacher.reshape(micro * SAMP, CLS)
    classifier, cls_moment = classifier.T, cls_moment.T
    da1, outgoing, ff_grads, ff_vecs, stu_grads, cls_grads = feed(
        info, tokens, o, matrices, vec, student, classifier, goals, send, send_col, returned
    )
    arrived = lax.all_to_all(outgoing, "batch", split_axis=0, concat_axis=0, tiled=True)
    input_grads, grads, at_vecs = attend_back(
        info, tokens, da1.reshape(micro, row_len, D), q, k, v, o, logs, matrices, ff_grads
    )
    own, vec_sum, stu_sum, cls_sum = reduce_grads(grads, ff_vecs, at_vecs, stu_grads, cls_grads)
    shard = lax.axis_index("shard").astype(jnp.int32).reshape(1)
    *updated, layer_out = update(
        own,
        blocks,
        left_stats,
        right_stats,
        left_root,
        right_root,
        shard,
        vec_sum,
        vectors,
        vec_moment,
        stu_sum,
        student,
        stu_moment,
        cls_sum,
        classifier,
        cls_moment,
        back,
        arrived,
    )
    classes = [a.T for a in updated[-3:]]
    return (layer_out[:, None], input_grads[:, None], *updated[:-3], *classes)


def solution(mesh):
    rows = P(None, ("batch", "shard"), None, None)
    tags = P(None, ("batch", "shard"), None)
    mats = P("shard", None, None)
    vecs = P("shard", None)
    return jax.shard_map(
        local,
        mesh=mesh,
        in_specs=(rows, rows, tags, tags, rows, mats, mats, mats, mats, mats, vecs, vecs)
        + (P(),) * 4,
        out_specs=(rows, rows, mats, mats, mats, mats, vecs, vecs, vecs) + (P(),) * 6,
        check_vma=False,
    )
```

```python
import functools

import jax
import jax.numpy as jnp
from jax import lax
from jax.experimental import pallas as pl
from jax.experimental.pallas import tpu as pltpu
from jax.sharding import PartitionSpec as P

D = 512
H = 8
DH = 64
FF = 2048
SW = 128
NMAT = 12
SAMP = 4
LAYER = 4
CLS = 14

decay_rate = 0.5
block_rate = 0.04
vector_rate = 0.05
head_rate = 0.05

QT = 256
STEP = 2
KG = 128
PAIRS = H // 2
LANES = 128
PART = 512
PARTS, CUT = FF // PART, D // PART
BIG = float(2**30)
EPS = 1e-6
VMEM = 60 * 1024 * 1024

F32 = jnp.float32
BF16 = jnp.bfloat16


def nn(a, b):
    return jnp.dot(a, b, preferred_element_type=F32)


def nt(a, b):
    return lax.dot_general(a, b, (((1,), (1,)), ((), ())), preferred_element_type=F32)


def tn(a, b):
    return lax.dot_general(a, b, (((0,), (0,)), ((), ())), preferred_element_type=F32)


def exact(a, b, dims=(((1,), (0,)), ((), ()))):
    return lax.dot_general(
        a, b, dims, preferred_element_type=F32, precision=lax.Precision.HIGHEST
    )


def row_sum(v):
    return jnp.sum(v, axis=0, keepdims=True)


def two_low(v, b):
    high = v.astype(BF16)
    return nn(high, b) + nn((v - high.astype(F32)).astype(BF16), b)


def split_low(v):
    high = v.astype(BF16).astype(F32)
    rest = v - high
    mid = rest.astype(BF16).astype(F32)
    return high, mid, rest - mid


def ends_of(info, row):
    ends, total = [], jnp.int32(0)
    for j in range(SAMP):
        total = total + info[row, j]
        ends.append(total)
    return ends


def live_of(info, row):
    return [(info[row, SAMP + j] >= LAYER).astype(jnp.int32) for j in range(SAMP)]


def sample_column(ends, first, count):
    place = first + lax.broadcasted_iota(jnp.int32, (count, 1), 0)
    total = jnp.zeros((count, 1), jnp.int32)
    for j in range(SAMP - 1):
        total = total + (place >= ends[j]).astype(jnp.int32)
    return total


def reach(ends, live, first, count, row_len):
    low, high = jnp.int32(row_len), jnp.int32(0)
    start = jnp.int32(0)
    for j in range(SAMP):
        end = ends[j]
        meets = (start < first + count) & (end > first) & (end > start) & (live[j] > 0)
        low = jnp.where(meets, jnp.minimum(low, start), low)
        high = jnp.where(meets, jnp.maximum(high, end), high)
        start = end
    begin = low // KG
    number = jnp.maximum((high + KG - 1) // KG - begin, 0)
    return begin, number


def lane_index(rows):
    return lax.broadcasted_iota(jnp.int32, (rows, LANES), 1)


TAG = 16


def key_spare(sample, rows, pair):
    lane = lane_index(rows) % DH
    own = (lane < 3 * PAIRS) & (lane % PAIRS == pair)
    return jnp.where(own | (lane == sample + TAG), 1.0, 0.0)


def query_spare(sample, rows):
    lane = lane_index(rows) % DH
    tag = (lane >= TAG) & (lane < TAG + SAMP) & (lane != sample + TAG)
    return jnp.where(tag, -BIG, 0.0)


def store_heads(ref, rows, p, pair, spare, first):
    ref[rows, 2 * p * LANES : (2 * p + 1) * LANES] = jnp.where(first, pair, spare).astype(BF16)
    ref[rows, (2 * p + 1) * LANES : (2 * p + 2) * LANES] = jnp.where(
        first, spare, pair
    ).astype(BF16)


def head_lanes(h):
    return slice(h * LANES, (h + 1) * LANES)


def widths(row_len):
    most = row_len // KG
    return list(range(most // 2, most + 1))


def chosen_span(ends, live, t, row_len):
    begin, number = reach(ends, live, t * QT, QT, row_len)
    least, most = widths(row_len)[0], row_len // KG
    number = jnp.where(number > 0, jnp.maximum(number, least), 0)
    return jnp.minimum(begin, most - number), number


def bits_of(size):
    return [1 << i for i in range(size.bit_length() - 1)]


def pick_kernel(place_ref, rows_ref, out_ref):
    group, _, slots, _ = out_ref.shape
    places = group * slots
    spot = lax.broadcasted_iota(jnp.int32, (places, rows_ref.shape[1]), 1)
    pick = jnp.where(spot == place_ref[0], 1.0, 0.0).astype(BF16)
    out_ref[:, 0] = nn(pick, rows_ref[0]).astype(BF16).reshape(group, slots, D)


def pick_rows(place_col, rows, group):
    micro, row_len, _ = rows.shape
    slots = row_len // group
    return pl.pallas_call(
        pick_kernel,
        grid=(micro,),
        in_specs=[
            pl.BlockSpec((1, row_len, 1), lambda m: (m, 0, 0)),
            pl.BlockSpec((1, row_len, D), lambda m: (m, 0, 0)),
        ],
        out_specs=pl.BlockSpec((group, 1, slots, D), lambda m: (0, m, 0, 0)),
        out_shape=jax.ShapeDtypeStruct((group, micro, slots, D), BF16),
        compiler_params=pltpu.CompilerParams(vmem_limit_bytes=VMEM),
    )(place_col, rows)


def attend_kernel(info, x_ref, w_ref, vec_ref, q_ref, k_ref, v_ref, o_ref, l_ref, qx, kx, vx):
    row = pl.program_id(0)
    row_len = x_ref.shape[1]
    ends, live = ends_of(info, row), live_of(info, row)
    first = lane_index(QT) < DH
    ones = jnp.ones((QT, LANES), F32)

    @pl.loop(0, row_len // QT)
    def _(t):
        rows = pl.ds(pl.multiple_of(t * QT, QT), QT)
        x = x_ref[0, rows, :]
        sample = sample_column(ends, t * QT, QT)
        q_extra = query_spare(sample, QT)
        q = ((nn(x, w_ref[0]) + vec_ref[0:1, :]).astype(BF16).astype(F32) * DH**-0.5).astype(BF16)
        k = nn(x, w_ref[1]).astype(BF16)
        v = (nn(x, w_ref[2]) + vec_ref[1:2, :]).astype(BF16)
        q_ref[0, rows, :] = q
        k_ref[0, rows, :] = k
        v_ref[0, rows, :] = v
        for p in range(PAIRS):
            pair = head_lanes(p)
            store_heads(qx, rows, p, q[:, pair].astype(F32), q_extra, first)
            store_heads(kx, rows, p, k[:, pair].astype(F32), key_spare(sample, QT, p), first)
            store_heads(vx, rows, p, v[:, pair].astype(F32), ones, first)

    @pl.loop(0, row_len // QT)
    def _(t):
        rows = pl.ds(pl.multiple_of(t * QT, QT), QT)
        begin, number = chosen_span(ends, live, t, row_len)

        @pl.when(number == 0)
        def _():
            o_ref[0, rows, :] = jnp.zeros((QT, D), BF16)
            l_ref[0, rows, :] = jnp.zeros((QT, LANES), F32)

        for n in widths(row_len):

            @pl.when(number == n)
            def _(n=n):
                span = pl.ds(pl.multiple_of(begin * KG, KG), n * KG)
                lane = lane_index(QT)
                scores, powers, got = {}, {}, {}
                peaks = jnp.zeros((QT, LANES), F32)
                totals = jnp.ones((QT, LANES), F32)
                for step in range(H + 2):
                    if step < H:
                        cols = head_lanes(step)
                        scores[step] = nt(qx[rows, cols], kx[span, cols])
                    h = step - 1
                    if 0 <= h < H:
                        s = scores.pop(h)
                        peak = jnp.max(s, axis=1, keepdims=True)
                        powers[h] = jnp.exp(s - peak).astype(BF16)
                        spot = lane == (h // 2 + DH if h % 2 == 0 else h // 2)
                        peaks = jnp.where(spot, peak, peaks)
                    h = step - 2
                    if 0 <= h < H:
                        got[h] = nn(powers.pop(h), vx[span, head_lanes(h)])
                        spot = lane == (h // 2 + DH if h % 2 == 0 else h // 2)
                        totals = jnp.where(spot, got[h], totals)
                        if h % 2 == 1:
                            left, right = got.pop(h - 1), got.pop(h)
                            top = jnp.where(first, left, right)
                            total = pltpu.roll(jnp.where(first, right, left), DH, 1)
                            o_ref[0, rows, head_lanes(h // 2)] = (top / total).astype(BF16)
                l_ref[0, rows, :] = jnp.where(
                    peaks > -0.5 * BIG, peaks + jnp.log(totals), 0.0
                )


def attend(info, tokens, blocks, vec):
    micro, row_len, _ = tokens.shape
    row_spec = lambda width: pl.BlockSpec((1, row_len, width), lambda r: (r, 0, 0))
    low = jax.ShapeDtypeStruct((micro, row_len, D), BF16)
    return pl.pallas_call(
        attend_kernel,
        grid=(micro,),
        in_specs=[
            pl.BlockSpec(memory_space=pltpu.SMEM),
            row_spec(D),
            pl.BlockSpec((3, D, D), lambda r: (0, 0, 0)),
            pl.BlockSpec((NMAT, D), lambda r: (0, 0)),
        ],
        out_specs=[row_spec(D)] * 4 + [row_spec(LANES)],
        out_shape=[low] * 4 + [jax.ShapeDtypeStruct((micro, row_len, LANES), F32)],
        scratch_shapes=[pltpu.VMEM((row_len, 2 * D), BF16)] * 3,
        compiler_params=pltpu.CompilerParams(vmem_limit_bytes=VMEM),
        cost_estimate=pl.CostEstimate(
            flops=micro * row_len * D * D * 6 + micro * H * row_len * row_len * DH * 16,
            bytes_accessed=micro * row_len * D * 16,
            transcendentals=micro * H * row_len * row_len,
        ),
    )(info, tokens, blocks, vec)


def gelu_both(u):
    share = 0.5 + 0.5 * lax.erf(u * 0.5**0.5)
    bell = jnp.exp2((-0.5 * 1.4426950408889634) * (u * u))
    return u * share, share + (u * 0.3989422804014327) * bell


def norm_parts(a):
    center = a - jnp.mean(a, axis=-1, keepdims=True)
    rate = lax.rsqrt(jnp.mean(center * center, axis=-1, keepdims=True) + EPS)
    return center * rate, rate


def norm_back(grad, unit, rate):
    return rate * (
        grad
        - jnp.mean(grad, axis=-1, keepdims=True)
        - unit * jnp.mean(grad * unit, axis=-1, keepdims=True)
    )


def feed_kernel(
    info,
    x_ref,
    o_ref,
    w_ref,
    vec_ref,
    stu_ref,
    cls_ref,
    goal_ref,
    send_row,
    send_col,
    back_ref,
    da1_ref,
    out_ref,
    wg_ref,
    vg_ref,
    sg_ref,
    cg_ref,
    unit1,
    rate1,
    h1b,
    act,
    slope,
    unit2,
    rate2,
    zb,
    head_in,
    head_low,
    *,
    tile,
    micro,
    row_len,
):
    step = pl.program_id(0)
    tiles = micro * row_len // tile
    group, _, slots, _ = out_ref.shape

    @pl.when(step == 0)
    def _():
        vg_ref[...] = jnp.zeros_like(vg_ref)

    @pl.when(step < tiles)
    def _():
        rows = pl.ds(pl.multiple_of(step * tile, tile), tile)
        a1 = x_ref[...].astype(F32) + (nn(o_ref[...], w_ref[3]) + vec_ref[2:3, :])
        unit, rate = norm_parts(a1)
        unit1[rows, :] = unit
        rate1[rows, :] = rate
        h1 = unit * vec_ref[3:4, :] + vec_ref[4:5, :]
        low = h1.astype(BF16)
        h1b[rows, :] = low
        total = h1 + vec_ref[9:10, :]
        raw, value = {}, {}
        for turn in range(PARTS + 2):
            if turn < PARTS:
                c, at = turn // CUT, slice(turn % CUT * PART, (turn % CUT + 1) * PART)
                raw[turn] = nn(low, w_ref[4 + c, :, at]) + vec_ref[5 + c : 6 + c, at]
            if 0 <= turn - 1 < PARTS:
                cols = slice((turn - 1) * PART, turn * PART)
                up, grad = gelu_both(raw.pop(turn - 1))
                value[turn - 1] = up.astype(BF16)
                act[rows, cols] = value[turn - 1]
                slope[rows, cols] = grad.astype(BF16)
            if 0 <= turn - 2 < PARTS:
                c = (turn - 2) // CUT
                at = slice((turn - 2) % CUT * PART, ((turn - 2) % CUT + 1) * PART)
                total = total + nn(value.pop(turn - 2), w_ref[8 + c, at, :])
        unit, rate = norm_parts(total)
        unit2[rows, :] = unit
        rate2[rows, :] = rate
        z = (unit * vec_ref[10:11, :] + vec_ref[11:12, :]).astype(BF16)
        zb[rows, :] = z
        head_in[rows, :] = nn(z, stu_ref[0:D, :].astype(BF16)) + stu_ref[D + SW : D + SW + 1, :]

    @pl.when(step == tiles)
    def _():
        head_phase(
            info, stu_ref, cls_ref, goal_ref, sg_ref, cg_ref, head_in, head_low, micro, row_len
        )
        sg_ref[0:D, :] = tn(zb[...], head_low[...])
        @pl.loop(0, micro)
        def _(m):
            place = send_row[pl.ds(m, 1), :]
            spot = lax.broadcasted_iota(jnp.int32, (group * slots, row_len), 0)
            pick = jnp.where(spot == place, 1.0, 0.0).astype(BF16)
            here = pl.ds(pl.multiple_of(m * row_len, row_len), row_len)
            moved = nn(pick, zb[here, :]).astype(BF16)
            out_ref[:, m] = moved.reshape(group, slots, D)

    @pl.when(step >= tiles)
    def _():
        t = step - tiles
        rows = pl.ds(pl.multiple_of(t * tile, tile), tile)
        m = (t * tile) // row_len
        spot = lax.broadcasted_iota(jnp.int32, (tile, group * slots), 1)
        pick = jnp.where(spot == send_col[...], 1.0, 0.0).astype(BF16)
        dz = nn(pick, back_ref[:, m].reshape(group * slots, D))
        dz = dz + nt(head_low[rows, :], stu_ref[0:D, :].astype(BF16))
        unit = unit2[rows, :]
        vg_ref[10:11, :] += row_sum(dz * unit)
        vg_ref[11:12, :] += row_sum(dz)
        da2 = norm_back(dz * vec_ref[10:11, :], unit, rate2[rows, :])
        low = da2.astype(BF16)
        zb[rows, :] = low
        vg_ref[9:10, :] += row_sum(low.astype(F32))
        dh1 = da2
        raw, value = {}, {}
        for turn in range(PARTS + 2):
            if turn < PARTS:
                c, at = turn // CUT, slice(turn % CUT * PART, (turn % CUT + 1) * PART)
                raw[turn] = nt(low, w_ref[8 + c, at, :])
            if 0 <= turn - 1 < PARTS:
                cols = slice((turn - 1) * PART, turn * PART)
                c = (turn - 1) // CUT
                at = slice((turn - 1) % CUT * PART, ((turn - 1) % CUT + 1) * PART)
                du = (raw.pop(turn - 1) * slope[rows, cols].astype(F32)).astype(BF16)
                value[turn - 1] = du
                slope[rows, cols] = du
                vg_ref[5 + c : 6 + c, at] += row_sum(du.astype(F32))
            if 0 <= turn - 2 < PARTS:
                c = (turn - 2) // CUT
                at = slice((turn - 2) % CUT * PART, ((turn - 2) % CUT + 1) * PART)
                dh1 = dh1 + nt(value.pop(turn - 2), w_ref[4 + c, :, at])
        unit = unit1[rows, :]
        vg_ref[3:4, :] += row_sum(dh1 * unit)
        vg_ref[4:5, :] += row_sum(dh1)
        da1_ref[...] = norm_back(dh1 * vec_ref[3:4, :], unit, rate1[rows, :])

    @pl.when(step == 2 * tiles - 1)
    def _():
        @pl.loop(0, FF // D)
        def _(c):
            cols = pl.ds(pl.multiple_of(c * D, D), D)
            wg_ref[c] = tn(h1b[...], slope[:, cols]).astype(BF16)
            wg_ref[4 + c] = tn(act[:, cols], zb[...]).astype(BF16)


def head_phase(info, stu_ref, cls_ref, goal_ref, sg_ref, cg_ref, head_in, head_low, micro, row_len):
    scale = DH**-0.5
    query = stu_ref[D + SW + 2 : D + SW + 3, :]
    same = (
        lax.broadcasted_iota(jnp.int32, (SW, SW), 0) // DH
        == lax.broadcasted_iota(jnp.int32, (SW, SW), 1) // DH
    )
    same = jnp.where(same, 1.0, 0.0).astype(BF16)
    pooled, weights, members = [], [], []
    for m in range(micro):
        rows = slice(m * row_len, (m + 1) * row_len)
        s = head_in[rows, :]
        e = two_low(s * query, same) * scale
        sample = sample_column(ends_of(info, m), 0, row_len)
        share = jnp.zeros_like(e)
        for j in range(SAMP):
            member = sample == j
            peak = jnp.max(jnp.where(member, e, -1e30), axis=0, keepdims=True)
            up = jnp.where(member, jnp.exp(jnp.where(member, e - peak, 0.0)), 0.0)
            up = up / row_sum(up)
            share = share + up
            pooled.append(row_sum(up * s))
            members.append(member)
        weights.append(share)
    pooled = jnp.concatenate(pooled, axis=0)
    pool_weight = stu_ref[D : D + SW, :]
    mixed = jnp.tanh(exact(pooled, pool_weight) + stu_ref[D + SW + 1 : D + SW + 2, :])
    classes = cls_ref[:, 0:SW]
    bias = cls_ref[:, SW : SW + 1].T
    logits = exact(mixed, classes, (((1,), (1,)), ((), ()))) + bias
    logits = logits - jnp.max(logits, axis=-1, keepdims=True)
    chance = jnp.exp(logits)
    chance = chance / jnp.sum(chance, axis=-1, keepdims=True)
    goal = goal_ref[...]
    index = lax.broadcasted_iota(jnp.int32, (micro * SAMP, 1), 0)
    alive = jnp.zeros((micro * SAMP, 1), F32)
    for m in range(micro):
        for j, flag in enumerate(live_of(info, m)):
            alive = jnp.where(index == m * SAMP + j, flag.astype(F32), alive)
    target = jnp.exp(goal - jnp.max(goal, axis=-1, keepdims=True))
    target = target / jnp.sum(target, axis=-1, keepdims=True)
    d_logits = alive * (chance - target)
    cg_ref[:, 0:SW] = exact(d_logits, mixed, (((0,), (0,)), ((), ())))
    cg_ref[:, SW : SW + 1] = row_sum(d_logits).T
    d_pre = exact(d_logits, classes) * (1.0 - mixed * mixed)
    sg_ref[D : D + SW, :] = exact(pooled, d_pre, (((0,), (0,)), ((), ())))
    sg_ref[D + SW + 1 : D + SW + 2, :] = row_sum(d_pre)
    d_pooled = exact(d_pre, pool_weight, (((1,), (1,)), ((), ())))
    inner = two_low(pooled * d_pooled, same)
    d_bias = jnp.zeros((1, SW), F32)
    d_query = jnp.zeros((1, SW), F32)
    for m in range(micro):
        rows = slice(m * row_len, (m + 1) * row_len)
        s = head_in[rows, :]
        spread = jnp.zeros((row_len, SW), F32)
        center = jnp.zeros((row_len, SW), F32)
        for j in range(SAMP):
            member = members[m * SAMP + j]
            at = m * SAMP + j
            spread = jnp.where(member, d_pooled[at : at + 1, :], spread)
            center = jnp.where(member, inner[at : at + 1, :], center)
        share = weights[m]
        d_e = share * (two_low(s * spread, same) - center) * scale
        d_s = (share * spread + d_e * query).astype(BF16)
        head_low[rows, :] = d_s
        d_bias = d_bias + row_sum(d_s.astype(F32))
        d_query = d_query + row_sum(d_e * s)
    sg_ref[D + SW : D + SW + 1, :] = d_bias
    sg_ref[D + SW + 2 : D + SW + 3, :] = d_query


def feed(info, x, o, blocks, vec, student, classifier, goals, send_row, send_col, returned):
    micro, row_len, _ = x.shape
    tokens = micro * row_len
    tile = 512
    tiles = tokens // tile
    group, _, slots, _ = returned.shape
    whole = lambda *shape: pl.BlockSpec(shape, lambda i: (0,) * len(shape))
    once = lambda *shape: pl.BlockSpec(
        shape, lambda i: (0,) * len(shape), pipeline_mode=pl.Buffered(1)
    )
    ahead = lambda width: pl.BlockSpec((tile, width), lambda i: (jnp.minimum(i, tiles - 1), 0))
    behind = lambda width: pl.BlockSpec((tile, width), lambda i: (jnp.maximum(i - tiles, 0), 0))
    return pl.pallas_call(
        functools.partial(feed_kernel, tile=tile, micro=micro, row_len=row_len),
        grid=(2 * tiles,),
        in_specs=[
            pl.BlockSpec(memory_space=pltpu.SMEM),
            ahead(D),
            ahead(D),
            once(NMAT, D, D),
            once(NMAT, D),
            once(*student.shape),
            once(*classifier.shape),
            once(*goals.shape),
            once(*send_row.shape),
            behind(1),
            once(*returned.shape),
        ],
        out_specs=[
            behind(D),
            once(*returned.shape),
            once(8, D, D),
            once(NMAT, D),
            once(*student.shape),
            once(*classifier.shape),
        ],
        out_shape=[
            jax.ShapeDtypeStruct((tokens, D), F32),
            jax.ShapeDtypeStruct(returned.shape, BF16),
            jax.ShapeDtypeStruct((NMAT, D, D), BF16),
            jax.ShapeDtypeStruct((NMAT, D), F32),
            jax.ShapeDtypeStruct(student.shape, F32),
            jax.ShapeDtypeStruct(classifier.shape, F32),
        ],
        scratch_shapes=[
            pltpu.VMEM((tokens, D), F32),
            pltpu.VMEM((tokens, 1), F32),
            pltpu.VMEM((tokens, D), BF16),
            pltpu.VMEM((tokens, FF), BF16),
            pltpu.VMEM((tokens, FF), BF16),
            pltpu.VMEM((tokens, D), F32),
            pltpu.VMEM((tokens, 1), F32),
            pltpu.VMEM((tokens, D), BF16),
            pltpu.VMEM((tokens, SW), F32),
            pltpu.VMEM((tokens, SW), BF16),
        ],
        compiler_params=pltpu.CompilerParams(vmem_limit_bytes=VMEM),
        cost_estimate=pl.CostEstimate(
            flops=tokens * D * FF * 12, bytes_accessed=tokens * D * 16, transcendentals=tokens * FF
        ),
    )(
        info,
        x.reshape(tokens, D),
        o.reshape(tokens, D),
        blocks,
        vec,
        student,
        classifier,
        goals,
        send_row,
        send_col,
        returned,
    )


def attend_back_kernel(
    info,
    x_ref,
    da1_ref,
    q_ref,
    k_ref,
    v_ref,
    o_ref,
    l_ref,
    w_ref,
    _,
    dx_ref,
    wg_ref,
    vg_ref,
    qx,
    kx,
    vx,
    dox,
    dq,
    dk,
    dv,
    dk_sum,
    dv_sum,
    wsum,
    *,
    micro,
):
    row = pl.program_id(0)
    row_len = x_ref.shape[1]
    ends, live = ends_of(info, row), live_of(info, row)
    first = lane_index(QT) < DH
    ones = jnp.ones((QT, LANES), F32)

    @pl.when(row == 0)
    def _():
        vg_ref[...] = jnp.zeros_like(vg_ref)
        wsum[...] = jnp.zeros_like(wsum)

    head = lax.broadcasted_iota(jnp.int32, (D, LANES), 0) // DH
    spot = head // 2 + DH * (1 - head % 2)
    gather = lax.broadcasted_iota(jnp.int32, (D, LANES), 1) == spot
    gather = jnp.where(gather, 1.0, 0.0).astype(BF16)

    dq[...] = jnp.zeros_like(dq)

    @pl.loop(0, row_len // QT)
    def _(t):
        rows = pl.ds(pl.multiple_of(t * QT, QT), QT)
        sample = sample_column(ends, t * QT, QT)
        lane = lane_index(QT) % DH
        high, mid, rest = split_low(jnp.where(lane < PAIRS, -l_ref[0, rows, :], 0.0))
        q_extra = (
            query_spare(sample, QT)
            + high
            + pltpu.roll(mid, PAIRS, 1)
            + pltpu.roll(rest, 2 * PAIRS, 1)
        )
        branch = da1_ref[0, rows, :].astype(BF16)
        vg_ref[2:3, :] += row_sum(branch.astype(F32))
        do = nt(branch, w_ref[3]).astype(BF16).astype(F32)
        delta = two_low(do * o_ref[0, rows, :].astype(F32), gather)
        high = delta.astype(BF16).astype(F32)
        do_extra = pltpu.roll(high - delta, PAIRS, 1) - high
        for p in range(PAIRS):
            pair = head_lanes(p)
            k_extra = key_spare(sample, QT, p)
            store_heads(dox, rows, p, do[:, pair], do_extra, first)
            store_heads(qx, rows, p, q_ref[0, rows, pair].astype(F32), q_extra, first)
            store_heads(kx, rows, p, k_ref[0, rows, pair].astype(F32), k_extra, first)
            store_heads(vx, rows, p, v_ref[0, rows, pair].astype(F32), k_extra, first)

    @pl.loop(0, row_len // QT)
    def _(t):
        rows = pl.ds(pl.multiple_of(t * QT, QT), QT)
        begin, number = reach(ends, live, t * QT, QT, row_len)
        number = (number + STEP - 1) // STEP
        begin = jnp.minimum(begin, row_len // KG - number * STEP)
        dk_sum[...] = jnp.zeros_like(dk_sum)
        dv_sum[...] = jnp.zeros_like(dv_sum)

        @pl.loop(0, number)
        def _(j):
            span = pl.ds(pl.multiple_of((begin + j * STEP) * KG, KG), STEP * KG)
            wide = lane_index(STEP * KG) < DH
            raw, done, got = {}, {}, {}
            for step in range(H + 2):
                if step < H:
                    cols = head_lanes(step)
                    raw[step] = (
                        nt(kx[rows, cols], qx[span, cols]),
                        nt(vx[rows, cols], dox[span, cols]),
                    )
                h = step - 1
                if 0 <= h < H:
                    s, dp = raw.pop(h)
                    prob = jnp.exp(s)
                    done[h] = (prob.astype(BF16), (prob * dp).astype(BF16))
                h = step - 2
                if 0 <= h < H:
                    cols = head_lanes(h)
                    prob, ds = done.pop(h)
                    got[h] = (
                        nn(prob, dox[span, cols]),
                        nn(ds, qx[span, cols]),
                        tn(ds, kx[rows, cols]),
                    )
                    if h % 2 == 1:
                        left, right = got.pop(h - 1), got.pop(h)
                        cols = head_lanes(h // 2)
                        dv_sum[:, cols] += jnp.where(first, left[0], right[0])
                        dk_sum[:, cols] += jnp.where(first, left[1], right[1])
                        dq[span, cols] += jnp.where(wide, left[2], right[2])

        dk[rows, :] = dk_sum[...].astype(BF16)
        dv[rows, :] = dv_sum[...].astype(BF16)

    @pl.loop(0, row_len // QT)
    def _(t):
        rows = pl.ds(pl.multiple_of(t * QT, QT), QT)
        dq_low = (dq[rows, :] * DH**-0.5).astype(BF16)
        dk_low, dv_low = dk[rows, :], dv[rows, :]
        vg_ref[0:1, :] += row_sum(dq_low.astype(F32))
        vg_ref[1:2, :] += row_sum(dv_low.astype(F32))
        dx_ref[0, rows, :] = (
            da1_ref[0, rows, :]
            + nt(dq_low, w_ref[0])
            + nt(dk_low, w_ref[1])
            + nt(dv_low, w_ref[2])
        ).astype(BF16)

    x = x_ref[0]
    wsum[0] += tn(x, (dq[...] * DH**-0.5).astype(BF16))
    wsum[1] += tn(x, dk[...])
    wsum[2] += tn(x, dv[...])
    wsum[3] += tn(o_ref[0], da1_ref[0].astype(BF16))

    @pl.when(row == micro - 1)
    def _():
        wg_ref[...] = wsum[...].astype(BF16)


def attend_back(info, tokens, da1, q, k, v, o, logs, blocks, grads):
    micro, row_len, _ = tokens.shape
    row_spec = lambda width: pl.BlockSpec((1, row_len, width), lambda r: (r, 0, 0))
    return pl.pallas_call(
        functools.partial(attend_back_kernel, micro=micro),
        grid=(micro,),
        in_specs=[
            pl.BlockSpec(memory_space=pltpu.SMEM),
            *[row_spec(D)] * 6,
            row_spec(LANES),
            pl.BlockSpec((4, D, D), lambda r: (0, 0, 0)),
            pl.BlockSpec(memory_space=pl.ANY),
        ],
        out_specs=[
            row_spec(D),
            pl.BlockSpec((4, D, D), lambda r: (2, 0, 0)),
            pl.BlockSpec((8, D), lambda r: (0, 0)),
        ],
        out_shape=[
            jax.ShapeDtypeStruct((micro, row_len, D), BF16),
            jax.ShapeDtypeStruct((NMAT, D, D), BF16),
            jax.ShapeDtypeStruct((8, D), F32),
        ],
        scratch_shapes=[
            *[pltpu.VMEM((row_len, 2 * D), BF16)] * 4,
            pltpu.VMEM((row_len, D), F32),
            pltpu.VMEM((row_len, D), BF16),
            pltpu.VMEM((row_len, D), BF16),
            pltpu.VMEM((QT, D), F32),
            pltpu.VMEM((QT, D), F32),
            pltpu.VMEM((4, D, D), F32),
        ],
        input_output_aliases={9: 1},
        compiler_params=pltpu.CompilerParams(vmem_limit_bytes=VMEM),
        cost_estimate=pl.CostEstimate(
            flops=micro * row_len * D * D * 16 + micro * H * row_len * row_len * DH * 10,
            bytes_accessed=micro * row_len * D * 16,
            transcendentals=micro * H * row_len * row_len,
        ),
    )(info, tokens, da1, q, k, v, o, logs, blocks, grads)


CROSS = 3
CHUNKS = 12
STU_ROWS, CLS_ROWS, VEC_ROWS = 656, 16, 16
SMALL_ROWS = 1024


def reduce_kernel(
    group,
    owners,
    grad_ref,
    ff_vec,
    at_vec,
    stu_ref,
    cls_ref,
    own_ref,
    vec_out,
    stu_out,
    cls_out,
    got_a,
    sum_a,
    got_b,
    part,
    got_c,
    final,
    small,
    small_got,
    small_sum,
    small_end,
    got_y,
    half_y,
    send_sem,
    recv_sem,
    small_send,
    small_recv,
):
    b, s = lax.axis_index("batch"), lax.axis_index("shard")
    per = NMAT // owners
    rows = per * D // CHUNKS
    batch_bits, shard_bits = bits_of(group), bits_of(owners)
    half = SMALL_ROWS // 2

    def copy(src, dst, sems, at, where):
        return pltpu.make_async_remote_copy(
            src_ref=src,
            dst_ref=dst,
            send_sem=sems[0].at[at],
            recv_sem=sems[1].at[at],
            device_id=where,
            device_id_type=pl.DeviceIdType.MESH,
        )

    peers = [(b, s ^ bit) for bit in shard_bits] + [(b ^ bit, s) for bit in batch_bits]
    barrier = pltpu.get_barrier_semaphore()
    for peer in peers:
        pl.semaphore_signal(
            barrier, inc=1, device_id=peer, device_id_type=pl.DeviceIdType.MESH
        )
    pl.semaphore_wait(barrier, len(peers))

    sems = (send_sem, recv_sem)
    small_sems = (small_send, small_recv)
    waits = []

    def begin(op):
        op.start()
        waits.append(op)
        return op

    def piece(owner, c):
        at = lax.rem(owner * per + c * per // CHUNKS + 8, NMAT)
        if rows == D:
            return grad_ref.at[at]
        step = D // rows
        return grad_ref.at[at, pl.ds((c % step) * rows, rows)]

    far = shard_bits[1]
    first = {}
    for c in range(CHUNKS):
        first[c] = [
            begin(copy(piece(s ^ 1 ^ far, c), got_a.at[c, 0], sems, (c, 0), peers[0])),
            begin(copy(piece(s ^ 1, c), got_a.at[c, 1], sems, (c, 1), peers[0])),
        ]

    small[...] = jnp.zeros_like(small)
    stu_count = stu_ref.shape[0]
    small[0:stu_count, :] = stu_ref[...].astype(BF16)
    small[STU_ROWS : STU_ROWS + CLS, :] = cls_ref[:, 0:SW].astype(BF16)
    small[STU_ROWS + CLS_ROWS : STU_ROWS + CLS_ROWS + CLS, 0:1] = cls_ref[:, SW:].astype(BF16)
    for i in range(4):
        at = STU_ROWS + 2 * CLS_ROWS + i * VEC_ROWS
        lanes = slice(i * LANES, (i + 1) * LANES)
        small[at : at + 3, :] = at_vec[0:3, lanes].astype(BF16)
        small[at + 3 : at + NMAT, :] = ff_vec[3:NMAT, lanes].astype(BF16)
    core = lax.rem(s, 2)
    mine = pl.ds(pl.multiple_of(core * half, 16), half)
    other = pl.ds(pl.multiple_of((1 - core) * half, 16), half)
    small_op = begin(copy(small.at[other], small_got.at[pl.ds(0, half)], small_sems, 0, peers[0]))

    def add(x, y):
        return (x.astype(F32) + y.astype(F32)).astype(BF16)

    def add_into(out, x, y, x_at=0, y_at=0, out_at=0):
        count = out[1]
        slab = 16 if count % 32 else 32

        @pl.loop(0, count // slab)
        def _(i):
            def rows_at(first):
                return pl.ds(pl.multiple_of(first + i * slab, 16), slab)

            out[0][rows_at(out_at), :] = add(x[rows_at(x_at), :], y[rows_at(y_at), :])

    second = {}
    copies = send_sem.shape[1]

    def crossed(c):
        return c % CROSS == CROSS - 1

    def start_second(c):
        for i, op in enumerate(first[c]):
            op.wait_recv()
            owner = s ^ far if i == 0 else s
            add_into((sum_a.at[c, i], rows), piece(owner, c), got_a.at[c, i])
        if crossed(c):
            count = rows // 2
            away = pl.ds(pl.multiple_of((1 - lax.rem(b, 2)) * count, 16), count)
            second[c] = [
                begin(copy(sum_a.at[c, i, away], got_y.at[c, i], sems, (c, at), (b ^ 1, s)))
                for i, at in ((0, 3), (1, copies - 1))
            ]
        else:
            second[c] = begin(copy(sum_a.at[c, 0], got_b.at[c], sems, (c, 2), peers[1]))

    start_second(0)
    start_second(1)

    spans = []
    size = rows
    for bit in batch_bits:
        halving = size >= 32
        spans.append((bit, size, halving))
        if halving:
            size //= 2
    offset_of = []
    offset = jnp.int32(0)
    slot_of = []
    slot = 0
    for bit, now, halving in spans:
        place = lax.rem(b // bit, 2)
        offset_of.append((offset, place))
        slot_of.append(slot)
        if halving:
            offset = offset + place * (now // 2)
            slot += now // 2
        else:
            slot += now
    last = offset

    def ranged(ref, c, start, count):
        return ref.at[c, pl.ds(pl.multiple_of(start, 16), count)]

    moving = {}

    def start_batch(c, k):
        bit, now, halving = spans[k]
        start, place = offset_of[k]
        if halving:
            count = now // 2
            src = ranged(part.at[k], c, start + (1 - place) * count, count)
        else:
            count = now
            src = ranged(part.at[k], c, start, count)
        dst = got_c.at[c, pl.ds(slot_of[k], count)]
        moving[c, k] = begin(copy(src, dst, sems, (c, 3 + k), (b ^ bit, s)))

    def end_batch(c, k):
        bit, now, halving = spans[k]
        start, place = offset_of[k]
        moving[c, k].wait_recv()
        count = now // 2 if halving else now
        if halving:
            start = start + place * count
        target = part.at[k + 1, c] if k + 1 < len(spans) else final.at[c]
        add_into(
            (target, count), part.at[k, c], got_c.at[c], x_at=start, y_at=slot_of[k], out_at=start
        )

    gathers = [k for k in reversed(range(len(spans))) if spans[k][2]]
    gathering = {}

    def start_gather(c, g):
        k = gathers[g]
        bit, now, _ = spans[k]
        start, place = offset_of[k]
        count = now // 2
        at = ranged(final, c, start + place * count, count)
        gathering[c, g] = begin(
            copy(at, at, sems, (c, 3 + len(spans) + g), (b ^ bit, s))
        )

    def stage(c, k):
        if crossed(c) and k < 2:
            count = rows // 2
            here = lax.rem(b, 2) * count
            if k == 0:
                for i, op in enumerate(second[c]):
                    op.wait_recv()
                    add_into((half_y.at[c, i], count), sum_a.at[c, i], got_y.at[c, i], x_at=here)
                dst = got_b.at[c, pl.ds(0, count)]
                second[c] = begin(copy(half_y.at[c, 0], dst, sems, (c, 2), peers[1]))
                if c + 2 < CHUNKS:
                    start_second(c + 2)
            else:
                second[c].wait_recv()
                add_into((part.at[1, c], count), half_y.at[c, 1], got_b.at[c], out_at=here)
                start_batch(c, 1)
        elif k == 0:
            second[c].wait_recv()
            if c + 2 < CHUNKS:
                start_second(c + 2)
            add_into((part.at[0, c], rows), sum_a.at[c, 1], got_b.at[c])
            start_batch(c, 0)
        elif k <= len(spans):
            end_batch(c, k - 1)
            if k < len(spans):
                start_batch(c, k)
            else:
                start_gather(c, 0)
        else:
            g = k - len(spans) - 1
            gathering[c, g].wait_recv()
            if g + 1 < len(gathers):
                start_gather(c, g + 1)
            else:
                per_block = CHUNKS // per
                block, within = c // per_block, c % per_block
                own_ref[block, within * rows : (within + 1) * rows, :] = final[c]

    stages = 1 + len(spans) + len(gathers)
    rest = [(s, bit) for bit in shard_bits[1:]] + [(b, bit) for bit in batch_bits]
    levels = []
    start, size, at = core * half, half, 0
    for index, (axis, bit) in enumerate(rest):
        place = lax.rem(axis // bit, 2)
        count = size // 2 if size >= 32 else size
        peer = (b, s ^ bit) if index < len(shard_bits) - 1 else (b ^ bit, s)
        levels.append((start, size, count, place, peer, at))
        at += count
        if count < size:
            start, size = start + place * count, count
    last_start, last_size = start, size
    backs = [k for k in reversed(range(len(levels))) if levels[k][2] < levels[k][1]]

    def small_rows(ref, first, count):
        return ref.at[pl.ds(pl.multiple_of(first, 16), count)]

    def small_begin(k):
        begin_at, now, count, place, peer, slot = levels[k]
        first = begin_at + (1 - place) * count if count < now else begin_at
        return begin(
            copy(
                small_rows(small_sum.at[k], first, count),
                small_got.at[pl.ds(half + slot, count)],
                small_sems,
                k + 1,
                peer,
            )
        )

    def small_back(g):
        if g == len(backs):
            at = small_rows(small_end, core * half, half)
            return begin(copy(at, at, small_sems, len(levels) + 1 + g, peers[0]))
        begin_at, now, count, place, peer, _ = levels[backs[g]]
        at = small_rows(small_end, begin_at + place * count, count)
        return begin(copy(at, at, small_sems, len(levels) + 1 + g, peer))

    def small_stage(k):
        nonlocal small_op
        small_op.wait_recv()
        if k == 0:
            add_into((small_sum.at[0], half), small, small_got, x_at=core * half, out_at=core * half)
            small_op = small_begin(0)
        elif k <= len(levels):
            begin_at, now, count, place, _, slot = levels[k - 1]
            first = begin_at + place * count if count < now else begin_at
            target = small_sum.at[k] if k < len(levels) else small_end
            add_into(
                (target, count),
                small_sum.at[k - 1],
                small_got,
                x_at=first,
                y_at=half + slot,
                out_at=first,
            )
            small_op = small_begin(k) if k < len(levels) else small_back(0)
        elif k - len(levels) <= len(backs):
            small_op = small_back(k - len(levels))

    small_last = len(levels) + len(backs) + 1
    small_k = 0
    for tick in range(CHUNKS + 2 * (stages - 1)):
        for k in reversed(range(stages)):
            c = tick - 2 * k
            if 0 <= c < CHUNKS:
                stage(c, k)
        if small_k <= small_last:
            small_stage(small_k)
            small_k += 1
    while small_k <= small_last:
        small_stage(small_k)
        small_k += 1

    for i in range(4):
        at = STU_ROWS + 2 * CLS_ROWS + i * VEC_ROWS
        lanes = slice(i * LANES, (i + 1) * LANES)
        vec_out[:, lanes] = small_end[at : at + VEC_ROWS, :].astype(F32)
    stu_out[...] = small_end[0:STU_ROWS, :].astype(F32)
    cls_out[:, 0:LANES] = small_end[STU_ROWS : STU_ROWS + CLS_ROWS, :].astype(F32)
    at = STU_ROWS + CLS_ROWS
    cls_out[:, LANES:] = small_end[at : at + CLS_ROWS, :].astype(F32)
    for op in waits:
        op.wait_send()


def reduce_grads(grads, ff_vec, at_vec, stu, cls):
    group, owners = lax.axis_size("batch"), lax.axis_size("shard")
    per = NMAT // owners
    rows = per * D // CHUNKS
    batch_count = len(bits_of(group))
    copies = 4 + 2 * batch_count
    small_count = len(bits_of(owners)) + batch_count + 1
    vmem = pl.BlockSpec(memory_space=pltpu.VMEM)
    return pl.pallas_call(
        functools.partial(reduce_kernel, group, owners),
        in_specs=[vmem] * 5,
        out_specs=[vmem] * 4,
        out_shape=[
            jax.ShapeDtypeStruct((per, D, D), BF16),
            jax.ShapeDtypeStruct((VEC_ROWS, D), F32),
            jax.ShapeDtypeStruct((STU_ROWS, SW), F32),
            jax.ShapeDtypeStruct((CLS_ROWS, 2 * LANES), F32),
        ],
        scratch_shapes=[
            pltpu.VMEM((CHUNKS, 2, rows, D), BF16),
            pltpu.VMEM((CHUNKS, 2, rows, D), BF16),
            pltpu.VMEM((CHUNKS, rows, D), BF16),
            pltpu.VMEM((batch_count, CHUNKS, rows, D), BF16),
            pltpu.VMEM((CHUNKS, rows + 16 * batch_count, D), BF16),
            pltpu.VMEM((CHUNKS, rows, D), BF16),
            pltpu.VMEM((SMALL_ROWS, LANES), BF16),
            pltpu.VMEM((SMALL_ROWS + 32 * small_count, LANES), BF16),
            pltpu.VMEM((small_count, SMALL_ROWS, LANES), BF16),
            pltpu.VMEM((SMALL_ROWS, LANES), BF16),
            pltpu.VMEM((CHUNKS, 2, rows // 2, D), BF16),
            pltpu.VMEM((CHUNKS, 2, rows // 2, D), BF16),
            pltpu.SemaphoreType.DMA((CHUNKS, copies)),
            pltpu.SemaphoreType.DMA((CHUNKS, copies)),
            pltpu.SemaphoreType.DMA((2 * small_count + 1,)),
            pltpu.SemaphoreType.DMA((2 * small_count + 1,)),
        ],
        compiler_params=pltpu.CompilerParams(
            collective_id=1, has_side_effects=True, vmem_limit_bytes=VMEM
        ),
        cost_estimate=pl.CostEstimate(
            flops=NMAT * D * D * 4, bytes_accessed=NMAT * D * D * 8, transcendentals=0
        ),
    )(grads, ff_vec, at_vec, stu, cls)


def update_kernel(
    own_ref,
    blocks_ref,
    left_ref,
    right_ref,
    lroot_ref,
    rroot_ref,
    shard_ref,
    vsum_ref,
    vec_ref,
    vmom_ref,
    ssum_ref,
    stu_ref,
    smom_ref,
    csum_ref,
    cls_ref,
    cmom_ref,
    back_ref,
    rows_ref,
    grad_out,
    new_out,
    left_out,
    right_out,
    vg_out,
    vm_out,
    v_out,
    sg_out,
    sm_out,
    s_out,
    cg_out,
    cm_out,
    c_out,
    layer_out,
    *,
    owners,
):
    step = pl.program_id(0)
    row_len = layer_out.shape[1]

    @pl.when(step < rows_ref.shape[1])
    def _():
        arrived = rows_ref[:, step].reshape(row_len, D)
        chunk = min(256, row_len)

        @pl.loop(0, row_len // chunk)
        def _(k):
            at = pl.multiple_of(k * chunk, chunk)
            spot = at + lax.broadcasted_iota(jnp.int32, (chunk, row_len), 0)
            pick = jnp.where(spot == back_ref[pl.ds(step, 1), :], 1.0, 0.0).astype(BF16)
            layer_out[0, pl.ds(at, chunk), :] = nn(pick, arrived).astype(BF16)

    g = own_ref[0]
    grad_out[0] = g.astype(F32)
    left_out[0] = decay_rate * left_ref[0] + (1.0 - decay_rate) * nt(g, g)
    right_out[0] = decay_rate * right_ref[0] + (1.0 - decay_rate) * tn(g, g)
    steered = nn(lroot_ref[0].astype(BF16), g).astype(BF16)
    steered = nn(steered, rroot_ref[0].astype(BF16))
    size = jnp.mean(steered * steered, keepdims=True)
    new_out[0] = blocks_ref[0].astype(F32) - steered * (block_rate * lax.rsqrt(size + 1e-06))

    @pl.when(pl.program_id(0) == 0)
    def _():
        per = NMAT // owners
        mine = vsum_ref[0:per, :]
        for i in range(1, owners):
            mine = jnp.where(shard_ref[0] == i, vsum_ref[i * per : (i + 1) * per, :], mine)

        def rule(grads, old, moment, rate, outs):
            renewed = decay_rate * moment + (1.0 - decay_rate) * grads * grads
            outs[0][...] = grads
            outs[1][...] = renewed
            outs[2][...] = old - rate * grads / (jnp.sqrt(renewed) + 1e-08)

        rule(mine, vec_ref[...], vmom_ref[...], vector_rate, (vg_out, vm_out, v_out))
        rule(
            ssum_ref[0 : stu_ref.shape[0], :],
            stu_ref[...],
            smom_ref[...],
            head_rate,
            (sg_out, sm_out, s_out),
        )
        rule(
            csum_ref[0:CLS, 0 : SW + 1],
            cls_ref[...],
            cmom_ref[...],
            head_rate,
            (cg_out, cm_out, c_out),
        )


def update(own, blocks, left, right, lroot, rroot, shard, vsum, vec, vmom, ssum, stu, smom, csum, cls, cmom, back, arrived):
    per = own.shape[0]
    micro, row_len = back.shape
    mat = pl.BlockSpec((1, D, D), lambda i: (i, 0, 0))
    whole = lambda a: pl.BlockSpec(a.shape, lambda i: (0,) * a.ndim)
    like = lambda a: jax.ShapeDtypeStruct(a.shape, F32)
    return pl.pallas_call(
        functools.partial(update_kernel, owners=NMAT // per),
        grid=(per,),
        in_specs=[mat] * 6
        + [pl.BlockSpec(memory_space=pltpu.SMEM)]
        + [whole(a) for a in (vsum, vec, vmom, ssum, stu, smom, csum, cls, cmom, back, arrived)],
        out_specs=[mat] * 4
        + [whole(a) for a in (vec,) * 3 + (stu,) * 3 + (cls,) * 3]
        + [pl.BlockSpec((1, row_len, D), lambda i: (jnp.minimum(i, micro - 1), 0, 0))],
        out_shape=[like(left)] * 4
        + [like(a) for a in (vec,) * 3 + (stu,) * 3 + (cls,) * 3]
        + [jax.ShapeDtypeStruct((micro, row_len, D), BF16)],
        compiler_params=pltpu.CompilerParams(vmem_limit_bytes=VMEM),
    )(
        own,
        blocks,
        left,
        right,
        lroot,
        rroot,
        shard,
        vsum,
        vec,
        vmom,
        ssum,
        stu,
        smom,
        csum,
        cls,
        cmom,
        back,
        arrived,
    )


def local(
    tokens,
    cotangent,
    lengths,
    exit_layers,
    teacher,
    blocks,
    left_stats,
    right_stats,
    left_root,
    right_root,
    vectors,
    vec_moment,
    student,
    stu_moment,
    classifier,
    cls_moment,
):
    group = lax.axis_size("batch")
    me = lax.axis_index("batch")
    micro, _, row_len, _ = tokens.shape
    slots = row_len // group
    tokens, cotangent = tokens[:, 0], cotangent[:, 0]
    ends = jnp.cumsum(lengths[:, 0], axis=-1, dtype=jnp.int32)
    live = (exit_layers[:, 0] >= LAYER).astype(jnp.int32)
    info = jnp.concatenate([lengths[:, 0], exit_layers[:, 0]], axis=1)
    alive_len = lengths[:, 0] * live
    counts = jnp.sum(alive_len, axis=1, dtype=jnp.int32)
    everyone = lax.all_gather(counts[None, :], "batch", axis=0, tiled=True)
    starts = jnp.cumsum(everyone, axis=0, dtype=jnp.int32) - everyone

    places = jnp.arange(row_len, dtype=jnp.int32)
    before = jnp.cumsum(alive_len, axis=1, dtype=jnp.int32) - alive_len
    sample = jnp.sum((places[None, :, None] >= ends[:, None, : SAMP - 1]).astype(jnp.int32), axis=-1)
    chosen = sample[..., None] == jnp.arange(SAMP, dtype=jnp.int32)
    shift = jnp.sum(jnp.where(chosen, (before - ends + lengths[:, 0])[:, None, :], 0), axis=-1)
    alive_tok = jnp.sum(jnp.where(chosen, live[:, None, :], 0), axis=-1)
    rank = places[None, :] + shift
    send = (starts[me][:, None] + rank) % group * slots + rank // group
    send = jnp.where(alive_tok > 0, send, row_len)
    start_of = jnp.repeat(starts.T, slots, axis=1)
    count_of = jnp.repeat(everyone.T, slots, axis=1)
    turn = (me - start_of) % group + group * (places % slots)[None, :]
    back = jnp.where(turn < count_of, (start_of + turn) // group, row_len)

    grad_outgoing = pick_rows(back[:, :, None], cotangent, group)
    returned = lax.all_to_all(grad_outgoing, "batch", split_axis=0, concat_axis=0, tiled=True)

    matrices = lax.all_gather(blocks, "shard", axis=0, tiled=True)
    vec = lax.all_gather(vectors.astype(BF16), "shard", axis=0, tiled=True).astype(F32)

    q, k, v, o, logs = attend(info, tokens, matrices, vec)
    goals = teacher.reshape(micro * SAMP, CLS)
    classifier, cls_moment = classifier.T, cls_moment.T
    da1, outgoing, ff_grads, ff_vecs, stu_grads, cls_grads = feed(
        info, tokens, o, matrices, vec, student, classifier, goals, send, send.reshape(-1, 1), returned
    )
    arrived = lax.all_to_all(outgoing, "batch", split_axis=0, concat_axis=0, tiled=True)
    input_grads, grads, at_vecs = attend_back(
        info, tokens, da1.reshape(micro, row_len, D), q, k, v, o, logs, matrices, ff_grads
    )
    own, vec_sum, stu_sum, cls_sum = reduce_grads(grads, ff_vecs, at_vecs, stu_grads, cls_grads)
    shard = lax.axis_index("shard").astype(jnp.int32).reshape(1)
    *updated, layer_out = update(
        own,
        blocks,
        left_stats,
        right_stats,
        left_root,
        right_root,
        shard,
        vec_sum,
        vectors,
        vec_moment,
        stu_sum,
        student,
        stu_moment,
        cls_sum,
        classifier,
        cls_moment,
        back,
        arrived,
    )
    classes = [a.T for a in updated[-3:]]
    return (layer_out[:, None], input_grads[:, None], *updated[:-3], *classes)


def solution(mesh):
    rows = P(None, ("batch", "shard"), None, None)
    tags = P(None, ("batch", "shard"), None)
    mats = P("shard", None, None)
    vecs = P("shard", None)
    return jax.shard_map(
        local,
        mesh=mesh,
        in_specs=(rows, rows, tags, tags, rows, mats, mats, mats, mats, mats, vecs, vecs)
        + (P(),) * 4,
        out_specs=(rows, rows, mats, mats, mats, mats, vecs, vecs, vecs) + (P(),) * 6,
        check_vma=False,
    )
```

```python
import functools

import jax
import jax.numpy as jnp
from jax import lax
from jax.experimental import pallas as pl
from jax.experimental.pallas import tpu as pltpu
from jax.sharding import PartitionSpec as P

D = 512
H = 8
DH = 64
FF = 2048
SW = 128
NMAT = 12
SAMP = 4
LAYER = 4
CLS = 14

decay_rate = 0.5
block_rate = 0.04
vector_rate = 0.05
head_rate = 0.05

QT = 256
STEP = 2
KG = 128
PAIRS = H // 2
LANES = 128
PART = 512
PARTS, CUT = FF // PART, D // PART
BIG = float(2**30)
EPS = 1e-6
VMEM = 60 * 1024 * 1024

F32 = jnp.float32
BF16 = jnp.bfloat16


def nn(a, b):
    return jnp.dot(a, b, preferred_element_type=F32)


def nt(a, b):
    return lax.dot_general(a, b, (((1,), (1,)), ((), ())), preferred_element_type=F32)


def tn(a, b):
    return lax.dot_general(a, b, (((0,), (0,)), ((), ())), preferred_element_type=F32)


def exact(a, b, dims=(((1,), (0,)), ((), ()))):
    return lax.dot_general(
        a, b, dims, preferred_element_type=F32, precision=lax.Precision.HIGHEST
    )


def row_sum(v):
    return jnp.sum(v, axis=0, keepdims=True)


def two_low(v, b):
    high = v.astype(BF16)
    return nn(high, b) + nn((v - high.astype(F32)).astype(BF16), b)


def split_low(v):
    high = v.astype(BF16).astype(F32)
    rest = v - high
    mid = rest.astype(BF16).astype(F32)
    return high, mid, rest - mid


def ends_of(info, row):
    ends, total = [], jnp.int32(0)
    for j in range(SAMP):
        total = total + info[row, j]
        ends.append(total)
    return ends


def live_of(info, row):
    return [(info[row, SAMP + j] >= LAYER).astype(jnp.int32) for j in range(SAMP)]


def sample_column(ends, first, count):
    place = first + lax.broadcasted_iota(jnp.int32, (count, 1), 0)
    total = jnp.zeros((count, 1), jnp.int32)
    for j in range(SAMP - 1):
        total = total + (place >= ends[j]).astype(jnp.int32)
    return total


def reach(ends, live, first, count, row_len):
    low, high = jnp.int32(row_len), jnp.int32(0)
    start = jnp.int32(0)
    for j in range(SAMP):
        end = ends[j]
        meets = (start < first + count) & (end > first) & (end > start) & (live[j] > 0)
        low = jnp.where(meets, jnp.minimum(low, start), low)
        high = jnp.where(meets, jnp.maximum(high, end), high)
        start = end
    begin = low // KG
    number = jnp.maximum((high + KG - 1) // KG - begin, 0)
    return begin, number


def lane_index(rows):
    return lax.broadcasted_iota(jnp.int32, (rows, LANES), 1)


TAG = 16


def key_spare(sample, rows, pair):
    lane = lane_index(rows) % DH
    own = (lane < 3 * PAIRS) & (lane % PAIRS == pair)
    return jnp.where(own | (lane == sample + TAG), 1.0, 0.0)


def query_spare(sample, rows):
    lane = lane_index(rows) % DH
    tag = (lane >= TAG) & (lane < TAG + SAMP) & (lane != sample + TAG)
    return jnp.where(tag, -BIG, 0.0)


def store_heads(ref, rows, p, pair, spare, first):
    pair, spare, last = pair.astype(BF16), spare.astype(BF16), 1 - first
    ref[rows, 2 * p * LANES : (2 * p + 1) * LANES] = pair * first + spare * last
    ref[rows, (2 * p + 1) * LANES : (2 * p + 2) * LANES] = pair * last + spare * first


def head_lanes(h):
    return slice(h * LANES, (h + 1) * LANES)


def widths(row_len):
    most = row_len // KG
    return list(range(most // 2, most + 1))


def chosen_span(ends, live, t, row_len):
    begin, number = reach(ends, live, t * QT, QT, row_len)
    least, most = widths(row_len)[0], row_len // KG
    number = jnp.where(number > 0, jnp.maximum(number, least), 0)
    return jnp.minimum(begin, most - number), number


def bits_of(size):
    return [1 << i for i in range(size.bit_length() - 1)]


def pick_kernel(place_ref, rows_ref, out_ref):
    group, _, slots, _ = out_ref.shape
    places = group * slots
    spot = lax.broadcasted_iota(jnp.int32, (places, rows_ref.shape[1]), 1)
    pick = jnp.where(spot == place_ref[0], 1.0, 0.0).astype(BF16)
    out_ref[:, 0] = nn(pick, rows_ref[0]).astype(BF16).reshape(group, slots, D)


def pick_rows(place_col, rows, group):
    micro, row_len, _ = rows.shape
    slots = row_len // group
    return pl.pallas_call(
        pick_kernel,
        grid=(micro,),
        in_specs=[
            pl.BlockSpec((1, row_len, 1), lambda m: (m, 0, 0)),
            pl.BlockSpec((1, row_len, D), lambda m: (m, 0, 0)),
        ],
        out_specs=pl.BlockSpec((group, 1, slots, D), lambda m: (0, m, 0, 0)),
        out_shape=jax.ShapeDtypeStruct((group, micro, slots, D), BF16),
        compiler_params=pltpu.CompilerParams(vmem_limit_bytes=VMEM),
    )(place_col, rows)


def attend_kernel(info, x_ref, w_ref, vec_ref, q_ref, k_ref, v_ref, o_ref, l_ref, qx, kx, vx):
    row = pl.program_id(0)
    row_len = x_ref.shape[1]
    ends, live = ends_of(info, row), live_of(info, row)
    first = lane_index(QT) < DH
    low_first = jnp.where(first, 1.0, 0.0).astype(BF16)
    ones = jnp.ones((QT, LANES), F32)

    @pl.loop(0, row_len // QT)
    def _(t):
        rows = pl.ds(pl.multiple_of(t * QT, QT), QT)
        x = x_ref[0, rows, :]
        sample = sample_column(ends, t * QT, QT)
        q_extra = query_spare(sample, QT)
        q = ((nn(x, w_ref[0]) + vec_ref[0:1, :]).astype(BF16).astype(F32) * DH**-0.5).astype(BF16)
        k = nn(x, w_ref[1]).astype(BF16)
        v = (nn(x, w_ref[2]) + vec_ref[1:2, :]).astype(BF16)
        q_ref[0, rows, :] = q
        k_ref[0, rows, :] = k
        v_ref[0, rows, :] = v
        for p in range(PAIRS):
            pair = head_lanes(p)
            store_heads(qx, rows, p, q[:, pair], q_extra, low_first)
            store_heads(kx, rows, p, k[:, pair], key_spare(sample, QT, p), low_first)
            store_heads(vx, rows, p, v[:, pair], ones, low_first)

    @pl.loop(0, row_len // QT)
    def _(t):
        rows = pl.ds(pl.multiple_of(t * QT, QT), QT)
        begin, number = chosen_span(ends, live, t, row_len)

        @pl.when(number == 0)
        def _():
            o_ref[0, rows, :] = jnp.zeros((QT, D), BF16)
            l_ref[0, rows, :] = jnp.zeros((QT, LANES), F32)

        for n in widths(row_len):

            @pl.when(number == n)
            def _(n=n):
                span = pl.ds(pl.multiple_of(begin * KG, KG), n * KG)
                lane = lane_index(QT)
                scores, powers, got = {}, {}, {}
                peaks = jnp.zeros((QT, LANES), F32)
                totals = jnp.ones((QT, LANES), F32)
                for step in range(H + 2):
                    if step < H:
                        cols = head_lanes(step)
                        scores[step] = nt(qx[rows, cols], kx[span, cols])
                    h = step - 1
                    if 0 <= h < H:
                        s = scores.pop(h)
                        peak = jnp.max(s, axis=1, keepdims=True)
                        powers[h] = jnp.exp(s - peak).astype(BF16)
                        spot = lane == (h // 2 + DH if h % 2 == 0 else h // 2)
                        peaks = jnp.where(spot, peak, peaks)
                    h = step - 2
                    if 0 <= h < H:
                        got[h] = nn(powers.pop(h), vx[span, head_lanes(h)])
                        spot = lane == (h // 2 + DH if h % 2 == 0 else h // 2)
                        totals = jnp.where(spot, got[h], totals)
                        if h % 2 == 1:
                            left, right = got.pop(h - 1), got.pop(h)
                            top = jnp.where(first, left, right)
                            total = pltpu.roll(jnp.where(first, right, left), DH, 1)
                            o_ref[0, rows, head_lanes(h // 2)] = (top / total).astype(BF16)
                l_ref[0, rows, :] = jnp.where(
                    peaks > -0.5 * BIG, peaks + jnp.log(totals), 0.0
                )


def attend(info, tokens, blocks, vec):
    micro, row_len, _ = tokens.shape
    row_spec = lambda width: pl.BlockSpec((1, row_len, width), lambda r: (r, 0, 0))
    low = jax.ShapeDtypeStruct((micro, row_len, D), BF16)
    return pl.pallas_call(
        attend_kernel,
        grid=(micro,),
        in_specs=[
            pl.BlockSpec(memory_space=pltpu.SMEM),
            row_spec(D),
            pl.BlockSpec((3, D, D), lambda r: (0, 0, 0)),
            pl.BlockSpec((NMAT, D), lambda r: (0, 0)),
        ],
        out_specs=[row_spec(D)] * 4 + [row_spec(LANES)],
        out_shape=[low] * 4 + [jax.ShapeDtypeStruct((micro, row_len, LANES), F32)],
        scratch_shapes=[pltpu.VMEM((row_len, 2 * D), BF16)] * 3,
        compiler_params=pltpu.CompilerParams(vmem_limit_bytes=VMEM),
        cost_estimate=pl.CostEstimate(
            flops=micro * row_len * D * D * 6 + micro * H * row_len * row_len * DH * 16,
            bytes_accessed=micro * row_len * D * 16,
            transcendentals=micro * H * row_len * row_len,
        ),
    )(info, tokens, blocks, vec)


def gelu_both(u):
    share = 0.5 + 0.5 * lax.erf(u * 0.5**0.5)
    bell = jnp.exp2((-0.5 * 1.4426950408889634) * (u * u))
    return u * share, share + (u * 0.3989422804014327) * bell


def norm_parts(a):
    center = a - jnp.mean(a, axis=-1, keepdims=True)
    rate = lax.rsqrt(jnp.mean(center * center, axis=-1, keepdims=True) + EPS)
    return center * rate, rate


def norm_back(grad, unit, rate):
    return rate * (
        grad
        - jnp.mean(grad, axis=-1, keepdims=True)
        - unit * jnp.mean(grad * unit, axis=-1, keepdims=True)
    )


def feed_kernel(
    info,
    x_ref,
    o_ref,
    w_ref,
    vec_ref,
    stu_ref,
    cls_ref,
    goal_ref,
    send_row,
    send_col,
    back_ref,
    da1_ref,
    out_ref,
    wg_ref,
    vg_ref,
    sg_ref,
    cg_ref,
    unit1,
    rate1,
    h1b,
    act,
    slope,
    unit2,
    rate2,
    zb,
    head_in,
    head_low,
    *,
    tile,
    micro,
    row_len,
):
    step = pl.program_id(0)
    tiles = micro * row_len // tile
    group, _, slots, _ = out_ref.shape

    @pl.when(step == 0)
    def _():
        vg_ref[...] = jnp.zeros_like(vg_ref)

    @pl.when(step < tiles)
    def _():
        rows = pl.ds(pl.multiple_of(step * tile, tile), tile)
        a1 = x_ref[...].astype(F32) + (nn(o_ref[...], w_ref[3]) + vec_ref[2:3, :])
        unit, rate = norm_parts(a1)
        unit1[rows, :] = unit
        rate1[rows, :] = rate
        h1 = unit * vec_ref[3:4, :] + vec_ref[4:5, :]
        low = h1.astype(BF16)
        h1b[rows, :] = low
        total = h1 + vec_ref[9:10, :]
        raw, value = {}, {}
        for turn in range(PARTS + 2):
            if turn < PARTS:
                c, at = turn // CUT, slice(turn % CUT * PART, (turn % CUT + 1) * PART)
                raw[turn] = nn(low, w_ref[4 + c, :, at]) + vec_ref[5 + c : 6 + c, at]
            if 0 <= turn - 1 < PARTS:
                cols = slice((turn - 1) * PART, turn * PART)
                up, grad = gelu_both(raw.pop(turn - 1))
                value[turn - 1] = up.astype(BF16)
                act[rows, cols] = value[turn - 1]
                slope[rows, cols] = grad.astype(BF16)
            if 0 <= turn - 2 < PARTS:
                c = (turn - 2) // CUT
                at = slice((turn - 2) % CUT * PART, ((turn - 2) % CUT + 1) * PART)
                total = total + nn(value.pop(turn - 2), w_ref[8 + c, at, :])
        unit, rate = norm_parts(total)
        unit2[rows, :] = unit
        rate2[rows, :] = rate
        z = (unit * vec_ref[10:11, :] + vec_ref[11:12, :]).astype(BF16)
        zb[rows, :] = z
        head_in[rows, :] = nn(z, stu_ref[0:D, :].astype(BF16)) + stu_ref[D + SW : D + SW + 1, :]

    @pl.when(step == tiles)
    def _():
        head_phase(
            info, stu_ref, cls_ref, goal_ref, sg_ref, cg_ref, head_in, head_low, micro, row_len
        )
        sg_ref[0:D, :] = tn(zb[...], head_low[...])
        @pl.loop(0, micro)
        def _(m):
            place = send_row[pl.ds(m, 1), :]
            spot = lax.broadcasted_iota(jnp.int32, (group * slots, row_len), 0)
            pick = jnp.where(spot == place, 1.0, 0.0).astype(BF16)
            here = pl.ds(pl.multiple_of(m * row_len, row_len), row_len)
            moved = nn(pick, zb[here, :]).astype(BF16)
            out_ref[:, m] = moved.reshape(group, slots, D)

    @pl.when(step >= tiles)
    def _():
        t = step - tiles
        rows = pl.ds(pl.multiple_of(t * tile, tile), tile)
        m = (t * tile) // row_len
        spot = lax.broadcasted_iota(jnp.int32, (tile, group * slots), 1)
        pick = jnp.where(spot == send_col[...], 1.0, 0.0).astype(BF16)
        dz = nn(pick, back_ref[:, m].reshape(group * slots, D))
        dz = dz + nt(head_low[rows, :], stu_ref[0:D, :].astype(BF16))
        unit = unit2[rows, :]
        vg_ref[10:11, :] += row_sum(dz * unit)
        vg_ref[11:12, :] += row_sum(dz)
        da2 = norm_back(dz * vec_ref[10:11, :], unit, rate2[rows, :])
        low = da2.astype(BF16)
        zb[rows, :] = low
        vg_ref[9:10, :] += row_sum(low.astype(F32))
        dh1 = da2
        raw, value = {}, {}
        for turn in range(PARTS + 2):
            if turn < PARTS:
                c, at = turn // CUT, slice(turn % CUT * PART, (turn % CUT + 1) * PART)
                raw[turn] = nt(low, w_ref[8 + c, at, :])
            if 0 <= turn - 1 < PARTS:
                cols = slice((turn - 1) * PART, turn * PART)
                c = (turn - 1) // CUT
                at = slice((turn - 1) % CUT * PART, ((turn - 1) % CUT + 1) * PART)
                du = (raw.pop(turn - 1) * slope[rows, cols].astype(F32)).astype(BF16)
                value[turn - 1] = du
                slope[rows, cols] = du
                vg_ref[5 + c : 6 + c, at] += row_sum(du.astype(F32))
            if 0 <= turn - 2 < PARTS:
                c = (turn - 2) // CUT
                at = slice((turn - 2) % CUT * PART, ((turn - 2) % CUT + 1) * PART)
                dh1 = dh1 + nt(value.pop(turn - 2), w_ref[4 + c, :, at])
        unit = unit1[rows, :]
        vg_ref[3:4, :] += row_sum(dh1 * unit)
        vg_ref[4:5, :] += row_sum(dh1)
        da1_ref[...] = norm_back(dh1 * vec_ref[3:4, :], unit, rate1[rows, :])

    @pl.when(step == 2 * tiles - 1)
    def _():
        @pl.loop(0, FF // D)
        def _(c):
            cols = pl.ds(pl.multiple_of(c * D, D), D)
            wg_ref[c] = tn(h1b[...], slope[:, cols]).astype(BF16)
            wg_ref[4 + c] = tn(act[:, cols], zb[...]).astype(BF16)


def head_phase(info, stu_ref, cls_ref, goal_ref, sg_ref, cg_ref, head_in, head_low, micro, row_len):
    scale = DH**-0.5
    query = stu_ref[D + SW + 2 : D + SW + 3, :]
    same = (
        lax.broadcasted_iota(jnp.int32, (SW, SW), 0) // DH
        == lax.broadcasted_iota(jnp.int32, (SW, SW), 1) // DH
    )
    same = jnp.where(same, 1.0, 0.0).astype(BF16)
    pooled, weights, members = [], [], []
    for m in range(micro):
        rows = slice(m * row_len, (m + 1) * row_len)
        s = head_in[rows, :]
        e = two_low(s * query, same) * scale
        sample = sample_column(ends_of(info, m), 0, row_len)
        share = jnp.zeros_like(e)
        for j in range(SAMP):
            member = sample == j
            peak = jnp.max(jnp.where(member, e, -1e30), axis=0, keepdims=True)
            up = jnp.where(member, jnp.exp(jnp.where(member, e - peak, 0.0)), 0.0)
            up = up / row_sum(up)
            share = share + up
            pooled.append(row_sum(up * s))
            members.append(member)
        weights.append(share)
    pooled = jnp.concatenate(pooled, axis=0)
    pool_weight = stu_ref[D : D + SW, :]
    mixed = jnp.tanh(exact(pooled, pool_weight) + stu_ref[D + SW + 1 : D + SW + 2, :])
    classes = cls_ref[:, 0:SW]
    bias = cls_ref[:, SW : SW + 1].T
    logits = exact(mixed, classes, (((1,), (1,)), ((), ()))) + bias
    logits = logits - jnp.max(logits, axis=-1, keepdims=True)
    chance = jnp.exp(logits)
    chance = chance / jnp.sum(chance, axis=-1, keepdims=True)
    goal = goal_ref[...]
    index = lax.broadcasted_iota(jnp.int32, (micro * SAMP, 1), 0)
    alive = jnp.zeros((micro * SAMP, 1), F32)
    for m in range(micro):
        for j, flag in enumerate(live_of(info, m)):
            alive = jnp.where(index == m * SAMP + j, flag.astype(F32), alive)
    target = jnp.exp(goal - jnp.max(goal, axis=-1, keepdims=True))
    target = target / jnp.sum(target, axis=-1, keepdims=True)
    d_logits = alive * (chance - target)
    cg_ref[:, 0:SW] = exact(d_logits, mixed, (((0,), (0,)), ((), ())))
    cg_ref[:, SW : SW + 1] = row_sum(d_logits).T
    d_pre = exact(d_logits, classes) * (1.0 - mixed * mixed)
    sg_ref[D : D + SW, :] = exact(pooled, d_pre, (((0,), (0,)), ((), ())))
    sg_ref[D + SW + 1 : D + SW + 2, :] = row_sum(d_pre)
    d_pooled = exact(d_pre, pool_weight, (((1,), (1,)), ((), ())))
    inner = two_low(pooled * d_pooled, same)
    d_bias = jnp.zeros((1, SW), F32)
    d_query = jnp.zeros((1, SW), F32)
    for m in range(micro):
        rows = slice(m * row_len, (m + 1) * row_len)
        s = head_in[rows, :]
        spread = jnp.zeros((row_len, SW), F32)
        center = jnp.zeros((row_len, SW), F32)
        for j in range(SAMP):
            member = members[m * SAMP + j]
            at = m * SAMP + j
            spread = jnp.where(member, d_pooled[at : at + 1, :], spread)
            center = jnp.where(member, inner[at : at + 1, :], center)
        share = weights[m]
        d_e = share * (two_low(s * spread, same) - center) * scale
        d_s = (share * spread + d_e * query).astype(BF16)
        head_low[rows, :] = d_s
        d_bias = d_bias + row_sum(d_s.astype(F32))
        d_query = d_query + row_sum(d_e * s)
    sg_ref[D + SW : D + SW + 1, :] = d_bias
    sg_ref[D + SW + 2 : D + SW + 3, :] = d_query


def feed(info, x, o, blocks, vec, student, classifier, goals, send_row, send_col, returned):
    micro, row_len, _ = x.shape
    tokens = micro * row_len
    tile = 512
    tiles = tokens // tile
    group, _, slots, _ = returned.shape
    whole = lambda *shape: pl.BlockSpec(shape, lambda i: (0,) * len(shape))
    once = lambda *shape: pl.BlockSpec(
        shape, lambda i: (0,) * len(shape), pipeline_mode=pl.Buffered(1)
    )
    ahead = lambda width: pl.BlockSpec((tile, width), lambda i: (jnp.minimum(i, tiles - 1), 0))
    behind = lambda width: pl.BlockSpec((tile, width), lambda i: (jnp.maximum(i - tiles, 0), 0))
    return pl.pallas_call(
        functools.partial(feed_kernel, tile=tile, micro=micro, row_len=row_len),
        grid=(2 * tiles,),
        in_specs=[
            pl.BlockSpec(memory_space=pltpu.SMEM),
            ahead(D),
            ahead(D),
            once(NMAT, D, D),
            once(NMAT, D),
            once(*student.shape),
            once(*classifier.shape),
            once(*goals.shape),
            once(*send_row.shape),
            behind(1),
            once(*returned.shape),
        ],
        out_specs=[
            behind(D),
            once(*returned.shape),
            once(8, D, D),
            once(NMAT, D),
            once(*student.shape),
            once(*classifier.shape),
        ],
        out_shape=[
            jax.ShapeDtypeStruct((tokens, D), F32),
            jax.ShapeDtypeStruct(returned.shape, BF16),
            jax.ShapeDtypeStruct((NMAT, D, D), BF16),
            jax.ShapeDtypeStruct((NMAT, D), F32),
            jax.ShapeDtypeStruct(student.shape, F32),
            jax.ShapeDtypeStruct(classifier.shape, F32),
        ],
        scratch_shapes=[
            pltpu.VMEM((tokens, D), F32),
            pltpu.VMEM((tokens, 1), F32),
            pltpu.VMEM((tokens, D), BF16),
            pltpu.VMEM((tokens, FF), BF16),
            pltpu.VMEM((tokens, FF), BF16),
            pltpu.VMEM((tokens, D), F32),
            pltpu.VMEM((tokens, 1), F32),
            pltpu.VMEM((tokens, D), BF16),
            pltpu.VMEM((tokens, SW), F32),
            pltpu.VMEM((tokens, SW), BF16),
        ],
        compiler_params=pltpu.CompilerParams(vmem_limit_bytes=VMEM),
        cost_estimate=pl.CostEstimate(
            flops=tokens * D * FF * 12, bytes_accessed=tokens * D * 16, transcendentals=tokens * FF
        ),
    )(
        info,
        x.reshape(tokens, D),
        o.reshape(tokens, D),
        blocks,
        vec,
        student,
        classifier,
        goals,
        send_row,
        send_col,
        returned,
    )


def attend_back_kernel(
    info,
    x_ref,
    da1_ref,
    q_ref,
    k_ref,
    v_ref,
    o_ref,
    l_ref,
    w_ref,
    _,
    dx_ref,
    wg_ref,
    vg_ref,
    qx,
    kx,
    vx,
    dox,
    dq,
    dk,
    dv,
    dkt,
    dvt,
    qt,
    dot,
    dq_sum,
    wsum,
    *,
    micro,
):
    row = pl.program_id(0)
    row_len = x_ref.shape[1]
    ends, live = ends_of(info, row), live_of(info, row)
    first = lane_index(QT) < DH
    low_first = jnp.where(first, 1.0, 0.0).astype(BF16)
    ones = jnp.ones((QT, LANES), F32)

    @pl.when(row == 0)
    def _():
        vg_ref[...] = jnp.zeros_like(vg_ref)
        wsum[...] = jnp.zeros_like(wsum)

    head = lax.broadcasted_iota(jnp.int32, (D, LANES), 0) // DH
    spot = head // 2 + DH * (1 - head % 2)
    gather = lax.broadcasted_iota(jnp.int32, (D, LANES), 1) == spot
    gather = jnp.where(gather, 1.0, 0.0).astype(BF16)

    dkt[...] = jnp.zeros_like(dkt)
    dvt[...] = jnp.zeros_like(dvt)

    @pl.loop(0, row_len // QT)
    def _(t):
        rows = pl.ds(pl.multiple_of(t * QT, QT), QT)
        sample = sample_column(ends, t * QT, QT)
        lane = lane_index(QT) % DH
        high, mid, rest = split_low(jnp.where(lane < PAIRS, -l_ref[0, rows, :], 0.0))
        q_extra = (
            query_spare(sample, QT)
            + high
            + pltpu.roll(mid, PAIRS, 1)
            + pltpu.roll(rest, 2 * PAIRS, 1)
        )
        branch = da1_ref[0, rows, :].astype(BF16)
        vg_ref[2:3, :] += row_sum(branch.astype(F32))
        do = nt(branch, w_ref[3]).astype(BF16).astype(F32)
        delta = two_low(do * o_ref[0, rows, :].astype(F32), gather)
        high = delta.astype(BF16).astype(F32)
        do_extra = pltpu.roll(high - delta, PAIRS, 1) - high
        for p in range(PAIRS):
            pair = head_lanes(p)
            k_extra = key_spare(sample, QT, p)
            store_heads(dox, rows, p, do[:, pair], do_extra, low_first)
            store_heads(qx, rows, p, q_ref[0, rows, pair], q_extra, low_first)
            store_heads(kx, rows, p, k_ref[0, rows, pair], k_extra, low_first)
            store_heads(vx, rows, p, v_ref[0, rows, pair], k_extra, low_first)

    @pl.loop(0, row_len // QT)
    def _(t):
        rows = pl.ds(pl.multiple_of(t * QT, QT), QT)
        begin, number = reach(ends, live, t * QT, QT, row_len)
        number = (number + STEP - 1) // STEP
        begin = jnp.minimum(begin, row_len // KG - number * STEP)
        dq_sum[...] = jnp.zeros_like(dq_sum)
        for h in range(H):
            qt[head_lanes(h), :] = qx[rows, head_lanes(h)].T
            dot[head_lanes(h), :] = dox[rows, head_lanes(h)].T

        @pl.loop(0, number)
        def _(j):
            span = pl.ds(pl.multiple_of((begin + j * STEP) * KG, KG), STEP * KG)
            raw, done, got = {}, {}, {}
            for step in range(H + 2):
                if step < H:
                    cols = head_lanes(step)
                    raw[step] = (
                        nt(qx[rows, cols], kx[span, cols]),
                        nt(dox[rows, cols], vx[span, cols]),
                    )
                h = step - 1
                if 0 <= h < H:
                    s, dp = raw.pop(h)
                    prob = jnp.exp(s)
                    done[h] = (prob.astype(BF16), (prob * dp).astype(BF16))
                h = step - 2
                if 0 <= h < H:
                    cols = head_lanes(h)
                    prob, ds = done.pop(h)
                    mine = slice(h * DH, (h + 1) * DH)
                    side = slice(h % 2 * DH, (h % 2 + 1) * DH)
                    dvt[mine, span] += nn(dot[cols, :], prob)[side]
                    dkt[mine, span] += nn(qt[cols, :], ds)[side]
                    got[h] = nn(ds, kx[span, cols])
                    if h % 2 == 1:
                        left, right = got.pop(h - 1), got.pop(h)
                        dq_sum[:, head_lanes(h // 2)] += jnp.where(first, left, right)

        dq[rows, :] = (dq_sum[...] * DH**-0.5).astype(BF16)

    @pl.loop(0, row_len // QT)
    def _(t):
        rows = pl.ds(pl.multiple_of(t * QT, QT), QT)
        dq_low = dq[rows, :]
        dk_low = dkt[:, rows].astype(BF16).T
        dv_low = dvt[:, rows].astype(BF16).T
        dk[rows, :] = dk_low
        dv[rows, :] = dv_low
        vg_ref[0:1, :] += row_sum(dq_low.astype(F32))
        vg_ref[1:2, :] += row_sum(dv_low.astype(F32))
        dx_ref[0, rows, :] = (
            da1_ref[0, rows, :]
            + nt(dq_low, w_ref[0])
            + nt(dk_low, w_ref[1])
            + nt(dv_low, w_ref[2])
        ).astype(BF16)

    x = x_ref[0]
    wsum[0] += tn(x, dq[...])
    wsum[1] += tn(x, dk[...])
    wsum[2] += tn(x, dv[...])
    wsum[3] += tn(o_ref[0], da1_ref[0].astype(BF16))

    @pl.when(row == micro - 1)
    def _():
        wg_ref[...] = wsum[...].astype(BF16)


def attend_back(info, tokens, da1, q, k, v, o, logs, blocks, grads):
    micro, row_len, _ = tokens.shape
    row_spec = lambda width: pl.BlockSpec((1, row_len, width), lambda r: (r, 0, 0))
    return pl.pallas_call(
        functools.partial(attend_back_kernel, micro=micro),
        grid=(micro,),
        in_specs=[
            pl.BlockSpec(memory_space=pltpu.SMEM),
            *[row_spec(D)] * 6,
            row_spec(LANES),
            pl.BlockSpec((4, D, D), lambda r: (0, 0, 0)),
            pl.BlockSpec(memory_space=pl.ANY),
        ],
        out_specs=[
            row_spec(D),
            pl.BlockSpec((4, D, D), lambda r: (2, 0, 0)),
            pl.BlockSpec((8, D), lambda r: (0, 0)),
        ],
        out_shape=[
            jax.ShapeDtypeStruct((micro, row_len, D), BF16),
            jax.ShapeDtypeStruct((NMAT, D, D), BF16),
            jax.ShapeDtypeStruct((8, D), F32),
        ],
        scratch_shapes=[
            *[pltpu.VMEM((row_len, 2 * D), BF16)] * 4,
            *[pltpu.VMEM((row_len, D), BF16)] * 3,
            *[pltpu.VMEM((D, row_len), F32)] * 2,
            *[pltpu.VMEM((2 * D, QT), BF16)] * 2,
            pltpu.VMEM((QT, D), F32),
            pltpu.VMEM((4, D, D), F32),
        ],
        input_output_aliases={9: 1},
        compiler_params=pltpu.CompilerParams(vmem_limit_bytes=VMEM),
        cost_estimate=pl.CostEstimate(
            flops=micro * row_len * D * D * 16 + micro * H * row_len * row_len * DH * 10,
            bytes_accessed=micro * row_len * D * 16,
            transcendentals=micro * H * row_len * row_len,
        ),
    )(info, tokens, da1, q, k, v, o, logs, blocks, grads)


CROSS = 3
CHUNKS = 12
STU_ROWS, CLS_ROWS, VEC_ROWS = 656, 16, 16
SMALL_ROWS = 1024


def reduce_kernel(
    group,
    owners,
    grad_ref,
    ff_vec,
    at_vec,
    stu_ref,
    cls_ref,
    own_ref,
    vec_out,
    stu_out,
    cls_out,
    got_a,
    sum_a,
    got_b,
    part,
    got_c,
    final,
    small,
    small_got,
    small_sum,
    small_end,
    got_y,
    half_y,
    send_sem,
    recv_sem,
    small_send,
    small_recv,
):
    b, s = lax.axis_index("batch"), lax.axis_index("shard")
    per = NMAT // owners
    rows = per * D // CHUNKS
    batch_bits, shard_bits = bits_of(group), bits_of(owners)
    half = SMALL_ROWS // 2

    def copy(src, dst, sems, at, where):
        return pltpu.make_async_remote_copy(
            src_ref=src,
            dst_ref=dst,
            send_sem=sems[0].at[at],
            recv_sem=sems[1].at[at],
            device_id=where,
            device_id_type=pl.DeviceIdType.MESH,
        )

    peers = [(b, s ^ bit) for bit in shard_bits] + [(b ^ bit, s) for bit in batch_bits]
    barrier = pltpu.get_barrier_semaphore()
    for peer in peers:
        pl.semaphore_signal(
            barrier, inc=1, device_id=peer, device_id_type=pl.DeviceIdType.MESH
        )
    pl.semaphore_wait(barrier, len(peers))

    sems = (send_sem, recv_sem)
    small_sems = (small_send, small_recv)
    waits = []

    def begin(op):
        op.start()
        waits.append(op)
        return op

    def piece(owner, c):
        at = lax.rem(owner * per + c * per // CHUNKS + 8, NMAT)
        if rows == D:
            return grad_ref.at[at]
        step = D // rows
        return grad_ref.at[at, pl.ds((c % step) * rows, rows)]

    far = shard_bits[1]
    first = {}
    for c in range(CHUNKS):
        first[c] = [
            begin(copy(piece(s ^ 1 ^ far, c), got_a.at[c, 0], sems, (c, 0), peers[0])),
            begin(copy(piece(s ^ 1, c), got_a.at[c, 1], sems, (c, 1), peers[0])),
        ]

    small[...] = jnp.zeros_like(small)
    stu_count = stu_ref.shape[0]
    small[0:stu_count, :] = stu_ref[...].astype(BF16)
    small[STU_ROWS : STU_ROWS + CLS, :] = cls_ref[:, 0:SW].astype(BF16)
    small[STU_ROWS + CLS_ROWS : STU_ROWS + CLS_ROWS + CLS, 0:1] = cls_ref[:, SW:].astype(BF16)
    for i in range(4):
        at = STU_ROWS + 2 * CLS_ROWS + i * VEC_ROWS
        lanes = slice(i * LANES, (i + 1) * LANES)
        small[at : at + 3, :] = at_vec[0:3, lanes].astype(BF16)
        small[at + 3 : at + NMAT, :] = ff_vec[3:NMAT, lanes].astype(BF16)
    core = lax.rem(s, 2)
    mine = pl.ds(pl.multiple_of(core * half, 16), half)
    other = pl.ds(pl.multiple_of((1 - core) * half, 16), half)
    small_op = begin(copy(small.at[other], small_got.at[pl.ds(0, half)], small_sems, 0, peers[0]))

    def add(x, y):
        return (x.astype(F32) + y.astype(F32)).astype(BF16)

    def add_into(out, x, y, x_at=0, y_at=0, out_at=0):
        count = out[1]
        slab = 16 if count % 32 else 32

        @pl.loop(0, count // slab)
        def _(i):
            def rows_at(first):
                return pl.ds(pl.multiple_of(first + i * slab, 16), slab)

            out[0][rows_at(out_at), :] = add(x[rows_at(x_at), :], y[rows_at(y_at), :])

    second = {}
    copies = send_sem.shape[1]

    def crossed(c):
        return c % CROSS == CROSS - 1

    def start_second(c):
        for i, op in enumerate(first[c]):
            op.wait_recv()
            owner = s ^ far if i == 0 else s
            add_into((sum_a.at[c, i], rows), piece(owner, c), got_a.at[c, i])
        if crossed(c):
            count = rows // 2
            away = pl.ds(pl.multiple_of((1 - lax.rem(b, 2)) * count, 16), count)
            second[c] = [
                begin(copy(sum_a.at[c, i, away], got_y.at[c, i], sems, (c, at), (b ^ 1, s)))
                for i, at in ((0, 3), (1, copies - 1))
            ]
        else:
            second[c] = begin(copy(sum_a.at[c, 0], got_b.at[c], sems, (c, 2), peers[1]))

    start_second(0)
    start_second(1)

    spans = []
    size = rows
    for bit in batch_bits:
        halving = size >= 32
        spans.append((bit, size, halving))
        if halving:
            size //= 2
    offset_of = []
    offset = jnp.int32(0)
    slot_of = []
    slot = 0
    for bit, now, halving in spans:
        place = lax.rem(b // bit, 2)
        offset_of.append((offset, place))
        slot_of.append(slot)
        if halving:
            offset = offset + place * (now // 2)
            slot += now // 2
        else:
            slot += now
    last = offset

    def ranged(ref, c, start, count):
        return ref.at[c, pl.ds(pl.multiple_of(start, 16), count)]

    moving = {}

    def start_batch(c, k):
        bit, now, halving = spans[k]
        start, place = offset_of[k]
        if halving:
            count = now // 2
            src = ranged(part.at[k], c, start + (1 - place) * count, count)
        else:
            count = now
            src = ranged(part.at[k], c, start, count)
        dst = got_c.at[c, pl.ds(slot_of[k], count)]
        moving[c, k] = begin(copy(src, dst, sems, (c, 3 + k), (b ^ bit, s)))

    def end_batch(c, k):
        bit, now, halving = spans[k]
        start, place = offset_of[k]
        moving[c, k].wait_recv()
        count = now // 2 if halving else now
        if halving:
            start = start + place * count
        target = part.at[k + 1, c] if k + 1 < len(spans) else final.at[c]
        add_into(
            (target, count), part.at[k, c], got_c.at[c], x_at=start, y_at=slot_of[k], out_at=start
        )

    gathers = [k for k in reversed(range(len(spans))) if spans[k][2]]
    gathering = {}

    def start_gather(c, g):
        k = gathers[g]
        bit, now, _ = spans[k]
        start, place = offset_of[k]
        count = now // 2
        at = ranged(final, c, start + place * count, count)
        gathering[c, g] = begin(
            copy(at, at, sems, (c, 3 + len(spans) + g), (b ^ bit, s))
        )

    def stage(c, k):
        if crossed(c) and k < 2:
            count = rows // 2
            here = lax.rem(b, 2) * count
            if k == 0:
                for i, op in enumerate(second[c]):
                    op.wait_recv()
                    add_into((half_y.at[c, i], count), sum_a.at[c, i], got_y.at[c, i], x_at=here)
                dst = got_b.at[c, pl.ds(0, count)]
                second[c] = begin(copy(half_y.at[c, 0], dst, sems, (c, 2), peers[1]))
                if c + 2 < CHUNKS:
                    start_second(c + 2)
            else:
                second[c].wait_recv()
                add_into((part.at[1, c], count), half_y.at[c, 1], got_b.at[c], out_at=here)
                start_batch(c, 1)
        elif k == 0:
            second[c].wait_recv()
            if c + 2 < CHUNKS:
                start_second(c + 2)
            add_into((part.at[0, c], rows), sum_a.at[c, 1], got_b.at[c])
            start_batch(c, 0)
        elif k <= len(spans):
            end_batch(c, k - 1)
            if k < len(spans):
                start_batch(c, k)
            else:
                start_gather(c, 0)
        else:
            g = k - len(spans) - 1
            gathering[c, g].wait_recv()
            if g + 1 < len(gathers):
                start_gather(c, g + 1)
            else:
                per_block = CHUNKS // per
                block, within = c // per_block, c % per_block
                own_ref[block, within * rows : (within + 1) * rows, :] = final[c]

    stages = 1 + len(spans) + len(gathers)
    rest = [(s, bit) for bit in shard_bits[1:]] + [(b, bit) for bit in batch_bits]
    levels = []
    start, size, at = core * half, half, 0
    for index, (axis, bit) in enumerate(rest):
        place = lax.rem(axis // bit, 2)
        count = size // 2 if size >= 32 else size
        peer = (b, s ^ bit) if index < len(shard_bits) - 1 else (b ^ bit, s)
        levels.append((start, size, count, place, peer, at))
        at += count
        if count < size:
            start, size = start + place * count, count
    last_start, last_size = start, size
    backs = [k for k in reversed(range(len(levels))) if levels[k][2] < levels[k][1]]

    def small_rows(ref, first, count):
        return ref.at[pl.ds(pl.multiple_of(first, 16), count)]

    def small_begin(k):
        begin_at, now, count, place, peer, slot = levels[k]
        first = begin_at + (1 - place) * count if count < now else begin_at
        return begin(
            copy(
                small_rows(small_sum.at[k], first, count),
                small_got.at[pl.ds(half + slot, count)],
                small_sems,
                k + 1,
                peer,
            )
        )

    def small_back(g):
        if g == len(backs):
            at = small_rows(small_end, core * half, half)
            return begin(copy(at, at, small_sems, len(levels) + 1 + g, peers[0]))
        begin_at, now, count, place, peer, _ = levels[backs[g]]
        at = small_rows(small_end, begin_at + place * count, count)
        return begin(copy(at, at, small_sems, len(levels) + 1 + g, peer))

    def small_stage(k):
        nonlocal small_op
        small_op.wait_recv()
        if k == 0:
            add_into((small_sum.at[0], half), small, small_got, x_at=core * half, out_at=core * half)
            small_op = small_begin(0)
        elif k <= len(levels):
            begin_at, now, count, place, _, slot = levels[k - 1]
            first = begin_at + place * count if count < now else begin_at
            target = small_sum.at[k] if k < len(levels) else small_end
            add_into(
                (target, count),
                small_sum.at[k - 1],
                small_got,
                x_at=first,
                y_at=half + slot,
                out_at=first,
            )
            small_op = small_begin(k) if k < len(levels) else small_back(0)
        elif k - len(levels) <= len(backs):
            small_op = small_back(k - len(levels))

    small_last = len(levels) + len(backs) + 1
    small_k = 0
    for tick in range(CHUNKS + 2 * (stages - 1)):
        for k in reversed(range(stages)):
            c = tick - 2 * k
            if 0 <= c < CHUNKS:
                stage(c, k)
        if small_k <= small_last:
            small_stage(small_k)
            small_k += 1
    while small_k <= small_last:
        small_stage(small_k)
        small_k += 1

    for i in range(4):
        at = STU_ROWS + 2 * CLS_ROWS + i * VEC_ROWS
        lanes = slice(i * LANES, (i + 1) * LANES)
        vec_out[:, lanes] = small_end[at : at + VEC_ROWS, :].astype(F32)
    stu_out[...] = small_end[0:STU_ROWS, :].astype(F32)
    cls_out[:, 0:LANES] = small_end[STU_ROWS : STU_ROWS + CLS_ROWS, :].astype(F32)
    at = STU_ROWS + CLS_ROWS
    cls_out[:, LANES:] = small_end[at : at + CLS_ROWS, :].astype(F32)
    for op in waits:
        op.wait_send()


def reduce_grads(grads, ff_vec, at_vec, stu, cls):
    group, owners = lax.axis_size("batch"), lax.axis_size("shard")
    per = NMAT // owners
    rows = per * D // CHUNKS
    batch_count = len(bits_of(group))
    copies = 4 + 2 * batch_count
    small_count = len(bits_of(owners)) + batch_count + 1
    vmem = pl.BlockSpec(memory_space=pltpu.VMEM)
    return pl.pallas_call(
        functools.partial(reduce_kernel, group, owners),
        in_specs=[vmem] * 5,
        out_specs=[vmem] * 4,
        out_shape=[
            jax.ShapeDtypeStruct((per, D, D), BF16),
            jax.ShapeDtypeStruct((VEC_ROWS, D), F32),
            jax.ShapeDtypeStruct((STU_ROWS, SW), F32),
            jax.ShapeDtypeStruct((CLS_ROWS, 2 * LANES), F32),
        ],
        scratch_shapes=[
            pltpu.VMEM((CHUNKS, 2, rows, D), BF16),
            pltpu.VMEM((CHUNKS, 2, rows, D), BF16),
            pltpu.VMEM((CHUNKS, rows, D), BF16),
            pltpu.VMEM((batch_count, CHUNKS, rows, D), BF16),
            pltpu.VMEM((CHUNKS, rows + 16 * batch_count, D), BF16),
            pltpu.VMEM((CHUNKS, rows, D), BF16),
            pltpu.VMEM((SMALL_ROWS, LANES), BF16),
            pltpu.VMEM((SMALL_ROWS + 32 * small_count, LANES), BF16),
            pltpu.VMEM((small_count, SMALL_ROWS, LANES), BF16),
            pltpu.VMEM((SMALL_ROWS, LANES), BF16),
            pltpu.VMEM((CHUNKS, 2, rows // 2, D), BF16),
            pltpu.VMEM((CHUNKS, 2, rows // 2, D), BF16),
            pltpu.SemaphoreType.DMA((CHUNKS, copies)),
            pltpu.SemaphoreType.DMA((CHUNKS, copies)),
            pltpu.SemaphoreType.DMA((2 * small_count + 1,)),
            pltpu.SemaphoreType.DMA((2 * small_count + 1,)),
        ],
        compiler_params=pltpu.CompilerParams(
            collective_id=1, has_side_effects=True, vmem_limit_bytes=VMEM
        ),
        cost_estimate=pl.CostEstimate(
            flops=NMAT * D * D * 4, bytes_accessed=NMAT * D * D * 8, transcendentals=0
        ),
    )(grads, ff_vec, at_vec, stu, cls)


def update_kernel(
    own_ref,
    blocks_ref,
    left_ref,
    right_ref,
    lroot_ref,
    rroot_ref,
    shard_ref,
    vsum_ref,
    vec_ref,
    vmom_ref,
    ssum_ref,
    stu_ref,
    smom_ref,
    csum_ref,
    cls_ref,
    cmom_ref,
    back_ref,
    rows_ref,
    grad_out,
    new_out,
    left_out,
    right_out,
    vg_out,
    vm_out,
    v_out,
    sg_out,
    sm_out,
    s_out,
    cg_out,
    cm_out,
    c_out,
    layer_out,
    *,
    owners,
):
    step = pl.program_id(0)
    row_len = layer_out.shape[1]

    @pl.when(step < rows_ref.shape[1])
    def _():
        arrived = rows_ref[:, step].reshape(row_len, D)
        chunk = min(256, row_len)

        @pl.loop(0, row_len // chunk)
        def _(k):
            at = pl.multiple_of(k * chunk, chunk)
            spot = at + lax.broadcasted_iota(jnp.int32, (chunk, row_len), 0)
            pick = jnp.where(spot == back_ref[pl.ds(step, 1), :], 1.0, 0.0).astype(BF16)
            layer_out[0, pl.ds(at, chunk), :] = nn(pick, arrived).astype(BF16)

    g = own_ref[0]
    grad_out[0] = g.astype(F32)
    left_out[0] = decay_rate * left_ref[0] + (1.0 - decay_rate) * nt(g, g)
    right_out[0] = decay_rate * right_ref[0] + (1.0 - decay_rate) * tn(g, g)
    steered = nn(lroot_ref[0].astype(BF16), g).astype(BF16)
    steered = nn(steered, rroot_ref[0].astype(BF16))
    size = jnp.mean(steered * steered, keepdims=True)
    new_out[0] = blocks_ref[0].astype(F32) - steered * (block_rate * lax.rsqrt(size + 1e-06))

    @pl.when(pl.program_id(0) == 0)
    def _():
        per = NMAT // owners
        mine = vsum_ref[0:per, :]
        for i in range(1, owners):
            mine = jnp.where(shard_ref[0] == i, vsum_ref[i * per : (i + 1) * per, :], mine)

        def rule(grads, old, moment, rate, outs):
            renewed = decay_rate * moment + (1.0 - decay_rate) * grads * grads
            outs[0][...] = grads
            outs[1][...] = renewed
            outs[2][...] = old - rate * grads / (jnp.sqrt(renewed) + 1e-08)

        rule(mine, vec_ref[...], vmom_ref[...], vector_rate, (vg_out, vm_out, v_out))
        rule(
            ssum_ref[0 : stu_ref.shape[0], :],
            stu_ref[...],
            smom_ref[...],
            head_rate,
            (sg_out, sm_out, s_out),
        )
        rule(
            csum_ref[0:CLS, 0 : SW + 1],
            cls_ref[...],
            cmom_ref[...],
            head_rate,
            (cg_out, cm_out, c_out),
        )


def update(own, blocks, left, right, lroot, rroot, shard, vsum, vec, vmom, ssum, stu, smom, csum, cls, cmom, back, arrived):
    per = own.shape[0]
    micro, row_len = back.shape
    mat = pl.BlockSpec((1, D, D), lambda i: (i, 0, 0))
    whole = lambda a: pl.BlockSpec(a.shape, lambda i: (0,) * a.ndim)
    like = lambda a: jax.ShapeDtypeStruct(a.shape, F32)
    return pl.pallas_call(
        functools.partial(update_kernel, owners=NMAT // per),
        grid=(per,),
        in_specs=[mat] * 6
        + [pl.BlockSpec(memory_space=pltpu.SMEM)]
        + [whole(a) for a in (vsum, vec, vmom, ssum, stu, smom, csum, cls, cmom, back, arrived)],
        out_specs=[mat] * 4
        + [whole(a) for a in (vec,) * 3 + (stu,) * 3 + (cls,) * 3]
        + [pl.BlockSpec((1, row_len, D), lambda i: (jnp.minimum(i, micro - 1), 0, 0))],
        out_shape=[like(left)] * 4
        + [like(a) for a in (vec,) * 3 + (stu,) * 3 + (cls,) * 3]
        + [jax.ShapeDtypeStruct((micro, row_len, D), BF16)],
        compiler_params=pltpu.CompilerParams(vmem_limit_bytes=VMEM),
    )(
        own,
        blocks,
        left,
        right,
        lroot,
        rroot,
        shard,
        vsum,
        vec,
        vmom,
        ssum,
        stu,
        smom,
        csum,
        cls,
        cmom,
        back,
        arrived,
    )


def local(
    tokens,
    cotangent,
    lengths,
    exit_layers,
    teacher,
    blocks,
    left_stats,
    right_stats,
    left_root,
    right_root,
    vectors,
    vec_moment,
    student,
    stu_moment,
    classifier,
    cls_moment,
):
    group = lax.axis_size("batch")
    me = lax.axis_index("batch")
    micro, _, row_len, _ = tokens.shape
    slots = row_len // group
    tokens, cotangent = tokens[:, 0], cotangent[:, 0]
    ends = jnp.cumsum(lengths[:, 0], axis=-1, dtype=jnp.int32)
    live = (exit_layers[:, 0] >= LAYER).astype(jnp.int32)
    info = jnp.concatenate([lengths[:, 0], exit_layers[:, 0]], axis=1)
    alive_len = lengths[:, 0] * live
    counts = jnp.sum(alive_len, axis=1, dtype=jnp.int32)
    everyone = lax.all_gather(counts[None, :], "batch", axis=0, tiled=True)
    starts = jnp.cumsum(everyone, axis=0, dtype=jnp.int32) - everyone

    places = jnp.arange(row_len, dtype=jnp.int32)
    before = jnp.cumsum(alive_len, axis=1, dtype=jnp.int32) - alive_len
    sample = jnp.sum((places[None, :, None] >= ends[:, None, : SAMP - 1]).astype(jnp.int32), axis=-1)
    chosen = sample[..., None] == jnp.arange(SAMP, dtype=jnp.int32)
    shift = jnp.sum(jnp.where(chosen, (before - ends + lengths[:, 0])[:, None, :], 0), axis=-1)
    alive_tok = jnp.sum(jnp.where(chosen, live[:, None, :], 0), axis=-1)
    rank = places[None, :] + shift
    send = (starts[me][:, None] + rank) % group * slots + rank // group
    send = jnp.where(alive_tok > 0, send, row_len)
    start_of = jnp.repeat(starts.T, slots, axis=1)
    count_of = jnp.repeat(everyone.T, slots, axis=1)
    turn = (me - start_of) % group + group * (places % slots)[None, :]
    back = jnp.where(turn < count_of, (start_of + turn) // group, row_len)

    grad_outgoing = pick_rows(back[:, :, None], cotangent, group)
    returned = lax.all_to_all(grad_outgoing, "batch", split_axis=0, concat_axis=0, tiled=True)

    matrices = lax.all_gather(blocks, "shard", axis=0, tiled=True)
    vec = lax.all_gather(vectors.astype(BF16), "shard", axis=0, tiled=True).astype(F32)

    q, k, v, o, logs = attend(info, tokens, matrices, vec)
    goals = teacher.reshape(micro * SAMP, CLS)
    classifier, cls_moment = classifier.T, cls_moment.T
    da1, outgoing, ff_grads, ff_vecs, stu_grads, cls_grads = feed(
        info, tokens, o, matrices, vec, student, classifier, goals, send, send.reshape(-1, 1), returned
    )
    arrived = lax.all_to_all(outgoing, "batch", split_axis=0, concat_axis=0, tiled=True)
    input_grads, grads, at_vecs = attend_back(
        info, tokens, da1.reshape(micro, row_len, D), q, k, v, o, logs, matrices, ff_grads
    )
    own, vec_sum, stu_sum, cls_sum = reduce_grads(grads, ff_vecs, at_vecs, stu_grads, cls_grads)
    shard = lax.axis_index("shard").astype(jnp.int32).reshape(1)
    *updated, layer_out = update(
        own,
        blocks,
        left_stats,
        right_stats,
        left_root,
        right_root,
        shard,
        vec_sum,
        vectors,
        vec_moment,
        stu_sum,
        student,
        stu_moment,
        cls_sum,
        classifier,
        cls_moment,
        back,
        arrived,
    )
    classes = [a.T for a in updated[-3:]]
    return (layer_out[:, None], input_grads[:, None], *updated[:-3], *classes)


def solution(mesh):
    rows = P(None, ("batch", "shard"), None, None)
    tags = P(None, ("batch", "shard"), None)
    mats = P("shard", None, None)
    vecs = P("shard", None)
    return jax.shard_map(
        local,
        mesh=mesh,
        in_specs=(rows, rows, tags, tags, rows, mats, mats, mats, mats, mats, vecs, vecs)
        + (P(),) * 4,
        out_specs=(rows, rows, mats, mats, mats, mats, vecs, vecs, vecs) + (P(),) * 6,
        check_vma=False,
    )
```

```python
import functools

import jax
import jax.numpy as jnp
from jax import lax
from jax.experimental import pallas as pl
from jax.experimental.pallas import tpu as pltpu
from jax.sharding import PartitionSpec as P

D = 512
H = 8
DH = 64
FF = 2048
SW = 128
NMAT = 12
SAMP = 4
LAYER = 4
CLS = 14

decay_rate = 0.5
block_rate = 0.04
vector_rate = 0.05
head_rate = 0.05

QT = 256
STEP = 2
KG = 128
PAIRS = H // 2
LANES = 128
PART = 512
PARTS, CUT = FF // PART, D // PART
BIG = float(2**30)
EPS = 1e-6
VMEM = 60 * 1024 * 1024

F32 = jnp.float32
BF16 = jnp.bfloat16


def nn(a, b):
    return jnp.dot(a, b, preferred_element_type=F32)


def nt(a, b):
    return lax.dot_general(a, b, (((1,), (1,)), ((), ())), preferred_element_type=F32)


def tn(a, b):
    return lax.dot_general(a, b, (((0,), (0,)), ((), ())), preferred_element_type=F32)


def exact(a, b, dims=(((1,), (0,)), ((), ()))):
    return lax.dot_general(
        a, b, dims, preferred_element_type=F32, precision=lax.Precision.HIGHEST
    )


def row_sum(v):
    return jnp.sum(v, axis=0, keepdims=True)


def two_low(v, b):
    high = v.astype(BF16)
    return nn(high, b) + nn((v - high.astype(F32)).astype(BF16), b)


def split_low(v):
    high = v.astype(BF16).astype(F32)
    rest = v - high
    mid = rest.astype(BF16).astype(F32)
    return high, mid, rest - mid


def ends_of(info, row):
    ends, total = [], jnp.int32(0)
    for j in range(SAMP):
        total = total + info[row, j]
        ends.append(total)
    return ends


def live_of(info, row):
    return [(info[row, SAMP + j] >= LAYER).astype(jnp.int32) for j in range(SAMP)]


def sample_column(ends, first, count):
    place = first + lax.broadcasted_iota(jnp.int32, (count, 1), 0)
    total = jnp.zeros((count, 1), jnp.int32)
    for j in range(SAMP - 1):
        total = total + (place >= ends[j]).astype(jnp.int32)
    return total


def reach(ends, live, first, count, row_len):
    low, high = jnp.int32(row_len), jnp.int32(0)
    start = jnp.int32(0)
    for j in range(SAMP):
        end = ends[j]
        meets = (start < first + count) & (end > first) & (end > start) & (live[j] > 0)
        low = jnp.where(meets, jnp.minimum(low, start), low)
        high = jnp.where(meets, jnp.maximum(high, end), high)
        start = end
    begin = low // KG
    number = jnp.maximum((high + KG - 1) // KG - begin, 0)
    return begin, number


def lane_index(rows):
    return lax.broadcasted_iota(jnp.int32, (rows, LANES), 1)


TAG = 16


def key_spare(sample, rows, pair):
    lane = lane_index(rows) % DH
    own = (lane < 3 * PAIRS) & (lane % PAIRS == pair)
    return jnp.where(own | (lane == sample + TAG), 1.0, 0.0)


def query_spare(sample, rows):
    lane = lane_index(rows) % DH
    tag = (lane >= TAG) & (lane < TAG + SAMP) & (lane != sample + TAG)
    return jnp.where(tag, -BIG, 0.0)


def store_heads(ref, rows, p, pair, spare, first):
    pair, spare, last = pair.astype(BF16), spare.astype(BF16), 1 - first
    ref[rows, 2 * p * LANES : (2 * p + 1) * LANES] = pair * first + spare * last
    ref[rows, (2 * p + 1) * LANES : (2 * p + 2) * LANES] = pair * last + spare * first


def head_lanes(h):
    return slice(h * LANES, (h + 1) * LANES)


def widths(row_len):
    most = row_len // KG
    return list(range(most // 2, most + 1))


def chosen_span(ends, live, t, row_len):
    begin, number = reach(ends, live, t * QT, QT, row_len)
    least, most = widths(row_len)[0], row_len // KG
    number = jnp.where(number > 0, jnp.maximum(number, least), 0)
    return jnp.minimum(begin, most - number), number


def bits_of(size):
    return [1 << i for i in range(size.bit_length() - 1)]


def pick_kernel(place_ref, rows_ref, out_ref):
    group, _, slots, _ = out_ref.shape
    places = group * slots
    spot = lax.broadcasted_iota(jnp.int32, (places, rows_ref.shape[1]), 1)
    pick = jnp.where(spot == place_ref[0], 1.0, 0.0).astype(BF16)
    out_ref[:, 0] = nn(pick, rows_ref[0]).astype(BF16).reshape(group, slots, D)


def pick_rows(place_col, rows, group):
    micro, row_len, _ = rows.shape
    slots = row_len // group
    return pl.pallas_call(
        pick_kernel,
        grid=(micro,),
        in_specs=[
            pl.BlockSpec((1, row_len, 1), lambda m: (m, 0, 0)),
            pl.BlockSpec((1, row_len, D), lambda m: (m, 0, 0)),
        ],
        out_specs=pl.BlockSpec((group, 1, slots, D), lambda m: (0, m, 0, 0)),
        out_shape=jax.ShapeDtypeStruct((group, micro, slots, D), BF16),
        compiler_params=pltpu.CompilerParams(vmem_limit_bytes=VMEM),
    )(place_col, rows)


def attend_kernel(info, x_ref, w_ref, vec_ref, q_ref, k_ref, v_ref, o_ref, l_ref, qx, kx, vx):
    row = pl.program_id(0)
    row_len = x_ref.shape[1]
    ends, live = ends_of(info, row), live_of(info, row)
    first = lane_index(QT) < DH
    low_first = jnp.where(first, 1.0, 0.0).astype(BF16)
    ones = jnp.ones((QT, LANES), F32)

    @pl.loop(0, row_len // QT)
    def _(t):
        rows = pl.ds(pl.multiple_of(t * QT, QT), QT)
        x = x_ref[0, rows, :]
        sample = sample_column(ends, t * QT, QT)
        q_extra = query_spare(sample, QT)
        q = ((nn(x, w_ref[0]) + vec_ref[0:1, :]).astype(BF16).astype(F32) * DH**-0.5).astype(BF16)
        k = nn(x, w_ref[1]).astype(BF16)
        v = (nn(x, w_ref[2]) + vec_ref[1:2, :]).astype(BF16)
        q_ref[0, rows, :] = q
        k_ref[0, rows, :] = k
        v_ref[0, rows, :] = v
        for p in range(PAIRS):
            pair = head_lanes(p)
            store_heads(qx, rows, p, q[:, pair], q_extra, low_first)
            store_heads(kx, rows, p, k[:, pair], key_spare(sample, QT, p), low_first)
            store_heads(vx, rows, p, v[:, pair], ones, low_first)

    @pl.loop(0, row_len // QT)
    def _(t):
        rows = pl.ds(pl.multiple_of(t * QT, QT), QT)
        begin, number = chosen_span(ends, live, t, row_len)

        @pl.when(number == 0)
        def _():
            o_ref[0, rows, :] = jnp.zeros((QT, D), BF16)
            l_ref[0, rows, :] = jnp.zeros((QT, LANES), F32)

        for n in widths(row_len):

            @pl.when(number == n)
            def _(n=n):
                span = pl.ds(pl.multiple_of(begin * KG, KG), n * KG)
                lane = lane_index(QT)
                scores, powers, got = {}, {}, {}
                peaks = jnp.zeros((QT, LANES), F32)
                totals = jnp.ones((QT, LANES), F32)
                for step in range(H + 2):
                    if step < H:
                        cols = head_lanes(step)
                        scores[step] = nt(qx[rows, cols], kx[span, cols])
                    h = step - 1
                    if 0 <= h < H:
                        s = scores.pop(h)
                        peak = jnp.max(s, axis=1, keepdims=True)
                        powers[h] = jnp.exp(s - peak).astype(BF16)
                        spot = lane == (h // 2 + DH if h % 2 == 0 else h // 2)
                        peaks = jnp.where(spot, peak, peaks)
                    h = step - 2
                    if 0 <= h < H:
                        got[h] = nn(powers.pop(h), vx[span, head_lanes(h)])
                        spot = lane == (h // 2 + DH if h % 2 == 0 else h // 2)
                        totals = jnp.where(spot, got[h], totals)
                        if h % 2 == 1:
                            left, right = got.pop(h - 1), got.pop(h)
                            top = jnp.where(first, left, right)
                            total = pltpu.roll(jnp.where(first, right, left), DH, 1)
                            o_ref[0, rows, head_lanes(h // 2)] = (top / total).astype(BF16)
                l_ref[0, rows, :] = jnp.where(
                    peaks > -0.5 * BIG, peaks + jnp.log(totals), 0.0
                )


def attend(info, tokens, blocks, vec):
    micro, row_len, _ = tokens.shape
    row_spec = lambda width: pl.BlockSpec((1, row_len, width), lambda r: (r, 0, 0))
    low = jax.ShapeDtypeStruct((micro, row_len, D), BF16)
    return pl.pallas_call(
        attend_kernel,
        grid=(micro,),
        in_specs=[
            pl.BlockSpec(memory_space=pltpu.SMEM),
            row_spec(D),
            pl.BlockSpec((3, D, D), lambda r: (0, 0, 0)),
            pl.BlockSpec((NMAT, D), lambda r: (0, 0)),
        ],
        out_specs=[row_spec(D)] * 4 + [row_spec(LANES)],
        out_shape=[low] * 4 + [jax.ShapeDtypeStruct((micro, row_len, LANES), F32)],
        scratch_shapes=[pltpu.VMEM((row_len, 2 * D), BF16)] * 3,
        compiler_params=pltpu.CompilerParams(vmem_limit_bytes=VMEM),
        cost_estimate=pl.CostEstimate(
            flops=micro * row_len * D * D * 6 + micro * H * row_len * row_len * DH * 16,
            bytes_accessed=micro * row_len * D * 16,
            transcendentals=micro * H * row_len * row_len,
        ),
    )(info, tokens, blocks, vec)


def gelu_both(u):
    share = 0.5 + 0.5 * lax.erf(u * 0.5**0.5)
    bell = jnp.exp2((-0.5 * 1.4426950408889634) * (u * u))
    return u * share, share + (u * 0.3989422804014327) * bell


def norm_parts(a):
    center = a - jnp.mean(a, axis=-1, keepdims=True)
    rate = lax.rsqrt(jnp.mean(center * center, axis=-1, keepdims=True) + EPS)
    return center * rate, rate


def norm_back(grad, unit, rate):
    return rate * (
        grad
        - jnp.mean(grad, axis=-1, keepdims=True)
        - unit * jnp.mean(grad * unit, axis=-1, keepdims=True)
    )


def feed_kernel(
    info,
    x_ref,
    o_ref,
    w_ref,
    vec_ref,
    stu_ref,
    cls_ref,
    goal_ref,
    send_row,
    send_col,
    back_hbm,
    da1_ref,
    out_hbm,
    wg_hbm,
    vg_ref,
    sg_ref,
    cg_ref,
    unit1,
    rate1,
    h1b,
    act,
    slope,
    unit2,
    rate2,
    zb,
    head_in,
    head_low,
    back_ref,
    out_ref,
    wg_ref,
    sems,
    *,
    tile,
    micro,
    row_len,
):
    step = pl.program_id(0)
    tiles = micro * row_len // tile
    group, _, slots, _ = out_ref.shape

    parts = FF // D
    bring = pltpu.make_async_copy(back_hbm, back_ref, sems.at[0])
    take = pltpu.make_async_copy(out_ref, out_hbm, sems.at[1])

    def leave(block, at):
        return pltpu.make_async_copy(wg_ref.at[block], wg_hbm.at[block], sems.at[at])

    @pl.when(step == 0)
    def _():
        bring.start()
        vg_ref[...] = jnp.zeros_like(vg_ref)

    @pl.when(step < tiles)
    def _():
        rows = pl.ds(pl.multiple_of(step * tile, tile), tile)
        a1 = x_ref[...].astype(F32) + (nn(o_ref[...], w_ref[3]) + vec_ref[2:3, :])
        unit, rate = norm_parts(a1)
        unit1[rows, :] = unit
        rate1[rows, :] = rate
        h1 = unit * vec_ref[3:4, :] + vec_ref[4:5, :]
        low = h1.astype(BF16)
        h1b[rows, :] = low
        total = h1 + vec_ref[9:10, :]
        raw, value = {}, {}
        for turn in range(PARTS + 2):
            if turn < PARTS:
                c, at = turn // CUT, slice(turn % CUT * PART, (turn % CUT + 1) * PART)
                raw[turn] = nn(low, w_ref[4 + c, :, at]) + vec_ref[5 + c : 6 + c, at]
            if 0 <= turn - 1 < PARTS:
                cols = slice((turn - 1) * PART, turn * PART)
                up, grad = gelu_both(raw.pop(turn - 1))
                value[turn - 1] = up.astype(BF16)
                act[rows, cols] = value[turn - 1]
                slope[rows, cols] = grad.astype(BF16)
            if 0 <= turn - 2 < PARTS:
                c = (turn - 2) // CUT
                at = slice((turn - 2) % CUT * PART, ((turn - 2) % CUT + 1) * PART)
                total = total + nn(value.pop(turn - 2), w_ref[8 + c, at, :])
        unit, rate = norm_parts(total)
        unit2[rows, :] = unit
        rate2[rows, :] = rate
        z = (unit * vec_ref[10:11, :] + vec_ref[11:12, :]).astype(BF16)
        zb[rows, :] = z
        head_in[rows, :] = nn(z, stu_ref[0:D, :].astype(BF16)) + stu_ref[D + SW : D + SW + 1, :]

    @pl.when(step == tiles)
    def _():
        head_phase(
            info, stu_ref, cls_ref, goal_ref, sg_ref, cg_ref, head_in, head_low, micro, row_len
        )
        sg_ref[0:D, :] = tn(zb[...], head_low[...])
        @pl.loop(0, micro)
        def _(m):
            place = send_row[pl.ds(m, 1), :]
            spot = lax.broadcasted_iota(jnp.int32, (group * slots, row_len), 0)
            pick = jnp.where(spot == place, 1.0, 0.0).astype(BF16)
            here = pl.ds(pl.multiple_of(m * row_len, row_len), row_len)
            moved = nn(pick, zb[here, :]).astype(BF16)
            out_ref[:, m] = moved.reshape(group, slots, D)

        take.start()
        bring.wait()

    @pl.when(step >= tiles)
    def _():
        t = step - tiles
        rows = pl.ds(pl.multiple_of(t * tile, tile), tile)
        m = (t * tile) // row_len
        spot = lax.broadcasted_iota(jnp.int32, (tile, group * slots), 1)
        pick = jnp.where(spot == send_col[...], 1.0, 0.0).astype(BF16)
        dz = nn(pick, back_ref[:, m].reshape(group * slots, D))
        dz = dz + nt(head_low[rows, :], stu_ref[0:D, :].astype(BF16))
        unit = unit2[rows, :]
        vg_ref[10:11, :] += row_sum(dz * unit)
        vg_ref[11:12, :] += row_sum(dz)
        da2 = norm_back(dz * vec_ref[10:11, :], unit, rate2[rows, :])
        low = da2.astype(BF16)
        zb[rows, :] = low
        vg_ref[9:10, :] += row_sum(low.astype(F32))
        dh1 = da2
        raw, value = {}, {}
        for turn in range(PARTS + 2):
            if turn < PARTS:
                c, at = turn // CUT, slice(turn % CUT * PART, (turn % CUT + 1) * PART)
                raw[turn] = nt(low, w_ref[8 + c, at, :])
            if 0 <= turn - 1 < PARTS:
                cols = slice((turn - 1) * PART, turn * PART)
                c = (turn - 1) // CUT
                at = slice((turn - 1) % CUT * PART, ((turn - 1) % CUT + 1) * PART)
                du = (raw.pop(turn - 1) * slope[rows, cols].astype(F32)).astype(BF16)
                value[turn - 1] = du
                slope[rows, cols] = du
                vg_ref[5 + c : 6 + c, at] += row_sum(du.astype(F32))
            if 0 <= turn - 2 < PARTS:
                c = (turn - 2) // CUT
                at = slice((turn - 2) % CUT * PART, ((turn - 2) % CUT + 1) * PART)
                dh1 = dh1 + nt(value.pop(turn - 2), w_ref[4 + c, :, at])
        unit = unit1[rows, :]
        vg_ref[3:4, :] += row_sum(dh1 * unit)
        vg_ref[4:5, :] += row_sum(dh1)
        da1_ref[...] = norm_back(dh1 * vec_ref[3:4, :], unit, rate1[rows, :])

    @pl.when(step == 2 * tiles - 1)
    def _():
        @pl.loop(0, FF // D)
        def _(c):
            cols = pl.ds(pl.multiple_of(c * D, D), D)
            wg_ref[c] = tn(h1b[...], slope[:, cols]).astype(BF16)
            leave(c, 2 + c).start()
            wg_ref[parts + c] = tn(act[:, cols], zb[...]).astype(BF16)
            leave(parts + c, 2 + parts + c).start()

        for block in range(2 * parts):
            leave(block, 2 + block).wait()
        take.wait()


def head_phase(info, stu_ref, cls_ref, goal_ref, sg_ref, cg_ref, head_in, head_low, micro, row_len):
    scale = DH**-0.5
    query = stu_ref[D + SW + 2 : D + SW + 3, :]
    same = (
        lax.broadcasted_iota(jnp.int32, (SW, SW), 0) // DH
        == lax.broadcasted_iota(jnp.int32, (SW, SW), 1) // DH
    )
    same = jnp.where(same, 1.0, 0.0).astype(BF16)
    pooled, weights, members = [], [], []
    for m in range(micro):
        rows = slice(m * row_len, (m + 1) * row_len)
        s = head_in[rows, :]
        e = two_low(s * query, same) * scale
        sample = sample_column(ends_of(info, m), 0, row_len)
        share = jnp.zeros_like(e)
        for j in range(SAMP):
            member = sample == j
            peak = jnp.max(jnp.where(member, e, -1e30), axis=0, keepdims=True)
            up = jnp.where(member, jnp.exp(jnp.where(member, e - peak, 0.0)), 0.0)
            up = up / row_sum(up)
            share = share + up
            pooled.append(row_sum(up * s))
            members.append(member)
        weights.append(share)
    pooled = jnp.concatenate(pooled, axis=0)
    pool_weight = stu_ref[D : D + SW, :]
    mixed = jnp.tanh(exact(pooled, pool_weight) + stu_ref[D + SW + 1 : D + SW + 2, :])
    classes = cls_ref[:, 0:SW]
    bias = cls_ref[:, SW : SW + 1].T
    logits = exact(mixed, classes, (((1,), (1,)), ((), ()))) + bias
    logits = logits - jnp.max(logits, axis=-1, keepdims=True)
    chance = jnp.exp(logits)
    chance = chance / jnp.sum(chance, axis=-1, keepdims=True)
    goal = goal_ref[...]
    index = lax.broadcasted_iota(jnp.int32, (micro * SAMP, 1), 0)
    alive = jnp.zeros((micro * SAMP, 1), F32)
    for m in range(micro):
        for j, flag in enumerate(live_of(info, m)):
            alive = jnp.where(index == m * SAMP + j, flag.astype(F32), alive)
    target = jnp.exp(goal - jnp.max(goal, axis=-1, keepdims=True))
    target = target / jnp.sum(target, axis=-1, keepdims=True)
    d_logits = alive * (chance - target)
    cg_ref[:, 0:SW] = exact(d_logits, mixed, (((0,), (0,)), ((), ())))
    cg_ref[:, SW : SW + 1] = row_sum(d_logits).T
    d_pre = exact(d_logits, classes) * (1.0 - mixed * mixed)
    sg_ref[D : D + SW, :] = exact(pooled, d_pre, (((0,), (0,)), ((), ())))
    sg_ref[D + SW + 1 : D + SW + 2, :] = row_sum(d_pre)
    d_pooled = exact(d_pre, pool_weight, (((1,), (1,)), ((), ())))
    inner = two_low(pooled * d_pooled, same)
    d_bias = jnp.zeros((1, SW), F32)
    d_query = jnp.zeros((1, SW), F32)
    for m in range(micro):
        rows = slice(m * row_len, (m + 1) * row_len)
        s = head_in[rows, :]
        spread = jnp.zeros((row_len, SW), F32)
        center = jnp.zeros((row_len, SW), F32)
        for j in range(SAMP):
            member = members[m * SAMP + j]
            at = m * SAMP + j
            spread = jnp.where(member, d_pooled[at : at + 1, :], spread)
            center = jnp.where(member, inner[at : at + 1, :], center)
        share = weights[m]
        d_e = share * (two_low(s * spread, same) - center) * scale
        d_s = (share * spread + d_e * query).astype(BF16)
        head_low[rows, :] = d_s
        d_bias = d_bias + row_sum(d_s.astype(F32))
        d_query = d_query + row_sum(d_e * s)
    sg_ref[D + SW : D + SW + 1, :] = d_bias
    sg_ref[D + SW + 2 : D + SW + 3, :] = d_query


def feed(info, x, o, blocks, vec, student, classifier, goals, send_row, send_col, returned):
    micro, row_len, _ = x.shape
    tokens = micro * row_len
    tile = 512
    tiles = tokens // tile
    group, _, slots, _ = returned.shape
    whole = lambda *shape: pl.BlockSpec(shape, lambda i: (0,) * len(shape))
    once = lambda *shape: pl.BlockSpec(
        shape, lambda i: (0,) * len(shape), pipeline_mode=pl.Buffered(1)
    )
    ahead = lambda width: pl.BlockSpec((tile, width), lambda i: (jnp.minimum(i, tiles - 1), 0))
    behind = lambda width: pl.BlockSpec((tile, width), lambda i: (jnp.maximum(i - tiles, 0), 0))
    return pl.pallas_call(
        functools.partial(feed_kernel, tile=tile, micro=micro, row_len=row_len),
        grid=(2 * tiles,),
        in_specs=[
            pl.BlockSpec(memory_space=pltpu.SMEM),
            ahead(D),
            ahead(D),
            once(NMAT, D, D),
            once(NMAT, D),
            once(*student.shape),
            once(*classifier.shape),
            once(*goals.shape),
            once(*send_row.shape),
            behind(1),
            pl.BlockSpec(memory_space=pl.ANY),
        ],
        out_specs=[
            behind(D),
            pl.BlockSpec(memory_space=pl.ANY),
            pl.BlockSpec(memory_space=pl.ANY),
            once(NMAT, D),
            once(*student.shape),
            once(*classifier.shape),
        ],
        out_shape=[
            jax.ShapeDtypeStruct((tokens, D), F32),
            jax.ShapeDtypeStruct(returned.shape, BF16),
            jax.ShapeDtypeStruct((NMAT, D, D), BF16),
            jax.ShapeDtypeStruct((NMAT, D), F32),
            jax.ShapeDtypeStruct(student.shape, F32),
            jax.ShapeDtypeStruct(classifier.shape, F32),
        ],
        scratch_shapes=[
            pltpu.VMEM((tokens, D), F32),
            pltpu.VMEM((tokens, 1), F32),
            pltpu.VMEM((tokens, D), BF16),
            pltpu.VMEM((tokens, FF), BF16),
            pltpu.VMEM((tokens, FF), BF16),
            pltpu.VMEM((tokens, D), F32),
            pltpu.VMEM((tokens, 1), F32),
            pltpu.VMEM((tokens, D), BF16),
            pltpu.VMEM((tokens, SW), F32),
            pltpu.VMEM((tokens, SW), BF16),
            pltpu.VMEM(returned.shape, BF16),
            pltpu.VMEM(returned.shape, BF16),
            pltpu.VMEM((2 * FF // D, D, D), BF16),
            pltpu.SemaphoreType.DMA((2 + 2 * FF // D,)),
        ],
        compiler_params=pltpu.CompilerParams(vmem_limit_bytes=VMEM),
        cost_estimate=pl.CostEstimate(
            flops=tokens * D * FF * 12, bytes_accessed=tokens * D * 16, transcendentals=tokens * FF
        ),
    )(
        info,
        x.reshape(tokens, D),
        o.reshape(tokens, D),
        blocks,
        vec,
        student,
        classifier,
        goals,
        send_row,
        send_col,
        returned,
    )


def attend_back_kernel(
    info,
    x_ref,
    da1_ref,
    q_ref,
    k_ref,
    v_ref,
    o_ref,
    l_ref,
    w_ref,
    _,
    dx_ref,
    wg_ref,
    vg_ref,
    qx,
    kx,
    vx,
    dox,
    dq,
    dk,
    dv,
    dkt,
    dvt,
    qt,
    dot,
    dq_sum,
    wsum,
    *,
    micro,
):
    row = pl.program_id(0)
    row_len = x_ref.shape[1]
    ends, live = ends_of(info, row), live_of(info, row)
    first = lane_index(QT) < DH
    low_first = jnp.where(first, 1.0, 0.0).astype(BF16)
    ones = jnp.ones((QT, LANES), F32)

    @pl.when(row == 0)
    def _():
        vg_ref[...] = jnp.zeros_like(vg_ref)
        wsum[...] = jnp.zeros_like(wsum)

    head = lax.broadcasted_iota(jnp.int32, (D, LANES), 0) // DH
    spot = head // 2 + DH * (1 - head % 2)
    gather = lax.broadcasted_iota(jnp.int32, (D, LANES), 1) == spot
    gather = jnp.where(gather, 1.0, 0.0).astype(BF16)

    dkt[...] = jnp.zeros_like(dkt)
    dvt[...] = jnp.zeros_like(dvt)

    @pl.loop(0, row_len // QT)
    def _(t):
        rows = pl.ds(pl.multiple_of(t * QT, QT), QT)
        sample = sample_column(ends, t * QT, QT)
        lane = lane_index(QT) % DH
        high, mid, rest = split_low(jnp.where(lane < PAIRS, -l_ref[0, rows, :], 0.0))
        q_extra = (
            query_spare(sample, QT)
            + high
            + pltpu.roll(mid, PAIRS, 1)
            + pltpu.roll(rest, 2 * PAIRS, 1)
        )
        branch = da1_ref[0, rows, :].astype(BF16)
        vg_ref[2:3, :] += row_sum(branch.astype(F32))
        do = nt(branch, w_ref[3]).astype(BF16).astype(F32)
        delta = two_low(do * o_ref[0, rows, :].astype(F32), gather)
        high = delta.astype(BF16).astype(F32)
        do_extra = pltpu.roll(high - delta, PAIRS, 1) - high
        for p in range(PAIRS):
            pair = head_lanes(p)
            k_extra = key_spare(sample, QT, p)
            store_heads(dox, rows, p, do[:, pair], do_extra, low_first)
            store_heads(qx, rows, p, q_ref[0, rows, pair], q_extra, low_first)
            store_heads(kx, rows, p, k_ref[0, rows, pair], k_extra, low_first)
            store_heads(vx, rows, p, v_ref[0, rows, pair], k_extra, low_first)

    @pl.loop(0, row_len // QT)
    def _(t):
        rows = pl.ds(pl.multiple_of(t * QT, QT), QT)
        begin, number = reach(ends, live, t * QT, QT, row_len)
        number = (number + STEP - 1) // STEP
        begin = jnp.minimum(begin, row_len // KG - number * STEP)
        dq_sum[...] = jnp.zeros_like(dq_sum)
        for h in range(H):
            qt[head_lanes(h), :] = qx[rows, head_lanes(h)].T
            dot[head_lanes(h), :] = dox[rows, head_lanes(h)].T

        @pl.loop(0, number)
        def _(j):
            span = pl.ds(pl.multiple_of((begin + j * STEP) * KG, KG), STEP * KG)
            raw, done, got = {}, {}, {}
            for step in range(H + 2):
                if step < H:
                    cols = head_lanes(step)
                    raw[step] = (
                        nt(qx[rows, cols], kx[span, cols]),
                        nt(dox[rows, cols], vx[span, cols]),
                    )
                h = step - 1
                if 0 <= h < H:
                    s, dp = raw.pop(h)
                    prob = jnp.exp(s)
                    done[h] = (prob.astype(BF16), (prob * dp).astype(BF16))
                h = step - 2
                if 0 <= h < H:
                    cols = head_lanes(h)
                    prob, ds = done.pop(h)
                    mine = slice(h * DH, (h + 1) * DH)
                    side = slice(h % 2 * DH, (h % 2 + 1) * DH)
                    dvt[mine, span] += nn(dot[cols, :], prob)[side]
                    dkt[mine, span] += nn(qt[cols, :], ds)[side]
                    got[h] = nn(ds, kx[span, cols])
                    if h % 2 == 1:
                        left, right = got.pop(h - 1), got.pop(h)
                        dq_sum[:, head_lanes(h // 2)] += jnp.where(first, left, right)

        dq[rows, :] = (dq_sum[...] * DH**-0.5).astype(BF16)

    @pl.loop(0, row_len // QT)
    def _(t):
        rows = pl.ds(pl.multiple_of(t * QT, QT), QT)
        dq_low = dq[rows, :]
        dk_low = dkt[:, rows].astype(BF16).T
        dv_low = dvt[:, rows].astype(BF16).T
        dk[rows, :] = dk_low
        dv[rows, :] = dv_low
        vg_ref[0:1, :] += row_sum(dq_low.astype(F32))
        vg_ref[1:2, :] += row_sum(dv_low.astype(F32))
        dx_ref[0, rows, :] = (
            da1_ref[0, rows, :]
            + nt(dq_low, w_ref[0])
            + nt(dk_low, w_ref[1])
            + nt(dv_low, w_ref[2])
        ).astype(BF16)

    x = x_ref[0]
    wsum[0] += tn(x, dq[...])
    wsum[1] += tn(x, dk[...])
    wsum[2] += tn(x, dv[...])
    wsum[3] += tn(o_ref[0], da1_ref[0].astype(BF16))

    @pl.when(row == micro - 1)
    def _():
        wg_ref[...] = wsum[...].astype(BF16)


def attend_back(info, tokens, da1, q, k, v, o, logs, blocks, grads):
    micro, row_len, _ = tokens.shape
    row_spec = lambda width: pl.BlockSpec((1, row_len, width), lambda r: (r, 0, 0))
    return pl.pallas_call(
        functools.partial(attend_back_kernel, micro=micro),
        grid=(micro,),
        in_specs=[
            pl.BlockSpec(memory_space=pltpu.SMEM),
            *[row_spec(D)] * 6,
            row_spec(LANES),
            pl.BlockSpec((4, D, D), lambda r: (0, 0, 0)),
            pl.BlockSpec(memory_space=pl.ANY),
        ],
        out_specs=[
            row_spec(D),
            pl.BlockSpec((4, D, D), lambda r: (2, 0, 0)),
            pl.BlockSpec((8, D), lambda r: (0, 0)),
        ],
        out_shape=[
            jax.ShapeDtypeStruct((micro, row_len, D), BF16),
            jax.ShapeDtypeStruct((NMAT, D, D), BF16),
            jax.ShapeDtypeStruct((8, D), F32),
        ],
        scratch_shapes=[
            *[pltpu.VMEM((row_len, 2 * D), BF16)] * 4,
            *[pltpu.VMEM((row_len, D), BF16)] * 3,
            *[pltpu.VMEM((D, row_len), F32)] * 2,
            *[pltpu.VMEM((2 * D, QT), BF16)] * 2,
            pltpu.VMEM((QT, D), F32),
            pltpu.VMEM((4, D, D), F32),
        ],
        input_output_aliases={9: 1},
        compiler_params=pltpu.CompilerParams(vmem_limit_bytes=VMEM),
        cost_estimate=pl.CostEstimate(
            flops=micro * row_len * D * D * 16 + micro * H * row_len * row_len * DH * 10,
            bytes_accessed=micro * row_len * D * 16,
            transcendentals=micro * H * row_len * row_len,
        ),
    )(info, tokens, da1, q, k, v, o, logs, blocks, grads)


CROSS = 3
CHUNKS = 12
STU_ROWS, CLS_ROWS, VEC_ROWS = 656, 16, 16
SMALL_ROWS = 1024


def reduce_kernel(
    group,
    owners,
    grad_ref,
    ff_vec,
    at_vec,
    stu_ref,
    cls_ref,
    own_ref,
    vec_out,
    stu_out,
    cls_out,
    got_a,
    sum_a,
    got_b,
    part,
    got_c,
    final,
    small,
    small_got,
    small_sum,
    small_end,
    got_y,
    half_y,
    held,
    held_sem,
    send_sem,
    recv_sem,
    small_send,
    small_recv,
):
    b, s = lax.axis_index("batch"), lax.axis_index("shard")
    per = NMAT // owners
    rows = per * D // CHUNKS
    batch_bits, shard_bits = bits_of(group), bits_of(owners)
    half = SMALL_ROWS // 2

    def copy(src, dst, sems, at, where):
        return pltpu.make_async_remote_copy(
            src_ref=src,
            dst_ref=dst,
            send_sem=sems[0].at[at],
            recv_sem=sems[1].at[at],
            device_id=where,
            device_id_type=pl.DeviceIdType.MESH,
        )

    far = shard_bits[1]

    def piece(owner, c):
        at = lax.rem(owner * per + c * per // CHUNKS + 8, NMAT)
        if rows == D:
            return grad_ref.at[at]
        step = D // rows
        return grad_ref.at[at, pl.ds((c % step) * rows, rows)]

    fetched = {}
    for c in range(CHUNKS):
        for i, owner in enumerate((s ^ far, s)):
            op = pltpu.make_async_copy(piece(owner, c), held.at[c, i], held_sem.at[c, i])
            op.start()
            fetched[c, i] = op

    peers = [(b, s ^ bit) for bit in shard_bits] + [(b ^ bit, s) for bit in batch_bits]
    barrier = pltpu.get_barrier_semaphore()
    for peer in peers:
        pl.semaphore_signal(
            barrier, inc=1, device_id=peer, device_id_type=pl.DeviceIdType.MESH
        )
    pl.semaphore_wait(barrier, len(peers))

    sems = (send_sem, recv_sem)
    small_sems = (small_send, small_recv)
    waits = []

    def begin(op):
        op.start()
        waits.append(op)
        return op

    first = {}
    for c in range(CHUNKS):
        first[c] = [
            begin(copy(piece(s ^ 1 ^ far, c), got_a.at[c, 0], sems, (c, 0), peers[0])),
            begin(copy(piece(s ^ 1, c), got_a.at[c, 1], sems, (c, 1), peers[0])),
        ]

    small[...] = jnp.zeros_like(small)
    stu_count = stu_ref.shape[0]
    small[0:stu_count, :] = stu_ref[...].astype(BF16)
    small[STU_ROWS : STU_ROWS + CLS, :] = cls_ref[:, 0:SW].astype(BF16)
    small[STU_ROWS + CLS_ROWS : STU_ROWS + CLS_ROWS + CLS, 0:1] = cls_ref[:, SW:].astype(BF16)
    for i in range(4):
        at = STU_ROWS + 2 * CLS_ROWS + i * VEC_ROWS
        lanes = slice(i * LANES, (i + 1) * LANES)
        small[at : at + 3, :] = at_vec[0:3, lanes].astype(BF16)
        small[at + 3 : at + NMAT, :] = ff_vec[3:NMAT, lanes].astype(BF16)
    core = lax.rem(s, 2)
    mine = pl.ds(pl.multiple_of(core * half, 16), half)
    other = pl.ds(pl.multiple_of((1 - core) * half, 16), half)
    small_op = begin(copy(small.at[other], small_got.at[pl.ds(0, half)], small_sems, 0, peers[0]))

    def add(x, y):
        return (x.astype(F32) + y.astype(F32)).astype(BF16)

    def add_into(out, x, y, x_at=0, y_at=0, out_at=0):
        count = out[1]
        slab = 16 if count % 32 else 32

        @pl.loop(0, count // slab)
        def _(i):
            def rows_at(first):
                return pl.ds(pl.multiple_of(first + i * slab, 16), slab)

            out[0][rows_at(out_at), :] = add(x[rows_at(x_at), :], y[rows_at(y_at), :])

    second = {}
    copies = send_sem.shape[1]

    def crossed(c):
        return c % CROSS == CROSS - 1

    def start_second(c):
        for i, op in enumerate(first[c]):
            op.wait_recv()
            fetched[c, i].wait()
            add_into((sum_a.at[c, i], rows), held.at[c, i], got_a.at[c, i])
        if crossed(c):
            count = rows // 2
            away = pl.ds(pl.multiple_of((1 - lax.rem(b, 2)) * count, 16), count)
            second[c] = [
                begin(copy(sum_a.at[c, i, away], got_y.at[c, i], sems, (c, at), (b ^ 1, s)))
                for i, at in ((0, 3), (1, copies - 1))
            ]
        else:
            second[c] = begin(copy(sum_a.at[c, 0], got_b.at[c], sems, (c, 2), peers[1]))

    start_second(0)
    start_second(1)

    spans = []
    size = rows
    for bit in batch_bits:
        halving = size >= 32
        spans.append((bit, size, halving))
        if halving:
            size //= 2
    offset_of = []
    offset = jnp.int32(0)
    slot_of = []
    slot = 0
    for bit, now, halving in spans:
        place = lax.rem(b // bit, 2)
        offset_of.append((offset, place))
        slot_of.append(slot)
        if halving:
            offset = offset + place * (now // 2)
            slot += now // 2
        else:
            slot += now
    last = offset

    def ranged(ref, c, start, count):
        return ref.at[c, pl.ds(pl.multiple_of(start, 16), count)]

    moving = {}

    def start_batch(c, k):
        bit, now, halving = spans[k]
        start, place = offset_of[k]
        if halving:
            count = now // 2
            src = ranged(part.at[k], c, start + (1 - place) * count, count)
        else:
            count = now
            src = ranged(part.at[k], c, start, count)
        dst = got_c.at[c, pl.ds(slot_of[k], count)]
        moving[c, k] = begin(copy(src, dst, sems, (c, 3 + k), (b ^ bit, s)))

    def end_batch(c, k):
        bit, now, halving = spans[k]
        start, place = offset_of[k]
        moving[c, k].wait_recv()
        count = now // 2 if halving else now
        if halving:
            start = start + place * count
        target = part.at[k + 1, c] if k + 1 < len(spans) else final.at[c]
        add_into(
            (target, count), part.at[k, c], got_c.at[c], x_at=start, y_at=slot_of[k], out_at=start
        )

    gathers = [k for k in reversed(range(len(spans))) if spans[k][2]]
    gathering = {}

    def start_gather(c, g):
        k = gathers[g]
        bit, now, _ = spans[k]
        start, place = offset_of[k]
        count = now // 2
        at = ranged(final, c, start + place * count, count)
        gathering[c, g] = begin(
            copy(at, at, sems, (c, 3 + len(spans) + g), (b ^ bit, s))
        )

    def stage(c, k):
        if crossed(c) and k < 2:
            count = rows // 2
            here = lax.rem(b, 2) * count
            if k == 0:
                for i, op in enumerate(second[c]):
                    op.wait_recv()
                    add_into((half_y.at[c, i], count), sum_a.at[c, i], got_y.at[c, i], x_at=here)
                dst = got_b.at[c, pl.ds(0, count)]
                second[c] = begin(copy(half_y.at[c, 0], dst, sems, (c, 2), peers[1]))
                if c + 2 < CHUNKS:
                    start_second(c + 2)
            else:
                second[c].wait_recv()
                add_into((part.at[1, c], count), half_y.at[c, 1], got_b.at[c], out_at=here)
                start_batch(c, 1)
        elif k == 0:
            second[c].wait_recv()
            if c + 2 < CHUNKS:
                start_second(c + 2)
            add_into((part.at[0, c], rows), sum_a.at[c, 1], got_b.at[c])
            start_batch(c, 0)
        elif k <= len(spans):
            end_batch(c, k - 1)
            if k < len(spans):
                start_batch(c, k)
            else:
                start_gather(c, 0)
        else:
            g = k - len(spans) - 1
            gathering[c, g].wait_recv()
            if g + 1 < len(gathers):
                start_gather(c, g + 1)
            else:
                per_block = CHUNKS // per
                block, within = c // per_block, c % per_block
                own_ref[block, within * rows : (within + 1) * rows, :] = final[c]

    stages = 1 + len(spans) + len(gathers)
    rest = [(s, bit) for bit in shard_bits[1:]] + [(b, bit) for bit in batch_bits]
    levels = []
    start, size, at = core * half, half, 0
    for index, (axis, bit) in enumerate(rest):
        place = lax.rem(axis // bit, 2)
        count = size // 2 if size >= 32 else size
        peer = (b, s ^ bit) if index < len(shard_bits) - 1 else (b ^ bit, s)
        levels.append((start, size, count, place, peer, at))
        at += count
        if count < size:
            start, size = start + place * count, count
    last_start, last_size = start, size
    backs = [k for k in reversed(range(len(levels))) if levels[k][2] < levels[k][1]]

    def small_rows(ref, first, count):
        return ref.at[pl.ds(pl.multiple_of(first, 16), count)]

    def small_begin(k):
        begin_at, now, count, place, peer, slot = levels[k]
        first = begin_at + (1 - place) * count if count < now else begin_at
        return begin(
            copy(
                small_rows(small_sum.at[k], first, count),
                small_got.at[pl.ds(half + slot, count)],
                small_sems,
                k + 1,
                peer,
            )
        )

    def small_back(g):
        if g == len(backs):
            at = small_rows(small_end, core * half, half)
            return begin(copy(at, at, small_sems, len(levels) + 1 + g, peers[0]))
        begin_at, now, count, place, peer, _ = levels[backs[g]]
        at = small_rows(small_end, begin_at + place * count, count)
        return begin(copy(at, at, small_sems, len(levels) + 1 + g, peer))

    def small_stage(k):
        nonlocal small_op
        small_op.wait_recv()
        if k == 0:
            add_into((small_sum.at[0], half), small, small_got, x_at=core * half, out_at=core * half)
            small_op = small_begin(0)
        elif k <= len(levels):
            begin_at, now, count, place, _, slot = levels[k - 1]
            first = begin_at + place * count if count < now else begin_at
            target = small_sum.at[k] if k < len(levels) else small_end
            add_into(
                (target, count),
                small_sum.at[k - 1],
                small_got,
                x_at=first,
                y_at=half + slot,
                out_at=first,
            )
            small_op = small_begin(k) if k < len(levels) else small_back(0)
        elif k - len(levels) <= len(backs):
            small_op = small_back(k - len(levels))

    small_last = len(levels) + len(backs) + 1
    small_k = 0
    for tick in range(CHUNKS + 2 * (stages - 1)):
        for k in reversed(range(stages)):
            c = tick - 2 * k
            if 0 <= c < CHUNKS:
                stage(c, k)
        if small_k <= small_last:
            small_stage(small_k)
            small_k += 1
    while small_k <= small_last:
        small_stage(small_k)
        small_k += 1

    for i in range(4):
        at = STU_ROWS + 2 * CLS_ROWS + i * VEC_ROWS
        lanes = slice(i * LANES, (i + 1) * LANES)
        vec_out[:, lanes] = small_end[at : at + VEC_ROWS, :].astype(F32)
    stu_out[...] = small_end[0:STU_ROWS, :].astype(F32)
    cls_out[:, 0:LANES] = small_end[STU_ROWS : STU_ROWS + CLS_ROWS, :].astype(F32)
    at = STU_ROWS + CLS_ROWS
    cls_out[:, LANES:] = small_end[at : at + CLS_ROWS, :].astype(F32)
    for op in waits:
        op.wait_send()


def reduce_grads(grads, ff_vec, at_vec, stu, cls):
    group, owners = lax.axis_size("batch"), lax.axis_size("shard")
    per = NMAT // owners
    rows = per * D // CHUNKS
    batch_count = len(bits_of(group))
    copies = 4 + 2 * batch_count
    small_count = len(bits_of(owners)) + batch_count + 1
    vmem = pl.BlockSpec(memory_space=pltpu.VMEM)
    return pl.pallas_call(
        functools.partial(reduce_kernel, group, owners),
        in_specs=[pl.BlockSpec(memory_space=pl.ANY)] + [vmem] * 4,
        out_specs=[vmem] * 4,
        out_shape=[
            jax.ShapeDtypeStruct((per, D, D), BF16),
            jax.ShapeDtypeStruct((VEC_ROWS, D), F32),
            jax.ShapeDtypeStruct((STU_ROWS, SW), F32),
            jax.ShapeDtypeStruct((CLS_ROWS, 2 * LANES), F32),
        ],
        scratch_shapes=[
            pltpu.VMEM((CHUNKS, 2, rows, D), BF16),
            pltpu.VMEM((CHUNKS, 2, rows, D), BF16),
            pltpu.VMEM((CHUNKS, rows, D), BF16),
            pltpu.VMEM((batch_count, CHUNKS, rows, D), BF16),
            pltpu.VMEM((CHUNKS, rows + 16 * batch_count, D), BF16),
            pltpu.VMEM((CHUNKS, rows, D), BF16),
            pltpu.VMEM((SMALL_ROWS, LANES), BF16),
            pltpu.VMEM((SMALL_ROWS + 32 * small_count, LANES), BF16),
            pltpu.VMEM((small_count, SMALL_ROWS, LANES), BF16),
            pltpu.VMEM((SMALL_ROWS, LANES), BF16),
            pltpu.VMEM((CHUNKS, 2, rows // 2, D), BF16),
            pltpu.VMEM((CHUNKS, 2, rows // 2, D), BF16),
            pltpu.VMEM((CHUNKS, 2, rows, D), BF16),
            pltpu.SemaphoreType.DMA((CHUNKS, 2)),
            pltpu.SemaphoreType.DMA((CHUNKS, copies)),
            pltpu.SemaphoreType.DMA((CHUNKS, copies)),
            pltpu.SemaphoreType.DMA((2 * small_count + 1,)),
            pltpu.SemaphoreType.DMA((2 * small_count + 1,)),
        ],
        compiler_params=pltpu.CompilerParams(
            collective_id=1, has_side_effects=True, vmem_limit_bytes=VMEM
        ),
        cost_estimate=pl.CostEstimate(
            flops=NMAT * D * D * 4, bytes_accessed=NMAT * D * D * 8, transcendentals=0
        ),
    )(grads, ff_vec, at_vec, stu, cls)


def update_kernel(
    own_ref,
    blocks_ref,
    left_ref,
    right_ref,
    lroot_ref,
    rroot_ref,
    shard_ref,
    vsum_ref,
    vec_ref,
    vmom_ref,
    ssum_ref,
    stu_ref,
    smom_ref,
    csum_ref,
    cls_ref,
    cmom_ref,
    back_ref,
    rows_ref,
    grad_out,
    new_out,
    left_out,
    right_out,
    vg_out,
    vm_out,
    v_out,
    sg_out,
    sm_out,
    s_out,
    cg_out,
    cm_out,
    c_out,
    layer_out,
    *,
    owners,
):
    step = pl.program_id(0)
    row_len = layer_out.shape[1]

    @pl.when(step < rows_ref.shape[1])
    def _():
        arrived = rows_ref[:, step].reshape(row_len, D)
        chunk = min(256, row_len)

        @pl.loop(0, row_len // chunk)
        def _(k):
            at = pl.multiple_of(k * chunk, chunk)
            spot = at + lax.broadcasted_iota(jnp.int32, (chunk, row_len), 0)
            pick = jnp.where(spot == back_ref[pl.ds(step, 1), :], 1.0, 0.0).astype(BF16)
            layer_out[0, pl.ds(at, chunk), :] = nn(pick, arrived).astype(BF16)

    g = own_ref[0]
    grad_out[0] = g.astype(F32)
    left_out[0] = decay_rate * left_ref[0] + (1.0 - decay_rate) * nt(g, g)
    right_out[0] = decay_rate * right_ref[0] + (1.0 - decay_rate) * tn(g, g)
    steered = nn(lroot_ref[0].astype(BF16), g).astype(BF16)
    steered = nn(steered, rroot_ref[0].astype(BF16))
    size = jnp.mean(steered * steered, keepdims=True)
    new_out[0] = blocks_ref[0].astype(F32) - steered * (block_rate * lax.rsqrt(size + 1e-06))

    @pl.when(pl.program_id(0) == 0)
    def _():
        per = NMAT // owners
        mine = vsum_ref[0:per, :]
        for i in range(1, owners):
            mine = jnp.where(shard_ref[0] == i, vsum_ref[i * per : (i + 1) * per, :], mine)

        def rule(grads, old, moment, rate, outs):
            renewed = decay_rate * moment + (1.0 - decay_rate) * grads * grads
            outs[0][...] = grads
            outs[1][...] = renewed
            outs[2][...] = old - rate * grads / (jnp.sqrt(renewed) + 1e-08)

        rule(mine, vec_ref[...], vmom_ref[...], vector_rate, (vg_out, vm_out, v_out))
        rule(
            ssum_ref[0 : stu_ref.shape[0], :],
            stu_ref[...],
            smom_ref[...],
            head_rate,
            (sg_out, sm_out, s_out),
        )
        rule(
            csum_ref[0:CLS, 0 : SW + 1],
            cls_ref[...],
            cmom_ref[...],
            head_rate,
            (cg_out, cm_out, c_out),
        )


def update(own, blocks, left, right, lroot, rroot, shard, vsum, vec, vmom, ssum, stu, smom, csum, cls, cmom, back, arrived):
    per = own.shape[0]
    micro, row_len = back.shape
    mat = pl.BlockSpec((1, D, D), lambda i: (i, 0, 0))
    whole = lambda a: pl.BlockSpec(a.shape, lambda i: (0,) * a.ndim)
    like = lambda a: jax.ShapeDtypeStruct(a.shape, F32)
    return pl.pallas_call(
        functools.partial(update_kernel, owners=NMAT // per),
        grid=(per,),
        in_specs=[mat] * 6
        + [pl.BlockSpec(memory_space=pltpu.SMEM)]
        + [whole(a) for a in (vsum, vec, vmom, ssum, stu, smom, csum, cls, cmom, back, arrived)],
        out_specs=[mat] * 4
        + [whole(a) for a in (vec,) * 3 + (stu,) * 3 + (cls,) * 3]
        + [pl.BlockSpec((1, row_len, D), lambda i: (jnp.minimum(i, micro - 1), 0, 0))],
        out_shape=[like(left)] * 4
        + [like(a) for a in (vec,) * 3 + (stu,) * 3 + (cls,) * 3]
        + [jax.ShapeDtypeStruct((micro, row_len, D), BF16)],
        compiler_params=pltpu.CompilerParams(vmem_limit_bytes=VMEM),
    )(
        own,
        blocks,
        left,
        right,
        lroot,
        rroot,
        shard,
        vsum,
        vec,
        vmom,
        ssum,
        stu,
        smom,
        csum,
        cls,
        cmom,
        back,
        arrived,
    )


def local(
    tokens,
    cotangent,
    lengths,
    exit_layers,
    teacher,
    blocks,
    left_stats,
    right_stats,
    left_root,
    right_root,
    vectors,
    vec_moment,
    student,
    stu_moment,
    classifier,
    cls_moment,
):
    group = lax.axis_size("batch")
    me = lax.axis_index("batch")
    micro, _, row_len, _ = tokens.shape
    slots = row_len // group
    tokens, cotangent = tokens[:, 0], cotangent[:, 0]
    ends = jnp.cumsum(lengths[:, 0], axis=-1, dtype=jnp.int32)
    live = (exit_layers[:, 0] >= LAYER).astype(jnp.int32)
    info = jnp.concatenate([lengths[:, 0], exit_layers[:, 0]], axis=1)
    alive_len = lengths[:, 0] * live
    counts = jnp.sum(alive_len, axis=1, dtype=jnp.int32)
    everyone = lax.all_gather(counts[None, :], "batch", axis=0, tiled=True)
    starts = jnp.cumsum(everyone, axis=0, dtype=jnp.int32) - everyone

    places = jnp.arange(row_len, dtype=jnp.int32)
    before = jnp.cumsum(alive_len, axis=1, dtype=jnp.int32) - alive_len
    sample = jnp.sum((places[None, :, None] >= ends[:, None, : SAMP - 1]).astype(jnp.int32), axis=-1)
    chosen = sample[..., None] == jnp.arange(SAMP, dtype=jnp.int32)
    shift = jnp.sum(jnp.where(chosen, (before - ends + lengths[:, 0])[:, None, :], 0), axis=-1)
    alive_tok = jnp.sum(jnp.where(chosen, live[:, None, :], 0), axis=-1)
    rank = places[None, :] + shift
    send = (starts[me][:, None] + rank) % group * slots + rank // group
    send = jnp.where(alive_tok > 0, send, row_len)
    start_of = jnp.repeat(starts.T, slots, axis=1)
    count_of = jnp.repeat(everyone.T, slots, axis=1)
    turn = (me - start_of) % group + group * (places % slots)[None, :]
    back = jnp.where(turn < count_of, (start_of + turn) // group, row_len)

    grad_outgoing = pick_rows(back[:, :, None], cotangent, group)
    returned = lax.all_to_all(grad_outgoing, "batch", split_axis=0, concat_axis=0, tiled=True)

    matrices = lax.all_gather(blocks, "shard", axis=0, tiled=True)
    vec = lax.all_gather(vectors.astype(BF16), "shard", axis=0, tiled=True).astype(F32)

    q, k, v, o, logs = attend(info, tokens, matrices, vec)
    goals = teacher.reshape(micro * SAMP, CLS)
    classifier, cls_moment = classifier.T, cls_moment.T
    da1, outgoing, ff_grads, ff_vecs, stu_grads, cls_grads = feed(
        info, tokens, o, matrices, vec, student, classifier, goals, send, send.reshape(-1, 1), returned
    )
    arrived = lax.all_to_all(outgoing, "batch", split_axis=0, concat_axis=0, tiled=True)
    input_grads, grads, at_vecs = attend_back(
        info, tokens, da1.reshape(micro, row_len, D), q, k, v, o, logs, matrices, ff_grads
    )
    own, vec_sum, stu_sum, cls_sum = reduce_grads(grads, ff_vecs, at_vecs, stu_grads, cls_grads)
    shard = lax.axis_index("shard").astype(jnp.int32).reshape(1)
    *updated, layer_out = update(
        own,
        blocks,
        left_stats,
        right_stats,
        left_root,
        right_root,
        shard,
        vec_sum,
        vectors,
        vec_moment,
        stu_sum,
        student,
        stu_moment,
        cls_sum,
        classifier,
        cls_moment,
        back,
        arrived,
    )
    classes = [a.T for a in updated[-3:]]
    return (layer_out[:, None], input_grads[:, None], *updated[:-3], *classes)


def solution(mesh):
    rows = P(None, ("batch", "shard"), None, None)
    tags = P(None, ("batch", "shard"), None)
    mats = P("shard", None, None)
    vecs = P("shard", None)
    return jax.shard_map(
        local,
        mesh=mesh,
        in_specs=(rows, rows, tags, tags, rows, mats, mats, mats, mats, mats, vecs, vecs)
        + (P(),) * 4,
        out_specs=(rows, rows, mats, mats, mats, mats, vecs, vecs, vecs) + (P(),) * 6,
        check_vma=False,
    )
```

```python
import functools

import jax
import jax.numpy as jnp
from jax import lax
from jax.experimental import pallas as pl
from jax.experimental.pallas import tpu as pltpu
from jax.sharding import PartitionSpec as P

D = 512
H = 8
DH = 64
FF = 2048
SW = 128
NMAT = 12
SAMP = 4
LAYER = 4
CLS = 14

decay_rate = 0.5
block_rate = 0.04
vector_rate = 0.05
head_rate = 0.05

QT = 256
STEP = 2
KG = 128
PAIRS = H // 2
LANES = 128
PART = 512
PARTS, CUT = FF // PART, D // PART
BIG = float(2**30)
EPS = 1e-6
VMEM = 60 * 1024 * 1024

F32 = jnp.float32
BF16 = jnp.bfloat16


def nn(a, b):
    return jnp.dot(a, b, preferred_element_type=F32)


def nt(a, b):
    return lax.dot_general(a, b, (((1,), (1,)), ((), ())), preferred_element_type=F32)


def tn(a, b):
    return lax.dot_general(a, b, (((0,), (0,)), ((), ())), preferred_element_type=F32)


def exact(a, b, dims=(((1,), (0,)), ((), ()))):
    return lax.dot_general(
        a, b, dims, preferred_element_type=F32, precision=lax.Precision.HIGHEST
    )


def row_sum(v):
    return jnp.sum(v, axis=0, keepdims=True)


def two_low(v, b):
    high = v.astype(BF16)
    return nn(high, b) + nn((v - high.astype(F32)).astype(BF16), b)


def split_low(v):
    high = v.astype(BF16).astype(F32)
    rest = v - high
    mid = rest.astype(BF16).astype(F32)
    return high, mid, rest - mid


def ends_of(info, row):
    ends, total = [], jnp.int32(0)
    for j in range(SAMP):
        total = total + info[row, j]
        ends.append(total)
    return ends


def live_of(info, row):
    return [(info[row, SAMP + j] >= LAYER).astype(jnp.int32) for j in range(SAMP)]


def sample_column(ends, first, count):
    place = first + lax.broadcasted_iota(jnp.int32, (count, 1), 0)
    total = jnp.zeros((count, 1), jnp.int32)
    for j in range(SAMP - 1):
        total = total + (place >= ends[j]).astype(jnp.int32)
    return total


def reach(ends, live, first, count, row_len):
    low, high = jnp.int32(row_len), jnp.int32(0)
    start = jnp.int32(0)
    for j in range(SAMP):
        end = ends[j]
        meets = (start < first + count) & (end > first) & (end > start) & (live[j] > 0)
        low = jnp.where(meets, jnp.minimum(low, start), low)
        high = jnp.where(meets, jnp.maximum(high, end), high)
        start = end
    begin = low // KG
    number = jnp.maximum((high + KG - 1) // KG - begin, 0)
    return begin, number


def lane_index(rows):
    return lax.broadcasted_iota(jnp.int32, (rows, LANES), 1)


TAG = 16


def key_spare(sample, rows, pair):
    lane = lane_index(rows) % DH
    own = (lane < 3 * PAIRS) & (lane % PAIRS == pair)
    return jnp.where(own | (lane == sample + TAG), 1.0, 0.0)


def query_spare(sample, rows):
    lane = lane_index(rows) % DH
    tag = (lane >= TAG) & (lane < TAG + SAMP) & (lane != sample + TAG)
    return jnp.where(tag, -BIG, 0.0)


def store_heads(ref, rows, p, pair, spare, first):
    pair, spare, last = pair.astype(BF16), spare.astype(BF16), 1 - first
    ref[rows, 2 * p * LANES : (2 * p + 1) * LANES] = pair * first + spare * last
    ref[rows, (2 * p + 1) * LANES : (2 * p + 2) * LANES] = pair * last + spare * first


def head_lanes(h):
    return slice(h * LANES, (h + 1) * LANES)


def widths(row_len):
    most = row_len // KG
    return list(range(most // 2, most + 1))


def chosen_span(ends, live, t, row_len):
    begin, number = reach(ends, live, t * QT, QT, row_len)
    least, most = widths(row_len)[0], row_len // KG
    number = jnp.where(number > 0, jnp.maximum(number, least), 0)
    return jnp.minimum(begin, most - number), number


def bits_of(size):
    return [1 << i for i in range(size.bit_length() - 1)]


def pick_kernel(place_ref, rows_ref, out_ref):
    group, _, slots, _ = out_ref.shape
    places = group * slots
    spot = lax.broadcasted_iota(jnp.int32, (places, rows_ref.shape[1]), 1)
    pick = jnp.where(spot == place_ref[0], 1.0, 0.0).astype(BF16)
    out_ref[:, 0] = nn(pick, rows_ref[0]).astype(BF16).reshape(group, slots, D)


def pick_rows(place_col, rows, group):
    micro, row_len, _ = rows.shape
    slots = row_len // group
    return pl.pallas_call(
        pick_kernel,
        grid=(micro,),
        in_specs=[
            pl.BlockSpec((1, row_len, 1), lambda m: (m, 0, 0)),
            pl.BlockSpec((1, row_len, D), lambda m: (m, 0, 0)),
        ],
        out_specs=pl.BlockSpec((group, 1, slots, D), lambda m: (0, m, 0, 0)),
        out_shape=jax.ShapeDtypeStruct((group, micro, slots, D), BF16),
        compiler_params=pltpu.CompilerParams(vmem_limit_bytes=VMEM),
    )(place_col, rows)


def attend_kernel(info, x_ref, w_ref, vec_ref, q_ref, k_ref, v_ref, o_ref, l_ref, qx, kx, vx):
    row = pl.program_id(0)
    row_len = x_ref.shape[1]
    ends, live = ends_of(info, row), live_of(info, row)
    first = lane_index(QT) < DH
    low_first = jnp.where(first, 1.0, 0.0).astype(BF16)
    ones = jnp.ones((QT, LANES), F32)

    @pl.loop(0, row_len // QT)
    def _(t):
        rows = pl.ds(pl.multiple_of(t * QT, QT), QT)
        x = x_ref[0, rows, :]
        sample = sample_column(ends, t * QT, QT)
        q_extra = query_spare(sample, QT)
        q = ((nn(x, w_ref[0]) + vec_ref[0:1, :]).astype(BF16).astype(F32) * DH**-0.5).astype(BF16)
        k = nn(x, w_ref[1]).astype(BF16)
        v = (nn(x, w_ref[2]) + vec_ref[1:2, :]).astype(BF16)
        q_ref[0, rows, :] = q
        k_ref[0, rows, :] = k
        v_ref[0, rows, :] = v
        for p in range(PAIRS):
            pair = head_lanes(p)
            store_heads(qx, rows, p, q[:, pair], q_extra, low_first)
            store_heads(kx, rows, p, k[:, pair], key_spare(sample, QT, p), low_first)
            store_heads(vx, rows, p, v[:, pair], ones, low_first)

    @pl.loop(0, row_len // QT)
    def _(t):
        rows = pl.ds(pl.multiple_of(t * QT, QT), QT)
        begin, number = chosen_span(ends, live, t, row_len)

        @pl.when(number == 0)
        def _():
            o_ref[0, rows, :] = jnp.zeros((QT, D), BF16)
            l_ref[0, rows, :] = jnp.zeros((QT, LANES), F32)

        for n in widths(row_len):

            @pl.when(number == n)
            def _(n=n):
                span = pl.ds(pl.multiple_of(begin * KG, KG), n * KG)
                lane = lane_index(QT)
                scores, powers, got = {}, {}, {}
                peaks = jnp.zeros((QT, LANES), F32)
                totals = jnp.ones((QT, LANES), F32)
                for step in range(H + 2):
                    if step < H:
                        cols = head_lanes(step)
                        scores[step] = nt(qx[rows, cols], kx[span, cols])
                    h = step - 1
                    if 0 <= h < H:
                        s = scores.pop(h)
                        peak = jnp.max(s, axis=1, keepdims=True)
                        powers[h] = jnp.exp(s - peak).astype(BF16)
                        spot = lane == (h // 2 + DH if h % 2 == 0 else h // 2)
                        peaks = jnp.where(spot, peak, peaks)
                    h = step - 2
                    if 0 <= h < H:
                        got[h] = nn(powers.pop(h), vx[span, head_lanes(h)])
                        spot = lane == (h // 2 + DH if h % 2 == 0 else h // 2)
                        totals = jnp.where(spot, got[h], totals)
                        if h % 2 == 1:
                            left, right = got.pop(h - 1), got.pop(h)
                            top = jnp.where(first, left, right)
                            total = pltpu.roll(jnp.where(first, right, left), DH, 1)
                            o_ref[0, rows, head_lanes(h // 2)] = (top / total).astype(BF16)
                l_ref[0, rows, :] = jnp.where(
                    peaks > -0.5 * BIG, peaks + jnp.log(totals), 0.0
                )


def attend(info, tokens, blocks, vec):
    micro, row_len, _ = tokens.shape
    row_spec = lambda width: pl.BlockSpec((1, row_len, width), lambda r: (r, 0, 0))
    low = jax.ShapeDtypeStruct((micro, row_len, D), BF16)
    return pl.pallas_call(
        attend_kernel,
        grid=(micro,),
        in_specs=[
            pl.BlockSpec(memory_space=pltpu.SMEM),
            row_spec(D),
            pl.BlockSpec((3, D, D), lambda r: (0, 0, 0)),
            pl.BlockSpec((NMAT, D), lambda r: (0, 0)),
        ],
        out_specs=[row_spec(D)] * 4 + [row_spec(LANES)],
        out_shape=[low] * 4 + [jax.ShapeDtypeStruct((micro, row_len, LANES), F32)],
        scratch_shapes=[pltpu.VMEM((row_len, 2 * D), BF16)] * 3,
        compiler_params=pltpu.CompilerParams(vmem_limit_bytes=VMEM),
        cost_estimate=pl.CostEstimate(
            flops=micro * row_len * D * D * 6 + micro * H * row_len * row_len * DH * 16,
            bytes_accessed=micro * row_len * D * 16,
            transcendentals=micro * H * row_len * row_len,
        ),
    )(info, tokens, blocks, vec)


def gelu_both(u):
    share = 0.5 + 0.5 * lax.erf(u * 0.5**0.5)
    bell = jnp.exp2((-0.5 * 1.4426950408889634) * (u * u))
    return u * share, share + (u * 0.3989422804014327) * bell


def norm_parts(a):
    center = a - jnp.mean(a, axis=-1, keepdims=True)
    rate = lax.rsqrt(jnp.mean(center * center, axis=-1, keepdims=True) + EPS)
    return center * rate, rate


def norm_back(grad, unit, rate):
    return rate * (
        grad
        - jnp.mean(grad, axis=-1, keepdims=True)
        - unit * jnp.mean(grad * unit, axis=-1, keepdims=True)
    )


def feed_kernel(
    info,
    x_ref,
    o_ref,
    w_ref,
    vec_ref,
    stu_ref,
    cls_ref,
    goal_ref,
    send_row,
    send_col,
    back_hbm,
    da1_ref,
    out_hbm,
    wg_hbm,
    vg_ref,
    sg_ref,
    cg_ref,
    unit1,
    rate1,
    h1b,
    act,
    slope,
    unit2,
    rate2,
    zb,
    head_in,
    head_low,
    back_ref,
    out_ref,
    wg_ref,
    sems,
    *,
    tile,
    micro,
    row_len,
):
    step = pl.program_id(0)
    tiles = micro * row_len // tile
    group, _, slots, _ = out_ref.shape

    parts = FF // D
    bring = pltpu.make_async_copy(back_hbm, back_ref, sems.at[0])
    take = pltpu.make_async_copy(out_ref, out_hbm, sems.at[1])

    def leave(block, at):
        return pltpu.make_async_copy(wg_ref.at[block], wg_hbm.at[block], sems.at[at])

    @pl.when(step == 0)
    def _():
        bring.start()
        vg_ref[...] = jnp.zeros_like(vg_ref)

    @pl.when(step < tiles)
    def _():
        rows = pl.ds(pl.multiple_of(step * tile, tile), tile)
        a1 = x_ref[...].astype(F32) + (nn(o_ref[...], w_ref[3]) + vec_ref[2:3, :])
        unit, rate = norm_parts(a1)
        unit1[rows, :] = unit
        rate1[rows, :] = rate
        h1 = unit * vec_ref[3:4, :] + vec_ref[4:5, :]
        low = h1.astype(BF16)
        h1b[rows, :] = low
        total = h1 + vec_ref[9:10, :]
        raw, value = {}, {}
        for turn in range(PARTS + 2):
            if turn < PARTS:
                c, at = turn // CUT, slice(turn % CUT * PART, (turn % CUT + 1) * PART)
                raw[turn] = nn(low, w_ref[4 + c, :, at]) + vec_ref[5 + c : 6 + c, at]
            if 0 <= turn - 1 < PARTS:
                cols = slice((turn - 1) * PART, turn * PART)
                up, grad = gelu_both(raw.pop(turn - 1))
                value[turn - 1] = up.astype(BF16)
                act[rows, cols] = value[turn - 1]
                slope[rows, cols] = grad.astype(BF16)
            if 0 <= turn - 2 < PARTS:
                c = (turn - 2) // CUT
                at = slice((turn - 2) % CUT * PART, ((turn - 2) % CUT + 1) * PART)
                total = total + nn(value.pop(turn - 2), w_ref[8 + c, at, :])
        unit, rate = norm_parts(total)
        unit2[rows, :] = unit
        rate2[rows, :] = rate
        z = (unit * vec_ref[10:11, :] + vec_ref[11:12, :]).astype(BF16)
        zb[rows, :] = z
        head_in[rows, :] = nn(z, stu_ref[0:D, :].astype(BF16)) + stu_ref[D + SW : D + SW + 1, :]

    @pl.when(step == tiles)
    def _():
        head_phase(
            info, stu_ref, cls_ref, goal_ref, sg_ref, cg_ref, head_in, head_low, micro, row_len
        )
        sg_ref[0:D, :] = tn(zb[...], head_low[...])
        @pl.loop(0, micro)
        def _(m):
            place = send_row[pl.ds(m, 1), :]
            spot = lax.broadcasted_iota(jnp.int32, (group * slots, row_len), 0)
            pick = jnp.where(spot == place, 1.0, 0.0).astype(BF16)
            here = pl.ds(pl.multiple_of(m * row_len, row_len), row_len)
            moved = nn(pick, zb[here, :]).astype(BF16)
            out_ref[:, m] = moved.reshape(group, slots, D)

        take.start()
        bring.wait()

    @pl.when(step >= tiles)
    def _():
        t = step - tiles
        rows = pl.ds(pl.multiple_of(t * tile, tile), tile)
        m = (t * tile) // row_len
        spot = lax.broadcasted_iota(jnp.int32, (tile, group * slots), 1)
        pick = jnp.where(spot == send_col[...], 1.0, 0.0).astype(BF16)
        dz = nn(pick, back_ref[:, m].reshape(group * slots, D))
        dz = dz + nt(head_low[rows, :], stu_ref[0:D, :].astype(BF16))
        unit = unit2[rows, :]
        vg_ref[10:11, :] += row_sum(dz * unit)
        vg_ref[11:12, :] += row_sum(dz)
        da2 = norm_back(dz * vec_ref[10:11, :], unit, rate2[rows, :])
        low = da2.astype(BF16)
        zb[rows, :] = low
        vg_ref[9:10, :] += row_sum(low.astype(F32))
        dh1 = da2
        raw, value = {}, {}
        for turn in range(PARTS + 2):
            if turn < PARTS:
                c, at = turn // CUT, slice(turn % CUT * PART, (turn % CUT + 1) * PART)
                raw[turn] = nt(low, w_ref[8 + c, at, :])
            if 0 <= turn - 1 < PARTS:
                cols = slice((turn - 1) * PART, turn * PART)
                c = (turn - 1) // CUT
                at = slice((turn - 1) % CUT * PART, ((turn - 1) % CUT + 1) * PART)
                du = (raw.pop(turn - 1) * slope[rows, cols].astype(F32)).astype(BF16)
                value[turn - 1] = du
                slope[rows, cols] = du
                vg_ref[5 + c : 6 + c, at] += row_sum(du.astype(F32))
            if 0 <= turn - 2 < PARTS:
                c = (turn - 2) // CUT
                at = slice((turn - 2) % CUT * PART, ((turn - 2) % CUT + 1) * PART)
                dh1 = dh1 + nt(value.pop(turn - 2), w_ref[4 + c, :, at])
        unit = unit1[rows, :]
        vg_ref[3:4, :] += row_sum(dh1 * unit)
        vg_ref[4:5, :] += row_sum(dh1)
        da1_ref[...] = norm_back(dh1 * vec_ref[3:4, :], unit, rate1[rows, :])

    @pl.when(step == 2 * tiles - 1)
    def _():
        @pl.loop(0, FF // D)
        def _(c):
            cols = pl.ds(pl.multiple_of(c * D, D), D)
            wg_ref[c] = tn(h1b[...], slope[:, cols]).astype(BF16)
            leave(c, 2 + c).start()
            wg_ref[parts + c] = tn(act[:, cols], zb[...]).astype(BF16)
            leave(parts + c, 2 + parts + c).start()

        for block in range(2 * parts):
            leave(block, 2 + block).wait()
        take.wait()


def head_phase(info, stu_ref, cls_ref, goal_ref, sg_ref, cg_ref, head_in, head_low, micro, row_len):
    scale = DH**-0.5
    query = stu_ref[D + SW + 2 : D + SW + 3, :]
    same = (
        lax.broadcasted_iota(jnp.int32, (SW, SW), 0) // DH
        == lax.broadcasted_iota(jnp.int32, (SW, SW), 1) // DH
    )
    same = jnp.where(same, 1.0, 0.0).astype(BF16)
    pooled, weights, members = [], [], []
    for m in range(micro):
        rows = slice(m * row_len, (m + 1) * row_len)
        s = head_in[rows, :]
        e = two_low(s * query, same) * scale
        sample = sample_column(ends_of(info, m), 0, row_len)
        share = jnp.zeros_like(e)
        for j in range(SAMP):
            member = sample == j
            peak = jnp.max(jnp.where(member, e, -1e30), axis=0, keepdims=True)
            up = jnp.where(member, jnp.exp(jnp.where(member, e - peak, 0.0)), 0.0)
            up = up / row_sum(up)
            share = share + up
            pooled.append(row_sum(up * s))
            members.append(member)
        weights.append(share)
    pooled = jnp.concatenate(pooled, axis=0)
    pool_weight = stu_ref[D : D + SW, :]
    mixed = jnp.tanh(exact(pooled, pool_weight) + stu_ref[D + SW + 1 : D + SW + 2, :])
    classes = cls_ref[:, 0:SW]
    bias = cls_ref[:, SW : SW + 1].T
    logits = exact(mixed, classes, (((1,), (1,)), ((), ()))) + bias
    logits = logits - jnp.max(logits, axis=-1, keepdims=True)
    chance = jnp.exp(logits)
    chance = chance / jnp.sum(chance, axis=-1, keepdims=True)
    goal = goal_ref[...]
    index = lax.broadcasted_iota(jnp.int32, (micro * SAMP, 1), 0)
    alive = jnp.zeros((micro * SAMP, 1), F32)
    for m in range(micro):
        for j, flag in enumerate(live_of(info, m)):
            alive = jnp.where(index == m * SAMP + j, flag.astype(F32), alive)
    target = jnp.exp(goal - jnp.max(goal, axis=-1, keepdims=True))
    target = target / jnp.sum(target, axis=-1, keepdims=True)
    d_logits = alive * (chance - target)
    cg_ref[:, 0:SW] = exact(d_logits, mixed, (((0,), (0,)), ((), ())))
    cg_ref[:, SW : SW + 1] = row_sum(d_logits).T
    d_pre = exact(d_logits, classes) * (1.0 - mixed * mixed)
    sg_ref[D : D + SW, :] = exact(pooled, d_pre, (((0,), (0,)), ((), ())))
    sg_ref[D + SW + 1 : D + SW + 2, :] = row_sum(d_pre)
    d_pooled = exact(d_pre, pool_weight, (((1,), (1,)), ((), ())))
    inner = two_low(pooled * d_pooled, same)
    d_bias = jnp.zeros((1, SW), F32)
    d_query = jnp.zeros((1, SW), F32)
    for m in range(micro):
        rows = slice(m * row_len, (m + 1) * row_len)
        s = head_in[rows, :]
        spread = jnp.zeros((row_len, SW), F32)
        center = jnp.zeros((row_len, SW), F32)
        for j in range(SAMP):
            member = members[m * SAMP + j]
            at = m * SAMP + j
            spread = jnp.where(member, d_pooled[at : at + 1, :], spread)
            center = jnp.where(member, inner[at : at + 1, :], center)
        share = weights[m]
        d_e = share * (two_low(s * spread, same) - center) * scale
        d_s = (share * spread + d_e * query).astype(BF16)
        head_low[rows, :] = d_s
        d_bias = d_bias + row_sum(d_s.astype(F32))
        d_query = d_query + row_sum(d_e * s)
    sg_ref[D + SW : D + SW + 1, :] = d_bias
    sg_ref[D + SW + 2 : D + SW + 3, :] = d_query


def feed(info, x, o, blocks, vec, student, classifier, goals, send_row, send_col, returned):
    micro, row_len, _ = x.shape
    tokens = micro * row_len
    tile = 512
    tiles = tokens // tile
    group, _, slots, _ = returned.shape
    whole = lambda *shape: pl.BlockSpec(shape, lambda i: (0,) * len(shape))
    once = lambda *shape: pl.BlockSpec(
        shape, lambda i: (0,) * len(shape), pipeline_mode=pl.Buffered(1)
    )
    ahead = lambda width: pl.BlockSpec((tile, width), lambda i: (jnp.minimum(i, tiles - 1), 0))
    behind = lambda width: pl.BlockSpec((tile, width), lambda i: (jnp.maximum(i - tiles, 0), 0))
    return pl.pallas_call(
        functools.partial(feed_kernel, tile=tile, micro=micro, row_len=row_len),
        grid=(2 * tiles,),
        in_specs=[
            pl.BlockSpec(memory_space=pltpu.SMEM),
            ahead(D),
            ahead(D),
            once(NMAT, D, D),
            once(NMAT, D),
            once(*student.shape),
            once(*classifier.shape),
            once(*goals.shape),
            once(*send_row.shape),
            behind(1),
            pl.BlockSpec(memory_space=pl.ANY),
        ],
        out_specs=[
            behind(D),
            pl.BlockSpec(memory_space=pl.ANY),
            pl.BlockSpec(memory_space=pl.ANY),
            once(NMAT, D),
            once(*student.shape),
            once(*classifier.shape),
        ],
        out_shape=[
            jax.ShapeDtypeStruct((tokens, D), F32),
            jax.ShapeDtypeStruct(returned.shape, BF16),
            jax.ShapeDtypeStruct((NMAT, D, D), BF16),
            jax.ShapeDtypeStruct((NMAT, D), F32),
            jax.ShapeDtypeStruct(student.shape, F32),
            jax.ShapeDtypeStruct(classifier.shape, F32),
        ],
        scratch_shapes=[
            pltpu.VMEM((tokens, D), F32),
            pltpu.VMEM((tokens, 1), F32),
            pltpu.VMEM((tokens, D), BF16),
            pltpu.VMEM((tokens, FF), BF16),
            pltpu.VMEM((tokens, FF), BF16),
            pltpu.VMEM((tokens, D), F32),
            pltpu.VMEM((tokens, 1), F32),
            pltpu.VMEM((tokens, D), BF16),
            pltpu.VMEM((tokens, SW), F32),
            pltpu.VMEM((tokens, SW), BF16),
            pltpu.VMEM(returned.shape, BF16),
            pltpu.VMEM(returned.shape, BF16),
            pltpu.VMEM((2 * FF // D, D, D), BF16),
            pltpu.SemaphoreType.DMA((2 + 2 * FF // D,)),
        ],
        compiler_params=pltpu.CompilerParams(vmem_limit_bytes=VMEM),
        cost_estimate=pl.CostEstimate(
            flops=tokens * D * FF * 12, bytes_accessed=tokens * D * 16, transcendentals=tokens * FF
        ),
    )(
        info,
        x.reshape(tokens, D),
        o.reshape(tokens, D),
        blocks,
        vec,
        student,
        classifier,
        goals,
        send_row,
        send_col,
        returned,
    )


def attend_back_kernel(
    info,
    x_hbm,
    da1_ref,
    q_ref,
    k_ref,
    v_ref,
    o_ref,
    l_ref,
    w_out_ref,
    w_hbm,
    _,
    dx_ref,
    wg_ref,
    vg_ref,
    qx,
    kx,
    vx,
    dox,
    dq,
    dk,
    dv,
    dkt,
    dvt,
    qt,
    dot,
    dq_sum,
    wsum,
    x_ref,
    w_ref,
    sems,
    *,
    micro,
):
    row = pl.program_id(0)
    row_len = da1_ref.shape[1]
    bring_x = pltpu.make_async_copy(x_hbm.at[row], x_ref, sems.at[0])
    bring_w = pltpu.make_async_copy(w_hbm.at[pl.ds(0, 3)], w_ref, sems.at[1])
    bring_x.start()
    ends, live = ends_of(info, row), live_of(info, row)
    first = lane_index(QT) < DH
    low_first = jnp.where(first, 1.0, 0.0).astype(BF16)
    ones = jnp.ones((QT, LANES), F32)

    @pl.when(row == 0)
    def _():
        bring_w.start()
        vg_ref[...] = jnp.zeros_like(vg_ref)
        wsum[...] = jnp.zeros_like(wsum)

    head = lax.broadcasted_iota(jnp.int32, (D, LANES), 0) // DH
    spot = head // 2 + DH * (1 - head % 2)
    gather = lax.broadcasted_iota(jnp.int32, (D, LANES), 1) == spot
    gather = jnp.where(gather, 1.0, 0.0).astype(BF16)

    dkt[...] = jnp.zeros_like(dkt)
    dvt[...] = jnp.zeros_like(dvt)

    @pl.loop(0, row_len // QT)
    def _(t):
        rows = pl.ds(pl.multiple_of(t * QT, QT), QT)
        sample = sample_column(ends, t * QT, QT)
        lane = lane_index(QT) % DH
        high, mid, rest = split_low(jnp.where(lane < PAIRS, -l_ref[0, rows, :], 0.0))
        q_extra = (
            query_spare(sample, QT)
            + high
            + pltpu.roll(mid, PAIRS, 1)
            + pltpu.roll(rest, 2 * PAIRS, 1)
        )
        branch = da1_ref[0, rows, :].astype(BF16)
        vg_ref[2:3, :] += row_sum(branch.astype(F32))
        do = nt(branch, w_out_ref[0]).astype(BF16).astype(F32)
        delta = two_low(do * o_ref[0, rows, :].astype(F32), gather)
        high = delta.astype(BF16).astype(F32)
        do_extra = pltpu.roll(high - delta, PAIRS, 1) - high
        for p in range(PAIRS):
            pair = head_lanes(p)
            k_extra = key_spare(sample, QT, p)
            store_heads(dox, rows, p, do[:, pair], do_extra, low_first)
            store_heads(qx, rows, p, q_ref[0, rows, pair], q_extra, low_first)
            store_heads(kx, rows, p, k_ref[0, rows, pair], k_extra, low_first)
            store_heads(vx, rows, p, v_ref[0, rows, pair], k_extra, low_first)

    @pl.loop(0, row_len // QT)
    def _(t):
        rows = pl.ds(pl.multiple_of(t * QT, QT), QT)
        begin, number = reach(ends, live, t * QT, QT, row_len)
        number = (number + STEP - 1) // STEP
        begin = jnp.minimum(begin, row_len // KG - number * STEP)
        dq_sum[...] = jnp.zeros_like(dq_sum)
        for h in range(H):
            qt[head_lanes(h), :] = qx[rows, head_lanes(h)].T
            dot[head_lanes(h), :] = dox[rows, head_lanes(h)].T

        @pl.loop(0, number)
        def _(j):
            span = pl.ds(pl.multiple_of((begin + j * STEP) * KG, KG), STEP * KG)
            raw, done, got = {}, {}, {}
            for step in range(H + 2):
                if step < H:
                    cols = head_lanes(step)
                    raw[step] = (
                        nt(qx[rows, cols], kx[span, cols]),
                        nt(dox[rows, cols], vx[span, cols]),
                    )
                h = step - 1
                if 0 <= h < H:
                    s, dp = raw.pop(h)
                    prob = jnp.exp(s)
                    done[h] = (prob.astype(BF16), (prob * dp).astype(BF16))
                h = step - 2
                if 0 <= h < H:
                    cols = head_lanes(h)
                    prob, ds = done.pop(h)
                    mine = slice(h * DH, (h + 1) * DH)
                    side = slice(h % 2 * DH, (h % 2 + 1) * DH)
                    dvt[mine, span] += nn(dot[cols, :], prob)[side]
                    dkt[mine, span] += nn(qt[cols, :], ds)[side]
                    got[h] = nn(ds, kx[span, cols])
                    if h % 2 == 1:
                        left, right = got.pop(h - 1), got.pop(h)
                        dq_sum[:, head_lanes(h // 2)] += jnp.where(first, left, right)

        dq[rows, :] = (dq_sum[...] * DH**-0.5).astype(BF16)

    @pl.when(row == 0)
    def _():
        bring_w.wait()

    @pl.loop(0, row_len // QT)
    def _(t):
        rows = pl.ds(pl.multiple_of(t * QT, QT), QT)
        dq_low = dq[rows, :]
        dk_low = dkt[:, rows].astype(BF16).T
        dv_low = dvt[:, rows].astype(BF16).T
        dk[rows, :] = dk_low
        dv[rows, :] = dv_low
        vg_ref[0:1, :] += row_sum(dq_low.astype(F32))
        vg_ref[1:2, :] += row_sum(dv_low.astype(F32))
        dx_ref[0, rows, :] = (
            da1_ref[0, rows, :]
            + nt(dq_low, w_ref[0])
            + nt(dk_low, w_ref[1])
            + nt(dv_low, w_ref[2])
        ).astype(BF16)

    bring_x.wait()
    x = x_ref[...]
    wsum[0] += tn(x, dq[...])
    wsum[1] += tn(x, dk[...])
    wsum[2] += tn(x, dv[...])
    wsum[3] += tn(o_ref[0], da1_ref[0].astype(BF16))

    @pl.when(row == micro - 1)
    def _():
        wg_ref[...] = wsum[...].astype(BF16)


def attend_back(info, tokens, da1, q, k, v, o, logs, blocks, grads):
    micro, row_len, _ = tokens.shape
    row_spec = lambda width: pl.BlockSpec((1, row_len, width), lambda r: (r, 0, 0))
    return pl.pallas_call(
        functools.partial(attend_back_kernel, micro=micro),
        grid=(micro,),
        in_specs=[
            pl.BlockSpec(memory_space=pltpu.SMEM),
            pl.BlockSpec(memory_space=pl.ANY),
            *[row_spec(D)] * 5,
            row_spec(LANES),
            pl.BlockSpec((1, D, D), lambda r: (3, 0, 0)),
            pl.BlockSpec(memory_space=pl.ANY),
            pl.BlockSpec(memory_space=pl.ANY),
        ],
        out_specs=[
            row_spec(D),
            pl.BlockSpec((4, D, D), lambda r: (2, 0, 0)),
            pl.BlockSpec((8, D), lambda r: (0, 0)),
        ],
        out_shape=[
            jax.ShapeDtypeStruct((micro, row_len, D), BF16),
            jax.ShapeDtypeStruct((NMAT, D, D), BF16),
            jax.ShapeDtypeStruct((8, D), F32),
        ],
        scratch_shapes=[
            *[pltpu.VMEM((row_len, 2 * D), BF16)] * 4,
            *[pltpu.VMEM((row_len, D), BF16)] * 3,
            *[pltpu.VMEM((D, row_len), F32)] * 2,
            *[pltpu.VMEM((2 * D, QT), BF16)] * 2,
            pltpu.VMEM((QT, D), F32),
            pltpu.VMEM((4, D, D), F32),
            pltpu.VMEM((row_len, D), BF16),
            pltpu.VMEM((3, D, D), BF16),
            pltpu.SemaphoreType.DMA((2,)),
        ],
        input_output_aliases={10: 1},
        compiler_params=pltpu.CompilerParams(vmem_limit_bytes=VMEM),
        cost_estimate=pl.CostEstimate(
            flops=micro * row_len * D * D * 16 + micro * H * row_len * row_len * DH * 10,
            bytes_accessed=micro * row_len * D * 16,
            transcendentals=micro * H * row_len * row_len,
        ),
    )(info, tokens, da1, q, k, v, o, logs, blocks, blocks, grads)


CROSS = 3
CHUNKS = 12
STU_ROWS, CLS_ROWS, VEC_ROWS = 656, 16, 16
SMALL_ROWS = 1024


def reduce_kernel(
    group,
    owners,
    grad_ref,
    ff_vec,
    at_vec,
    stu_ref,
    cls_ref,
    own_ref,
    vec_out,
    stu_out,
    cls_out,
    got_a,
    sum_a,
    got_b,
    part,
    got_c,
    final,
    small,
    small_got,
    small_sum,
    small_end,
    got_y,
    half_y,
    held,
    held_sem,
    send_sem,
    recv_sem,
    small_send,
    small_recv,
):
    b, s = lax.axis_index("batch"), lax.axis_index("shard")
    per = NMAT // owners
    rows = per * D // CHUNKS
    batch_bits, shard_bits = bits_of(group), bits_of(owners)
    half = SMALL_ROWS // 2

    def copy(src, dst, sems, at, where):
        return pltpu.make_async_remote_copy(
            src_ref=src,
            dst_ref=dst,
            send_sem=sems[0].at[at],
            recv_sem=sems[1].at[at],
            device_id=where,
            device_id_type=pl.DeviceIdType.MESH,
        )

    far = shard_bits[1]

    def piece(owner, c):
        at = lax.rem(owner * per + c * per // CHUNKS + 8, NMAT)
        if rows == D:
            return grad_ref.at[at]
        step = D // rows
        return grad_ref.at[at, pl.ds((c % step) * rows, rows)]

    fetched = {}
    for c in range(CHUNKS):
        for i, owner in enumerate((s ^ far, s)):
            op = pltpu.make_async_copy(piece(owner, c), held.at[c, i], held_sem.at[c, i])
            op.start()
            fetched[c, i] = op

    peers = [(b, s ^ bit) for bit in shard_bits] + [(b ^ bit, s) for bit in batch_bits]
    barrier = pltpu.get_barrier_semaphore()
    for peer in peers:
        pl.semaphore_signal(
            barrier, inc=1, device_id=peer, device_id_type=pl.DeviceIdType.MESH
        )
    pl.semaphore_wait(barrier, len(peers))

    sems = (send_sem, recv_sem)
    small_sems = (small_send, small_recv)
    waits = []

    def begin(op):
        op.start()
        waits.append(op)
        return op

    first = {}
    for c in range(CHUNKS):
        first[c] = [
            begin(copy(piece(s ^ 1 ^ far, c), got_a.at[c, 0], sems, (c, 0), peers[0])),
            begin(copy(piece(s ^ 1, c), got_a.at[c, 1], sems, (c, 1), peers[0])),
        ]

    small[...] = jnp.zeros_like(small)
    stu_count = stu_ref.shape[0]
    small[0:stu_count, :] = stu_ref[...].astype(BF16)
    small[STU_ROWS : STU_ROWS + CLS, :] = cls_ref[:, 0:SW].astype(BF16)
    small[STU_ROWS + CLS_ROWS : STU_ROWS + CLS_ROWS + CLS, 0:1] = cls_ref[:, SW:].astype(BF16)
    for i in range(4):
        at = STU_ROWS + 2 * CLS_ROWS + i * VEC_ROWS
        lanes = slice(i * LANES, (i + 1) * LANES)
        small[at : at + 3, :] = at_vec[0:3, lanes].astype(BF16)
        small[at + 3 : at + NMAT, :] = ff_vec[3:NMAT, lanes].astype(BF16)
    core = lax.rem(s, 2)
    mine = pl.ds(pl.multiple_of(core * half, 16), half)
    other = pl.ds(pl.multiple_of((1 - core) * half, 16), half)
    small_op = begin(copy(small.at[other], small_got.at[pl.ds(0, half)], small_sems, 0, peers[0]))

    def add(x, y):
        return (x.astype(F32) + y.astype(F32)).astype(BF16)

    def add_into(out, x, y, x_at=0, y_at=0, out_at=0):
        count = out[1]
        slab = 16 if count % 32 else 32

        @pl.loop(0, count // slab)
        def _(i):
            def rows_at(first):
                return pl.ds(pl.multiple_of(first + i * slab, 16), slab)

            out[0][rows_at(out_at), :] = add(x[rows_at(x_at), :], y[rows_at(y_at), :])

    second = {}
    copies = send_sem.shape[1]

    def crossed(c):
        return c % CROSS == CROSS - 1

    def start_second(c):
        for i, op in enumerate(first[c]):
            op.wait_recv()
            fetched[c, i].wait()
            add_into((sum_a.at[c, i], rows), held.at[c, i], got_a.at[c, i])
        if crossed(c):
            count = rows // 2
            away = pl.ds(pl.multiple_of((1 - lax.rem(b, 2)) * count, 16), count)
            second[c] = [
                begin(copy(sum_a.at[c, i, away], got_y.at[c, i], sems, (c, at), (b ^ 1, s)))
                for i, at in ((0, 3), (1, copies - 1))
            ]
        else:
            second[c] = begin(copy(sum_a.at[c, 0], got_b.at[c], sems, (c, 2), peers[1]))

    start_second(0)
    start_second(1)

    spans = []
    size = rows
    for bit in batch_bits:
        halving = size >= 32
        spans.append((bit, size, halving))
        if halving:
            size //= 2
    offset_of = []
    offset = jnp.int32(0)
    slot_of = []
    slot = 0
    for bit, now, halving in spans:
        place = lax.rem(b // bit, 2)
        offset_of.append((offset, place))
        slot_of.append(slot)
        if halving:
            offset = offset + place * (now // 2)
            slot += now // 2
        else:
            slot += now
    last = offset

    def ranged(ref, c, start, count):
        return ref.at[c, pl.ds(pl.multiple_of(start, 16), count)]

    moving = {}

    def start_batch(c, k):
        bit, now, halving = spans[k]
        start, place = offset_of[k]
        if halving:
            count = now // 2
            src = ranged(part.at[k], c, start + (1 - place) * count, count)
        else:
            count = now
            src = ranged(part.at[k], c, start, count)
        dst = got_c.at[c, pl.ds(slot_of[k], count)]
        moving[c, k] = begin(copy(src, dst, sems, (c, 3 + k), (b ^ bit, s)))

    def end_batch(c, k):
        bit, now, halving = spans[k]
        start, place = offset_of[k]
        moving[c, k].wait_recv()
        count = now // 2 if halving else now
        if halving:
            start = start + place * count
        target = part.at[k + 1, c] if k + 1 < len(spans) else final.at[c]
        add_into(
            (target, count), part.at[k, c], got_c.at[c], x_at=start, y_at=slot_of[k], out_at=start
        )

    gathers = [k for k in reversed(range(len(spans))) if spans[k][2]]
    gathering = {}

    def start_gather(c, g):
        k = gathers[g]
        bit, now, _ = spans[k]
        start, place = offset_of[k]
        count = now // 2
        at = ranged(final, c, start + place * count, count)
        gathering[c, g] = begin(
            copy(at, at, sems, (c, 3 + len(spans) + g), (b ^ bit, s))
        )

    def stage(c, k):
        if crossed(c) and k < 2:
            count = rows // 2
            here = lax.rem(b, 2) * count
            if k == 0:
                for i, op in enumerate(second[c]):
                    op.wait_recv()
                    add_into((half_y.at[c, i], count), sum_a.at[c, i], got_y.at[c, i], x_at=here)
                dst = got_b.at[c, pl.ds(0, count)]
                second[c] = begin(copy(half_y.at[c, 0], dst, sems, (c, 2), peers[1]))
                if c + 2 < CHUNKS:
                    start_second(c + 2)
            else:
                second[c].wait_recv()
                add_into((part.at[1, c], count), half_y.at[c, 1], got_b.at[c], out_at=here)
                start_batch(c, 1)
        elif k == 0:
            second[c].wait_recv()
            if c + 2 < CHUNKS:
                start_second(c + 2)
            add_into((part.at[0, c], rows), sum_a.at[c, 1], got_b.at[c])
            start_batch(c, 0)
        elif k <= len(spans):
            end_batch(c, k - 1)
            if k < len(spans):
                start_batch(c, k)
            else:
                start_gather(c, 0)
        else:
            g = k - len(spans) - 1
            gathering[c, g].wait_recv()
            if g + 1 < len(gathers):
                start_gather(c, g + 1)
            else:
                per_block = CHUNKS // per
                block, within = c // per_block, c % per_block
                own_ref[block, within * rows : (within + 1) * rows, :] = final[c]

    stages = 1 + len(spans) + len(gathers)
    rest = [(s, bit) for bit in shard_bits[1:]] + [(b, bit) for bit in batch_bits]
    levels = []
    start, size, at = core * half, half, 0
    for index, (axis, bit) in enumerate(rest):
        place = lax.rem(axis // bit, 2)
        count = size // 2 if size >= 32 else size
        peer = (b, s ^ bit) if index < len(shard_bits) - 1 else (b ^ bit, s)
        levels.append((start, size, count, place, peer, at))
        at += count
        if count < size:
            start, size = start + place * count, count
    last_start, last_size = start, size
    backs = [k for k in reversed(range(len(levels))) if levels[k][2] < levels[k][1]]

    def small_rows(ref, first, count):
        return ref.at[pl.ds(pl.multiple_of(first, 16), count)]

    def small_begin(k):
        begin_at, now, count, place, peer, slot = levels[k]
        first = begin_at + (1 - place) * count if count < now else begin_at
        return begin(
            copy(
                small_rows(small_sum.at[k], first, count),
                small_got.at[pl.ds(half + slot, count)],
                small_sems,
                k + 1,
                peer,
            )
        )

    def small_back(g):
        if g == len(backs):
            at = small_rows(small_end, core * half, half)
            return begin(copy(at, at, small_sems, len(levels) + 1 + g, peers[0]))
        begin_at, now, count, place, peer, _ = levels[backs[g]]
        at = small_rows(small_end, begin_at + place * count, count)
        return begin(copy(at, at, small_sems, len(levels) + 1 + g, peer))

    def small_stage(k):
        nonlocal small_op
        small_op.wait_recv()
        if k == 0:
            add_into((small_sum.at[0], half), small, small_got, x_at=core * half, out_at=core * half)
            small_op = small_begin(0)
        elif k <= len(levels):
            begin_at, now, count, place, _, slot = levels[k - 1]
            first = begin_at + place * count if count < now else begin_at
            target = small_sum.at[k] if k < len(levels) else small_end
            add_into(
                (target, count),
                small_sum.at[k - 1],
                small_got,
                x_at=first,
                y_at=half + slot,
                out_at=first,
            )
            small_op = small_begin(k) if k < len(levels) else small_back(0)
        elif k - len(levels) <= len(backs):
            small_op = small_back(k - len(levels))

    small_last = len(levels) + len(backs) + 1
    small_k = 0
    for tick in range(CHUNKS + 2 * (stages - 1)):
        for k in reversed(range(stages)):
            c = tick - 2 * k
            if 0 <= c < CHUNKS:
                stage(c, k)
        if small_k <= small_last:
            small_stage(small_k)
            small_k += 1
    while small_k <= small_last:
        small_stage(small_k)
        small_k += 1

    for i in range(4):
        at = STU_ROWS + 2 * CLS_ROWS + i * VEC_ROWS
        lanes = slice(i * LANES, (i + 1) * LANES)
        vec_out[:, lanes] = small_end[at : at + VEC_ROWS, :].astype(F32)
    stu_out[...] = small_end[0:STU_ROWS, :].astype(F32)
    cls_out[:, 0:LANES] = small_end[STU_ROWS : STU_ROWS + CLS_ROWS, :].astype(F32)
    at = STU_ROWS + CLS_ROWS
    cls_out[:, LANES:] = small_end[at : at + CLS_ROWS, :].astype(F32)
    for op in waits:
        op.wait_send()


def reduce_grads(grads, ff_vec, at_vec, stu, cls):
    group, owners = lax.axis_size("batch"), lax.axis_size("shard")
    per = NMAT // owners
    rows = per * D // CHUNKS
    batch_count = len(bits_of(group))
    copies = 4 + 2 * batch_count
    small_count = len(bits_of(owners)) + batch_count + 1
    vmem = pl.BlockSpec(memory_space=pltpu.VMEM)
    return pl.pallas_call(
        functools.partial(reduce_kernel, group, owners),
        in_specs=[pl.BlockSpec(memory_space=pl.ANY)] + [vmem] * 4,
        out_specs=[vmem] * 4,
        out_shape=[
            jax.ShapeDtypeStruct((per, D, D), BF16),
            jax.ShapeDtypeStruct((VEC_ROWS, D), F32),
            jax.ShapeDtypeStruct((STU_ROWS, SW), F32),
            jax.ShapeDtypeStruct((CLS_ROWS, 2 * LANES), F32),
        ],
        scratch_shapes=[
            pltpu.VMEM((CHUNKS, 2, rows, D), BF16),
            pltpu.VMEM((CHUNKS, 2, rows, D), BF16),
            pltpu.VMEM((CHUNKS, rows, D), BF16),
            pltpu.VMEM((batch_count, CHUNKS, rows, D), BF16),
            pltpu.VMEM((CHUNKS, rows + 16 * batch_count, D), BF16),
            pltpu.VMEM((CHUNKS, rows, D), BF16),
            pltpu.VMEM((SMALL_ROWS, LANES), BF16),
            pltpu.VMEM((SMALL_ROWS + 32 * small_count, LANES), BF16),
            pltpu.VMEM((small_count, SMALL_ROWS, LANES), BF16),
            pltpu.VMEM((SMALL_ROWS, LANES), BF16),
            pltpu.VMEM((CHUNKS, 2, rows // 2, D), BF16),
            pltpu.VMEM((CHUNKS, 2, rows // 2, D), BF16),
            pltpu.VMEM((CHUNKS, 2, rows, D), BF16),
            pltpu.SemaphoreType.DMA((CHUNKS, 2)),
            pltpu.SemaphoreType.DMA((CHUNKS, copies)),
            pltpu.SemaphoreType.DMA((CHUNKS, copies)),
            pltpu.SemaphoreType.DMA((2 * small_count + 1,)),
            pltpu.SemaphoreType.DMA((2 * small_count + 1,)),
        ],
        compiler_params=pltpu.CompilerParams(
            collective_id=1, has_side_effects=True, vmem_limit_bytes=VMEM
        ),
        cost_estimate=pl.CostEstimate(
            flops=NMAT * D * D * 4, bytes_accessed=NMAT * D * D * 8, transcendentals=0
        ),
    )(grads, ff_vec, at_vec, stu, cls)


def update_kernel(
    own_ref,
    blocks_ref,
    left_ref,
    right_ref,
    lroot_ref,
    rroot_ref,
    shard_ref,
    vsum_ref,
    vec_ref,
    vmom_ref,
    ssum_ref,
    stu_ref,
    smom_ref,
    csum_ref,
    cls_ref,
    cmom_ref,
    back_ref,
    rows_ref,
    grad_out,
    new_out,
    left_out,
    right_out,
    vg_out,
    vm_out,
    v_out,
    sg_out,
    sm_out,
    s_out,
    cg_out,
    cm_out,
    c_out,
    layer_out,
    *,
    owners,
):
    step = pl.program_id(0)
    row_len = layer_out.shape[1]

    @pl.when(step < rows_ref.shape[1])
    def _():
        arrived = rows_ref[:, step].reshape(row_len, D)
        chunk = min(256, row_len)

        @pl.loop(0, row_len // chunk)
        def _(k):
            at = pl.multiple_of(k * chunk, chunk)
            spot = at + lax.broadcasted_iota(jnp.int32, (chunk, row_len), 0)
            pick = jnp.where(spot == back_ref[pl.ds(step, 1), :], 1.0, 0.0).astype(BF16)
            layer_out[0, pl.ds(at, chunk), :] = nn(pick, arrived).astype(BF16)

    g = own_ref[0]
    grad_out[0] = g.astype(F32)
    left_out[0] = decay_rate * left_ref[0] + (1.0 - decay_rate) * nt(g, g)
    right_out[0] = decay_rate * right_ref[0] + (1.0 - decay_rate) * tn(g, g)
    steered = nn(lroot_ref[0].astype(BF16), g).astype(BF16)
    steered = nn(steered, rroot_ref[0].astype(BF16))
    size = jnp.mean(steered * steered, keepdims=True)
    new_out[0] = blocks_ref[0].astype(F32) - steered * (block_rate * lax.rsqrt(size + 1e-06))

    @pl.when(pl.program_id(0) == 0)
    def _():
        per = NMAT // owners
        mine = vsum_ref[0:per, :]
        for i in range(1, owners):
            mine = jnp.where(shard_ref[0] == i, vsum_ref[i * per : (i + 1) * per, :], mine)

        def rule(grads, old, moment, rate, outs):
            renewed = decay_rate * moment + (1.0 - decay_rate) * grads * grads
            outs[0][...] = grads
            outs[1][...] = renewed
            outs[2][...] = old - rate * grads / (jnp.sqrt(renewed) + 1e-08)

        rule(mine, vec_ref[...], vmom_ref[...], vector_rate, (vg_out, vm_out, v_out))
        rule(
            ssum_ref[0 : stu_ref.shape[0], :],
            stu_ref[...],
            smom_ref[...],
            head_rate,
            (sg_out, sm_out, s_out),
        )
        rule(
            csum_ref[0:CLS, 0 : SW + 1],
            cls_ref[...],
            cmom_ref[...],
            head_rate,
            (cg_out, cm_out, c_out),
        )


def update(own, blocks, left, right, lroot, rroot, shard, vsum, vec, vmom, ssum, stu, smom, csum, cls, cmom, back, arrived):
    per = own.shape[0]
    micro, row_len = back.shape
    mat = pl.BlockSpec((1, D, D), lambda i: (i, 0, 0))
    whole = lambda a: pl.BlockSpec(a.shape, lambda i: (0,) * a.ndim)
    like = lambda a: jax.ShapeDtypeStruct(a.shape, F32)
    return pl.pallas_call(
        functools.partial(update_kernel, owners=NMAT // per),
        grid=(per,),
        in_specs=[mat] * 6
        + [pl.BlockSpec(memory_space=pltpu.SMEM)]
        + [whole(a) for a in (vsum, vec, vmom, ssum, stu, smom, csum, cls, cmom, back, arrived)],
        out_specs=[mat] * 4
        + [whole(a) for a in (vec,) * 3 + (stu,) * 3 + (cls,) * 3]
        + [pl.BlockSpec((1, row_len, D), lambda i: (jnp.minimum(i, micro - 1), 0, 0))],
        out_shape=[like(left)] * 4
        + [like(a) for a in (vec,) * 3 + (stu,) * 3 + (cls,) * 3]
        + [jax.ShapeDtypeStruct((micro, row_len, D), BF16)],
        compiler_params=pltpu.CompilerParams(vmem_limit_bytes=VMEM),
    )(
        own,
        blocks,
        left,
        right,
        lroot,
        rroot,
        shard,
        vsum,
        vec,
        vmom,
        ssum,
        stu,
        smom,
        csum,
        cls,
        cmom,
        back,
        arrived,
    )


def local(
    tokens,
    cotangent,
    lengths,
    exit_layers,
    teacher,
    blocks,
    left_stats,
    right_stats,
    left_root,
    right_root,
    vectors,
    vec_moment,
    student,
    stu_moment,
    classifier,
    cls_moment,
):
    group = lax.axis_size("batch")
    me = lax.axis_index("batch")
    micro, _, row_len, _ = tokens.shape
    slots = row_len // group
    tokens, cotangent = tokens[:, 0], cotangent[:, 0]
    ends = jnp.cumsum(lengths[:, 0], axis=-1, dtype=jnp.int32)
    live = (exit_layers[:, 0] >= LAYER).astype(jnp.int32)
    info = jnp.concatenate([lengths[:, 0], exit_layers[:, 0]], axis=1)
    alive_len = lengths[:, 0] * live
    counts = jnp.sum(alive_len, axis=1, dtype=jnp.int32)
    everyone = lax.all_gather(counts[None, :], "batch", axis=0, tiled=True)
    starts = jnp.cumsum(everyone, axis=0, dtype=jnp.int32) - everyone

    places = jnp.arange(row_len, dtype=jnp.int32)
    before = jnp.cumsum(alive_len, axis=1, dtype=jnp.int32) - alive_len
    sample = jnp.sum((places[None, :, None] >= ends[:, None, : SAMP - 1]).astype(jnp.int32), axis=-1)
    chosen = sample[..., None] == jnp.arange(SAMP, dtype=jnp.int32)
    shift = jnp.sum(jnp.where(chosen, (before - ends + lengths[:, 0])[:, None, :], 0), axis=-1)
    alive_tok = jnp.sum(jnp.where(chosen, live[:, None, :], 0), axis=-1)
    rank = places[None, :] + shift
    send = (starts[me][:, None] + rank) % group * slots + rank // group
    send = jnp.where(alive_tok > 0, send, row_len)
    start_of = jnp.repeat(starts.T, slots, axis=1)
    count_of = jnp.repeat(everyone.T, slots, axis=1)
    turn = (me - start_of) % group + group * (places % slots)[None, :]
    back = jnp.where(turn < count_of, (start_of + turn) // group, row_len)

    grad_outgoing = pick_rows(back[:, :, None], cotangent, group)
    returned = lax.all_to_all(grad_outgoing, "batch", split_axis=0, concat_axis=0, tiled=True)

    matrices = lax.all_gather(blocks, "shard", axis=0, tiled=True)
    vec = lax.all_gather(vectors.astype(BF16), "shard", axis=0, tiled=True).astype(F32)

    q, k, v, o, logs = attend(info, tokens, matrices, vec)
    goals = teacher.reshape(micro * SAMP, CLS)
    classifier, cls_moment = classifier.T, cls_moment.T
    da1, outgoing, ff_grads, ff_vecs, stu_grads, cls_grads = feed(
        info, tokens, o, matrices, vec, student, classifier, goals, send, send.reshape(-1, 1), returned
    )
    arrived = lax.all_to_all(outgoing, "batch", split_axis=0, concat_axis=0, tiled=True)
    input_grads, grads, at_vecs = attend_back(
        info, tokens, da1.reshape(micro, row_len, D), q, k, v, o, logs, matrices, ff_grads
    )
    own, vec_sum, stu_sum, cls_sum = reduce_grads(grads, ff_vecs, at_vecs, stu_grads, cls_grads)
    shard = lax.axis_index("shard").astype(jnp.int32).reshape(1)
    *updated, layer_out = update(
        own,
        blocks,
        left_stats,
        right_stats,
        left_root,
        right_root,
        shard,
        vec_sum,
        vectors,
        vec_moment,
        stu_sum,
        student,
        stu_moment,
        cls_sum,
        classifier,
        cls_moment,
        back,
        arrived,
    )
    classes = [a.T for a in updated[-3:]]
    return (layer_out[:, None], input_grads[:, None], *updated[:-3], *classes)


def solution(mesh):
    rows = P(None, ("batch", "shard"), None, None)
    tags = P(None, ("batch", "shard"), None)
    mats = P("shard", None, None)
    vecs = P("shard", None)
    return jax.shard_map(
        local,
        mesh=mesh,
        in_specs=(rows, rows, tags, tags, rows, mats, mats, mats, mats, mats, vecs, vecs)
        + (P(),) * 4,
        out_specs=(rows, rows, mats, mats, mats, mats, vecs, vecs, vecs) + (P(),) * 6,
        check_vma=False,
    )
```
